32 devices in a mesh: fsdp: 2 (over y), ctx: 8 (over z, x), tp: 2 (over core).
Axes of the slice: x: 2, y: 2, z: 4, core: 2. Of those that a mesh axis runs over, the one named last changes fastest.
Arguments:
- hidden_in: bfloat16 [8192, 2048], P(('fsdp', 'ctx')), may hold values from -6 to 6
- block_order: int32 [2, 16], P('fsdp'), may hold values from 0 to 15, as said below
- attn_norm_gain: bfloat16 [2048], replicated, may hold values from 0.25 to 1.75
- attn_norm_bias: bfloat16 [2048], replicated, may hold values from -1.75 to 1.75
- query_weight: bfloat16 [2048, 2048], P(('fsdp', 'ctx'), 'tp'), may hold values from -0.125 to 0.125
- query_bias: bfloat16 [2048], P('tp'), may hold values from -1.75 to 1.75
- keyval_weight: bfloat16 [2048, 256], P(('fsdp', 'ctx')), may hold values from -0.125 to 0.125
- value_bias: bfloat16 [128], replicated, may hold values from -0.3125 to 0.3125
- proj_weight: bfloat16 [2048, 2048], P(('fsdp', 'ctx'), 'tp'), may hold values from -4 to 4
- proj_bias: bfloat16 [2048], replicated, may hold values from -1.75 to 1.75
- mlp_norm_gain: bfloat16 [2048], replicated, may hold values from 0.25 to 1.75
- mlp_norm_bias: bfloat16 [2048], replicated, may hold values from -1.75 to 1.75
- up_weight: bfloat16 [2048, 8192], P(('fsdp', 'ctx'), 'tp'), may hold values from -0.125 to 0.125
- up_bias: bfloat16 [8192], P('tp'), may hold values from -1.75 to 1.75
- down_weight: bfloat16 [2048, 8192], P(('fsdp', 'ctx'), 'tp'), may hold values from -0.0625 to 0.0625
- down_bias: bfloat16 [2048], replicated, may hold values from -1.75 to 1.75
- out_cotangent: bfloat16 [8192, 2048], P(('fsdp', 'ctx')), may hold values from -8 to 8
Outputs:
- layer_out: bfloat16 [8192, 2048], P(('fsdp', 'ctx'))
- input_grad: bfloat16 [8192, 2048], P(('fsdp', 'ctx'))
- grad_attn_norm_gain: float32 [2048], replicated
- grad_attn_norm_bias: float32 [2048], replicated
- grad_query_weight: float32 [2048, 2048], P(('fsdp', 'ctx'), 'tp')
- grad_query_bias: float32 [2048], P('tp')
- grad_keyval_weight: float32 [2048, 256], P(('fsdp', 'ctx'))
- grad_value_bias: float32 [128], replicated
- grad_proj_weight: float32 [2048, 2048], P(('fsdp', 'ctx'), 'tp')
- grad_proj_bias: float32 [2048], replicated
- grad_mlp_norm_gain: float32 [2048], replicated
- grad_mlp_norm_bias: float32 [2048], replicated
- grad_up_weight: float32 [2048, 8192], P(('fsdp', 'ctx'), 'tp')
- grad_up_bias: float32 [8192], P('tp')
- grad_down_weight: float32 [2048, 8192], P(('fsdp', 'ctx'), 'tp')
- grad_down_bias: float32 [2048], replicated
The draws below stay inside these ranges and needn't reach their ends.
Inputs may be any that keep to these rules, and one draw needn't show every extreme that they name: `block_order`: each row is a permutation of the 16 block numbers. In each row the first, the middle (8) and the last slot hold prompt blocks of one group.
All inputs are finite; a program needn't handle non-finite values.
Results may differ from the reference program's by a relative error of at most 0.012.
Values may be sent and summed in bfloat16 or wider, within the bound.
A program may use at most 256 MiB of HBM per device.

```python
import jax
import jax.numpy as jnp
from jax import lax

D = 2048
H = 16
HD = 128
FF = 8192
BLK = 256
PBLK = 8
CONTS = 8
BPD = 2
TOKENS = 8192
N_FSDP = 2
N_CTX = 8


def draw_block_order(key, part):
    key = jax.random.fold_in(key, 11)
    slot_count = N_CTX * BPD
    group_blocks = PBLK + CONTS
    group_total = slot_count // group_blocks
    targets = (0, slot_count // 2, slot_count - 1)

    def one_row(row_key):
        perm_key, group_key, choose_key = jax.random.split(row_key, 3)
        ordering = jax.random.permutation(perm_key, slot_count).astype(jnp.int32)
        chosen = jax.random.randint(group_key, (), 0, group_total).astype(jnp.int32)
        prompt_pick = jax.random.permutation(choose_key, PBLK).astype(jnp.int32)
        slot_ids = jnp.arange(slot_count, dtype=jnp.int32)
        for number in range(3):
            wanted = chosen * group_blocks + prompt_pick[number]
            where_now = jnp.argmax(ordering == wanted)
            current = ordering[targets[number]]
            ordering = jnp.where(slot_ids == where_now, current, ordering)
            ordering = ordering.at[targets[number]].set(wanted)
        return ordering
    row_keys = jax.random.split(key, N_FSDP)
    return jax.vmap(one_row)(row_keys).astype(jnp.int32)


def raised(values, own_key, source, target, shards_of, factor):
    def block_of(axis_at):
        return (jnp.arange(values.shape[axis_at]) // (values.shape[axis_at] // shards_of)).reshape((-1,) + (1,) * (values.ndim - 1 - axis_at))

    near = jax.random.permutation(own_key, shards_of)[block_of(target)]
    other_side = (block_of(target) + shards_of // 2) % shards_of
    return jnp.where((block_of(source) == near) | (block_of(source) == other_side), factor * values, values)


def steps_of(own_key, shape, pieces, least, top_value):
    gain, own = 1.0, jax.random.fold_in(own_key, 6)
    for dim, shards_of in pieces:
        heights = jnp.exp(jax.random.uniform(jax.random.fold_in(own, dim), (shards_of,), jnp.float32, least / len(pieces), top_value / len(pieces)))
        gain = gain * jnp.repeat(heights, shape[dim] // shards_of).reshape([-1 if axis == dim else 1 for axis in range(len(shape))])
    return gain


def gaussian(stream_key, shape, width, limit, cuts=(), held_as=jnp.bfloat16):
    drawn = jax.random.normal(stream_key, shape, jnp.float32) * width
    if len(cuts) > 0:
        drawn = steps_of(stream_key, shape, cuts, -0.22, 0.18) * drawn
    return jnp.clip(drawn, min=-limit, max=limit).astype(held_as)


def gaussian_with(key, extent, scale, most, cuts, heavy, kind=jnp.bfloat16):
    array = scale * jax.random.normal(key, extent, jnp.float32)
    if cuts:
        array = array * steps_of(key, extent, cuts, -0.22, 0.18)
    return jnp.clip(raised(array, jax.random.fold_in(key, 3), *heavy), -most, most).astype(kind)


def setup_inputs(seed: int = 0) -> dict:
    keys = jax.random.split(jax.random.key(seed), 18)
    hidden_in = gaussian(keys[0], (TOKENS, D), 1.0, 6.0, ((0, 16),))
    block_order = draw_block_order(jax.random.fold_in(keys[17], 71), 0)
    attn_norm_gain = jnp.clip(1.0 + 0.15 * jax.random.normal(keys[2], (D,), jnp.float32), 0.25, 1.75).astype(jnp.bfloat16)
    attn_norm_bias = gaussian(keys[3], (D,), 0.3, 1.75)
    query_weight = gaussian(keys[4], (D, D), D ** -0.5, 0.125, ((0, 16), (1, 2)))
    query_bias = gaussian(keys[5], (D,), 0.3, 1.75, ((0, 2),))
    keyval_weight = gaussian(keys[6], (D, 2 * HD), D ** -0.5, 0.125, ((0, 16),))
    value_bias = gaussian(keys[7], (HD,), 0.05, 0.3125)
    proj_weight = gaussian(keys[8], (D, D), (D * 2 // (PBLK * BLK)) ** -0.5, 4.0, ((0, 16), (1, 2)))
    proj_bias = gaussian(keys[9], (D,), 0.3, 1.75)
    mlp_norm_gain = jnp.clip(1.0 + 0.15 * jax.random.normal(keys[10], (D,), jnp.float32), 0.25, 1.75).astype(jnp.bfloat16)
    mlp_norm_bias = gaussian(keys[11], (D,), 0.3, 1.75)
    up_weight = gaussian(keys[12], (D, FF), D ** -0.5, 0.125, ((0, 16), (1, 2)))
    up_bias = gaussian(keys[13], (FF,), 0.3, 1.75, ((0, 2),))
    down_weight = gaussian(keys[14], (D, FF), FF ** -0.5, 0.0625, ((0, 16), (1, 2)))
    down_bias = gaussian(keys[15], (D,), 0.3, 1.75)
    out_cotangent = gaussian_with(keys[16], (TOKENS, D), 1.0, 8.0, ((0, 16),), (0, 1, 16, 2.0))
    return dict(hidden_in=hidden_in, block_order=block_order, attn_norm_gain=attn_norm_gain, attn_norm_bias=attn_norm_bias, query_weight=query_weight, query_bias=query_bias, keyval_weight=keyval_weight, value_bias=value_bias, proj_weight=proj_weight, proj_bias=proj_bias, mlp_norm_gain=mlp_norm_gain, mlp_norm_bias=mlp_norm_bias, up_weight=up_weight, up_bias=up_bias, down_weight=down_weight, down_bias=down_bias, out_cotangent=out_cotangent)


EPSILON = 1e-05
MASKED = -1e+30
HIGHEST = lax.Precision.HIGHEST

@jax.custom_vjp
def low(v):
    return lax.optimization_barrier(v.astype(jnp.bfloat16)).astype(jnp.float32)

@jax.custom_vjp
def low_back(v):
    return v

def low_keep(v):
    return (low(v), None)

def low_pass(kept, grad):
    return (grad,)

def back_keep(v):
    return (v, None)

def back_low(kept, grad):
    return (low(grad),)
low.defvjp(low_keep, low_pass)
low_back.defvjp(back_keep, back_low)

def layer_norm(values, norm_gain, norm_shift):
    average = lax.optimization_barrier(jnp.mean(values, axis=-1, keepdims=True))
    centered = values - average
    spread = lax.optimization_barrier(jnp.mean(centered * centered, axis=-1, keepdims=True))
    return centered * lax.rsqrt(spread + EPSILON) * norm_gain + norm_shift

def gelu_tanh(values):
    return jax.nn.gelu(values, approximate=True)

def visible_group(position, key_count):
    prompt_len = PBLK * BLK
    key_index = lax.broadcasted_iota(jnp.int32, (BLK, key_count), 1)
    query_index = lax.broadcasted_iota(jnp.int32, (BLK, key_count), 0)
    key_block = key_index // BLK
    key_pos = jnp.where(key_block < PBLK, key_index, prompt_len + key_index % BLK)
    query_pos = jnp.where(position < PBLK, position * BLK + query_index, prompt_len + query_index)
    same_place = (key_block < PBLK) | (key_block == position)
    return (key_pos <= query_pos) & same_place

def group_layer(params, stream):
    gain_one, shift_one, query_weight, query_bias, keyval_weight, value_bias, proj_weight, proj_bias, gain_two, shift_two, up_weight, up_bias, down_weight, down_bias = params
    token_count = stream.shape[0]
    normed_one = low(layer_norm(stream, gain_one, shift_one))
    query_rows = low(low_back(jnp.dot(normed_one, query_weight, precision=HIGHEST) + query_bias))
    value_shift = jnp.concatenate([jnp.zeros_like(value_bias), value_bias])
    keyval = low(low_back(jnp.dot(normed_one, keyval_weight, precision=HIGHEST) + value_shift))
    key_rows = keyval[:, :HD]
    value_rows = keyval[:, HD:]
    queries = query_rows.reshape(PBLK + CONTS, BLK, H, HD)

    def attend_one(inputs):
        block_query, position = inputs
        raw_scores = jnp.einsum('qhd,kd->hqk', block_query, key_rows, precision=HIGHEST)
        scores = low_back(raw_scores * HD ** (-0.5))
        allowed = visible_group(position, token_count)
        masked = jnp.where(allowed[None], scores, MASKED)
        largest = lax.optimization_barrier(jnp.max(masked, axis=-1, keepdims=True))
        exponent = jnp.exp(masked - largest)
        attention = exponent / lax.optimization_barrier(jnp.sum(exponent, axis=-1, keepdims=True))
        return jnp.einsum('hqk,kd->qhd', low(attention), value_rows, precision=HIGHEST)
    mixed_heads = lax.map(jax.checkpoint(attend_one), (queries, jnp.arange(PBLK + CONTS, dtype=jnp.int32)))
    mixed_heads = low(low_back(mixed_heads.reshape(token_count, H * HD)))
    attn_out = low_back(jnp.dot(mixed_heads, proj_weight.T, precision=HIGHEST) + proj_bias)
    middle = stream + attn_out
    normed_two = low(layer_norm(middle, gain_two, shift_two))
    pre_act = low_back(jnp.dot(normed_two, up_weight, precision=HIGHEST) + up_bias)
    activation = low(gelu_tanh(pre_act))
    return middle + low_back(jnp.dot(activation, down_weight.T, precision=HIGHEST) + down_bias)

def pick_rows(row_blocks, row_index):
    return jnp.take(row_blocks, row_index.astype(jnp.int32), axis=0)

def reference(hidden_in, block_order, attn_norm_gain, attn_norm_bias, query_weight, query_bias, keyval_weight, value_bias, proj_weight, proj_bias, mlp_norm_gain, mlp_norm_bias, up_weight, up_bias, down_weight, down_bias, out_cotangent):
    slot_count = N_CTX * BPD
    group_blocks = PBLK + CONTS
    inverse = jnp.argsort(block_order, axis=1).astype(jnp.int32)
    float_args = tuple((member.astype(jnp.float32) for member in (hidden_in, attn_norm_gain, attn_norm_bias, query_weight, query_bias, keyval_weight, value_bias, proj_weight, proj_bias, mlp_norm_gain, mlp_norm_bias, up_weight, up_bias, down_weight, down_bias)))

    def forward(stream, *params):
        blocks = stream.reshape(N_FSDP, slot_count, BLK, D)
        logical = jax.vmap(pick_rows)(blocks, inverse)
        grouped = logical.reshape(N_FSDP * slot_count // group_blocks, group_blocks * BLK, D)

        def one_group(carry_over, group_rows):
            return (carry_over, group_layer(params, group_rows))
        outputs = lax.scan(jax.checkpoint(one_group), jnp.zeros((), stream.dtype), grouped)[1]
        outputs = outputs.reshape(N_FSDP, slot_count, BLK, D)
        physical = jax.vmap(pick_rows)(outputs, block_order)
        return physical.reshape(N_FSDP * slot_count * BLK, D)
    layer_out, pullback = jax.vjp(forward, *float_args)
    grads = pullback(out_cotangent.astype(jnp.float32))
    return (layer_out.astype(jnp.bfloat16), grads[0].astype(jnp.bfloat16), grads[1], grads[2], grads[3], grads[4], grads[5], grads[6], grads[7], grads[8], grads[9], grads[10], grads[11], grads[12], grads[13], grads[14])
```

```python
import jax
import jax.numpy as jnp
from jax import lax
from jax.sharding import Mesh, PartitionSpec as P

HD = 128
BLK = 256
PBLK = 8
CONTS = 8
EPSILON = 1e-05
MASKED = -1e30
F32 = jnp.float32
BF16 = jnp.bfloat16
ROWS = ("fsdp", "line", "pair")
PLANE = ("fsdp", "pair")
CTX = ("line", "pair")
EVERY = ("fsdp", "line", "pair", "tp")


def layer_norm(values, norm_gain, norm_shift):
    average = jnp.mean(values, axis=-1, keepdims=True)
    centered = values - average
    spread = jnp.mean(centered * centered, axis=-1, keepdims=True)
    return centered * lax.rsqrt(spread + EPSILON) * norm_gain + norm_shift


def gelu_tanh(values):
    return jax.nn.gelu(values, approximate=True)


def visible_mask(position, query_rows, key_count):
    prompt_len = PBLK * BLK
    key_index = lax.broadcasted_iota(jnp.int32, (query_rows, key_count), 1)
    query_index = lax.broadcasted_iota(jnp.int32, (query_rows, key_count), 0)
    key_block = key_index // BLK
    key_pos = jnp.where(key_block < PBLK, key_index, prompt_len + key_index % BLK)
    is_prompt = position < PBLK
    query_pos = jnp.where(is_prompt, position * BLK + query_index, prompt_len + query_index)
    own_slot = key_block == PBLK
    return (key_pos <= query_pos) & jnp.logical_not(is_prompt & own_slot)


def attend_block(inputs):
    queries, keyset, position = inputs
    head_size = queries.shape[-1]
    key_part = keyset[:, :head_size]
    value_part = keyset[:, head_size:]
    scores = jnp.einsum(
        "hqd,kd->hqk", queries, key_part, preferred_element_type=jnp.float32
    ) * head_size ** (-0.5)
    allowed = visible_mask(position, queries.shape[1], key_part.shape[0])
    masked = jnp.where(allowed[None], scores, MASKED)
    largest = jnp.max(masked, axis=-1, keepdims=True)
    exponent = jnp.exp(masked - largest)
    row_total = jnp.sum(exponent, axis=-1, keepdims=True)
    attention = (exponent / row_total).astype(jnp.bfloat16)
    mixed = jnp.einsum("hqk,kd->hqd", attention, value_part, preferred_element_type=jnp.float32)
    return (mixed, (largest + jnp.log(row_total))[..., 0])


def attend_back(inputs):
    queries, keyset, position, logsum, grad_mixed = inputs
    head_size = queries.shape[-1]
    scale = head_size ** (-0.5)
    key_part = keyset[:, :head_size]
    value_part = keyset[:, head_size:]
    scores = (
        jnp.einsum("hqd,kd->hqk", queries, key_part, preferred_element_type=jnp.float32) * scale
    )
    allowed = visible_mask(position, queries.shape[1], key_part.shape[0])
    attention = jnp.where(allowed[None], jnp.exp(scores - logsum[..., None]), 0.0)
    grad_probs = jnp.einsum(
        "hqd,kd->hqk", grad_mixed, value_part, preferred_element_type=jnp.float32
    )
    inner = jnp.sum(grad_probs * attention, axis=-1, keepdims=True)
    grad_scores = (attention * (grad_probs - inner)).astype(jnp.bfloat16)
    grad_queries = (
        jnp.einsum("hqk,kd->hqd", grad_scores, key_part, preferred_element_type=jnp.float32) * scale
    )
    grad_keys = (
        jnp.einsum("hqk,hqd->kd", grad_scores, queries, preferred_element_type=jnp.float32) * scale
    )
    grad_values = jnp.einsum(
        "hqk,hqd->kd",
        attention.astype(jnp.bfloat16),
        grad_mixed,
        preferred_element_type=jnp.float32,
    )
    return (grad_queries, jnp.concatenate([grad_keys, grad_values], axis=1))


def swap_tp(values):
    return lax.ppermute(values, "tp", [(0, 1), (1, 0)])


def gather_rows(values):
    return lax.all_gather(values, ROWS, axis=0, tiled=True)


def sum_rows(values):
    return lax.psum_scatter(values.astype(BF16), ROWS, scatter_dimension=0, tiled=True).astype(F32)


def gather_plane(values):
    return lax.all_gather(values, PLANE + ("tp",), axis=0, tiled=True)


def sum_plane(values):
    return lax.psum_scatter(values, PLANE + ("tp",), scatter_dimension=0, tiled=True).astype(F32)


def spread_columns(values):
    quarters = lax.axis_size("fsdp") * lax.axis_size("pair")
    rows, columns = values.shape
    cut = values.reshape(rows, quarters, columns // quarters).transpose(1, 0, 2)
    return lax.all_to_all(cut, PLANE, split_axis=0, concat_axis=0, tiled=True)


def collect_columns(values):
    quarters, rows, columns = values.shape
    back = lax.all_to_all(values, PLANE, split_axis=0, concat_axis=0, tiled=True)
    return back.transpose(1, 0, 2).reshape(rows, quarters * columns)


def gather_line(values):
    lines = lax.axis_size("line")
    quarters, rows, columns = values.shape
    fsdp = lax.axis_size("fsdp")
    every = lax.all_gather(values, "line", axis=0, tiled=False)
    every = every.reshape(lines, fsdp, quarters // fsdp, rows, columns).transpose(1, 0, 2, 3, 4)
    return every.reshape(lines * quarters * rows, columns)


def sum_line(values):
    lines, fsdp, pair = lax.axis_size("line"), lax.axis_size("fsdp"), lax.axis_size("pair")
    total, columns = values.shape
    rows = total // (lines * fsdp * pair)
    ordered = values.reshape(fsdp, lines, pair, rows, columns).transpose(1, 0, 2, 3, 4)
    ordered = ordered.reshape(total, columns).astype(BF16)
    summed = lax.psum_scatter(ordered, "line", scatter_dimension=0, tiled=True)
    return summed.reshape(fsdp * pair, rows, columns)


def gather_ctx(values):
    return lax.all_gather(values, CTX, axis=0, tiled=True)


def sum_ctx(values):
    return lax.psum_scatter(values, CTX, scatter_dimension=0, tiled=True).astype(F32)


def body(
    hidden_in,
    block_order,
    attn_norm_gain,
    attn_norm_bias,
    query_weight,
    query_bias,
    keyval_weight,
    value_bias,
    proj_weight,
    proj_bias,
    mlp_norm_gain,
    mlp_norm_bias,
    up_weight,
    up_bias,
    down_weight,
    down_bias,
    out_cotangent,
):
    rows_dev = hidden_in.shape[0]
    half_rows = rows_dev // 2
    width = hidden_in.shape[1]
    blocks_dev = rows_dev // BLK
    slot_count = block_order.shape[1]
    group_blocks = PBLK + CONTS
    heads_dev = query_bias.shape[0] // HD
    head_width = heads_dev * HD
    core = lax.axis_index("tp")
    quarter = lax.axis_index("fsdp") * lax.axis_size("pair") + lax.axis_index("pair")
    quarters = lax.axis_size("fsdp") * lax.axis_size("pair")
    hidden_dev = up_weight.shape[1] // quarters

    def own_half(values):
        return lax.dynamic_slice_in_dim(values, core * half_rows, half_rows, axis=0)

    def other_half(values):
        return lax.dynamic_slice_in_dim(values, (1 - core) * half_rows, half_rows, axis=0)

    def in_order(mine, other, axis=0):
        first = jnp.where(core == 0, mine, other)
        second = jnp.where(core == 0, other, mine)
        return jnp.concatenate([first, second], axis=axis)

    def sum_halves(values):
        return own_half(values) + swap_tp(other_half(values))

    def join_halves(values):
        return in_order(values, swap_tp(values))

    gain_one = attn_norm_gain.astype(F32)
    shift_one = attn_norm_bias.astype(F32)
    gain_two = mlp_norm_gain.astype(F32)
    shift_two = mlp_norm_bias.astype(F32)

    slot_ids = jnp.arange(slot_count, dtype=jnp.int32)
    ordering = block_order[0]
    inverse = jnp.sum(
        jnp.where(ordering[None, :] == slot_ids[:, None], slot_ids[None, :], 0), axis=1
    )
    ctx_index = lax.axis_index("line") * lax.axis_size("pair") + lax.axis_index("pair")
    first_slot = ctx_index * blocks_dev
    my_slots = first_slot + jnp.arange(blocks_dev, dtype=jnp.int32)
    my_blocks = lax.dynamic_slice_in_dim(ordering, first_slot, blocks_dev)
    positions = my_blocks % group_blocks
    group_base = my_blocks // group_blocks * group_blocks
    prompt_slots = jnp.take(
        inverse, group_base[:, None] + jnp.arange(PBLK, dtype=jnp.int32)[None, :]
    )
    key_slots = jnp.concatenate([prompt_slots, my_slots[:, None]], axis=1)

    keyval_cut = lax.dynamic_slice_in_dim(keyval_weight, core * HD, HD, axis=1)
    first_all = gather_rows(jnp.concatenate([query_weight, keyval_cut], axis=1))
    proj_all = gather_rows(proj_weight)
    down_all = gather_line(spread_columns(down_weight))
    up_all = gather_line(spread_columns(up_weight))

    stream = hidden_in.astype(F32)
    normed_one = layer_norm(stream, gain_one, shift_one).astype(BF16)
    value_shift = jnp.where(core == 1, value_bias.astype(F32), 0.0)
    first_shift = jnp.concatenate([query_bias.astype(F32), value_shift])
    first_low = (jnp.dot(normed_one, first_all, preferred_element_type=F32) + first_shift).astype(
        BF16
    )
    query_low = first_low[:, :head_width]
    part_low = first_low[:, head_width:]
    part_every = gather_ctx(part_low)
    keyval_every = in_order(part_every, swap_tp(part_every), axis=1)
    keyval_low = in_order(part_low, swap_tp(part_low), axis=1)
    keyval_table = keyval_every.reshape(slot_count, BLK, 2 * HD)
    own_table = keyval_low.reshape(blocks_dev, 1, BLK, 2 * HD)
    keysets = jnp.concatenate([keyval_table[prompt_slots], own_table], axis=1)
    keysets = keysets.reshape(blocks_dev, (PBLK + 1) * BLK, 2 * HD)
    queries = query_low.reshape(blocks_dev, BLK, heads_dev, HD).transpose(0, 2, 1, 3)
    mixed, logsums = lax.map(attend_block, (queries, keysets, positions))
    mixed_low = mixed.transpose(0, 2, 1, 3).reshape(rows_dev, head_width).astype(BF16)
    proj_part = jnp.einsum("rk,ok->ro", mixed_low, proj_all, preferred_element_type=F32)
    middle = own_half(stream) + sum_halves(proj_part) + proj_bias.astype(F32)

    normed_two = layer_norm(middle, gain_two, shift_two).astype(BF16)
    cotangent = own_half(out_cotangent)
    cotangent_all = gather_plane(cotangent)
    normed_two_all = gather_plane(normed_two)
    up_shift = lax.dynamic_slice_in_dim(up_bias, quarter * hidden_dev, hidden_dev).astype(F32)
    grad_act = jnp.dot(cotangent_all, down_all, preferred_element_type=F32)
    pre_act = jnp.dot(normed_two_all, up_all, preferred_element_type=F32) + up_shift
    act, gelu_pull = jax.vjp(gelu_tanh, pre_act)
    act_low = act.astype(BF16)
    grad_pre_wide = gelu_pull(grad_act)[0]
    grad_pre = grad_pre_wide.astype(BF16)
    normed_two_part = jnp.einsum("rf,df->rd", grad_pre, up_all, preferred_element_type=F32)
    grad_normed_two = sum_plane(normed_two_part.astype(BF16))
    down_part = jnp.einsum("rf,of->ro", act_low, down_all, preferred_element_type=F32)
    mlp_out = sum_plane(down_part.astype(BF16)) + down_bias.astype(F32)
    layer_out = join_halves((middle + mlp_out).astype(BF16))
    grad_up_bias = jnp.sum(grad_pre, axis=0, dtype=F32)
    down_weight_grad = jnp.einsum("ro,rf->of", cotangent_all, act_low, preferred_element_type=F32)
    up_weight_grad = jnp.einsum("rd,rf->df", normed_two_all, grad_pre, preferred_element_type=F32)
    grad_down_weight = collect_columns(sum_line(down_weight_grad)).astype(F32)
    grad_up_weight = collect_columns(sum_line(up_weight_grad)).astype(F32)

    norm_two_pull = jax.vjp(layer_norm, middle, gain_two, shift_two)[1]
    grad_mid_norm, grad_mlp_norm_gain, grad_mlp_norm_bias = norm_two_pull(grad_normed_two)
    grad_middle = cotangent.astype(F32) + grad_mid_norm
    grad_down_bias = jnp.sum(cotangent, axis=0, dtype=F32)

    grad_attn_half = grad_middle.astype(BF16)
    grad_proj_bias = jnp.sum(grad_attn_half, axis=0, dtype=F32)
    grad_attn = join_halves(grad_attn_half)
    proj_weight_grad = jnp.einsum("ro,rk->ok", grad_attn, mixed_low, preferred_element_type=F32)
    grad_proj_weight = sum_rows(proj_weight_grad)
    grad_mixed = jnp.einsum("ro,ok->rk", grad_attn, proj_all, preferred_element_type=F32).astype(
        BF16
    )
    grad_mixed_heads = grad_mixed.reshape(blocks_dev, BLK, heads_dev, HD).transpose(0, 2, 1, 3)
    grad_queries, grad_keysets = lax.map(
        attend_back, (queries, keysets, positions, logsums, grad_mixed_heads)
    )
    grad_query = grad_queries.transpose(0, 2, 1, 3).reshape(rows_dev, head_width).astype(BF16)
    grad_query_bias = jnp.sum(grad_query, axis=0, dtype=F32)
    keyset_terms = grad_keysets.reshape(blocks_dev, PBLK + 1, BLK * 2 * HD)
    target_hits = (key_slots[:, :, None] == slot_ids[None, None, :]).astype(F32)
    spread_back = jnp.einsum(
        "bts,btc->sc",
        target_hits,
        keyset_terms,
        precision=lax.Precision.HIGHEST,
        preferred_element_type=F32,
    ).reshape(slot_count * BLK, 2 * HD)
    own_part = lax.dynamic_slice_in_dim(spread_back, core * HD, HD, axis=1)
    other_part = lax.dynamic_slice_in_dim(spread_back, (1 - core) * HD, HD, axis=1)
    part_sum = (own_part + swap_tp(other_part)).astype(BF16)
    grad_part = sum_ctx(part_sum).astype(BF16)
    grad_value_bias = jnp.where(core == 1, jnp.sum(grad_part, axis=0, dtype=F32), 0.0)
    grad_first = jnp.concatenate([grad_query, grad_part], axis=1)
    normed_one_part = jnp.einsum("rk,dk->rd", grad_first, first_all, preferred_element_type=F32)
    grad_normed_one = sum_halves(normed_one_part)
    first_weight_grad = jnp.einsum("rd,rk->dk", normed_one, grad_first, preferred_element_type=F32)
    grad_first_weight = sum_rows(first_weight_grad)
    grad_query_weight = grad_first_weight[:, :head_width]
    grad_cut = grad_first_weight[:, head_width:]
    grad_keyval_weight = in_order(grad_cut, swap_tp(grad_cut), axis=1)
    norm_one_pull = jax.vjp(layer_norm, own_half(stream), gain_one, shift_one)[1]
    grad_in_norm, grad_attn_norm_gain, grad_attn_norm_bias = norm_one_pull(grad_normed_one)
    input_grad = join_halves((grad_middle + grad_in_norm).astype(BF16))

    query_slots = jnp.zeros((2 * head_width,), F32)
    query_slots = lax.dynamic_update_slice_in_dim(
        query_slots, grad_query_bias, core * head_width, axis=0
    )
    hidden_slots = jnp.zeros((2 * quarters * hidden_dev,), F32)
    hidden_slots = lax.dynamic_update_slice_in_dim(
        hidden_slots, grad_up_bias, (core * quarters + quarter) * hidden_dev, axis=0
    )
    pieces = [
        grad_attn_norm_gain,
        grad_attn_norm_bias,
        grad_proj_bias,
        grad_mlp_norm_gain,
        grad_mlp_norm_bias,
        grad_down_bias,
        grad_value_bias,
        query_slots,
        hidden_slots,
    ]
    summed = lax.psum(jnp.concatenate(pieces), EVERY)
    cuts, start = [], 0
    for piece in pieces:
        cuts.append(summed[start : start + piece.shape[0]])
        start += piece.shape[0]
    sum_query = lax.dynamic_slice_in_dim(cuts[7], core * head_width, head_width)
    sum_up = lax.dynamic_slice_in_dim(cuts[8], core * quarters * hidden_dev, quarters * hidden_dev)
    return (
        layer_out,
        input_grad,
        cuts[0],
        cuts[1],
        grad_query_weight,
        sum_query,
        grad_keyval_weight,
        cuts[6],
        grad_proj_weight,
        cuts[2],
        cuts[3],
        cuts[4],
        grad_up_weight,
        sum_up,
        grad_down_weight,
        cuts[5],
    )


def solution(mesh):
    fsdp, ctx, tp = mesh.devices.shape
    grid = Mesh(mesh.devices.reshape(fsdp, ctx // 2, 2, tp), EVERY)
    by_rows = P(ROWS, None)
    by_both = P(ROWS, "tp")
    return jax.shard_map(
        body,
        mesh=grid,
        in_specs=(
            by_rows,
            P("fsdp", None),
            P(),
            P(),
            by_both,
            P("tp"),
            by_rows,
            P(),
            by_both,
            P(),
            P(),
            P(),
            by_both,
            P("tp"),
            by_both,
            P(),
            by_rows,
        ),
        out_specs=(
            by_rows,
            by_rows,
            P(),
            P(),
            by_both,
            P("tp"),
            by_rows,
            P(),
            by_both,
            P(),
            P(),
            P(),
            by_both,
            P("tp"),
            by_both,
            P(),
        ),
        check_vma=False,
    )
```

```python
import functools

import jax
import jax.numpy as jnp
from jax import lax
from jax.experimental import pallas as pl
from jax.experimental.pallas import tpu as pltpu
from jax.sharding import Mesh, PartitionSpec as P

HD = 128
BLK = 256
PBLK = 8
CONTS = 8
EPSILON = 1e-05
MASKED = -1e30
F32 = jnp.float32
BF16 = jnp.bfloat16
ROWS = ("fsdp", "line", "pair")
EVERY = ("fsdp", "line", "pair", "tp")


def layer_norm(values, norm_gain, norm_shift):
    average = jnp.mean(values, axis=-1, keepdims=True)
    centered = values - average
    spread = jnp.mean(centered * centered, axis=-1, keepdims=True)
    return centered * lax.rsqrt(spread + EPSILON) * norm_gain + norm_shift


def gelu_tanh(values):
    return jax.nn.gelu(values, approximate=True)


MESH_ID = pl.DeviceIdType.MESH
VMEM_BYTES = 56 * 1024 * 1024
SIDE = ("pair", "fsdp")
FRONT = ("fsdp", "pair")


def here():
    return {name: lax.axis_index(name) for name in EVERY}


def flip(place, step):
    place = dict(place)
    if isinstance(step, str):
        place[step] = 1 - place[step]
    else:
        core = place["tp"]
        for name, used in ((step[0], 1 - core), (step[1], core)):
            place[name] = place[name] + (1 - 2 * place[name]) * used
    return place


def along(place, amount):
    return dict(place, line=place["line"] + amount)


def greet(me, steps, lines):
    barrier = pltpu.get_barrier_semaphore()
    for step in steps:
        pl.semaphore_signal(barrier, inc=1, device_id=flip(me, step), device_id_type=MESH_ID)
    count = len(steps)
    if lines > 1:
        for amount in (-1, 1):
            there = me["line"] + amount
            inside = (there >= 0) & (there < lines)

            @pl.when(inside)
            def _():
                pl.semaphore_signal(
                    barrier, inc=1, device_id=along(me, amount), device_id_type=MESH_ID
                )

            count = count + inside.astype(jnp.int32)
    pl.semaphore_wait(barrier, count)


def remote(source, target, send_sem, recv_sem, place):
    return pltpu.make_async_remote_copy(
        src_ref=source,
        dst_ref=target,
        send_sem=send_sem,
        recv_sem=recv_sem,
        device_id=place,
        device_id_type=MESH_ID,
    )


def top_bit(bits):
    return bits.bit_length() - 1


def gather_kernel(steps, lines, slot, x_ref, out_ref, own_sem, line_send, line_recv, send, recv):
    me = here()
    count = len(steps)
    my_line = me["line"] if lines > 1 else 0

    def origin(bits, shard):
        place = me
        for k in reversed(range(count)):
            if bits >> k & 1:
                place = flip(place, steps[k])
        return dict(place, line=shard)

    def block(bits, shard):
        return slot(out_ref, origin(bits, shard))

    def to_step(k, bits, shard, source):
        return remote(
            source,
            block(bits, shard),
            send.at[shard, k * (1 << count) + bits],
            recv.at[shard, bits | 1 << k],
            flip(me, steps[k]),
        )

    def to_line(amount, shard, source):
        return remote(
            source,
            block(0, shard),
            line_send.at[(amount + 1) // 2, shard],
            line_recv.at[shard],
            along(me, amount),
        )

    def arrived(bits, shard):
        remote(
            block(bits, shard),
            block(bits, shard),
            send.at[shard, 0],
            recv.at[shard, bits],
            me,
        ).wait_recv()

    def send_on(bits, shard, source):
        for k in range(top_bit(bits) + 1, count):
            to_step(k, bits, shard, source).start()

    def at_distance(distance, work):
        if distance == 0:
            work(my_line, 0)
            return
        for amount in (1, -1):
            shard = my_line - amount * distance
            pl.when((shard >= 0) & (shard < lines))(functools.partial(work, shard, amount))

    def line_inside(amount):
        there = my_line + amount
        return (there >= 0) & (there < lines)

    greet(me, steps, lines)
    own = pltpu.make_async_copy(x_ref, block(0, my_line), own_sem)
    own.start()
    if lines > 1:
        for amount in (1, -1):
            pl.when(line_inside(amount))(
                lambda amount=amount: to_line(amount, my_line, x_ref).start()
            )
    send_on(0, my_line, x_ref)

    def line_arrival(shard, amount):
        remote(
            block(0, shard), block(0, shard), line_send.at[0, shard], line_recv.at[shard], me
        ).wait_recv()
        pl.when(line_inside(amount))(lambda: to_line(amount, shard, block(0, shard)).start())
        send_on(0, shard, block(0, shard))

    def level_arrival(level, shard, amount):
        del amount
        for bits in range(1 << level, 2 << level):
            arrived(bits, shard)
            send_on(bits, shard, block(bits, shard))

    for tick in range(1, lines + count):
        if tick < lines:
            at_distance(tick, line_arrival)
        for level in range(count):
            distance = tick - 1 - level
            if 0 <= distance < lines:
                at_distance(distance, functools.partial(level_arrival, level))

    own.wait()
    if lines > 1:
        for amount in (1, -1):
            for distance in range(lines):
                shard = my_line - amount * distance
                pl.when((shard >= 0) & (shard < lines) & line_inside(amount))(
                    lambda amount=amount, shard=shard: to_line(
                        amount, shard, block(0, shard)
                    ).wait_send()
                )
    for shard in range(lines):
        for bits in range(1 << count):
            for k in range(top_bit(bits) + 1, count):
                to_step(k, bits, shard, block(bits, shard)).wait_send()


def gather(values, steps, lines, shape, slot, number):
    parts = 1 << len(steps)
    return pl.pallas_call(
        functools.partial(gather_kernel, steps, lines, slot),
        out_shape=jax.ShapeDtypeStruct(shape, values.dtype),
        in_specs=[pl.BlockSpec(memory_space=pl.ANY)],
        out_specs=pl.BlockSpec(memory_space=pl.ANY),
        scratch_shapes=[
            pltpu.SemaphoreType.DMA(()),
            pltpu.SemaphoreType.DMA((2, lines)),
            pltpu.SemaphoreType.DMA((lines,)),
            pltpu.SemaphoreType.DMA((lines, len(steps) * parts)),
            pltpu.SemaphoreType.DMA((lines, parts)),
        ],
        compiler_params=pltpu.CompilerParams(collective_id=number, has_side_effects=True),
    )(values)


def add_blocks(target, first, second, rows):
    tile = min(rows, 64)

    def one(index, carry):
        cut = pl.ds(pl.multiple_of(index * tile, tile), tile)
        total = first(cut).astype(F32) + second(cut).astype(F32)
        target[cut, :] = total.astype(target.dtype)
        return carry

    lax.fori_loop(0, rows // tile, one, 0)


def sum_kernel(steps, lines, rows, read, x_ref, slot, out_ref, held, on_line, sems):
    send, recv, line_send, line_recv = sems
    me = here()
    count = len(steps)
    my_line = me["line"] if lines > 1 else 0

    def target_of(bits, shard):
        place = me
        for k in range(count):
            if bits >> k & 1:
                place = flip(place, steps[k])
        return dict(place, line=shard)

    def store(k, shard, bits):
        return held[k].at[shard, bits >> (k + 1)]

    def copy(k, shard, bits):
        source = slot(x_ref, target_of(bits, shard)) if k == 0 else store(k - 1, shard, bits)
        return remote(
            source,
            store(k, shard, bits ^ (1 << k)),
            send[k].at[shard, bits >> (k + 1)],
            recv[k].at[shard, bits >> (k + 1)],
            flip(me, steps[k]),
        )

    def parts_of(k):
        return [high << (k + 1) for high in reversed(range(1 << (count - 1 - k)))]

    def send_step(k, shard):
        for bits in parts_of(k):
            copy(k, shard, bits | 1 << k).start()

    def take_step(k, shard):
        for bits in parts_of(k):
            copy(k, shard, bits | 1 << k).wait_recv()
            here_ref = store(k, shard, bits)
            if k == 0:
                place = target_of(bits, shard)
                mine = lambda cut, place=place: read(x_ref, place, cut)
            else:
                before = store(k - 1, shard, bits)
                mine = lambda cut, before=before: before[cut, :]
            add_blocks(here_ref, mine, lambda cut, here_ref=here_ref: here_ref[cut, :], rows)
            if k + 1 < count and bits >> (k + 1) & 1:
                copy(k + 1, shard, bits).start()

    def line_inside(amount):
        there = my_line + amount
        return (there >= 0) & (there < lines)

    def line_copy(amount, shard):
        way = (amount + 1) // 2
        return remote(
            on_line.at[way, shard],
            on_line.at[way, shard],
            line_send.at[way, shard],
            line_recv.at[way, shard],
            along(me, amount),
        )

    last = count - 1

    def each(distance, work):
        if distance == 0:
            work(my_line, 0)
            return
        for amount in (1, -1):
            shard = my_line + amount * distance
            pl.when((shard >= 0) & (shard < lines))(functools.partial(work, shard, amount))

    def line_step(shard, amount):
        done = held[last].at[shard, 0]
        moving = on_line.at[(amount + 1) // 2, shard]

        @pl.when(line_inside(-amount))
        def _():
            line_copy(amount, shard).wait_recv()
            add_blocks(moving, lambda cut: moving[cut, :], lambda cut: done[cut, :], rows)

        @pl.when(jnp.logical_not(line_inside(-amount)))
        def _():
            add_blocks(moving, lambda cut: done[cut, :], lambda cut: jnp.zeros_like(done[cut, :]), rows)

        line_copy(amount, shard).start()

    greet(me, steps, lines)
    order = list(reversed(range(lines)))
    for distance in order:
        each(distance, lambda shard, amount: send_step(0, shard))
    for tick in range(lines + count):
        for k in reversed(range(count)):
            index = tick - k
            if 0 <= index < lines:
                each(order[index], lambda shard, amount, k=k: take_step(k, shard))
        index = tick - count
        if 0 <= index < lines and order[index] > 0:
            each(order[index], line_step)
    final = held[last].at[my_line, 0]
    if lines == 1:
        add_blocks(out_ref, lambda cut: final[cut, :], lambda cut: jnp.zeros_like(final[cut, :]), rows)
    else:
        add_blocks(out_ref, lambda cut: final[cut, :], lambda cut: jnp.zeros_like(final[cut, :]), rows)
        for amount in (1, -1):

            @pl.when(line_inside(-amount))
            def _():
                line_copy(amount, my_line).wait_recv()
                moving = on_line.at[(amount + 1) // 2, my_line]
                add_blocks(
                    out_ref, lambda cut: out_ref[cut, :], lambda cut: moving[cut, :], rows
                )

        for amount in (1, -1):
            for distance in range(1, lines):
                shard = my_line + amount * distance
                pl.when((shard >= 0) & (shard < lines))(
                    lambda amount=amount, shard=shard: line_copy(amount, shard).wait_send()
                )
    for k in range(count):
        for shard in range(lines):
            for bits in parts_of(k):
                copy(k, shard, bits | 1 << k).wait_send()


def sum_parts(values, steps, lines, rows, columns, slot, read, number, kind=F32):
    count = len(steps)

    def kernel(x_ref, out_ref, *rest):
        held, rest = rest[:count], rest[count:]
        on_line, rest = rest[0], rest[1:]
        send, rest = rest[:count], rest[count:]
        recv, rest = rest[:count], rest[count:]
        sum_kernel(
            steps, lines, rows, read, x_ref, slot, out_ref, held, on_line, (send, recv) + rest
        )

    sizes = [1 << (count - 1 - k) for k in range(count)]
    return pl.pallas_call(
        kernel,
        out_shape=jax.ShapeDtypeStruct((rows, columns), kind),
        in_specs=[pl.BlockSpec(memory_space=pltpu.VMEM)],
        out_specs=pl.BlockSpec(memory_space=pltpu.VMEM),
        scratch_shapes=[pltpu.VMEM((lines, size, rows, columns), BF16) for size in sizes]
        + [pltpu.VMEM((2, lines, rows, columns), BF16) if lines > 1 else pltpu.VMEM((2, 1, 16, 128), BF16)]
        + [pltpu.SemaphoreType.DMA((lines, size)) for size in sizes] * 2
        + [pltpu.SemaphoreType.DMA((2, lines))] * 2,
        compiler_params=pltpu.CompilerParams(
            collective_id=number, has_side_effects=True, vmem_limit_bytes=VMEM_BYTES
        ),
    )(values)


def gather_rows(values, number):
    lines, (rows, columns) = lax.axis_size("line"), values.shape
    out = gather(
        values,
        (SIDE, FRONT),
        lines,
        (2, lines, 2, rows, columns),
        lambda ref, at: ref.at[at["fsdp"], at["line"], at["pair"]],
        number,
    )
    return out.reshape(4 * lines * rows, columns)


def sum_rows(values, number):
    lines, (total, columns) = lax.axis_size("line"), values.shape
    rows = total // (4 * lines)
    return sum_parts(
        values.astype(BF16).reshape(2, lines, 2, rows, columns),
        (FRONT, SIDE),
        lines,
        rows,
        columns,
        lambda ref, at: ref.at[at["fsdp"], at["line"], at["pair"]],
        lambda ref, at, cut: ref[at["fsdp"], at["line"], at["pair"], cut, :],
        number,
    )


def gather_plane(values, number):
    rows, columns = values.shape
    out = gather(
        values,
        (SIDE, FRONT, "tp"),
        1,
        (2, 2, 2, rows, columns),
        lambda ref, at: ref.at[at["fsdp"], at["pair"], at["tp"]],
        number,
    )
    return out.reshape(8 * rows, columns)


def sum_plane(values, number):
    total, columns = values.shape
    rows = total // 8
    return sum_parts(
        values.reshape(2, 2, 2, rows, columns),
        ("tp", FRONT, SIDE),
        1,
        rows,
        columns,
        lambda ref, at: ref.at[at["fsdp"], at["pair"], at["tp"]],
        lambda ref, at, cut: ref[at["fsdp"], at["pair"], at["tp"], cut, :],
        number,
    )


def gather_ctx(values, number):
    lines, (rows, columns) = lax.axis_size("line"), values.shape
    out = gather(
        values,
        ("pair", "tp"),
        lines,
        (lines, 2, 2, rows, columns),
        lambda ref, at: ref.at[at["line"], at["pair"], at["tp"]],
        number,
    )
    return out


def sum_ctx(values, number):
    lines, _, _, rows, columns = values.shape
    return sum_parts(
        values,
        ("tp", "pair"),
        lines,
        rows,
        columns,
        lambda ref, at: ref.at[at["line"], at["pair"], at["tp"]],
        lambda ref, at, cut: ref[at["line"], at["pair"], at["tp"], cut, :],
        number,
    )


DIRECT = (("pair",), ("fsdp",), ("pair", "fsdp"))


def move(me, names):
    place = me
    for name in names:
        place = flip(place, name)
    return place


def quarter_of(place):
    return place["fsdp"] * 2 + place["pair"]


def exchange_kernel(count, spread, *refs):
    sources, targets = refs[:count], refs[count : 2 * count]
    own_sem, send, recv = refs[2 * count :]
    me = here()

    def wide(ref, quarter):
        columns = ref.shape[1] // 4
        return ref.at[:, pl.ds(pl.multiple_of(quarter * columns, columns), columns)]

    def narrow(ref, quarter):
        return ref.at[quarter]

    cut, put = (wide, narrow) if spread else (narrow, wide)
    barrier = pltpu.get_barrier_semaphore()
    for names in DIRECT:
        pl.semaphore_signal(barrier, inc=1, device_id=move(me, names), device_id_type=MESH_ID)
    pl.semaphore_wait(barrier, len(DIRECT))
    copies = []
    for n in range(count):
        for k, names in reversed(list(enumerate(DIRECT))):
            there = move(me, names)
            copies.append(
                remote(
                    cut(sources[n], quarter_of(there)),
                    put(targets[n], quarter_of(me)),
                    send.at[n, k],
                    recv.at[n, k],
                    there,
                )
            )
        copies.append(
            pltpu.make_async_copy(
                cut(sources[n], quarter_of(me)), put(targets[n], quarter_of(me)), own_sem.at[n]
            )
        )
    for one in copies:
        one.start()
    for one in copies:
        one.wait()


def exchange_columns(arrays, spread, number):
    count = len(arrays)
    if spread:
        shapes = [(4, a.shape[0], a.shape[1] // 4) for a in arrays]
    else:
        shapes = [(a.shape[1], a.shape[2] * 4) for a in arrays]
    return pl.pallas_call(
        functools.partial(exchange_kernel, count, spread),
        out_shape=[jax.ShapeDtypeStruct(s, a.dtype) for s, a in zip(shapes, arrays)],
        in_specs=[pl.BlockSpec(memory_space=pl.ANY)] * count,
        out_specs=[pl.BlockSpec(memory_space=pl.ANY)] * count,
        scratch_shapes=[
            pltpu.SemaphoreType.DMA((count,)),
            pltpu.SemaphoreType.DMA((count, 3)),
            pltpu.SemaphoreType.DMA((count, 3)),
        ],
        compiler_params=pltpu.CompilerParams(collective_id=number, has_side_effects=True),
    )(*arrays)


def total_kernel(lines, x_ref, out_ref, moved, on_line, send, recv, line_send, line_recv):
    me = here()
    steps = ("tp", "pair", "fsdp")
    greet(me, steps, lines)
    out_ref[...] = x_ref[...]
    for k, step in enumerate(steps):
        swap = remote(moved.at[k, 0], moved.at[k, 1], send.at[k], recv.at[k], flip(me, step))
        moved[k, 0] = out_ref[...]
        swap.start()
        swap.wait()
        out_ref[...] = out_ref[...] + moved[k, 1]
    on_line[me["line"]] = out_ref[...]

    def copy(amount, shard):
        return remote(
            on_line.at[shard],
            on_line.at[shard],
            line_send.at[(amount + 1) // 2, shard],
            line_recv.at[shard],
            along(me, amount),
        )

    def inside(amount):
        there = me["line"] + amount
        return (there >= 0) & (there < lines)

    for amount in (1, -1):
        pl.when(inside(amount))(lambda amount=amount: copy(amount, me["line"]).start())
    for distance in range(1, lines):
        for amount in (1, -1):
            shard = me["line"] - amount * distance

            @pl.when((shard >= 0) & (shard < lines))
            def _():
                copy(amount, shard).wait_recv()
                pl.when(inside(amount))(lambda: copy(amount, shard).start())

    total = on_line[0]
    for shard in range(1, lines):
        total = total + on_line[shard]
    out_ref[...] = total
    for amount in (1, -1):
        for distance in range(lines):
            shard = me["line"] - amount * distance
            pl.when((shard >= 0) & (shard < lines) & inside(amount))(
                lambda amount=amount, shard=shard: copy(amount, shard).wait_send()
            )


def total_sum(values, number):
    lines = lax.axis_size("line")
    size = values.shape[0]
    shape = (-(-size // 1024) * 8, 128)
    padded = jnp.pad(values, (0, shape[0] * 128 - size)).reshape(shape)
    out = pl.pallas_call(
        functools.partial(total_kernel, lines),
        out_shape=jax.ShapeDtypeStruct(shape, F32),
        in_specs=[pl.BlockSpec(memory_space=pltpu.VMEM)],
        out_specs=pl.BlockSpec(memory_space=pltpu.VMEM),
        scratch_shapes=[
            pltpu.VMEM((3, 2) + shape, F32),
            pltpu.VMEM((lines,) + shape, F32),
            pltpu.SemaphoreType.DMA((3,)),
            pltpu.SemaphoreType.DMA((3,)),
            pltpu.SemaphoreType.DMA((2, lines)),
            pltpu.SemaphoreType.DMA((lines,)),
        ],
        compiler_params=pltpu.CompilerParams(
            collective_id=number, has_side_effects=True, vmem_limit_bytes=VMEM_BYTES
        ),
    )(padded)
    return out.reshape(-1)[:size]


def swap_tp(values):
    return lax.ppermute(values, "tp", [(0, 1), (1, 0)])


def gather_line(values):
    lines = lax.axis_size("line")
    quarters, rows, columns = values.shape
    fsdp = lax.axis_size("fsdp")
    every = lax.all_gather(values, "line", axis=0, tiled=False)
    every = every.reshape(lines, fsdp, quarters // fsdp, rows, columns).transpose(1, 0, 2, 3, 4)
    return every.reshape(lines * quarters * rows, columns)


def sum_line(values):
    lines, fsdp, pair = lax.axis_size("line"), lax.axis_size("fsdp"), lax.axis_size("pair")
    total, columns = values.shape
    rows = total // (lines * fsdp * pair)
    ordered = values.reshape(fsdp, lines, pair, rows, columns).transpose(1, 0, 2, 3, 4)
    ordered = ordered.reshape(total, columns).astype(BF16)
    summed = lax.psum_scatter(ordered, "line", scatter_dimension=0, tiled=True)
    return summed.reshape(fsdp * pair, rows, columns)


LOG2E = 1.4426950408889634


def visible_bias(bias_ref, position, chunks):
    prompt = position < PBLK
    row = lax.broadcasted_iota(jnp.int32, (BLK, BLK), 0)
    column = lax.broadcasted_iota(jnp.int32, (BLK, BLK), 1)
    limit = jnp.where(prompt, position * BLK + column, PBLK * BLK)
    for chunk in range(chunks - 1):
        bias_ref[chunk] = jnp.where(row + chunk * BLK <= limit, 0.0, MASKED)
    own_limit = jnp.where(prompt, -1, column)
    bias_ref[chunks - 1] = jnp.where(row <= own_limit, 0.0, MASKED)


def rows_by_rows(left, right):
    return lax.dot_general(left, right, (((1,), (1,)), ((), ())), preferred_element_type=F32)


def attend_kernel(position_ref, query_ref, key_ref, value_t_ref, mixed_ref, logsum_ref, bias_ref, score_ref):
    chunks = PBLK + 1
    factor = HD**-0.5 * LOG2E

    @pl.when(pl.program_id(1) == 0)
    def _():
        visible_bias(bias_ref, position_ref[pl.program_id(0)], chunks)

    query = query_ref[...]
    largest = None
    for chunk in range(chunks):
        keys = key_ref[0, chunk * BLK : (chunk + 1) * BLK, :]
        score = rows_by_rows(keys, query) + bias_ref[chunk]
        score_ref[chunk] = score
        top = jnp.max(score.reshape(BLK // 8, 8, BLK), axis=0)
        largest = top if largest is None else jnp.maximum(largest, top)
    largest = jnp.max(largest, axis=0, keepdims=True)
    total = jnp.zeros((8, BLK), F32)
    mixed = jnp.zeros((HD, BLK), F32)
    for chunk in range(chunks):
        weight = jnp.exp2((score_ref[chunk] - largest) * factor)
        total = total + jnp.sum(weight.reshape(BLK // 8, 8, BLK), axis=0)
        values = value_t_ref[0, :, chunk * BLK : (chunk + 1) * BLK]
        mixed = mixed + jnp.dot(values, weight.astype(BF16), preferred_element_type=F32)
    total = jnp.sum(total, axis=0, keepdims=True)
    mixed_ref[...] = (mixed / total).T.astype(BF16)
    logsum_ref[0, 0] = largest * factor + jnp.log2(total)


def attend(queries, keysets, positions):
    rows, width = queries.shape
    blocks, heads = rows // BLK, width // HD
    keys = keysets[:, :, :HD]
    values_t = keysets[:, :, HD:].transpose(0, 2, 1)
    count = keysets.shape[1]
    return pl.pallas_call(
        attend_kernel,
        grid=(blocks, heads),
        out_shape=[
            jax.ShapeDtypeStruct((rows, width), BF16),
            jax.ShapeDtypeStruct((blocks, heads, 1, BLK), F32),
        ],
        in_specs=[
            pl.BlockSpec(memory_space=pltpu.SMEM),
            pl.BlockSpec((BLK, HD), lambda b, h: (b, h)),
            pl.BlockSpec((1, count, HD), lambda b, h: (b, 0, 0)),
            pl.BlockSpec((1, HD, count), lambda b, h: (b, 0, 0)),
        ],
        out_specs=[
            pl.BlockSpec((BLK, HD), lambda b, h: (b, h)),
            pl.BlockSpec((1, 1, 1, BLK), lambda b, h: (b, h, 0, 0)),
        ],
        scratch_shapes=[
            pltpu.VMEM((PBLK + 1, BLK, BLK), F32),
            pltpu.VMEM((PBLK + 1, BLK, BLK), F32),
        ],
        compiler_params=pltpu.CompilerParams(vmem_limit_bytes=VMEM_BYTES),
        cost_estimate=pl.CostEstimate(
            flops=4 * rows * width * count, bytes_accessed=8 * rows * width, transcendentals=rows * heads * count
        ),
    )(positions, queries, keys, values_t)


def attend_back_kernel(
    position_ref, slot_ref, query_ref, grad_ref, mixed_ref, logsum_ref, key_ref, key_t_ref, value_ref,
    grad_query_ref, table_out_ref, bias_ref, set_ref, table_ref,
):
    chunks = PBLK + 1
    scale = HD**-0.5
    block, head = pl.program_id(0), pl.program_id(1)

    @pl.when(head == 0)
    def _():
        visible_bias(bias_ref, position_ref[block], chunks)
        set_ref[...] = jnp.zeros_like(set_ref)

    @pl.when((head == 0) & (block == 0))
    def _():
        def clear(index, carry):
            table_ref[index] = jnp.zeros(table_ref.shape[1:], F32)
            return carry

        lax.fori_loop(0, table_ref.shape[0], clear, 0)

    query, grad = query_ref[...], grad_ref[...]
    inner = jnp.sum(grad.astype(F32) * mixed_ref[...].astype(F32), axis=1, keepdims=True)
    inner = jnp.broadcast_to(inner, (BLK, HD)).T[:1, :]
    logsum = logsum_ref[0, 0]
    grad_query = jnp.zeros((HD, BLK), F32)
    for chunk in range(chunks):
        cut = slice(chunk * BLK, (chunk + 1) * BLK)
        score = rows_by_rows(key_ref[0, cut, :], query)
        weight = jnp.exp2(score * (scale * LOG2E) + bias_ref[chunk] - logsum)
        grad_weight = rows_by_rows(value_ref[0, cut, :], grad)
        grad_score = (weight * (grad_weight - inner)).astype(BF16)
        set_ref[cut, :HD] += jnp.dot(grad_score, query, preferred_element_type=F32)
        set_ref[cut, HD:] += jnp.dot(weight.astype(BF16), grad, preferred_element_type=F32)
        grad_query = grad_query + jnp.dot(key_t_ref[0, :, cut], grad_score, preferred_element_type=F32)
    grad_query_ref[...] = (grad_query * scale).T.astype(BF16)

    @pl.when(head == pl.num_programs(1) - 1)
    def _():
        for chunk in range(chunks):
            slot = slot_ref[block, chunk]
            cut = slice(chunk * BLK, (chunk + 1) * BLK)
            table_ref[slot, :, :HD] += set_ref[cut, :HD] * scale
            table_ref[slot, :, HD:] += set_ref[cut, HD:]

    @pl.when((head == pl.num_programs(1) - 1) & (block == pl.num_programs(0) - 1))
    def _():
        per_device = table_out_ref.shape[2] // BLK

        def give(index, carry):
            holder, place = index // per_device, index % per_device
            rows = pl.ds(pl.multiple_of(place * BLK, BLK), BLK)
            table_out_ref[holder, 0, rows, :] = table_ref[index, :, :HD].astype(BF16)
            table_out_ref[holder, 1, rows, :] = table_ref[index, :, HD:].astype(BF16)
            return carry

        lax.fori_loop(0, table_ref.shape[0], give, 0)


def attend_back(queries, grads, mixed, logsums, keysets, positions, key_slots, slot_count):
    rows, width = queries.shape
    blocks, heads = rows // BLK, width // HD
    keys, values = keysets[:, :, :HD], keysets[:, :, HD:]
    count = keysets.shape[1]
    by_head = pl.BlockSpec((BLK, HD), lambda b, h: (b, h))
    by_block = pl.BlockSpec((1, count, HD), lambda b, h: (b, 0, 0))
    table = (slot_count // blocks, 2, blocks * BLK, HD)
    return pl.pallas_call(
        attend_back_kernel,
        grid=(blocks, heads),
        out_shape=[
            jax.ShapeDtypeStruct((rows, width), BF16),
            jax.ShapeDtypeStruct(table, BF16),
        ],
        in_specs=[
            pl.BlockSpec(memory_space=pltpu.SMEM),
            pl.BlockSpec(memory_space=pltpu.SMEM),
            by_head,
            by_head,
            by_head,
            pl.BlockSpec((1, 1, 1, BLK), lambda b, h: (b, h, 0, 0)),
            by_block,
            pl.BlockSpec((1, HD, count), lambda b, h: (b, 0, 0)),
            by_block,
        ],
        out_specs=[by_head, pl.BlockSpec(table, lambda b, h: (0, 0, 0, 0))],
        scratch_shapes=[
            pltpu.VMEM((PBLK + 1, BLK, BLK), F32),
            pltpu.VMEM((count, 2 * HD), F32),
            pltpu.VMEM((slot_count, BLK, 2 * HD), F32),
        ],
        compiler_params=pltpu.CompilerParams(vmem_limit_bytes=VMEM_BYTES),
        cost_estimate=pl.CostEstimate(
            flops=10 * rows * width * count, bytes_accessed=16 * rows * width, transcendentals=rows * heads * count
        ),
    )(positions, key_slots, queries, grads, mixed, logsums, keys, keys.transpose(0, 2, 1), values)


def body(
    hidden_in,
    block_order,
    attn_norm_gain,
    attn_norm_bias,
    query_weight,
    query_bias,
    keyval_weight,
    value_bias,
    proj_weight,
    proj_bias,
    mlp_norm_gain,
    mlp_norm_bias,
    up_weight,
    up_bias,
    down_weight,
    down_bias,
    out_cotangent,
):
    rows_dev = hidden_in.shape[0]
    half_rows = rows_dev // 2
    width = hidden_in.shape[1]
    blocks_dev = rows_dev // BLK
    slot_count = block_order.shape[1]
    group_blocks = PBLK + CONTS
    heads_dev = query_bias.shape[0] // HD
    head_width = heads_dev * HD
    core = lax.axis_index("tp")
    quarter = lax.axis_index("fsdp") * lax.axis_size("pair") + lax.axis_index("pair")
    quarters = lax.axis_size("fsdp") * lax.axis_size("pair")
    hidden_dev = up_weight.shape[1] // quarters

    def own_half(values):
        return lax.dynamic_slice_in_dim(values, core * half_rows, half_rows, axis=0)

    def other_half(values):
        return lax.dynamic_slice_in_dim(values, (1 - core) * half_rows, half_rows, axis=0)

    def in_order(mine, other, axis=0):
        first = jnp.where(core == 0, mine, other)
        second = jnp.where(core == 0, other, mine)
        return jnp.concatenate([first, second], axis=axis)

    def sum_halves(values):
        return own_half(values) + swap_tp(other_half(values))

    def join_halves(values):
        return in_order(values, swap_tp(values))

    gain_one = attn_norm_gain.astype(F32)
    shift_one = attn_norm_bias.astype(F32)
    gain_two = mlp_norm_gain.astype(F32)
    shift_two = mlp_norm_bias.astype(F32)

    slot_ids = jnp.arange(slot_count, dtype=jnp.int32)
    ordering = block_order[0]
    inverse = jnp.sum(
        jnp.where(ordering[None, :] == slot_ids[:, None], slot_ids[None, :], 0), axis=1
    )
    ctx_index = lax.axis_index("line") * lax.axis_size("pair") + lax.axis_index("pair")
    first_slot = ctx_index * blocks_dev
    my_slots = first_slot + jnp.arange(blocks_dev, dtype=jnp.int32)
    my_blocks = lax.dynamic_slice_in_dim(ordering, first_slot, blocks_dev)
    positions = my_blocks % group_blocks
    group_base = my_blocks // group_blocks * group_blocks
    prompt_slots = jnp.take(
        inverse, group_base[:, None] + jnp.arange(PBLK, dtype=jnp.int32)[None, :]
    )
    key_slots = jnp.concatenate([prompt_slots, my_slots[:, None]], axis=1)

    keyval_cut = lax.dynamic_slice_in_dim(keyval_weight, core * HD, HD, axis=1)
    first_all = gather_rows(jnp.concatenate([query_weight, keyval_cut], axis=1), 1)
    proj_all = gather_rows(proj_weight, 2)
    down_cut, up_cut = exchange_columns([down_weight, up_weight], True, 3)
    down_all = gather_line(down_cut)
    up_all = gather_line(up_cut)

    stream = hidden_in.astype(F32)
    normed_one = layer_norm(stream, gain_one, shift_one).astype(BF16)
    value_shift = jnp.where(core == 1, value_bias.astype(F32), 0.0)
    first_shift = jnp.concatenate([query_bias.astype(F32), value_shift])
    first_low = (jnp.dot(normed_one, first_all, preferred_element_type=F32) + first_shift).astype(
        BF16
    )
    query_low = first_low[:, :head_width]
    part_low = first_low[:, head_width:]
    keyval_every = gather_ctx(part_low, 4)
    keyval_low = in_order(part_low, swap_tp(part_low), axis=1)
    keyval_table = keyval_every.transpose(0, 1, 3, 2, 4).reshape(slot_count, BLK, 2 * HD)
    own_table = keyval_low.reshape(blocks_dev, 1, BLK, 2 * HD)
    keysets = jnp.concatenate([keyval_table[prompt_slots], own_table], axis=1)
    keysets = keysets.reshape(blocks_dev, (PBLK + 1) * BLK, 2 * HD)
    mixed_low, logsums = attend(query_low, keysets, positions)
    proj_part = jnp.einsum("rk,ok->ro", mixed_low, proj_all, preferred_element_type=F32)
    middle = own_half(stream) + sum_halves(proj_part) + proj_bias.astype(F32)

    normed_two = layer_norm(middle, gain_two, shift_two).astype(BF16)
    cotangent = own_half(out_cotangent)
    cotangent_all = gather_plane(cotangent, 5)
    normed_two_all = gather_plane(normed_two, 6)
    up_shift = lax.dynamic_slice_in_dim(up_bias, quarter * hidden_dev, hidden_dev).astype(F32)
    grad_act = jnp.dot(cotangent_all, down_all, preferred_element_type=F32)
    pre_act = jnp.dot(normed_two_all, up_all, preferred_element_type=F32) + up_shift
    act, gelu_pull = jax.vjp(gelu_tanh, pre_act)
    act_low = act.astype(BF16)
    grad_pre_wide = gelu_pull(grad_act)[0]
    grad_pre = grad_pre_wide.astype(BF16)
    normed_two_part = jnp.einsum("rf,df->rd", grad_pre, up_all, preferred_element_type=F32)
    grad_normed_two = sum_plane(normed_two_part.astype(BF16), 7)
    down_part = jnp.einsum("rf,of->ro", act_low, down_all, preferred_element_type=F32)
    mlp_out = sum_plane(down_part.astype(BF16), 8) + down_bias.astype(F32)
    layer_out = join_halves((middle + mlp_out).astype(BF16))
    grad_up_bias = jnp.sum(grad_pre, axis=0, dtype=F32)
    down_weight_grad = jnp.einsum("ro,rf->of", cotangent_all, act_low, preferred_element_type=F32)
    up_weight_grad = jnp.einsum("rd,rf->df", normed_two_all, grad_pre, preferred_element_type=F32)
    down_cut_grad = sum_line(down_weight_grad)
    up_cut_grad = sum_line(up_weight_grad)
    wide_grads = exchange_columns([down_cut_grad, up_cut_grad], False, 9)
    grad_down_weight, grad_up_weight = [one.astype(F32) for one in wide_grads]

    norm_two_pull = jax.vjp(layer_norm, middle, gain_two, shift_two)[1]
    grad_mid_norm, grad_mlp_norm_gain, grad_mlp_norm_bias = norm_two_pull(grad_normed_two)
    grad_middle = cotangent.astype(F32) + grad_mid_norm
    grad_down_bias = jnp.sum(cotangent, axis=0, dtype=F32)

    grad_attn_half = grad_middle.astype(BF16)
    grad_proj_bias = jnp.sum(grad_attn_half, axis=0, dtype=F32)
    grad_attn = join_halves(grad_attn_half)
    proj_weight_grad = jnp.einsum("ro,rk->ok", grad_attn, mixed_low, preferred_element_type=F32)
    grad_proj_weight = sum_rows(proj_weight_grad, 10)
    grad_mixed = jnp.einsum("ro,ok->rk", grad_attn, proj_all, preferred_element_type=F32).astype(
        BF16
    )
    grad_query, grad_table = attend_back(
        query_low, grad_mixed, mixed_low, logsums, keysets, positions, key_slots, slot_count
    )
    grad_query_bias = jnp.sum(grad_query, axis=0, dtype=F32)
    grad_parts = grad_table.reshape(
        lax.axis_size("line"), lax.axis_size("pair"), 2, rows_dev, HD
    )
    grad_part = sum_ctx(grad_parts, 12).astype(BF16)
    grad_value_bias = jnp.where(core == 1, jnp.sum(grad_part, axis=0, dtype=F32), 0.0)
    grad_first = jnp.concatenate([grad_query, grad_part], axis=1)
    normed_one_part = jnp.einsum("rk,dk->rd", grad_first, first_all, preferred_element_type=F32)
    grad_normed_one = sum_halves(normed_one_part)
    first_weight_grad = jnp.einsum("rd,rk->dk", normed_one, grad_first, preferred_element_type=F32)
    grad_first_weight = sum_rows(first_weight_grad, 11)
    grad_query_weight = grad_first_weight[:, :head_width]
    grad_cut = grad_first_weight[:, head_width:]
    grad_keyval_weight = in_order(grad_cut, swap_tp(grad_cut), axis=1)
    norm_one_pull = jax.vjp(layer_norm, own_half(stream), gain_one, shift_one)[1]
    grad_in_norm, grad_attn_norm_gain, grad_attn_norm_bias = norm_one_pull(grad_normed_one)
    input_grad = join_halves((grad_middle + grad_in_norm).astype(BF16))

    query_slots = jnp.zeros((2 * head_width,), F32)
    query_slots = lax.dynamic_update_slice_in_dim(
        query_slots, grad_query_bias, core * head_width, axis=0
    )
    hidden_slots = jnp.zeros((2 * quarters * hidden_dev,), F32)
    hidden_slots = lax.dynamic_update_slice_in_dim(
        hidden_slots, grad_up_bias, (core * quarters + quarter) * hidden_dev, axis=0
    )
    pieces = [
        grad_attn_norm_gain,
        grad_attn_norm_bias,
        grad_proj_bias,
        grad_mlp_norm_gain,
        grad_mlp_norm_bias,
        grad_down_bias,
        grad_value_bias,
        query_slots,
        hidden_slots,
    ]
    summed = total_sum(jnp.concatenate(pieces), 13)
    cuts, start = [], 0
    for piece in pieces:
        cuts.append(summed[start : start + piece.shape[0]])
        start += piece.shape[0]
    sum_query = lax.dynamic_slice_in_dim(cuts[7], core * head_width, head_width)
    sum_up = lax.dynamic_slice_in_dim(cuts[8], core * quarters * hidden_dev, quarters * hidden_dev)
    return (
        layer_out,
        input_grad,
        cuts[0],
        cuts[1],
        grad_query_weight,
        sum_query,
        grad_keyval_weight,
        cuts[6],
        grad_proj_weight,
        cuts[2],
        cuts[3],
        cuts[4],
        grad_up_weight,
        sum_up,
        grad_down_weight,
        cuts[5],
    )


def solution(mesh):
    fsdp, ctx, tp = mesh.devices.shape
    grid = Mesh(mesh.devices.reshape(fsdp, ctx // 2, 2, tp), EVERY)
    by_rows = P(ROWS, None)
    by_both = P(ROWS, "tp")
    return jax.shard_map(
        body,
        mesh=grid,
        in_specs=(
            by_rows,
            P("fsdp", None),
            P(),
            P(),
            by_both,
            P("tp"),
            by_rows,
            P(),
            by_both,
            P(),
            P(),
            P(),
            by_both,
            P("tp"),
            by_both,
            P(),
            by_rows,
        ),
        out_specs=(
            by_rows,
            by_rows,
            P(),
            P(),
            by_both,
            P("tp"),
            by_rows,
            P(),
            by_both,
            P(),
            P(),
            P(),
            by_both,
            P("tp"),
            by_both,
            P(),
        ),
        check_vma=False,
    )
```

```python
import functools

import jax
import jax.numpy as jnp
from jax import lax
from jax.experimental import pallas as pl
from jax.experimental.pallas import tpu as pltpu
from jax.sharding import Mesh, PartitionSpec as P

HD = 128
BLK = 256
PBLK = 8
CONTS = 8
EPSILON = 1e-05
MASKED = -1e30
F32 = jnp.float32
BF16 = jnp.bfloat16
ROWS = ("fsdp", "line", "pair")
EVERY = ("fsdp", "line", "pair", "tp")


def layer_norm(values, norm_gain, norm_shift):
    average = jnp.mean(values, axis=-1, keepdims=True)
    centered = values - average
    spread = jnp.mean(centered * centered, axis=-1, keepdims=True)
    return centered * lax.rsqrt(spread + EPSILON) * norm_gain + norm_shift


def gelu_tanh(values):
    return jax.nn.gelu(values, approximate=True)


MESH_ID = pl.DeviceIdType.MESH
VMEM_BYTES = 60 * 1024 * 1024
SIDE = ("pair", "fsdp")
FRONT = ("fsdp", "pair")


def here():
    return {name: lax.axis_index(name) for name in EVERY}


def flip(place, step):
    place = dict(place)
    if isinstance(step, str):
        place[step] = 1 - place[step]
    else:
        core = place["tp"]
        for name, used in ((step[0], 1 - core), (step[1], core)):
            place[name] = place[name] + (1 - 2 * place[name]) * used
    return place


def along(place, amount):
    return dict(place, line=place["line"] + amount)


def remote(source, target, send_sem, recv_sem, place):
    return pltpu.make_async_remote_copy(
        src_ref=source,
        dst_ref=target,
        send_sem=send_sem,
        recv_sem=recv_sem,
        device_id=place,
        device_id_type=MESH_ID,
    )


def top_bit(bits):
    return bits.bit_length() - 1


def add_blocks(target, first, second, rows):
    tile = min(rows, 64)

    def one(index, carry):
        cut = pl.ds(pl.multiple_of(index * tile, tile), tile)
        total = first(cut).astype(F32)
        if second is not None:
            total = total + second(cut).astype(F32)
        target[cut, :] = total.astype(target.dtype)
        return carry

    lax.fori_loop(0, rows // tile, one, 0)


def rows_of(ref):
    return lambda cut: ref[cut, :]


class Gather:
    def __init__(self, values, steps, lines, shape, slot):
        self.steps, self.lines, self.slot = steps, lines, slot
        self.out = jax.ShapeDtypeStruct(shape, values.dtype)
        self.in_spec = self.out_spec = pl.BlockSpec(memory_space=pl.ANY)

    def scratch(self):
        parts = 1 << len(self.steps)
        return [
            pltpu.SemaphoreType.DMA(()),
            pltpu.SemaphoreType.DMA((2, self.lines)),
            pltpu.SemaphoreType.DMA((self.lines,)),
            pltpu.SemaphoreType.DMA((self.lines, len(self.steps) * parts)),
            pltpu.SemaphoreType.DMA((self.lines, parts)),
        ]

    def stages(self, me, x_ref, out_ref, own_sem, line_send, line_recv, send, recv):
        steps, lines, slot = self.steps, self.lines, self.slot
        count = len(steps)
        my_line = me["line"] if lines > 1 else 0

        def block(bits, shard):
            place = me
            for k in reversed(range(count)):
                if bits >> k & 1:
                    place = flip(place, steps[k])
            return slot(out_ref, dict(place, line=shard))

        def to_step(k, bits, shard, source):
            return remote(
                source,
                block(bits, shard),
                send.at[shard, k * (1 << count) + bits],
                recv.at[shard, bits | 1 << k],
                flip(me, steps[k]),
            )

        def to_line(amount, shard, source):
            return remote(
                source,
                block(0, shard),
                line_send.at[(amount + 1) // 2, shard],
                line_recv.at[shard],
                along(me, amount),
            )

        def send_on(bits, shard, source):
            for k in range(top_bit(bits) + 1, count):
                to_step(k, bits, shard, source).start()

        def at_distance(distance, work):
            if distance == 0:
                work(my_line, 0)
                return
            for amount in (1, -1):
                shard = my_line - amount * distance
                pl.when((shard >= 0) & (shard < lines))(functools.partial(work, shard, amount))

        def line_inside(amount):
            there = my_line + amount
            return (there >= 0) & (there < lines)

        own = pltpu.make_async_copy(x_ref, block(0, my_line), own_sem)

        def begin():
            if lines > 1:
                for amount in (1, -1):
                    pl.when(line_inside(amount))(
                        lambda amount=amount: to_line(amount, my_line, x_ref).start()
                    )
            send_on(0, my_line, x_ref)
            own.start()

        def line_arrival(shard, amount):
            remote(
                block(0, shard), block(0, shard), line_send.at[0, shard], line_recv.at[shard], me
            ).wait_recv()
            pl.when(line_inside(amount))(lambda: to_line(amount, shard, block(0, shard)).start())
            send_on(0, shard, block(0, shard))

        def level_arrival(level, shard, amount):
            for bits in range(1 << level, 2 << level):
                remote(
                    block(bits, shard),
                    block(bits, shard),
                    send.at[shard, 0],
                    recv.at[shard, bits],
                    me,
                ).wait_recv()
                send_on(bits, shard, block(bits, shard))

        def tick(number):
            if number < lines:
                at_distance(number, line_arrival)
            for level in range(count):
                distance = number - 1 - level
                if 0 <= distance < lines:
                    at_distance(distance, functools.partial(level_arrival, level))

        def end():
            own.wait()
            if lines > 1:
                for amount in (1, -1):
                    for distance in range(lines):
                        shard = my_line - amount * distance
                        pl.when((shard >= 0) & (shard < lines) & line_inside(amount))(
                            lambda amount=amount, shard=shard: to_line(
                                amount, shard, block(0, shard)
                            ).wait_send()
                        )
            for shard in range(lines):
                for bits in range(1 << count):
                    for k in range(top_bit(bits) + 1, count):
                        to_step(k, bits, shard, block(bits, shard)).wait_send()

        ticks = [functools.partial(tick, number) for number in range(1, lines + count)]
        return [begin] + ticks + [end]


class Sum:
    def __init__(self, steps, lines, rows, columns, slot):
        self.steps, self.lines, self.rows, self.columns = steps, lines, rows, columns
        self.slot = slot
        self.out = jax.ShapeDtypeStruct((rows, columns), F32)
        self.in_spec = pl.BlockSpec(memory_space=pl.ANY)
        self.out_spec = pl.BlockSpec(memory_space=pltpu.VMEM)

    def scratch(self):
        count, lines = len(self.steps), self.lines
        sizes = [1 << (count - 1 - k) for k in range(count)]
        block = (self.rows, self.columns)
        return (
            [pltpu.VMEM((lines, sizes[0]) + block, BF16)]
            + [pltpu.VMEM((lines, size) + block, BF16) for size in sizes]
            + [pltpu.VMEM((2, lines) + (block if lines > 1 else (16, 128)), BF16)]
            + [pltpu.SemaphoreType.DMA((lines, sizes[0]))]
            + [pltpu.SemaphoreType.DMA((lines, size)) for size in sizes] * 2
            + [pltpu.SemaphoreType.DMA((2, lines))] * 2
        )

    def stages(self, me, x_ref, out_ref, own, *rest):
        steps, lines, rows, slot = self.steps, self.lines, self.rows, self.slot
        count = len(steps)
        held, rest = rest[:count], rest[count:]
        on_line, own_sem, rest = rest[0], rest[1], rest[2:]
        send, recv, (line_send, line_recv) = rest[:count], rest[count : 2 * count], rest[2 * count :]
        my_line = me["line"] if lines > 1 else 0
        last = count - 1

        def target_of(bits, shard):
            place = me
            for k in range(count):
                if bits >> k & 1:
                    place = flip(place, steps[k])
            return dict(place, line=shard)

        def store(k, shard, bits):
            return held[k].at[shard, bits >> (k + 1)]

        def own_copy(shard, bits):
            return pltpu.make_async_copy(
                slot(x_ref, target_of(bits, shard)),
                own.at[shard, bits >> 1],
                own_sem.at[shard, bits >> 1],
            )

        def copy(k, shard, bits):
            source = slot(x_ref, target_of(bits, shard)) if k == 0 else store(k - 1, shard, bits)
            return remote(
                source,
                store(k, shard, bits ^ (1 << k)),
                send[k].at[shard, bits >> (k + 1)],
                recv[k].at[shard, bits >> (k + 1)],
                flip(me, steps[k]),
            )

        def parts_of(k):
            return [high << (k + 1) for high in reversed(range(1 << (count - 1 - k)))]

        def send_first(shard, amount):
            for bits in parts_of(0):
                copy(0, shard, bits | 1).start()

        def own_first(shard, amount):
            for bits in parts_of(0):
                own_copy(shard, bits).start()

        def take_step(k, shard, amount):
            for bits in parts_of(k):
                copy(k, shard, bits | 1 << k).wait_recv()
                arrived = store(k, shard, bits)
                if k == 0:
                    own_copy(shard, bits).wait()
                    mine = own.at[shard, bits >> 1]
                else:
                    mine = store(k - 1, shard, bits)
                add_blocks(arrived, rows_of(mine), rows_of(arrived), rows)
                if k + 1 < count and bits >> (k + 1) & 1:
                    copy(k + 1, shard, bits).start()

        def line_inside(amount):
            there = my_line + amount
            return (there >= 0) & (there < lines)

        def line_copy(amount, shard):
            way = (amount + 1) // 2
            return remote(
                on_line.at[way, shard],
                on_line.at[way, shard],
                line_send.at[way, shard],
                line_recv.at[way, shard],
                along(me, amount),
            )

        def each(distance, work):
            if distance == 0:
                work(my_line, 0)
                return
            for amount in (1, -1):
                shard = my_line + amount * distance
                pl.when((shard >= 0) & (shard < lines))(functools.partial(work, shard, amount))

        def line_step(shard, amount):
            done = held[last].at[shard, 0]
            moving = on_line.at[(amount + 1) // 2, shard]

            @pl.when(line_inside(-amount))
            def _():
                line_copy(amount, shard).wait_recv()
                add_blocks(moving, rows_of(moving), rows_of(done), rows)

            @pl.when(jnp.logical_not(line_inside(-amount)))
            def _():
                add_blocks(moving, rows_of(done), None, rows)

            line_copy(amount, shard).start()

        order = list(reversed(range(lines)))

        def begin():
            for distance in order:
                each(distance, send_first)
            for distance in order:
                each(distance, own_first)

        def tick(number):
            for k in reversed(range(count)):
                index = number - k
                if 0 <= index < lines:
                    each(order[index], functools.partial(take_step, k))
            index = number - count
            if 0 <= index < lines and order[index] > 0:
                each(order[index], line_step)

        def end():
            final = held[last].at[my_line, 0]
            add_blocks(out_ref, rows_of(final), None, rows)
            if lines > 1:
                for amount in (1, -1):

                    @pl.when(line_inside(-amount))
                    def _():
                        line_copy(amount, my_line).wait_recv()
                        moving = on_line.at[(amount + 1) // 2, my_line]
                        add_blocks(out_ref, rows_of(out_ref), rows_of(moving), rows)

                for amount in (1, -1):
                    for distance in range(1, lines):
                        shard = my_line + amount * distance
                        pl.when((shard >= 0) & (shard < lines))(
                            lambda amount=amount, shard=shard: line_copy(amount, shard).wait_send()
                        )
            for k in range(count):
                for shard in range(lines):
                    for bits in parts_of(k):
                        copy(k, shard, bits | 1 << k).wait_send()

        ticks = [functools.partial(tick, number) for number in range(lines + count)]
        return [begin] + ticks + [end]


DIRECT = (("pair",), ("fsdp",), ("pair", "fsdp"))


def move(me, names):
    place = me
    for name in names:
        place = flip(place, name)
    return place


def quarter_of(place):
    return place["fsdp"] * 2 + place["pair"]


class Exchange:
    steps, lines, corner = ("pair", "fsdp"), 1, True

    def __init__(self, values, spread):
        self.spread = spread
        if spread:
            shape = (4, values.shape[0], values.shape[1] // 4)
        else:
            shape = (values.shape[1], values.shape[2] * 4)
        self.out = jax.ShapeDtypeStruct(shape, values.dtype)
        self.in_spec = self.out_spec = pl.BlockSpec(memory_space=pl.ANY)

    def scratch(self):
        return [
            pltpu.SemaphoreType.DMA(()),
            pltpu.SemaphoreType.DMA((3,)),
            pltpu.SemaphoreType.DMA((3,)),
        ]

    def stages(self, me, x_ref, out_ref, own_sem, send, recv):
        def wide(ref, quarter):
            columns = ref.shape[1] // 4
            return ref.at[:, pl.ds(pl.multiple_of(quarter * columns, columns), columns)]

        def narrow(ref, quarter):
            return ref.at[quarter]

        cut, put = (wide, narrow) if self.spread else (narrow, wide)
        copies = []
        for k, names in reversed(list(enumerate(DIRECT))):
            there = move(me, names)
            copies.append(
                remote(
                    cut(x_ref, quarter_of(there)),
                    put(out_ref, quarter_of(me)),
                    send.at[k],
                    recv.at[k],
                    there,
                )
            )
        copies.append(
            pltpu.make_async_copy(
                cut(x_ref, quarter_of(me)), put(out_ref, quarter_of(me)), own_sem
            )
        )

        def begin():
            for one in copies:
                one.start()

        def end():
            for one in copies:
                one.wait()

        return [begin, end]


class Total:
    steps = ("tp", "pair", "fsdp")

    def __init__(self, values, lines):
        self.lines, self.out = lines, jax.ShapeDtypeStruct(values.shape, F32)
        self.in_spec = self.out_spec = pl.BlockSpec(memory_space=pltpu.VMEM)

    def scratch(self):
        shape, lines = self.out.shape, self.lines
        return [
            pltpu.VMEM((3, 2) + shape, F32),
            pltpu.VMEM((lines,) + shape, F32),
            pltpu.SemaphoreType.DMA((3,)),
            pltpu.SemaphoreType.DMA((3,)),
            pltpu.SemaphoreType.DMA((2, lines)),
            pltpu.SemaphoreType.DMA((lines,)),
        ]

    def stages(self, me, x_ref, out_ref, moved, on_line, send, recv, line_send, line_recv):
        lines = self.lines

        def swap(k):
            return remote(
                moved.at[k, 0], moved.at[k, 1], send.at[k], recv.at[k], flip(me, self.steps[k])
            )

        def copy(amount, shard):
            return remote(
                on_line.at[shard],
                on_line.at[shard],
                line_send.at[(amount + 1) // 2, shard],
                line_recv.at[shard],
                along(me, amount),
            )

        def inside(amount):
            there = me["line"] + amount
            return (there >= 0) & (there < lines)

        def begin():
            moved[0, 0] = x_ref[...]
            swap(0).start()

        def after(k):
            swap(k).wait()
            if k < 2:
                moved[k + 1, 0] = moved[k, 0] + moved[k, 1]
                swap(k + 1).start()
                return
            on_line[me["line"]] = moved[k, 0] + moved[k, 1]
            for amount in (1, -1):
                pl.when(inside(amount))(lambda amount=amount: copy(amount, me["line"]).start())

        def hop(distance):
            for amount in (1, -1):
                shard = me["line"] - amount * distance

                @pl.when((shard >= 0) & (shard < lines))
                def _():
                    copy(amount, shard).wait_recv()
                    pl.when(inside(amount))(lambda: copy(amount, shard).start())

        def end():
            total = on_line[0]
            for shard in range(1, lines):
                total = total + on_line[shard]
            out_ref[...] = total
            for amount in (1, -1):
                for distance in range(lines):
                    shard = me["line"] - amount * distance
                    pl.when((shard >= 0) & (shard < lines) & inside(amount))(
                        lambda amount=amount, shard=shard: copy(amount, shard).wait_send()
                    )

        return (
            [begin]
            + [functools.partial(after, k) for k in range(3)]
            + [functools.partial(hop, distance) for distance in range(1, lines)]
            + [end]
        )


def greet(me, programs):
    barrier = pltpu.get_barrier_semaphore()
    lines = max(one.lines for one in programs)
    steps = list(dict.fromkeys(step for one in programs for step in one.steps))
    if SIDE in steps:
        steps = [step for step in steps if step not in ("pair", "fsdp")]
    places = [flip(me, step) for step in steps]
    if any(isinstance(one, Exchange) for one in programs):
        places.append(move(me, ("pair", "fsdp")))
    for place in places:
        pl.semaphore_signal(barrier, inc=1, device_id=place, device_id_type=MESH_ID)
    count = len(places)
    if lines > 1:
        for amount in (-1, 1):
            there = me["line"] + amount
            inside = (there >= 0) & (there < lines)

            @pl.when(inside)
            def _():
                pl.semaphore_signal(
                    barrier, inc=1, device_id=along(me, amount), device_id_type=MESH_ID
                )

            count = count + inside.astype(jnp.int32)
    pl.semaphore_wait(barrier, count)


def split_scratch(programs, refs):
    parts, start = [], 0
    for one in programs:
        size = len(one.scratch())
        parts.append(refs[start : start + size])
        start += size
    return parts


def schedule(programs, x_refs, out_refs, scratch):
    me = here()
    works = [(0.0, functools.partial(greet, me, programs))]
    for one, x_ref, out_ref, held in zip(programs, x_refs, out_refs, split_scratch(programs, scratch)):
        stages = one.stages(me, x_ref, out_ref, *held)
        works += [(k / (len(stages) - 1), stage) for k, stage in enumerate(stages)]
    return sorted(works, key=lambda work: work[0])


def run_programs(programs, arrays, number):
    count = len(programs)

    def kernel(*refs):
        for _, work in schedule(programs, refs[:count], refs[count : 2 * count], refs[2 * count :]):
            work()

    return pl.pallas_call(
        kernel,
        out_shape=[one.out for one in programs],
        in_specs=[one.in_spec for one in programs],
        out_specs=[one.out_spec for one in programs],
        scratch_shapes=[held for one in programs for held in one.scratch()],
        compiler_params=pltpu.CompilerParams(
            collective_id=number, has_side_effects=True, vmem_limit_bytes=VMEM_BYTES
        ),
    )(*arrays)


def by_rows_slot(ref, at):
    return ref.at[at["fsdp"], at["line"], at["pair"]]


def by_plane_slot(ref, at):
    return ref.at[at["fsdp"], at["pair"], at["tp"]]


def by_ctx_slot(ref, at):
    return ref.at[at["line"], at["pair"], at["tp"]]


def rows_gather(values):
    lines = lax.axis_size("line")
    return Gather(values, (SIDE, FRONT), lines, (2, lines, 2) + values.shape, by_rows_slot)


def rows_sum(values):
    lines, (total, columns) = lax.axis_size("line"), values.shape
    rows = total // (4 * lines)
    parts = values.astype(BF16).reshape(2, lines, 2, rows, columns)
    return Sum((FRONT, SIDE), lines, rows, columns, by_rows_slot), parts


def plane_gather(values):
    return Gather(values, (SIDE, FRONT, "tp"), 1, (2, 2, 2) + values.shape, by_plane_slot)


def plane_sum(values):
    rows, columns = values.shape[0] // 8, values.shape[1]
    parts = values.astype(BF16).reshape(2, 2, 2, rows, columns)
    return Sum(("tp", FRONT, SIDE), 1, rows, columns, by_plane_slot), parts


def flat(values):
    return values.reshape(-1, values.shape[-1])


def gather_ctx(values, number):
    lines = lax.axis_size("line")
    one = Gather(values, ("pair", "tp"), lines, (lines, 2, 2) + values.shape, by_ctx_slot)
    return run_programs([one], [values], number)[0]


def sum_ctx(values, number):
    lines, _, _, rows, columns = values.shape
    one = Sum(("tp", "pair"), lines, rows, columns, by_ctx_slot)
    return run_programs([one], [values], number)[0]


def total_of(values):
    size = values.shape[0]
    rows = -(-size // 1024) * 8
    padded = jnp.pad(values, (0, rows * 128 - size)).reshape(rows, 128)
    return Total(padded, lax.axis_size("line")), padded


def swap_tp(values):
    return lax.ppermute(values, "tp", [(0, 1), (1, 0)])


def gather_line(values):
    quarters, rows, columns = values.shape
    every = lax.all_gather(values, "line", axis=0, tiled=False)
    return every.reshape(-1, columns)


def sum_line(values):
    total, columns = values.shape
    lines = lax.axis_size("line")
    summed = lax.psum_scatter(values.astype(BF16), "line", scatter_dimension=0, tiled=True)
    return summed.reshape(4, total // (4 * lines), columns)


def to_line_order(values):
    lines = lax.axis_size("line")
    size = values.shape[1] // (2 * lines)
    cuts = [(half * lines + shard) * size for shard in range(lines) for half in range(2)]
    return jnp.concatenate([values[:, cut : cut + size] for cut in cuts], axis=1)


def from_line_order(values):
    lines = lax.axis_size("line")
    size = values.shape[1] // (2 * lines)
    cuts = [(shard * 2 + half) * size for half in range(2) for shard in range(lines)]
    return jnp.concatenate([values[:, cut : cut + size] for cut in cuts], axis=1)


LOG2E = 1.4426950408889634


def visible_bias(bias_ref, position, chunks):
    prompt = position < PBLK
    row = lax.broadcasted_iota(jnp.int32, (BLK, BLK), 0)
    column = lax.broadcasted_iota(jnp.int32, (BLK, BLK), 1)
    limit = jnp.where(prompt, position * BLK + column, PBLK * BLK)
    for chunk in range(chunks - 1):
        bias_ref[chunk] = jnp.where(row + chunk * BLK <= limit, 0.0, MASKED)
    own_limit = jnp.where(prompt, -1, column)
    bias_ref[chunks - 1] = jnp.where(row <= own_limit, 0.0, MASKED)


def rows_by_rows(left, right):
    return lax.dot_general(left, right, (((1,), (1,)), ((), ())), preferred_element_type=F32)


def beside(programs, in_refs, out_refs, scratch, steps):
    step = pl.program_id(0) * pl.num_programs(1) + pl.program_id(1)
    for place, work in schedule(programs, in_refs, out_refs, scratch):
        pl.when(step == min(steps - 1, int(place * steps)))(work)


def attend_kernel(programs, steps, *refs):
    count = len(programs)
    (position_ref, query_ref, key_ref, value_t_ref), refs = refs[:4], refs[4:]
    others, refs = refs[:count], refs[count:]
    (mixed_ref, logsum_ref), refs = refs[:2], refs[2:]
    other_outs, refs = refs[:count], refs[count:]
    (bias_ref, score_ref), scratch = refs[:2], refs[2:]
    chunks = PBLK + 1
    factor = HD**-0.5 * LOG2E
    beside(programs, others, other_outs, scratch, steps)

    @pl.when(pl.program_id(1) == 0)
    def _():
        visible_bias(bias_ref, position_ref[pl.program_id(0)], chunks)

    query = query_ref[...]
    largest = None
    for chunk in range(chunks):
        keys = key_ref[0, chunk * BLK : (chunk + 1) * BLK, :]
        score = rows_by_rows(keys, query) + bias_ref[chunk]
        score_ref[chunk] = score
        top = jnp.max(score.reshape(BLK // 8, 8, BLK), axis=0)
        largest = top if largest is None else jnp.maximum(largest, top)
    largest = jnp.max(largest, axis=0, keepdims=True)
    total = jnp.zeros((8, BLK), F32)
    mixed = jnp.zeros((HD, BLK), F32)
    for chunk in range(chunks):
        weight = jnp.exp2((score_ref[chunk] - largest) * factor)
        total = total + jnp.sum(weight.reshape(BLK // 8, 8, BLK), axis=0)
        values = value_t_ref[0, :, chunk * BLK : (chunk + 1) * BLK]
        mixed = mixed + jnp.dot(values, weight.astype(BF16), preferred_element_type=F32)
    total = jnp.sum(total, axis=0, keepdims=True)
    mixed_ref[...] = (mixed / total).T.astype(BF16)
    logsum_ref[0, 0] = largest * factor + jnp.log2(total)


def attend(queries, keysets, positions, programs, arrays, number):
    rows, width = queries.shape
    blocks, heads = rows // BLK, width // HD
    keys = keysets[:, :, :HD]
    values_t = keysets[:, :, HD:].transpose(0, 2, 1)
    count = keysets.shape[1]
    out = pl.pallas_call(
        functools.partial(attend_kernel, programs, blocks * heads),
        grid=(blocks, heads),
        out_shape=[
            jax.ShapeDtypeStruct((rows, width), BF16),
            jax.ShapeDtypeStruct((blocks, heads, 1, BLK), F32),
        ]
        + [one.out for one in programs],
        in_specs=[
            pl.BlockSpec(memory_space=pltpu.SMEM),
            pl.BlockSpec((BLK, HD), lambda b, h: (b, h)),
            pl.BlockSpec((1, count, HD), lambda b, h: (b, 0, 0)),
            pl.BlockSpec((1, HD, count), lambda b, h: (b, 0, 0)),
        ]
        + [one.in_spec for one in programs],
        out_specs=[
            pl.BlockSpec((BLK, HD), lambda b, h: (b, h)),
            pl.BlockSpec((1, 1, 1, BLK), lambda b, h: (b, h, 0, 0)),
        ]
        + [one.out_spec for one in programs],
        scratch_shapes=[
            pltpu.VMEM((PBLK + 1, BLK, BLK), F32),
            pltpu.VMEM((PBLK + 1, BLK, BLK), F32),
        ]
        + [held for one in programs for held in one.scratch()],
        compiler_params=pltpu.CompilerParams(
            collective_id=number, has_side_effects=True, vmem_limit_bytes=VMEM_BYTES
        ),
        cost_estimate=pl.CostEstimate(
            flops=4 * rows * width * count,
            bytes_accessed=8 * rows * width,
            transcendentals=rows * heads * count,
        ),
    )(positions, queries, keys, values_t, *arrays)
    return out[0], out[1], out[2:]


def attend_back_kernel(programs, steps, *refs):
    count = len(programs)
    (position_ref, query_ref, grad_ref, mixed_ref, logsum_ref), refs = refs[:5], refs[5:]
    (key_ref, key_t_ref, value_ref), refs = refs[:3], refs[3:]
    others, refs = refs[:count], refs[count:]
    (grad_query_ref, set_ref), refs = refs[:2], refs[2:]
    other_outs, refs = refs[:count], refs[count:]
    bias_ref, scratch = refs[0], refs[1:]
    chunks = PBLK + 1
    scale = HD**-0.5
    block, head = pl.program_id(0), pl.program_id(1)
    beside(programs, others, other_outs, scratch, steps)

    @pl.when(head == 0)
    def _():
        visible_bias(bias_ref, position_ref[block], chunks)
        set_ref[...] = jnp.zeros_like(set_ref)

    query, grad = query_ref[...], grad_ref[...]
    inner = jnp.sum(grad.astype(F32) * mixed_ref[...].astype(F32), axis=1, keepdims=True)
    inner = jnp.broadcast_to(inner, (BLK, HD)).T[:1, :]
    logsum = logsum_ref[0, 0]
    grad_query = jnp.zeros((HD, BLK), F32)
    for chunk in range(chunks):
        cut = slice(chunk * BLK, (chunk + 1) * BLK)
        score = rows_by_rows(key_ref[0, cut, :], query)
        weight = jnp.exp2(score * (scale * LOG2E) + bias_ref[chunk] - logsum)
        grad_weight = rows_by_rows(value_ref[0, cut, :], grad)
        grad_score = (weight * (grad_weight - inner)).astype(BF16)
        set_ref[0, cut, :HD] += jnp.dot(grad_score, query, preferred_element_type=F32)
        set_ref[0, cut, HD:] += jnp.dot(weight.astype(BF16), grad, preferred_element_type=F32)
        grad_query = grad_query + jnp.dot(
            key_t_ref[0, :, cut], grad_score, preferred_element_type=F32
        )
    grad_query_ref[...] = (grad_query * scale).T.astype(BF16)

    @pl.when(head == pl.num_programs(1) - 1)
    def _():
        set_ref[0, :, :HD] = set_ref[0, :, :HD] * scale


def attend_back(queries, grads, mixed, logsums, keysets, positions, programs, arrays, number):
    rows, width = queries.shape
    blocks, heads = rows // BLK, width // HD
    keys, values = keysets[:, :, :HD], keysets[:, :, HD:]
    count = keysets.shape[1]
    by_head = pl.BlockSpec((BLK, HD), lambda b, h: (b, h))
    by_block = pl.BlockSpec((1, count, HD), lambda b, h: (b, 0, 0))
    out = pl.pallas_call(
        functools.partial(attend_back_kernel, programs, blocks * heads),
        grid=(blocks, heads),
        out_shape=[
            jax.ShapeDtypeStruct((rows, width), BF16),
            jax.ShapeDtypeStruct((blocks, count, 2 * HD), F32),
        ]
        + [one.out for one in programs],
        in_specs=[
            pl.BlockSpec(memory_space=pltpu.SMEM),
            by_head,
            by_head,
            by_head,
            pl.BlockSpec((1, 1, 1, BLK), lambda b, h: (b, h, 0, 0)),
            by_block,
            pl.BlockSpec((1, HD, count), lambda b, h: (b, 0, 0)),
            by_block,
        ]
        + [one.in_spec for one in programs],
        out_specs=[by_head, pl.BlockSpec((1, count, 2 * HD), lambda b, h: (b, 0, 0))]
        + [one.out_spec for one in programs],
        scratch_shapes=[pltpu.VMEM((PBLK + 1, BLK, BLK), F32)]
        + [held for one in programs for held in one.scratch()],
        compiler_params=pltpu.CompilerParams(
            collective_id=number, has_side_effects=True, vmem_limit_bytes=VMEM_BYTES
        ),
        cost_estimate=pl.CostEstimate(
            flops=10 * rows * width * count,
            bytes_accessed=16 * rows * width,
            transcendentals=rows * heads * count,
        ),
    )(positions, queries, grads, mixed, logsums, keys, keys.transpose(0, 2, 1), values, *arrays)
    return out[0], out[1], out[2:]


def by_slot_kernel(slot_ref, set_ref, out_ref, table_ref):
    blocks, chunks = slot_ref.shape
    per_device = out_ref.shape[2] // BLK

    def clear(index, carry):
        table_ref[index] = jnp.zeros(table_ref.shape[1:], F32)
        return carry

    def give(index, carry):
        holder, place = index // per_device, index % per_device
        rows = pl.ds(pl.multiple_of(place * BLK, BLK), BLK)
        out_ref[holder, 0, rows, :] = table_ref[index, :, :HD].astype(BF16)
        out_ref[holder, 1, rows, :] = table_ref[index, :, HD:].astype(BF16)
        return carry

    lax.fori_loop(0, table_ref.shape[0], clear, 0)
    for block in range(blocks):
        for chunk in range(chunks):
            cut = slice(chunk * BLK, (chunk + 1) * BLK)
            table_ref[slot_ref[block, chunk]] += set_ref[block, cut, :]
    lax.fori_loop(0, table_ref.shape[0], give, 0)


def by_slot(sets, key_slots, slot_count):
    blocks = sets.shape[0]
    return pl.pallas_call(
        by_slot_kernel,
        out_shape=jax.ShapeDtypeStruct((slot_count // blocks, 2, blocks * BLK, HD), BF16),
        in_specs=[
            pl.BlockSpec(memory_space=pltpu.SMEM),
            pl.BlockSpec(memory_space=pltpu.VMEM),
        ],
        out_specs=pl.BlockSpec(memory_space=pltpu.VMEM),
        scratch_shapes=[pltpu.VMEM((slot_count, BLK, 2 * HD), F32)],
        compiler_params=pltpu.CompilerParams(vmem_limit_bytes=VMEM_BYTES),
    )(key_slots, sets)


def body(
    hidden_in,
    block_order,
    attn_norm_gain,
    attn_norm_bias,
    query_weight,
    query_bias,
    keyval_weight,
    value_bias,
    proj_weight,
    proj_bias,
    mlp_norm_gain,
    mlp_norm_bias,
    up_weight,
    up_bias,
    down_weight,
    down_bias,
    out_cotangent,
):
    rows_dev = hidden_in.shape[0]
    half_rows = rows_dev // 2
    width = hidden_in.shape[1]
    blocks_dev = rows_dev // BLK
    slot_count = block_order.shape[1]
    group_blocks = PBLK + CONTS
    heads_dev = query_bias.shape[0] // HD
    head_width = heads_dev * HD
    core = lax.axis_index("tp")
    quarter = lax.axis_index("fsdp") * lax.axis_size("pair") + lax.axis_index("pair")
    quarters = lax.axis_size("fsdp") * lax.axis_size("pair")
    hidden_dev = up_weight.shape[1] // quarters

    def own_half(values):
        return lax.dynamic_slice_in_dim(values, core * half_rows, half_rows, axis=0)

    def other_half(values):
        return lax.dynamic_slice_in_dim(values, (1 - core) * half_rows, half_rows, axis=0)

    def in_order(mine, other, axis=0):
        first = jnp.where(core == 0, mine, other)
        second = jnp.where(core == 0, other, mine)
        return jnp.concatenate([first, second], axis=axis)

    def sum_halves(values):
        return own_half(values) + swap_tp(other_half(values))

    def join_halves(values):
        return in_order(values, swap_tp(values))

    gain_one = attn_norm_gain.astype(F32)
    shift_one = attn_norm_bias.astype(F32)
    gain_two = mlp_norm_gain.astype(F32)
    shift_two = mlp_norm_bias.astype(F32)

    slot_ids = jnp.arange(slot_count, dtype=jnp.int32)
    ordering = block_order[0]
    inverse = jnp.sum(
        jnp.where(ordering[None, :] == slot_ids[:, None], slot_ids[None, :], 0), axis=1
    )
    ctx_index = lax.axis_index("line") * lax.axis_size("pair") + lax.axis_index("pair")
    first_slot = ctx_index * blocks_dev
    my_slots = first_slot + jnp.arange(blocks_dev, dtype=jnp.int32)
    my_blocks = lax.dynamic_slice_in_dim(ordering, first_slot, blocks_dev)
    positions = my_blocks % group_blocks
    group_base = my_blocks // group_blocks * group_blocks
    prompt_slots = jnp.take(
        inverse, group_base[:, None] + jnp.arange(PBLK, dtype=jnp.int32)[None, :]
    )
    key_slots = jnp.concatenate([prompt_slots, my_slots[:, None]], axis=1)

    keyval_cut = lax.dynamic_slice_in_dim(keyval_weight, core * HD, HD, axis=1)
    first_cut = jnp.concatenate([query_weight, keyval_cut], axis=1)
    down_cut, up_cut, first_all = run_programs(
        [Exchange(down_weight, True), Exchange(up_weight, True), rows_gather(first_cut)],
        [down_weight, up_weight, first_cut],
        1,
    )
    first_all = flat(first_all)

    stream = hidden_in.astype(F32)
    normed_one = layer_norm(stream, gain_one, shift_one).astype(BF16)
    value_shift = jnp.where(core == 1, value_bias.astype(F32), 0.0)
    first_shift = jnp.concatenate([query_bias.astype(F32), value_shift])
    first_low = (jnp.dot(normed_one, first_all, preferred_element_type=F32) + first_shift).astype(
        BF16
    )
    query_low = first_low[:, :head_width]
    part_low = first_low[:, head_width:]
    keyval_every = gather_ctx(part_low, 4)
    keyval_every, down_cut, up_cut = lax.optimization_barrier((keyval_every, down_cut, up_cut))
    down_all = gather_line(down_cut)
    up_all = gather_line(up_cut)
    keyval_low = in_order(part_low, swap_tp(part_low), axis=1)
    keyval_table = keyval_every.transpose(0, 1, 3, 2, 4).reshape(slot_count, BLK, 2 * HD)
    own_table = keyval_low.reshape(blocks_dev, 1, BLK, 2 * HD)
    keysets = jnp.concatenate([keyval_table[prompt_slots], own_table], axis=1)
    keysets = keysets.reshape(blocks_dev, (PBLK + 1) * BLK, 2 * HD)
    cotangent = own_half(out_cotangent)
    cotangent_line = to_line_order(cotangent)
    mixed_low, logsums, (proj_all, cotangent_all) = attend(
        query_low,
        keysets,
        positions,
        [rows_gather(proj_weight), plane_gather(cotangent_line)],
        [proj_weight, cotangent_line],
        2,
    )
    proj_all, cotangent_all = flat(proj_all), flat(cotangent_all)
    proj_part = jnp.einsum("rk,ok->ro", mixed_low, proj_all, preferred_element_type=F32)
    middle = own_half(stream) + sum_halves(proj_part) + proj_bias.astype(F32)

    normed_two = layer_norm(middle, gain_two, shift_two).astype(BF16)
    normed_two_line = to_line_order(normed_two)
    normed_two_all = run_programs([plane_gather(normed_two_line)], [normed_two_line], 6)[0]
    normed_two_all = flat(normed_two_all)
    up_shift = lax.dynamic_slice_in_dim(up_bias, quarter * hidden_dev, hidden_dev).astype(F32)
    grad_act = jnp.dot(cotangent_all, down_all, preferred_element_type=F32)
    pre_act = jnp.dot(normed_two_all, up_all, preferred_element_type=F32) + up_shift
    act, gelu_pull = jax.vjp(gelu_tanh, pre_act)
    act_low = act.astype(BF16)
    grad_pre_wide = gelu_pull(grad_act)[0]
    grad_pre = grad_pre_wide.astype(BF16)
    normed_two_part = jnp.einsum("rf,df->rd", grad_pre, up_all, preferred_element_type=F32)
    plane_two, plane_parts = plane_sum(normed_two_part)
    grad_normed_two = from_line_order(run_programs([plane_two], [plane_parts], 7)[0])
    down_part = jnp.einsum("rf,of->ro", act_low, down_all, preferred_element_type=F32)
    grad_up_bias = jnp.sum(grad_pre, axis=0, dtype=F32)
    down_weight_grad = jnp.einsum("ro,rf->of", cotangent_all, act_low, preferred_element_type=F32)
    up_weight_grad = jnp.einsum("rd,rf->df", normed_two_all, grad_pre, preferred_element_type=F32)
    down_cut_grad = sum_line(down_weight_grad)
    up_cut_grad = sum_line(up_weight_grad)

    norm_two_pull = jax.vjp(layer_norm, middle, gain_two, shift_two)[1]
    grad_mid_norm, grad_mlp_norm_gain, grad_mlp_norm_bias = norm_two_pull(grad_normed_two)
    grad_middle = cotangent.astype(F32) + grad_mid_norm
    grad_down_bias = jnp.sum(cotangent, axis=0, dtype=F32)

    grad_attn_half = grad_middle.astype(BF16)
    grad_proj_bias = jnp.sum(grad_attn_half, axis=0, dtype=F32)
    grad_attn = join_halves(grad_attn_half)
    proj_weight_grad = jnp.einsum("ro,rk->ok", grad_attn, mixed_low, preferred_element_type=F32)
    grad_mixed = jnp.einsum("ro,ok->rk", grad_attn, proj_all, preferred_element_type=F32).astype(
        BF16
    )
    sum_proj, proj_parts = rows_sum(proj_weight_grad)
    sum_down, down_parts = plane_sum(down_part)
    grad_query, grad_sets, (grad_proj_weight, mlp_out) = attend_back(
        query_low,
        grad_mixed,
        mixed_low,
        logsums,
        keysets,
        positions,
        [sum_proj, sum_down],
        [proj_parts, down_parts],
        3,
    )
    mlp_out = from_line_order(mlp_out) + down_bias.astype(F32)
    layer_out = join_halves((middle + mlp_out).astype(BF16))
    grad_table = by_slot(grad_sets, key_slots, slot_count)
    grad_query_bias = jnp.sum(grad_query, axis=0, dtype=F32)
    grad_parts = grad_table.reshape(
        lax.axis_size("line"), lax.axis_size("pair"), 2, rows_dev, HD
    )
    grad_part = sum_ctx(grad_parts, 12).astype(BF16)
    grad_value_bias = jnp.where(core == 1, jnp.sum(grad_part, axis=0, dtype=F32), 0.0)
    grad_first = jnp.concatenate([grad_query, grad_part], axis=1)
    normed_one_part = jnp.einsum("rk,dk->rd", grad_first, first_all, preferred_element_type=F32)
    grad_normed_one = sum_halves(normed_one_part)
    first_weight_grad = jnp.einsum("rd,rk->dk", normed_one, grad_first, preferred_element_type=F32)
    norm_one_pull = jax.vjp(layer_norm, own_half(stream), gain_one, shift_one)[1]
    grad_in_norm, grad_attn_norm_gain, grad_attn_norm_bias = norm_one_pull(grad_normed_one)
    input_grad = join_halves((grad_middle + grad_in_norm).astype(BF16))

    query_slots = jnp.zeros((2 * head_width,), F32)
    query_slots = lax.dynamic_update_slice_in_dim(
        query_slots, grad_query_bias, core * head_width, axis=0
    )
    hidden_slots = jnp.zeros((2 * quarters * hidden_dev,), F32)
    hidden_slots = lax.dynamic_update_slice_in_dim(
        hidden_slots, grad_up_bias, (core * quarters + quarter) * hidden_dev, axis=0
    )
    pieces = [
        grad_attn_norm_gain,
        grad_attn_norm_bias,
        grad_proj_bias,
        grad_mlp_norm_gain,
        grad_mlp_norm_bias,
        grad_down_bias,
        grad_value_bias,
        query_slots,
        hidden_slots,
    ]
    sum_first, first_parts = rows_sum(first_weight_grad)
    total, padded = total_of(jnp.concatenate(pieces))
    grad_first_weight, grad_down_weight, grad_up_weight, summed = run_programs(
        [sum_first, Exchange(down_cut_grad, False), Exchange(up_cut_grad, False), total],
        [first_parts, down_cut_grad, up_cut_grad, padded],
        13,
    )
    grad_down_weight, grad_up_weight = grad_down_weight.astype(F32), grad_up_weight.astype(F32)
    grad_query_weight = grad_first_weight[:, :head_width]
    grad_cut = grad_first_weight[:, head_width:]
    grad_keyval_weight = in_order(grad_cut, swap_tp(grad_cut), axis=1)
    summed = summed.reshape(-1)
    cuts, start = [], 0
    for piece in pieces:
        cuts.append(summed[start : start + piece.shape[0]])
        start += piece.shape[0]
    sum_query = lax.dynamic_slice_in_dim(cuts[7], core * head_width, head_width)
    sum_up = lax.dynamic_slice_in_dim(cuts[8], core * quarters * hidden_dev, quarters * hidden_dev)
    return (
        layer_out,
        input_grad,
        cuts[0],
        cuts[1],
        grad_query_weight,
        sum_query,
        grad_keyval_weight,
        cuts[6],
        grad_proj_weight,
        cuts[2],
        cuts[3],
        cuts[4],
        grad_up_weight,
        sum_up,
        grad_down_weight,
        cuts[5],
    )


def solution(mesh):
    fsdp, ctx, tp = mesh.devices.shape
    grid = Mesh(mesh.devices.reshape(fsdp, ctx // 2, 2, tp), EVERY)
    by_rows = P(ROWS, None)
    by_both = P(ROWS, "tp")
    return jax.shard_map(
        body,
        mesh=grid,
        in_specs=(
            by_rows,
            P("fsdp", None),
            P(),
            P(),
            by_both,
            P("tp"),
            by_rows,
            P(),
            by_both,
            P(),
            P(),
            P(),
            by_both,
            P("tp"),
            by_both,
            P(),
            by_rows,
        ),
        out_specs=(
            by_rows,
            by_rows,
            P(),
            P(),
            by_both,
            P("tp"),
            by_rows,
            P(),
            by_both,
            P(),
            P(),
            P(),
            by_both,
            P("tp"),
            by_both,
            P(),
        ),
        check_vma=False,
    )
```

```python
import functools

import jax
import jax.numpy as jnp
from jax import lax
from jax.experimental import pallas as pl
from jax.experimental.pallas import tpu as pltpu
from jax.sharding import Mesh, PartitionSpec as P

HD = 128
BLK = 256
PBLK = 8
CONTS = 8
EPSILON = 1e-05
MASKED = -1e30
F32 = jnp.float32
BF16 = jnp.bfloat16
ROWS = ("fsdp", "line", "pair")
EVERY = ("fsdp", "line", "pair", "tp")


def layer_norm(values, norm_gain, norm_shift):
    average = jnp.mean(values, axis=-1, keepdims=True)
    centered = values - average
    spread = jnp.mean(centered * centered, axis=-1, keepdims=True)
    return centered * lax.rsqrt(spread + EPSILON) * norm_gain + norm_shift


MESH_ID = pl.DeviceIdType.MESH
VMEM_BYTES = 60 * 1024 * 1024
SIDE = ("pair", "fsdp")
FRONT = ("fsdp", "pair")


def here():
    return {name: lax.axis_index(name) for name in EVERY}


def flip(place, step):
    place = dict(place)
    if isinstance(step, str):
        place[step] = 1 - place[step]
    else:
        core = place["tp"]
        for name, used in ((step[0], 1 - core), (step[1], core)):
            place[name] = place[name] + (1 - 2 * place[name]) * used
    return place


def along(place, amount):
    return dict(place, line=place["line"] + amount)


def remote(source, target, send_sem, recv_sem, place):
    return pltpu.make_async_remote_copy(
        src_ref=source,
        dst_ref=target,
        send_sem=send_sem,
        recv_sem=recv_sem,
        device_id=place,
        device_id_type=MESH_ID,
    )


def top_bit(bits):
    return bits.bit_length() - 1


def add_blocks(target, first, second, rows):
    tile = min(rows, 64)

    def one(index, carry):
        cut = pl.ds(pl.multiple_of(index * tile, tile), tile)
        total = first(cut).astype(F32)
        if second is not None:
            total = total + second(cut).astype(F32)
        target[cut, :] = total.astype(target.dtype)
        return carry

    lax.fori_loop(0, rows // tile, one, 0)


def rows_of(ref):
    return lambda cut: ref[cut, :]


class Gather:
    def __init__(self, values, steps, lines, shape, slot):
        self.steps, self.lines, self.slot = steps, lines, slot
        self.out = jax.ShapeDtypeStruct(shape, values.dtype)
        self.in_spec = self.out_spec = pl.BlockSpec(memory_space=pl.ANY)

    def scratch(self):
        parts = 1 << len(self.steps)
        return [
            pltpu.SemaphoreType.DMA(()),
            pltpu.SemaphoreType.DMA((2, self.lines)),
            pltpu.SemaphoreType.DMA((self.lines,)),
            pltpu.SemaphoreType.DMA((self.lines, max(1, len(self.steps)) * parts)),
            pltpu.SemaphoreType.DMA((self.lines, parts)),
        ]

    def stages(self, me, x_ref, out_ref, own_sem, line_send, line_recv, send, recv):
        steps, lines, slot = self.steps, self.lines, self.slot
        count = len(steps)
        my_line = me["line"] if lines > 1 else 0

        def block(bits, shard):
            place = me
            for k in reversed(range(count)):
                if bits >> k & 1:
                    place = flip(place, steps[k])
            return slot(out_ref, dict(place, line=shard))

        def to_step(k, bits, shard, source):
            return remote(
                source,
                block(bits, shard),
                send.at[shard, k * (1 << count) + bits],
                recv.at[shard, bits | 1 << k],
                flip(me, steps[k]),
            )

        def to_line(amount, shard, source):
            return remote(
                source,
                block(0, shard),
                line_send.at[(amount + 1) // 2, shard],
                line_recv.at[shard],
                along(me, amount),
            )

        def send_on(bits, shard, source):
            for k in range(top_bit(bits) + 1, count):
                to_step(k, bits, shard, source).start()

        def at_distance(distance, work):
            if distance == 0:
                work(my_line, 0)
                return
            for amount in (1, -1):
                shard = my_line - amount * distance
                pl.when((shard >= 0) & (shard < lines))(functools.partial(work, shard, amount))

        def line_inside(amount):
            there = my_line + amount
            return (there >= 0) & (there < lines)

        own = pltpu.make_async_copy(x_ref, block(0, my_line), own_sem)

        def begin():
            if lines > 1:
                for amount in (1, -1):
                    pl.when(line_inside(amount))(
                        lambda amount=amount: to_line(amount, my_line, x_ref).start()
                    )
            send_on(0, my_line, x_ref)
            own.start()

        def line_arrival(shard, amount):
            remote(
                block(0, shard), block(0, shard), line_send.at[0, shard], line_recv.at[shard], me
            ).wait_recv()
            pl.when(line_inside(amount))(lambda: to_line(amount, shard, block(0, shard)).start())
            send_on(0, shard, block(0, shard))

        def level_arrival(level, shard, amount):
            for bits in range(1 << level, 2 << level):
                remote(
                    block(bits, shard),
                    block(bits, shard),
                    send.at[shard, 0],
                    recv.at[shard, bits],
                    me,
                ).wait_recv()
                send_on(bits, shard, block(bits, shard))

        def tick(number):
            if number < lines:
                at_distance(number, line_arrival)
            for level in range(count):
                distance = number - 1 - level
                if 0 <= distance < lines:
                    at_distance(distance, functools.partial(level_arrival, level))

        def end():
            own.wait()
            if lines > 1:
                for amount in (1, -1):
                    for distance in range(lines):
                        shard = my_line - amount * distance
                        pl.when((shard >= 0) & (shard < lines) & line_inside(amount))(
                            lambda amount=amount, shard=shard: to_line(
                                amount, shard, block(0, shard)
                            ).wait_send()
                        )
            for shard in range(lines):
                for bits in range(1 << count):
                    for k in range(top_bit(bits) + 1, count):
                        to_step(k, bits, shard, block(bits, shard)).wait_send()

        ticks = [functools.partial(tick, number) for number in range(1, lines + count)]
        return [begin] + ticks + [end]


class Sum:
    def __init__(self, steps, lines, rows, columns, slot, shared=0):
        self.steps, self.lines, self.rows, self.columns = steps, lines, rows, columns
        self.slot, self.shared = slot, shared
        self.out = jax.ShapeDtypeStruct((rows, columns + shared), F32)
        self.in_spec = pl.BlockSpec(memory_space=pl.ANY)
        self.out_spec = pl.BlockSpec(memory_space=pltpu.VMEM)

    def scratch(self):
        count, lines = len(self.steps), self.lines
        sizes = [1 << (count - 1 - k) for k in range(count)]
        block = (self.rows, self.columns)
        return (
            [pltpu.VMEM((lines, sizes[0]) + block, BF16)]
            + [pltpu.VMEM((lines, size) + block, BF16) for size in sizes]
            + [pltpu.VMEM((2, lines) + (block if lines > 1 else (16, 128)), BF16)]
            + [pltpu.SemaphoreType.DMA((lines, sizes[0]))]
            + [pltpu.SemaphoreType.DMA((lines, size)) for size in sizes] * 2
            + [pltpu.SemaphoreType.DMA((2, lines))] * 2
            + [pltpu.SemaphoreType.DMA((2,))]
        )

    def stages(self, me, x_ref, whole_ref, own, *rest):
        out_ref = whole_ref.at[:, : self.columns] if self.shared else whole_ref
        steps, lines, rows, slot = self.steps, self.lines, self.rows, self.slot
        count = len(steps)
        held, rest = rest[:count], rest[count:]
        on_line, own_sem, rest = rest[0], rest[1], rest[2:]
        send, recv = rest[:count], rest[count : 2 * count]
        line_send, line_recv, share_sem = rest[2 * count :]
        my_line = me["line"] if lines > 1 else 0
        last = count - 1

        def target_of(bits, shard):
            place = me
            for k in range(count):
                if bits >> k & 1:
                    place = flip(place, steps[k])
            return dict(place, line=shard)

        def store(k, shard, bits):
            return held[k].at[shard, bits >> (k + 1)]

        def own_copy(shard, bits):
            return pltpu.make_async_copy(
                slot(x_ref, target_of(bits, shard)),
                own.at[shard, bits >> 1],
                own_sem.at[shard, bits >> 1],
            )

        def copy(k, shard, bits):
            source = slot(x_ref, target_of(bits, shard)) if k == 0 else store(k - 1, shard, bits)
            return remote(
                source,
                store(k, shard, bits ^ (1 << k)),
                send[k].at[shard, bits >> (k + 1)],
                recv[k].at[shard, bits >> (k + 1)],
                flip(me, steps[k]),
            )

        def parts_of(k):
            return [high << (k + 1) for high in reversed(range(1 << (count - 1 - k)))]

        def send_first(shard, amount):
            for bits in parts_of(0):
                copy(0, shard, bits | 1).start()

        def own_first(shard, amount):
            for bits in parts_of(0):
                own_copy(shard, bits).start()

        def take_step(k, shard, amount, parts=None):
            for bits in parts or parts_of(k):
                copy(k, shard, bits | 1 << k).wait_recv()
                arrived = store(k, shard, bits)
                if k == 0:
                    own_copy(shard, bits).wait()
                    mine = own.at[shard, bits >> 1]
                else:
                    mine = store(k - 1, shard, bits)
                add_blocks(arrived, rows_of(mine), rows_of(arrived), rows)
                if k + 1 < count and bits >> (k + 1) & 1:
                    copy(k + 1, shard, bits).start()

        def line_inside(amount):
            there = my_line + amount
            return (there >= 0) & (there < lines)

        def line_copy(amount, shard):
            way = (amount + 1) // 2
            return remote(
                on_line.at[way, shard],
                on_line.at[way, shard],
                line_send.at[way, shard],
                line_recv.at[way, shard],
                along(me, amount),
            )

        def each(distance, work):
            if distance == 0:
                work(my_line, 0)
                return
            for amount in (1, -1):
                shard = my_line + amount * distance
                pl.when((shard >= 0) & (shard < lines))(functools.partial(work, shard, amount))

        def line_step(shard, amount):
            done = held[last].at[shard, 0]
            moving = on_line.at[(amount + 1) // 2, shard]

            @pl.when(line_inside(-amount))
            def _():
                line_copy(amount, shard).wait_recv()
                add_blocks(moving, rows_of(moving), rows_of(done), rows)

            @pl.when(jnp.logical_not(line_inside(-amount)))
            def _():
                add_blocks(moving, rows_of(done), None, rows)

            line_copy(amount, shard).start()

        order = list(reversed(range(lines)))

        def begin():
            for distance in order:
                each(distance, send_first)
            for distance in order:
                each(distance, own_first)

        def tick(number):
            for k in reversed(range(count)):
                index = number - k
                if 0 <= index < lines:
                    each(order[index], functools.partial(take_step, k))
            index = number - count
            if 0 <= index < lines and order[index] > 0:
                each(order[index], line_step)

        def end():
            final = held[last].at[my_line, 0]
            add_blocks(out_ref, rows_of(final), None, rows)
            if lines > 1:
                for amount in (1, -1):

                    @pl.when(line_inside(-amount))
                    def _():
                        line_copy(amount, my_line).wait_recv()
                        moving = on_line.at[(amount + 1) // 2, my_line]
                        add_blocks(out_ref, rows_of(out_ref), rows_of(moving), rows)

                for amount in (1, -1):
                    for distance in range(1, lines):
                        shard = my_line + amount * distance
                        pl.when((shard >= 0) & (shard < lines))(
                            lambda amount=amount, shard=shard: line_copy(amount, shard).wait_send()
                        )
            if self.shared:
                share = remote(
                    whole_ref.at[:, self.columns - self.shared : self.columns],
                    whole_ref.at[:, self.columns :],
                    share_sem.at[0],
                    share_sem.at[1],
                    flip(me, "tp"),
                )
                share.start()
                share.wait()
            for k in range(count):
                for shard in range(lines):
                    for bits in parts_of(k):
                        copy(k, shard, bits | 1 << k).wait_send()

        if lines == 1:
            ticks = [
                functools.partial(take_step, k, 0, 0, [bits]) for k in range(count) for bits in parts_of(k)
            ]
        else:
            ticks = [functools.partial(tick, number) for number in range(lines + count)]
        return [begin] + ticks + [end]


DIRECT = (("pair",), ("fsdp",), ("pair", "fsdp"))


def move(me, names):
    place = me
    for name in names:
        place = flip(place, name)
    return place


def quarter_of(place):
    return place["fsdp"] * 2 + place["pair"]


class Exchange:
    steps, lines, corner = ("pair", "fsdp"), 1, True

    def __init__(self, values, spread):
        self.spread = spread
        if spread:
            shape = (4, values.shape[0], values.shape[1] // 4)
        else:
            shape = (values.shape[1], values.shape[2] * 4)
        self.out = jax.ShapeDtypeStruct(shape, values.dtype)
        self.in_spec = self.out_spec = pl.BlockSpec(memory_space=pl.ANY)

    def scratch(self):
        return [
            pltpu.SemaphoreType.DMA(()),
            pltpu.SemaphoreType.DMA((3,)),
            pltpu.SemaphoreType.DMA((3,)),
        ]

    def stages(self, me, x_ref, out_ref, own_sem, send, recv):
        def wide(ref, quarter):
            columns = ref.shape[1] // 4
            return ref.at[:, pl.ds(pl.multiple_of(quarter * columns, columns), columns)]

        def narrow(ref, quarter):
            return ref.at[quarter]

        cut, put = (wide, narrow) if self.spread else (narrow, wide)
        copies = []
        for k, names in reversed(list(enumerate(DIRECT))):
            there = move(me, names)
            copies.append(
                remote(
                    cut(x_ref, quarter_of(there)),
                    put(out_ref, quarter_of(me)),
                    send.at[k],
                    recv.at[k],
                    there,
                )
            )
        copies.append(
            pltpu.make_async_copy(
                cut(x_ref, quarter_of(me)), put(out_ref, quarter_of(me)), own_sem
            )
        )

        def begin():
            for one in copies:
                one.start()

        def end():
            for one in copies:
                one.wait()

        return [begin, end]


class Total:
    steps = ("tp", "pair", "fsdp")

    def __init__(self, values, lines):
        self.lines, self.out = lines, jax.ShapeDtypeStruct(values.shape, F32)
        self.in_spec = self.out_spec = pl.BlockSpec(memory_space=pltpu.VMEM)

    def scratch(self):
        shape, lines = self.out.shape, self.lines
        return [
            pltpu.VMEM((3, 2) + shape, F32),
            pltpu.VMEM((lines,) + shape, F32),
            pltpu.SemaphoreType.DMA((3,)),
            pltpu.SemaphoreType.DMA((3,)),
            pltpu.SemaphoreType.DMA((2, lines)),
            pltpu.SemaphoreType.DMA((lines,)),
        ]

    def stages(self, me, x_ref, out_ref, moved, on_line, send, recv, line_send, line_recv):
        lines = self.lines

        def swap(k):
            return remote(
                moved.at[k, 0], moved.at[k, 1], send.at[k], recv.at[k], flip(me, self.steps[k])
            )

        def copy(amount, shard):
            return remote(
                on_line.at[shard],
                on_line.at[shard],
                line_send.at[(amount + 1) // 2, shard],
                line_recv.at[shard],
                along(me, amount),
            )

        def inside(amount):
            there = me["line"] + amount
            return (there >= 0) & (there < lines)

        def begin():
            moved[0, 0] = x_ref[...]
            swap(0).start()

        def after(k):
            swap(k).wait()
            if k < 2:
                moved[k + 1, 0] = moved[k, 0] + moved[k, 1]
                swap(k + 1).start()
                return
            on_line[me["line"]] = moved[k, 0] + moved[k, 1]
            for amount in (1, -1):
                pl.when(inside(amount))(lambda amount=amount: copy(amount, me["line"]).start())

        def hop(distance):
            for amount in (1, -1):
                shard = me["line"] - amount * distance

                @pl.when((shard >= 0) & (shard < lines))
                def _():
                    copy(amount, shard).wait_recv()
                    pl.when(inside(amount))(lambda: copy(amount, shard).start())

        def end():
            total = on_line[0]
            for shard in range(1, lines):
                total = total + on_line[shard]
            out_ref[...] = total
            for amount in (1, -1):
                for distance in range(lines):
                    shard = me["line"] - amount * distance
                    pl.when((shard >= 0) & (shard < lines) & inside(amount))(
                        lambda amount=amount, shard=shard: copy(amount, shard).wait_send()
                    )

        return (
            [begin]
            + [functools.partial(after, k) for k in range(3)]
            + [functools.partial(hop, distance) for distance in range(1, lines)]
            + [end]
        )


def greet(me, programs):
    barrier = pltpu.get_barrier_semaphore()
    lines = max(one.lines for one in programs)
    steps = list(dict.fromkeys(step for one in programs for step in one.steps))
    if SIDE in steps:
        steps = [step for step in steps if step not in ("pair", "fsdp")]
    places = [flip(me, step) for step in steps]
    if any(isinstance(one, Exchange) for one in programs):
        places.append(move(me, ("pair", "fsdp")))
    for place in places:
        pl.semaphore_signal(barrier, inc=1, device_id=place, device_id_type=MESH_ID)
    count = len(places)
    if lines > 1:
        for amount in (-1, 1):
            there = me["line"] + amount
            inside = (there >= 0) & (there < lines)

            @pl.when(inside)
            def _():
                pl.semaphore_signal(
                    barrier, inc=1, device_id=along(me, amount), device_id_type=MESH_ID
                )

            count = count + inside.astype(jnp.int32)
    pl.semaphore_wait(barrier, count)


def split_scratch(programs, refs):
    parts, start = [], 0
    for one in programs:
        size = len(one.scratch())
        parts.append(refs[start : start + size])
        start += size
    return parts


def schedule(programs, x_refs, out_refs, scratch):
    me = here()
    works = [(0.0, functools.partial(greet, me, programs))]
    for one, x_ref, out_ref, held in zip(programs, x_refs, out_refs, split_scratch(programs, scratch)):
        stages = one.stages(me, x_ref, out_ref, *held)
        places = getattr(one, "places", (0.0, 1.0))
        if len(places) == 2:
            places = spaced(places[0], places[1], len(stages))
        last = len(places) - 2
        works += [
            (places[-1] if k == len(stages) - 1 else places[min(k, last)], stage)
            for k, stage in enumerate(stages)
        ]
    return sorted(works, key=lambda work: work[0])


def placed(program, *places):
    program.places = list(places)
    return program


def spaced(start, stop, count):
    return [start + (stop - start) * k / (count - 1) for k in range(count)]


def run_programs(programs, arrays, number):
    count = len(programs)
    given = [k for k, array in enumerate(arrays) if not callable(array)]

    def kernel(*refs):
        in_refs, out_refs = refs[: len(given)], refs[len(given) : len(given) + count]
        in_refs = [
            array(out_refs) if callable(array) else in_refs[given.index(k)]
            for k, array in enumerate(arrays)
        ]
        for _, work in schedule(programs, in_refs, out_refs, refs[len(given) + count :]):
            work()

    return pl.pallas_call(
        kernel,
        out_shape=[one.out for one in programs],
        in_specs=[programs[k].in_spec for k in given],
        out_specs=[one.out_spec for one in programs],
        scratch_shapes=[held for one in programs for held in one.scratch()],
        compiler_params=pltpu.CompilerParams(
            collective_id=number, has_side_effects=True, vmem_limit_bytes=VMEM_BYTES
        ),
    )(*[arrays[k] for k in given])


def by_rows_slot(ref, at):
    return ref.at[at["fsdp"], at["line"], at["pair"]]


def by_plane_slot(ref, at):
    return ref.at[at["fsdp"], at["pair"], at["tp"]]


def by_ctx_slot(ref, at):
    return ref.at[at["tp"], at["line"], at["pair"]]


def rows_gather(values):
    lines = lax.axis_size("line")
    return Gather(values, (SIDE, FRONT), lines, (2, lines, 2) + values.shape, by_rows_slot)


def line_gather(shape, kind):
    lines = lax.axis_size("line")
    like = jax.ShapeDtypeStruct(shape, kind)
    return Gather(like, (), lines, (lines,) + shape, lambda ref, at: ref.at[at["line"]])


def columns_gather(values):
    lines, rows, columns = values.shape
    return Gather(
        values, (SIDE, FRONT), 1, (2, lines, 2, rows, columns), lambda ref, at: ref.at[at["fsdp"], :, at["pair"]]
    )


def rows_sum(values, shared=0):
    lines, (total, columns) = lax.axis_size("line"), values.shape
    rows = total // (4 * lines)
    parts = values.astype(BF16).reshape(2, lines, 2, rows, columns)
    return Sum((FRONT, SIDE), lines, rows, columns, by_rows_slot, shared), parts


def plane_gather(values):
    return Gather(values, (SIDE, FRONT, "tp"), 1, (2, 2, 2) + values.shape, by_plane_slot)


def plane_sum(values):
    rows, columns = values.shape[0] // 8, values.shape[1]
    parts = values.astype(BF16).reshape(2, 2, 2, rows, columns)
    return Sum(("tp", FRONT, SIDE), 1, rows, columns, by_plane_slot), parts


def flat(values):
    return values.reshape(-1, values.shape[-1])


def gather_ctx(values, number):
    lines = lax.axis_size("line")
    one = Gather(values, ("pair", "tp"), lines, (2, lines, 2) + values.shape, by_ctx_slot)
    return run_programs([one], [values], number)[0]


def ctx_sum(values):
    _, lines, _, rows, columns = values.shape
    return Sum(("tp", "pair"), lines, rows, columns, by_ctx_slot)


def total_of(values):
    size = values.shape[0]
    rows = -(-size // 1024) * 8
    padded = jnp.pad(values, (0, rows * 128 - size)).reshape(rows, 128)
    return Total(padded, lax.axis_size("line")), padded


LOG2E = 1.4426950408889634


def visible_bias(bias_ref, position, chunks):
    prompt = position < PBLK
    row = lax.broadcasted_iota(jnp.int32, (BLK, BLK), 0)
    column = lax.broadcasted_iota(jnp.int32, (BLK, BLK), 1)
    limit = jnp.where(prompt, position * BLK + column, PBLK * BLK)
    for chunk in range(chunks - 1):
        bias_ref[chunk] = jnp.where(row + chunk * BLK <= limit, 0.0, MASKED)
    own_limit = jnp.where(prompt, -1, column)
    bias_ref[chunks - 1] = jnp.where(row <= own_limit, 0.0, MASKED)


def rows_by_rows(left, right):
    return lax.dot_general(left, right, (((1,), (1,)), ((), ())), preferred_element_type=F32)


def beside(programs, in_refs, out_refs, scratch, step, steps):
    late = []
    for place, work in schedule(programs, in_refs, out_refs, scratch):
        if place < 1:
            pl.when(step == int(place * steps))(work)
        else:
            late.append(work)

    def finish():
        @pl.when(step == steps - 1)
        def _():
            for work in late:
                work()

    return finish


def attend_kernel(programs, steps, *refs):
    count = len(programs)
    (position_ref, slot_ref, query_ref, table_ref), refs = refs[:4], refs[4:]
    others, refs = refs[:count], refs[count:]
    (mixed_ref, logsum_ref), refs = refs[:2], refs[2:]
    other_outs, refs = refs[:count], refs[count:]
    (bias_ref, score_ref, value_t_ref), scratch = refs[:3], refs[3:]
    chunks = PBLK + 1
    block = pl.program_id(0)
    factor = HD**-0.5 * LOG2E
    step = pl.program_id(0) * pl.num_programs(1) + pl.program_id(1)
    finish = beside(programs, others, other_outs, scratch, step, steps)

    @pl.when(pl.program_id(1) == 0)
    def _():
        visible_bias(bias_ref, position_ref[block], chunks)
        for chunk in range(chunks):
            value_t_ref[chunk] = table_ref[1, slot_ref[block, chunk]].astype(F32).T.astype(BF16)

    query = query_ref[...]
    largest = None
    for chunk in range(chunks):
        keys = table_ref[0, slot_ref[block, chunk]]
        score = rows_by_rows(keys, query) + bias_ref[chunk]
        score_ref[chunk] = score
        top = jnp.max(score.reshape(BLK // 8, 8, BLK), axis=0)
        largest = top if largest is None else jnp.maximum(largest, top)
    largest = jnp.max(largest, axis=0, keepdims=True)
    total = jnp.zeros((8, BLK), F32)
    mixed = jnp.zeros((HD, BLK), F32)
    for chunk in range(chunks):
        weight = jnp.exp2((score_ref[chunk] - largest) * factor)
        total = total + jnp.sum(weight.reshape(BLK // 8, 8, BLK), axis=0)
        mixed = mixed + jnp.dot(
            value_t_ref[chunk], weight.astype(BF16), preferred_element_type=F32
        )
    total = jnp.sum(total, axis=0, keepdims=True)
    mixed_ref[...] = (mixed / total).T.astype(BF16)
    logsum_ref[0, 0] = largest * factor + jnp.log2(total)
    finish()


def attend(queries, table, positions, key_slots, programs, arrays, number):
    rows, width = queries.shape
    blocks, heads = rows // BLK, width // HD
    count = (PBLK + 1) * BLK
    out = pl.pallas_call(
        functools.partial(attend_kernel, programs, blocks * heads),
        grid=(blocks, heads),
        out_shape=[
            jax.ShapeDtypeStruct((rows, width), BF16),
            jax.ShapeDtypeStruct((blocks, heads, 1, BLK), F32),
        ]
        + [one.out for one in programs],
        in_specs=[
            pl.BlockSpec(memory_space=pltpu.SMEM),
            pl.BlockSpec(memory_space=pltpu.SMEM),
            pl.BlockSpec((BLK, HD), lambda b, h: (b, h)),
            pl.BlockSpec(memory_space=pltpu.VMEM),
        ]
        + [one.in_spec for one in programs],
        out_specs=[
            pl.BlockSpec((BLK, HD), lambda b, h: (b, h)),
            pl.BlockSpec((1, 1, 1, BLK), lambda b, h: (b, h, 0, 0)),
        ]
        + [one.out_spec for one in programs],
        scratch_shapes=[
            pltpu.VMEM((PBLK + 1, BLK, BLK), F32),
            pltpu.VMEM((PBLK + 1, BLK, BLK), F32),
            pltpu.VMEM((PBLK + 1, HD, BLK), BF16),
        ]
        + [held for one in programs for held in one.scratch()],
        compiler_params=pltpu.CompilerParams(
            collective_id=number, has_side_effects=True, vmem_limit_bytes=VMEM_BYTES
        ),
        cost_estimate=pl.CostEstimate(
            flops=4 * rows * width * count,
            bytes_accessed=8 * rows * width,
            transcendentals=rows * heads * count,
        ),
    )(positions, key_slots, queries, table, *arrays)
    return out[0], out[1], out[2:]


def attend_back_kernel(programs, steps, *refs):
    count = len(programs)
    (position_ref, slot_ref, query_ref, grad_ref, mixed_ref), refs = refs[:5], refs[5:]
    (logsum_ref, table_ref), refs = refs[:2], refs[2:]
    others, refs = refs[:count], refs[count:]
    (grad_query_ref, set_ref), refs = refs[:2], refs[2:]
    other_outs, refs = refs[:count], refs[count:]
    (bias_ref, key_t_ref), scratch = refs[:2], refs[2:]
    chunks = PBLK + 1
    scale = HD**-0.5
    block, head = pl.program_id(0), pl.program_id(1)
    step = pl.program_id(0) * pl.num_programs(1) + pl.program_id(1)
    finish = beside(programs, others, other_outs, scratch, step, steps)

    @pl.when(head == 0)
    def _():
        visible_bias(bias_ref, position_ref[block], chunks)
        set_ref[...] = jnp.zeros_like(set_ref)
        for chunk in range(chunks):
            key_t_ref[chunk] = table_ref[0, slot_ref[block, chunk]].astype(F32).T.astype(BF16)

    query, grad = query_ref[...], grad_ref[...]
    inner = jnp.sum(grad.astype(F32) * mixed_ref[...].astype(F32), axis=1, keepdims=True)
    inner = jnp.broadcast_to(inner, (BLK, HD)).T[:1, :]
    logsum = logsum_ref[0, 0]
    grad_query = jnp.zeros((HD, BLK), F32)
    for chunk in range(chunks):
        cut = slice(chunk * BLK, (chunk + 1) * BLK)
        slot = slot_ref[block, chunk]
        score = rows_by_rows(table_ref[0, slot], query)
        weight = jnp.exp2(score * (scale * LOG2E) + bias_ref[chunk] - logsum)
        grad_weight = rows_by_rows(table_ref[1, slot], grad)
        grad_score = (weight * (grad_weight - inner)).astype(BF16)
        set_ref[0, cut, :HD] += jnp.dot(grad_score, query, preferred_element_type=F32)
        set_ref[0, cut, HD:] += jnp.dot(weight.astype(BF16), grad, preferred_element_type=F32)
        grad_query = grad_query + jnp.dot(
            key_t_ref[chunk], grad_score, preferred_element_type=F32
        )
    grad_query_ref[...] = (grad_query * scale).T.astype(BF16)

    @pl.when(head == pl.num_programs(1) - 1)
    def _():
        set_ref[0, :, :HD] = set_ref[0, :, :HD] * scale

    finish()


def attend_back(
    queries, grads, mixed, logsums, table, positions, key_slots, programs, arrays, number
):
    rows, width = queries.shape
    blocks, heads = rows // BLK, width // HD
    count = (PBLK + 1) * BLK
    by_head = pl.BlockSpec((BLK, HD), lambda b, h: (b, h))
    out = pl.pallas_call(
        functools.partial(attend_back_kernel, programs, blocks * heads),
        grid=(blocks, heads),
        out_shape=[
            jax.ShapeDtypeStruct((rows, width), BF16),
            jax.ShapeDtypeStruct((blocks, count, 2 * HD), F32),
        ]
        + [one.out for one in programs],
        in_specs=[
            pl.BlockSpec(memory_space=pltpu.SMEM),
            pl.BlockSpec(memory_space=pltpu.SMEM),
            by_head,
            by_head,
            by_head,
            pl.BlockSpec((1, 1, 1, BLK), lambda b, h: (b, h, 0, 0)),
            pl.BlockSpec(memory_space=pltpu.VMEM),
        ]
        + [one.in_spec for one in programs],
        out_specs=[by_head, pl.BlockSpec((1, count, 2 * HD), lambda b, h: (b, 0, 0))]
        + [one.out_spec for one in programs],
        scratch_shapes=[
            pltpu.VMEM((PBLK + 1, BLK, BLK), F32),
            pltpu.VMEM((PBLK + 1, HD, BLK), BF16),
        ]
        + [held for one in programs for held in one.scratch()],
        compiler_params=pltpu.CompilerParams(
            collective_id=number, has_side_effects=True, vmem_limit_bytes=VMEM_BYTES
        ),
        cost_estimate=pl.CostEstimate(
            flops=10 * rows * width * count,
            bytes_accessed=16 * rows * width,
            transcendentals=rows * heads * count,
        ),
    )(positions, key_slots, queries, grads, mixed, logsums, table, *arrays)
    return out[0], out[1], out[2:]


def by_slot_kernel(slot_ref, set_ref, out_ref, table_ref):
    blocks, chunks = slot_ref.shape

    def clear(index, carry):
        table_ref[index] = jnp.zeros(table_ref.shape[1:], F32)
        return carry

    def give(index, carry):
        out_ref[0, index] = table_ref[index, :, :HD].astype(BF16)
        out_ref[1, index] = table_ref[index, :, HD:].astype(BF16)
        return carry

    lax.fori_loop(0, table_ref.shape[0], clear, 0)
    for block in range(blocks):
        for chunk in range(chunks):
            cut = slice(chunk * BLK, (chunk + 1) * BLK)
            table_ref[slot_ref[block, chunk]] += set_ref[block, cut, :]
    lax.fori_loop(0, table_ref.shape[0], give, 0)


def by_slot(sets, key_slots, slot_count):
    return pl.pallas_call(
        by_slot_kernel,
        out_shape=jax.ShapeDtypeStruct((2, slot_count, BLK, HD), BF16),
        in_specs=[
            pl.BlockSpec(memory_space=pltpu.SMEM),
            pl.BlockSpec(memory_space=pltpu.VMEM),
        ],
        out_specs=pl.BlockSpec(memory_space=pltpu.VMEM),
        scratch_shapes=[pltpu.VMEM((slot_count, BLK, 2 * HD), F32)],
        compiler_params=pltpu.CompilerParams(vmem_limit_bytes=VMEM_BYTES),
    )(key_slots, sets)


GELU_OUTER = 0.7978845608028654
GELU_INNER = 0.044715


def down_copies(piece_ref, rest_ref, down_own, sems):
    first, rows = piece_ref.shape[2], down_own.shape[2]
    return [
        pltpu.make_async_copy(piece_ref, down_own.at[:, :, :first], sems.at[0]),
        pltpu.make_async_copy(
            rest_ref.at[:, :, : rows - first], down_own.at[:, :, first:], sems.at[1]
        ),
    ]


def forward_kernel(
    x_ref,
    cotangent_ref,
    piece_ref,
    rest_ref,
    shift_ref,
    all_ref,
    act_ref,
    pre_ref,
    part_ref,
    bias_ref,
    up_own,
    down_own,
    rows_own,
    cotangent_own,
    act_own,
    pre_own,
    part_own,
    weight_sem,
    load_sem,
    store_sem,
    own_sem,
    send,
    recv,
):
    me = here()
    steps = (SIDE, FRONT, "tp")
    half, width = x_ref.shape
    hidden = rest_ref.shape[3]

    def place(bits):
        at = me
        for k in (2, 1, 0):
            if bits >> k & 1:
                at = flip(at, steps[k])
        return at

    def block(bits):
        return by_plane_slot(all_ref, place(bits))

    def to_step(k, bits):
        source = block(bits) if bits else x_ref
        return remote(
            source, block(bits), send.at[k, bits], recv.at[bits | 1 << k], flip(me, steps[k])
        )

    def arrived(bits):
        remote(block(bits), block(bits), send.at[0, 0], recv.at[bits], me).wait_recv()

    def loads(number):
        slot, copies = number % 2, []
        for side, bits in enumerate((number, number + 4)):
            rows = pl.ds(side * half, half)
            copies.append(
                pltpu.make_async_copy(
                    by_plane_slot(cotangent_ref, place(bits)),
                    cotangent_own.at[slot, rows],
                    load_sem.at[slot, 0, side],
                )
            )
            copies.append(
                pltpu.make_async_copy(
                    block(bits) if bits else x_ref,
                    rows_own.at[slot, rows],
                    load_sem.at[slot, 1, side],
                )
            )
        return copies

    def stores(number, kind):
        slot = number % 2
        source, target = ((act_own, act_ref), (pre_own, pre_ref), (part_own, part_ref))[kind]
        return [
            pltpu.make_async_copy(
                source.at[slot, pl.ds(side * half, half)],
                by_plane_slot(target, place(bits)),
                store_sem.at[slot, kind, side],
            )
            for side, bits in enumerate((number, number + 4))
        ]

    def products(number):
        slot = number % 2
        tile = 256

        def one(index, carry):
            cut = pl.ds(pl.multiple_of(index * tile, tile), tile)
            down = down_own[:, :, :, cut].reshape(width, tile)
            up = up_own[:, :, :, cut].reshape(width, tile)
            grad_act = jnp.dot(cotangent_own[slot], down, preferred_element_type=F32)
            value = jnp.dot(rows_own[slot], up, preferred_element_type=F32)
            value = value + shift_ref[:, cut]
            square = value * value
            bend = jnp.tanh(GELU_OUTER * value * (1.0 + GELU_INNER * square))
            act_own[slot, :, cut] = (0.5 * value * (1.0 + bend)).astype(BF16)
            slope = 0.5 * (1.0 + bend) + 0.5 * GELU_OUTER * value * (1.0 - bend * bend) * (
                1.0 + 3.0 * GELU_INNER * square
            )
            grad_pre = (grad_act * slope).astype(BF16)
            pre_own[slot, :, cut] = grad_pre
            bias_ref[:, cut] += jnp.sum(
                grad_pre.astype(F32).reshape(2 * half // 8, 8, tile), axis=0
            )
            return carry

        lax.fori_loop(0, hidden // tile, one, 0)

    def back(number):
        slot = number % 2
        tile = up_own.shape[1] * up_own.shape[2]

        def one(index, carry):
            cut = pl.ds(pl.multiple_of(index * tile, tile), tile)
            up = up_own[index].reshape(tile, hidden)
            part_own[slot, :, cut] = rows_by_rows(pre_own[slot], up).astype(BF16)
            return carry

        lax.fori_loop(0, width // tile, one, 0)

    def pass_on(bits, *ways):
        arrived(bits)
        for k in ways:
            to_step(k, bits).start()

    def second():
        to_step(0, 0).wait_send()
        to_step(1, 0).start()

    between = [
        second,
        functools.partial(pass_on, 2, 2),
        functools.partial(pass_on, 3, 2),
        lambda: None,
    ]
    barrier = pltpu.get_barrier_semaphore()
    for step in steps:
        pl.semaphore_signal(barrier, inc=1, device_id=flip(me, step), device_id_type=MESH_ID)
    pl.semaphore_wait(barrier, 3)
    to_step(0, 0).start()
    to_step(2, 0).start()
    own = pltpu.make_async_copy(x_ref, block(0), own_sem)
    own.start()
    weights = down_copies(piece_ref, rest_ref, down_own, weight_sem)
    weights.append(
        pltpu.make_async_copy(
            rest_ref.at[:, :, rest_ref.shape[2] - up_own.shape[2] :], up_own, weight_sem.at[2]
        )
    )
    for one in weights:
        one.start()
    bias_ref[...] = jnp.zeros_like(bias_ref)
    for number in range(4):
        if number == 1:
            pass_on(1, 1, 2)
        arrived(4 + number)
        copies = loads(number)
        for one in copies:
            one.start()
        if number == 0:
            for one in weights:
                one.wait()
        if number >= 2:
            for kind in range(3):
                for one in stores(number - 2, kind):
                    one.wait()
        for one in copies:
            one.wait()
        products(number)
        between[number]()
        for kind in range(2):
            for one in stores(number, kind):
                one.start()
        back(number)
        for one in stores(number, 2):
            one.start()
    for number in (2, 3):
        for kind in range(3):
            for one in stores(number, kind):
                one.wait()
    own.wait()
    for k, bits in ((1, 0), (2, 0), (1, 1), (2, 1), (2, 2), (2, 3)):
        to_step(k, bits).wait_send()


def forward_products(rows, cotangent_all, piece, rest, shift, number):
    half, width = rows.shape
    lines, quarters, _, hidden = rest.shape
    weights = (lines, quarters, width // (lines * quarters), hidden)
    anywhere = pl.BlockSpec(memory_space=pl.ANY)
    inside = pl.BlockSpec(memory_space=pltpu.VMEM)
    lead = (2, 2, 2, half)
    return pl.pallas_call(
        forward_kernel,
        out_shape=[
            jax.ShapeDtypeStruct(lead + (width,), BF16),
            jax.ShapeDtypeStruct(lead + (hidden,), BF16),
            jax.ShapeDtypeStruct(lead + (hidden,), BF16),
            jax.ShapeDtypeStruct(lead + (width,), BF16),
            jax.ShapeDtypeStruct((8, hidden), F32),
        ],
        in_specs=[anywhere] * 4 + [inside],
        out_specs=[anywhere] * 4 + [inside],
        scratch_shapes=[
            pltpu.VMEM(weights, BF16),
            pltpu.VMEM(weights, BF16),
            pltpu.VMEM((2, 2 * half, width), BF16),
            pltpu.VMEM((2, 2 * half, width), BF16),
            pltpu.VMEM((2, 2 * half, hidden), BF16),
            pltpu.VMEM((2, 2 * half, hidden), BF16),
            pltpu.VMEM((2, 2 * half, width), BF16),
            pltpu.SemaphoreType.DMA((3,)),
            pltpu.SemaphoreType.DMA((2, 2, 2)),
            pltpu.SemaphoreType.DMA((2, 3, 2)),
            pltpu.SemaphoreType.DMA(()),
            pltpu.SemaphoreType.DMA((3, 4)),
            pltpu.SemaphoreType.DMA((8,)),
        ],
        compiler_params=pltpu.CompilerParams(
            collective_id=number, has_side_effects=True, vmem_limit_bytes=VMEM_BYTES
        ),
        cost_estimate=pl.CostEstimate(
            flops=48 * half * width * hidden,
            bytes_accessed=32 * half * width * 3,
            transcendentals=8 * half * hidden,
        ),
    )(rows, cotangent_all, piece, rest, shift)


def grads_kernel(programs, steps, *refs):
    count = len(programs)
    (cotangent_ref, rows_ref, act_ref, pre_ref, piece_ref, rest_ref), refs = refs[:6], refs[6:]
    others, refs = refs[:count], refs[count:]
    (down_part_ref, weight_grad_ref), refs = refs[:2], refs[2:]
    other_outs, refs = refs[:count], refs[count:]
    (act_own, pre_own, down_own, load_sem), scratch = refs[:4], refs[4:]
    step = pl.program_id(0)
    finish = beside(programs, others, other_outs, scratch, step, steps)

    @pl.when(step == 0)
    def _():
        copies = [
            pltpu.make_async_copy(act_ref, act_own, load_sem.at[2]),
            pltpu.make_async_copy(pre_ref, pre_own, load_sem.at[3]),
        ] + down_copies(piece_ref, rest_ref, down_own, load_sem)
        for one in copies:
            one.start()
        for one in copies:
            one.wait()

    def by_columns(left, right):
        return lax.dot_general(left, right, (((0,), (0,)), ((), ())), preferred_element_type=F32)

    tile = down_part_ref.shape[0]
    rows = pl.ds(pl.multiple_of(step * tile, tile), tile)
    shards, _, shard_rows, hidden = weight_grad_ref.shape
    for kind, (left, right) in enumerate(((cotangent_ref, act_own), (rows_ref, pre_own))):
        grad = by_columns(left[...], right[...]).astype(BF16)
        weight_grad_ref[:, kind] = grad.reshape(shards, shard_rows, hidden)
    down = down_own[...].reshape(down_part_ref.shape[1], hidden)
    down_part_ref[...] = rows_by_rows(act_own[rows, :], down).astype(BF16)
    finish()


def grad_products(cotangent_all, rows_all, act, grad_pre, piece, rest, programs, arrays, number):
    rows, width = cotangent_all.shape
    hidden = act.shape[1]
    lines, quarters = rest.shape[:2]
    shards, shard_rows = lines * quarters, width // (lines * quarters)
    steps = 8
    columns = pl.BlockSpec((rows, width // steps), lambda i: (0, i))
    anywhere = pl.BlockSpec(memory_space=pl.ANY)
    grads = pl.BlockSpec((shards // steps, 2, shard_rows, hidden), lambda i: (i, 0, 0, 0))
    out = pl.pallas_call(
        functools.partial(grads_kernel, programs, steps),
        grid=(steps,),
        out_shape=[
            jax.ShapeDtypeStruct((rows, width), BF16),
            jax.ShapeDtypeStruct((shards, 2, shard_rows, hidden), BF16),
        ]
        + [one.out for one in programs],
        in_specs=[columns, columns] + [anywhere] * 4 + [one.in_spec for one in programs],
        out_specs=[pl.BlockSpec((rows // steps, width), lambda i: (i, 0)), grads]
        + [one.out_spec for one in programs],
        scratch_shapes=[
            pltpu.VMEM((rows, hidden), BF16),
            pltpu.VMEM((rows, hidden), BF16),
            pltpu.VMEM((lines, quarters, shard_rows, hidden), BF16),
            pltpu.SemaphoreType.DMA((4,)),
        ]
        + [held for one in programs for held in one.scratch()],
        compiler_params=pltpu.CompilerParams(
            collective_id=number, has_side_effects=True, vmem_limit_bytes=VMEM_BYTES
        ),
        cost_estimate=pl.CostEstimate(
            flops=6 * rows * width * hidden,
            bytes_accessed=8 * rows * width,
            transcendentals=0,
        ),
    )(cotangent_all, rows_all, act, grad_pre, piece, rest, *arrays)
    return out[0], out[1], out[2:]


def reorder_kernel(cuts, size, x_ref, out_ref):
    for index, cut in enumerate(cuts):
        out_ref[:, index * size : (index + 1) * size] = x_ref[:, cut : cut + size]


def reorder(values, cuts):
    size = values.shape[1] // len(cuts)
    if size % 128:
        return jnp.concatenate([values[:, cut : cut + size] for cut in cuts], axis=1)
    return pl.pallas_call(
        functools.partial(reorder_kernel, cuts, size),
        out_shape=jax.ShapeDtypeStruct(values.shape, values.dtype),
        compiler_params=pltpu.CompilerParams(vmem_limit_bytes=VMEM_BYTES),
    )(values)


def to_line_order(values):
    lines = lax.axis_size("line")
    size = values.shape[1] // (2 * lines)
    return reorder(
        values, [(half * lines + shard) * size for shard in range(lines) for half in range(2)]
    )


def from_line_order(values):
    lines = lax.axis_size("line")
    size = values.shape[1] // (2 * lines)
    return reorder(
        values, [(shard * 2 + half) * size for half in range(2) for shard in range(lines)]
    )


def meet_sibling(me):
    barrier = pltpu.get_barrier_semaphore()
    pl.semaphore_signal(barrier, inc=1, device_id=flip(me, "tp"), device_id_type=MESH_ID)
    pl.semaphore_wait(barrier, 1)


def half_rows_of(core, rows):
    return pl.ds(pl.multiple_of(core * rows, rows), rows)


def each_rows(total, tile, work):
    def one(index, carry):
        work(pl.ds(pl.multiple_of(index * tile, tile), tile))
        return carry

    lax.fori_loop(0, total // tile, one, 0)


def each_columns(total, tile, work):
    each_rows(total, tile, work)


def moments(values):
    centered = values - jnp.mean(values, axis=1, keepdims=True)
    spread = jnp.mean(centered * centered, axis=1, keepdims=True)
    return centered, lax.rsqrt(spread + EPSILON)


def norm_back(values, gain, grad):
    centered, rstd = moments(values)
    xhat = centered * rstd
    scaled = grad * gain
    inner = jnp.mean(scaled * xhat, axis=1, keepdims=True)
    return xhat, rstd * (scaled - jnp.mean(scaled, axis=1, keepdims=True) - xhat * inner)


def fold_rows(values):
    return jnp.sum(values.reshape(values.shape[0] // 8, 8, values.shape[1]), axis=0)


def shuffled(cuts, ref, rows):
    if cuts is None:
        return ref[rows, :]
    size = ref.shape[1] // len(cuts)
    return jnp.concatenate([ref[rows, cut : cut + size] for cut in cuts], axis=1)


def project_kernel(
    cuts,
    mixed_ref,
    proj_ref,
    stream_ref,
    bias_ref,
    gain_ref,
    shift_ref,
    middle_ref,
    normed_ref,
    sent_ref,
    got_ref,
    sems,
):
    me = here()
    half, width = middle_ref.shape
    mine, other = half_rows_of(me["tp"], half), half_rows_of(1 - me["tp"], half)
    tile = 512
    meet_sibling(me)
    copy = remote(sent_ref, got_ref, sems.at[0], sems.at[1], flip(me, "tp"))

    def part(rows, target):
        def work(cut):
            target[:, cut] = rows_by_rows(mixed_ref[rows, :], proj_ref[cut, :])

        each_columns(width, tile, work)

    part(other, sent_ref)
    copy.start()
    part(mine, middle_ref)
    copy.wait_recv()
    bias, gain = bias_ref[...].astype(F32), gain_ref[...].astype(F32)
    shift = shift_ref[...].astype(F32)
    few = 32

    def finish(rows):
        start = pl.multiple_of(me["tp"] * half + rows.start, few)
        stream = stream_ref[pl.ds(start, few), :].astype(F32)
        middle = stream + (middle_ref[rows, :] + got_ref[rows, :] + bias)
        middle_ref[rows, :] = middle
        centered, rstd = moments(middle)
        normed = (centered * rstd * gain + shift).astype(BF16)
        if cuts is None:
            normed_ref[rows, :] = normed
            return
        size = width // len(cuts)
        for index, cut in enumerate(cuts):
            normed_ref[rows, index * size : (index + 1) * size] = normed[:, cut : cut + size]

    each_rows(half, few, finish)
    copy.wait_send()


def in_vmem(count):
    return [pl.BlockSpec(memory_space=pltpu.VMEM)] * count


def kernel_params(number):
    return pltpu.CompilerParams(
        collective_id=number, has_side_effects=True, vmem_limit_bytes=VMEM_BYTES
    )


def line_cuts(width, back):
    lines = lax.axis_size("line")
    size = width // (2 * lines)
    if size % 128:
        return None
    if back:
        return [(shard * 2 + half) * size for half in range(2) for shard in range(lines)]
    return [(half * lines + shard) * size for shard in range(lines) for half in range(2)]


def project(mixed, proj_all, stream, bias, gain, shift, number):
    rows, width = stream.shape
    half = rows // 2
    cuts = line_cuts(width, False)
    middle, normed = pl.pallas_call(
        functools.partial(project_kernel, cuts),
        out_shape=[
            jax.ShapeDtypeStruct((half, width), F32),
            jax.ShapeDtypeStruct((half, width), BF16),
        ],
        in_specs=in_vmem(6),
        out_specs=in_vmem(2),
        scratch_shapes=[
            pltpu.VMEM((half, width), F32),
            pltpu.VMEM((half, width), F32),
            pltpu.SemaphoreType.DMA((2,)),
        ],
        compiler_params=kernel_params(number),
        cost_estimate=pl.CostEstimate(
            flops=2 * rows * width * mixed.shape[1], bytes_accessed=8 * rows * width, transcendentals=0
        ),
    )(mixed, proj_all, stream, bias[None], gain[None], shift[None])
    return middle, normed if cuts else to_line_order(normed)


def middle_back_kernel(
    cuts,
    sum_ref,
    middle_ref,
    cotangent_ref,
    mixed_ref,
    proj_ref,
    gain_ref,
    grad_middle_ref,
    grad_mixed_ref,
    proj_grad_ref,
    sums_ref,
    attn_ref,
    sums_own,
    sems,
):
    me = here()
    half, width = middle_ref.shape
    mine, other = half_rows_of(me["tp"], half), half_rows_of(1 - me["tp"], half)
    few = 32
    gain = gain_ref[...].astype(F32)
    meet_sibling(me)
    sums_own[...] = jnp.zeros_like(sums_own)

    def norm(rows):
        start = pl.multiple_of(me["tp"] * half + rows.start, few)
        cotangent = cotangent_ref[pl.ds(start, few), :].astype(F32)
        grad = shuffled(cuts, sum_ref, rows)
        xhat, back = norm_back(middle_ref[rows, :], gain, grad)
        grad_middle = cotangent + back
        grad_middle_ref[rows, :] = grad_middle
        attn = grad_middle.astype(BF16)
        attn_ref[pl.ds(start, few), :] = attn
        sums_own[0] += fold_rows(grad * xhat)
        sums_own[1] += fold_rows(grad)
        sums_own[2] += fold_rows(attn.astype(F32))
        sums_own[3] += fold_rows(cotangent)

    each_rows(half, few, norm)
    copy = remote(attn_ref.at[mine], attn_ref.at[mine], sems.at[0], sems.at[1], flip(me, "tp"))
    copy.start()

    def to_heads(rows):
        def work(cut):
            grad = jnp.dot(attn_ref[rows, :], proj_ref[:, cut], preferred_element_type=F32)
            grad_mixed_ref[rows, cut] = grad.astype(BF16)

        each_columns(proj_ref.shape[1], 256, work)

    to_heads(mine)
    for kind in range(4):
        sums_ref[kind : kind + 1, :] = jnp.sum(sums_own[kind], axis=0, keepdims=True)
    sums_ref[4:8, :] = jnp.zeros((4, width), F32)
    copy.wait_recv()
    to_heads(other)

    def weight(cut):
        grad = lax.dot_general(
            attn_ref[:, cut], mixed_ref[...], (((0,), (0,)), ((), ())), preferred_element_type=F32
        )
        proj_grad_ref[cut, :] = grad.astype(BF16)

    each_columns(width, 256, weight)
    copy.wait_send()


def middle_back(grad_sum, middle, cotangent, mixed, proj_all, gain, number):
    rows, width = cotangent.shape
    half, heads = rows // 2, mixed.shape[1]
    cuts = line_cuts(width, True)
    return pl.pallas_call(
        functools.partial(middle_back_kernel, cuts),
        out_shape=[
            jax.ShapeDtypeStruct((half, width), F32),
            jax.ShapeDtypeStruct((rows, heads), BF16),
            jax.ShapeDtypeStruct((width, heads), BF16),
            jax.ShapeDtypeStruct((8, width), F32),
        ],
        in_specs=in_vmem(6),
        out_specs=in_vmem(4),
        scratch_shapes=[
            pltpu.VMEM((rows, width), BF16),
            pltpu.VMEM((4, 8, width), F32),
            pltpu.SemaphoreType.DMA((2,)),
        ],
        compiler_params=kernel_params(number),
        cost_estimate=pl.CostEstimate(
            flops=4 * rows * width * heads, bytes_accessed=16 * rows * width, transcendentals=0
        ),
    )(grad_sum if cuts else from_line_order(grad_sum), middle, cotangent, mixed, proj_all, gain[None])


def first_back_kernel(
    cuts,
    grad_query_ref,
    grad_part_ref,
    first_ref,
    stream_ref,
    normed_ref,
    gain_ref,
    grad_middle_ref,
    mlp_ref,
    middle_ref,
    bias_ref,
    input_ref,
    layer_ref,
    weight_ref,
    sums_ref,
    query_sums_ref,
    part_sums_ref,
    sent_ref,
    got_ref,
    grad_first_ref,
    sums_own,
    sems,
):
    me = here()
    rows, width = stream_ref.shape
    half, heads = rows // 2, grad_query_ref.shape[1]
    mine, other = half_rows_of(me["tp"], half), half_rows_of(1 - me["tp"], half)
    few = 32
    sibling = flip(me, "tp")
    meet_sibling(me)

    grad_first_ref[:, :heads] = grad_query_ref[...]
    grad_first_ref[:, heads:] = grad_part_ref[...].astype(BF16)

    def part(at, target):
        def work(cut):
            target[:, cut] = rows_by_rows(grad_first_ref[at, :], first_ref[cut, :])

        each_columns(width, 512, work)

    part(other, sent_ref)
    sums_copy = remote(sent_ref, got_ref, sems.at[0], sems.at[1], sibling)
    sums_copy.start()
    bias = bias_ref[...].astype(F32)

    def layer(at):
        start = pl.multiple_of(me["tp"] * half + at.start, few)
        out = middle_ref[at, :] + (shuffled(cuts, mlp_ref, at) + bias)
        layer_ref[pl.ds(start, few), :] = out.astype(BF16)

    each_rows(half, few, layer)
    layer_copy = remote(layer_ref.at[mine], layer_ref.at[mine], sems.at[2], sems.at[3], sibling)
    layer_copy.start()
    part(mine, grad_own := sums_own.at[0])
    sums_copy.wait_recv()
    gain = gain_ref[...].astype(F32)
    folded = sums_own.at[1]
    folded[0:16, :] = jnp.zeros((16, width), F32)

    def norm(at):
        start = pl.multiple_of(me["tp"] * half + at.start, few)
        grad = grad_own[at, :] + got_ref[at, :]
        xhat, back = norm_back(stream_ref[pl.ds(start, few), :].astype(F32), gain, grad)
        input_ref[pl.ds(start, few), :] = (grad_middle_ref[at, :] + back).astype(BF16)
        folded[0:8, :] += fold_rows(grad * xhat)
        folded[8:16, :] += fold_rows(grad)

    each_rows(half, few, norm)
    input_copy = remote(input_ref.at[mine], input_ref.at[mine], sems.at[4], sems.at[5], sibling)
    input_copy.start()
    sums_ref[0:1, :] = jnp.sum(folded[0:8, :], axis=0, keepdims=True)
    sums_ref[1:2, :] = jnp.sum(folded[8:16, :], axis=0, keepdims=True)
    sums_ref[2:8, :] = jnp.zeros((6, width), F32)

    def weight(cut):
        grad = lax.dot_general(
            normed_ref[:, cut],
            grad_first_ref[:, heads:],
            (((0,), (0,)), ((), ())),
            preferred_element_type=F32,
        )
        weight_ref[cut, :] = grad.astype(BF16)

    each_columns(width, 512, weight)
    query_sums_ref[...] = fold_rows(grad_query_ref[...].astype(F32))
    part_sums_ref[...] = fold_rows(grad_first_ref[:, heads:].astype(F32))
    layer_copy.wait()
    input_copy.wait()
    sums_copy.wait_send()


def first_back(
    grad_query, grad_part, first_all, stream, normed, gain, grad_middle, mlp_sum, middle, bias, number
):
    rows, width = stream.shape
    half, heads, part = rows // 2, grad_query.shape[1], grad_part.shape[1]
    cuts = line_cuts(width, True)
    return pl.pallas_call(
        functools.partial(first_back_kernel, cuts),
        out_shape=[
            jax.ShapeDtypeStruct((rows, width), BF16),
            jax.ShapeDtypeStruct((rows, width), BF16),
            jax.ShapeDtypeStruct((width, part), BF16),
            jax.ShapeDtypeStruct((8, width), F32),
            jax.ShapeDtypeStruct((8, heads), F32),
            jax.ShapeDtypeStruct((8, part), F32),
        ],
        in_specs=in_vmem(10),
        out_specs=in_vmem(6),
        scratch_shapes=[
            pltpu.VMEM((half, width), F32),
            pltpu.VMEM((half, width), F32),
            pltpu.VMEM((rows, heads + part), BF16),
            pltpu.VMEM((2, half, width), F32),
            pltpu.SemaphoreType.DMA((6,)),
        ],
        compiler_params=kernel_params(number),
        cost_estimate=pl.CostEstimate(
            flops=2 * rows * width * (heads + 2 * part),
            bytes_accessed=24 * rows * width,
            transcendentals=0,
        ),
    )(
        grad_query,
        grad_part,
        first_all,
        stream,
        normed,
        gain[None],
        grad_middle,
        mlp_sum if cuts else from_line_order(mlp_sum),
        middle,
        bias[None],
    )


def body(
    hidden_in,
    block_order,
    attn_norm_gain,
    attn_norm_bias,
    query_weight,
    query_bias,
    keyval_weight,
    value_bias,
    proj_weight,
    proj_bias,
    mlp_norm_gain,
    mlp_norm_bias,
    up_weight,
    up_bias,
    down_weight,
    down_bias,
    out_cotangent,
):
    rows_dev = hidden_in.shape[0]
    half_rows = rows_dev // 2
    width = hidden_in.shape[1]
    blocks_dev = rows_dev // BLK
    slot_count = block_order.shape[1]
    group_blocks = PBLK + CONTS
    heads_dev = query_bias.shape[0] // HD
    head_width = heads_dev * HD
    core = lax.axis_index("tp")
    quarter = lax.axis_index("fsdp") * lax.axis_size("pair") + lax.axis_index("pair")
    quarters = lax.axis_size("fsdp") * lax.axis_size("pair")
    hidden_dev = up_weight.shape[1] // quarters

    def own_half(values):
        return lax.dynamic_slice_in_dim(values, core * half_rows, half_rows, axis=0)

    def in_order(mine, other, axis=0):
        first = jnp.where(core == 0, mine, other)
        second = jnp.where(core == 0, other, mine)
        return jnp.concatenate([first, second], axis=axis)

    gain_one = attn_norm_gain.astype(F32)
    shift_one = attn_norm_bias.astype(F32)

    slot_ids = jnp.arange(slot_count, dtype=jnp.int32)
    ordering = block_order[0]
    inverse = jnp.sum(
        jnp.where(ordering[None, :] == slot_ids[:, None], slot_ids[None, :], 0), axis=1
    )
    ctx_index = lax.axis_index("line") * lax.axis_size("pair") + lax.axis_index("pair")
    first_slot = ctx_index * blocks_dev
    my_slots = first_slot + jnp.arange(blocks_dev, dtype=jnp.int32)
    my_blocks = lax.dynamic_slice_in_dim(ordering, first_slot, blocks_dev)
    positions = my_blocks % group_blocks
    group_base = my_blocks // group_blocks * group_blocks
    prompt_slots = jnp.take(
        inverse, group_base[:, None] + jnp.arange(PBLK, dtype=jnp.int32)[None, :]
    )
    key_slots = jnp.concatenate([prompt_slots, my_slots[:, None]], axis=1)

    keyval_cut = lax.dynamic_slice_in_dim(keyval_weight, core * HD, HD, axis=1)
    first_cut = jnp.concatenate([query_weight, keyval_cut], axis=1)
    mlp_weights = jnp.concatenate([down_weight, up_weight], axis=0)
    shard_rows = down_weight.shape[0]
    first_rows = shard_rows // 2
    first_line = line_gather(first_cut.shape, BF16)
    first_like = jax.ShapeDtypeStruct(first_line.out.shape, BF16)
    _, mlp_cut, proj_line, mlp_piece, first_all = run_programs(
        [
            placed(first_line, 0.0, 0.17),
            placed(Exchange(mlp_weights, True), 0.0, 0.18),
            placed(line_gather(proj_weight.shape, BF16), 0.06, 0.28),
            placed(line_gather((quarters, first_rows, hidden_dev), BF16), 0.3, 0.5, 0.65, 0.8, 0.8, 1.0),
            placed(columns_gather(first_like), 0.19, 0.4, 0.7, 1.0),
        ],
        [
            first_cut,
            mlp_weights,
            proj_weight,
            lambda outs: outs[1].at[:, :first_rows],
            lambda outs: outs[0],
        ],
        1,
    )
    first_all = flat(first_all)

    stream = hidden_in.astype(F32)
    normed_one = layer_norm(stream, gain_one, shift_one).astype(BF16)
    value_shift = jnp.where(core == 1, value_bias.astype(F32), 0.0)
    first_shift = jnp.concatenate([query_bias.astype(F32), value_shift])
    first_low = (jnp.dot(normed_one, first_all, preferred_element_type=F32) + first_shift).astype(
        BF16
    )
    query_low = first_low[:, :head_width]
    part_low = first_low[:, head_width:]
    keyval_every = gather_ctx(part_low, 4)
    keyval_every, mlp_cut = lax.optimization_barrier((keyval_every, mlp_cut))
    mlp_rest = lax.all_gather(mlp_cut[:, first_rows:], "line", axis=0, tiled=False)
    table = keyval_every.reshape(2, slot_count, BLK, HD)
    cotangent_line = to_line_order(own_half(out_cotangent))
    mixed_low, logsums, (proj_all, cotangent_all) = attend(
        query_low,
        table,
        positions,
        key_slots,
        [
            placed(columns_gather(proj_line), 0.0, 0.9, 1.0, 1.0),
            placed(plane_gather(cotangent_line), 0.0, 0.9, 1.0, 1.0),
        ],
        [proj_line, cotangent_line],
        2,
    )
    proj_all = flat(proj_all)
    middle, normed_two_line = project(
        mixed_low, proj_all, hidden_in, proj_bias, mlp_norm_gain, mlp_norm_bias, 5
    )

    up_shift = lax.dynamic_slice_in_dim(up_bias, quarter * hidden_dev, hidden_dev).astype(F32)
    normed_two_all, act_low, grad_pre, normed_two_part, up_bias_parts = forward_products(
        normed_two_line, cotangent_all, mlp_piece, mlp_rest, up_shift[None], 6
    )
    plane_two, plane_parts = plane_sum(flat(normed_two_part))
    placed(plane_two, 0.0, 0.13, 0.13, 0.13, 0.13, 0.38, 0.8, 1.0, 1.0)
    down_part, mlp_weight_grad, (grad_normed_two,) = grad_products(
        flat(cotangent_all),
        flat(normed_two_all),
        flat(act_low),
        flat(grad_pre),
        mlp_piece,
        mlp_rest,
        [plane_two],
        [plane_parts],
        7,
    )
    grad_up_bias = jnp.sum(up_bias_parts, axis=0)
    mlp_cut_grad = lax.psum_scatter(mlp_weight_grad, "line", scatter_dimension=0, tiled=True)
    mlp_cut_grad = mlp_cut_grad.reshape(quarters, 2 * shard_rows, hidden_dev)

    grad_middle, grad_mixed, proj_weight_grad, middle_sums = middle_back(
        grad_normed_two, middle, out_cotangent, mixed_low, proj_all, mlp_norm_gain, 8
    )
    sum_proj, proj_parts = rows_sum(proj_weight_grad)
    sum_down, down_parts = plane_sum(down_part)
    grad_query, grad_sets, (grad_proj_weight, mlp_out) = attend_back(
        query_low,
        grad_mixed,
        mixed_low,
        logsums,
        table,
        positions,
        key_slots,
        [
            placed(sum_proj, 0.0, 0.13, 0.26, 0.38, 0.51, 0.63, 0.7, 0.9),
            placed(sum_down, 0.0, 0.45, 0.45, 0.45, 0.45, 0.76, 0.95, 1.0, 1.0),
        ],
        [proj_parts, down_parts],
        3,
    )
    grad_table = by_slot(grad_sets, key_slots, slot_count)
    grad_parts = grad_table.reshape(
        2, lax.axis_size("line"), lax.axis_size("pair"), rows_dev, HD
    )
    query_weight_grad = jnp.einsum("rd,rk->dk", normed_one, grad_query, preferred_element_type=F32)
    sum_query, query_parts = rows_sum(query_weight_grad)
    grad_part, grad_query_weight = run_programs(
        [ctx_sum(grad_parts), sum_query], [grad_parts, query_parts], 12
    )
    input_grad, layer_out, part_weight_grad, first_sums, query_sums, part_sums = first_back(
        grad_query,
        grad_part,
        first_all,
        hidden_in,
        normed_one,
        attn_norm_gain,
        grad_middle,
        mlp_out,
        middle,
        down_bias,
        9,
    )
    grad_query_bias = jnp.sum(query_sums, axis=0)
    grad_value_bias = jnp.where(core == 1, jnp.sum(part_sums, axis=0), 0.0)

    query_slots = jnp.zeros((2 * head_width,), F32)
    query_slots = lax.dynamic_update_slice_in_dim(
        query_slots, grad_query_bias, core * head_width, axis=0
    )
    hidden_slots = jnp.zeros((2 * quarters * hidden_dev,), F32)
    hidden_slots = lax.dynamic_update_slice_in_dim(
        hidden_slots, grad_up_bias, (core * quarters + quarter) * hidden_dev, axis=0
    )
    pieces = [
        first_sums[0],
        first_sums[1],
        middle_sums[2],
        middle_sums[0],
        middle_sums[1],
        middle_sums[3],
        grad_value_bias,
        query_slots,
        hidden_slots,
    ]
    sum_part, weight_parts = rows_sum(part_weight_grad, HD)
    total, padded = total_of(jnp.concatenate(pieces))
    summed, grad_part_weight, mlp_grads = run_programs(
        [placed(total, 0.0, 0.8), placed(sum_part, 0.1, 0.9), placed(Exchange(mlp_cut_grad, False), 0.3, 1.0)],
        [padded, weight_parts, mlp_cut_grad],
        13,
    )
    grad_down_weight = mlp_grads[:shard_rows].astype(F32)
    grad_up_weight = mlp_grads[shard_rows:].astype(F32)
    grad_keyval_weight = in_order(grad_part_weight[:, :HD], grad_part_weight[:, HD:], axis=1)
    summed = summed.reshape(-1)
    cuts, start = [], 0
    for piece in pieces:
        cuts.append(summed[start : start + piece.shape[0]])
        start += piece.shape[0]
    sum_query = lax.dynamic_slice_in_dim(cuts[7], core * head_width, head_width)
    sum_up = lax.dynamic_slice_in_dim(cuts[8], core * quarters * hidden_dev, quarters * hidden_dev)
    return (
        layer_out,
        input_grad,
        cuts[0],
        cuts[1],
        grad_query_weight,
        sum_query,
        grad_keyval_weight,
        cuts[6],
        grad_proj_weight,
        cuts[2],
        cuts[3],
        cuts[4],
        grad_up_weight,
        sum_up,
        grad_down_weight,
        cuts[5],
    )


def solution(mesh):
    fsdp, ctx, tp = mesh.devices.shape
    grid = Mesh(mesh.devices.reshape(fsdp, ctx // 2, 2, tp), EVERY)
    by_rows = P(ROWS, None)
    by_both = P(ROWS, "tp")
    return jax.shard_map(
        body,
        mesh=grid,
        in_specs=(
            by_rows,
            P("fsdp", None),
            P(),
            P(),
            by_both,
            P("tp"),
            by_rows,
            P(),
            by_both,
            P(),
            P(),
            P(),
            by_both,
            P("tp"),
            by_both,
            P(),
            by_rows,
        ),
        out_specs=(
            by_rows,
            by_rows,
            P(),
            P(),
            by_both,
            P("tp"),
            by_rows,
            P(),
            by_both,
            P(),
            P(),
            P(),
            by_both,
            P("tp"),
            by_both,
            P(),
        ),
        check_vma=False,
    )
```

```python
import functools

import jax
import jax.numpy as jnp
from jax import lax
from jax.experimental import pallas as pl
from jax.experimental.pallas import tpu as pltpu
from jax.sharding import Mesh, PartitionSpec as P

HD = 128
BLK = 256
PBLK = 8
CONTS = 8
EPSILON = 1e-05
MASKED = -1e30
F32 = jnp.float32
BF16 = jnp.bfloat16
ROWS = ("fsdp", "line", "pair")
EVERY = ("fsdp", "line", "pair", "tp")


MESH_ID = pl.DeviceIdType.MESH
VMEM_BYTES = 60 * 1024 * 1024
SMALL = pl.CostEstimate(flops=1, bytes_accessed=1, transcendentals=0)
SIDE = ("pair", "fsdp")
FRONT = ("fsdp", "pair")


def here():
    return {name: lax.axis_index(name) for name in EVERY}


def flip(place, step):
    place = dict(place)
    if isinstance(step, str):
        place[step] = 1 - place[step]
    else:
        core = place["tp"]
        for name, used in ((step[0], 1 - core), (step[1], core)):
            place[name] = place[name] + (1 - 2 * place[name]) * used
    return place


def along(place, amount):
    return dict(place, line=place["line"] + amount)


def remote(source, target, send_sem, recv_sem, place):
    return pltpu.make_async_remote_copy(
        src_ref=source,
        dst_ref=target,
        send_sem=send_sem,
        recv_sem=recv_sem,
        device_id=place,
        device_id_type=MESH_ID,
    )


def top_bit(bits):
    return bits.bit_length() - 1


def add_blocks(target, first, second, rows):
    tile = min(rows, 64)

    def one(index, carry):
        cut = pl.ds(pl.multiple_of(index * tile, tile), tile)
        total = first(cut).astype(F32)
        if second is not None:
            total = total + second(cut).astype(F32)
        target[cut, :] = total.astype(target.dtype)
        return carry

    lax.fori_loop(0, rows // tile, one, 0)


def rows_of(ref):
    return lambda cut: ref[cut, :]


class Gather:
    def __init__(self, values, steps, lines, shape, slot):
        self.steps, self.lines, self.slot = steps, lines, slot
        self.out = jax.ShapeDtypeStruct(shape, values.dtype)
        self.in_spec = self.out_spec = pl.BlockSpec(memory_space=pl.ANY)

    def scratch(self):
        parts = 1 << len(self.steps)
        return [
            pltpu.SemaphoreType.DMA(()),
            pltpu.SemaphoreType.DMA((2, self.lines)),
            pltpu.SemaphoreType.DMA((self.lines,)),
            pltpu.SemaphoreType.DMA((self.lines, max(1, len(self.steps)) * parts)),
            pltpu.SemaphoreType.DMA((self.lines, parts)),
        ]

    def stages(self, me, x_ref, out_ref, own_sem, line_send, line_recv, send, recv):
        steps, lines, slot = self.steps, self.lines, self.slot
        count = len(steps)
        my_line = me["line"] if lines > 1 else 0

        def block(bits, shard):
            place = me
            for k in reversed(range(count)):
                if bits >> k & 1:
                    place = flip(place, steps[k])
            return slot(out_ref, dict(place, line=shard))

        def to_step(k, bits, shard, source):
            return remote(
                source,
                block(bits, shard),
                send.at[shard, k * (1 << count) + bits],
                recv.at[shard, bits | 1 << k],
                flip(me, steps[k]),
            )

        def to_line(amount, shard, source):
            return remote(
                source,
                block(0, shard),
                line_send.at[(amount + 1) // 2, shard],
                line_recv.at[shard],
                along(me, amount),
            )

        def send_on(bits, shard, source):
            for k in range(top_bit(bits) + 1, count):
                to_step(k, bits, shard, source).start()

        def at_distance(distance, work):
            if distance == 0:
                work(my_line, 0)
                return
            for amount in (1, -1):
                shard = my_line - amount * distance
                pl.when((shard >= 0) & (shard < lines))(functools.partial(work, shard, amount))

        def line_inside(amount):
            there = my_line + amount
            return (there >= 0) & (there < lines)

        own = pltpu.make_async_copy(x_ref, block(0, my_line), own_sem)

        def begin():
            if lines > 1:
                for amount in (1, -1):
                    pl.when(line_inside(amount))(
                        lambda amount=amount: to_line(amount, my_line, x_ref).start()
                    )
            send_on(0, my_line, x_ref)
            own.start()

        def line_arrival(shard, amount):
            remote(
                block(0, shard), block(0, shard), line_send.at[0, shard], line_recv.at[shard], me
            ).wait_recv()
            pl.when(line_inside(amount))(lambda: to_line(amount, shard, block(0, shard)).start())
            send_on(0, shard, block(0, shard))

        def level_arrival(level, shard, amount):
            for bits in range(1 << level, 2 << level):
                remote(
                    block(bits, shard),
                    block(bits, shard),
                    send.at[shard, 0],
                    recv.at[shard, bits],
                    me,
                ).wait_recv()
                send_on(bits, shard, block(bits, shard))

        def end():
            own.wait()
            if lines > 1:
                for amount in (1, -1):
                    for distance in range(lines):
                        shard = my_line - amount * distance
                        pl.when((shard >= 0) & (shard < lines) & line_inside(amount))(
                            lambda amount=amount, shard=shard: to_line(
                                amount, shard, block(0, shard)
                            ).wait_send()
                        )
            for shard in range(lines):
                for bits in range(1 << count):
                    for k in range(top_bit(bits) + 1, count):
                        to_step(k, bits, shard, block(bits, shard)).wait_send()

        line = [functools.partial(at_distance, number, line_arrival) for number in range(1, lines)]
        levels = [
            functools.partial(at_distance, number - level, functools.partial(level_arrival, level))
            for number in range(lines + count - 1)
            for level in range(count)
            if 0 <= number - level < lines
        ]
        return [begin] + line + levels + [end]


class Sum:
    def __init__(self, steps, lines, rows, columns, slot, shared=0):
        self.steps, self.lines, self.rows, self.columns = steps, lines, rows, columns
        self.slot, self.shared = slot, shared
        self.out = jax.ShapeDtypeStruct((rows, columns + shared), F32)
        self.in_spec = pl.BlockSpec(memory_space=pl.ANY)
        self.out_spec = pl.BlockSpec(memory_space=pltpu.VMEM)

    def scratch(self):
        count, lines = len(self.steps), self.lines
        sizes = [1 << (count - 1 - k) for k in range(count)]
        block = (self.rows, self.columns)
        return (
            [pltpu.VMEM((lines, sizes[0]) + block, BF16)]
            + [pltpu.VMEM((lines, size) + block, BF16) for size in sizes]
            + [pltpu.VMEM((2, lines) + (block if lines > 1 else (16, 128)), BF16)]
            + [pltpu.SemaphoreType.DMA((lines, sizes[0]))]
            + [pltpu.SemaphoreType.DMA((lines, size)) for size in sizes] * 2
            + [pltpu.SemaphoreType.DMA((2, lines))] * 2
            + [pltpu.SemaphoreType.DMA((2,))]
        )

    def stages(self, me, x_ref, whole_ref, own, *rest):
        out_ref = whole_ref.at[:, : self.columns] if self.shared else whole_ref
        steps, lines, rows, slot = self.steps, self.lines, self.rows, self.slot
        count = len(steps)
        held, rest = rest[:count], rest[count:]
        on_line, own_sem, rest = rest[0], rest[1], rest[2:]
        send, recv = rest[:count], rest[count : 2 * count]
        line_send, line_recv, share_sem = rest[2 * count :]
        my_line = me["line"] if lines > 1 else 0
        last = count - 1

        def target_of(bits, shard):
            place = me
            for k in range(count):
                if bits >> k & 1:
                    place = flip(place, steps[k])
            return dict(place, line=shard)

        def store(k, shard, bits):
            return held[k].at[shard, bits >> (k + 1)]

        def own_copy(shard, bits):
            return pltpu.make_async_copy(
                slot(x_ref, target_of(bits, shard)),
                own.at[shard, bits >> 1],
                own_sem.at[shard, bits >> 1],
            )

        def copy(k, shard, bits):
            source = slot(x_ref, target_of(bits, shard)) if k == 0 else store(k - 1, shard, bits)
            return remote(
                source,
                store(k, shard, bits ^ (1 << k)),
                send[k].at[shard, bits >> (k + 1)],
                recv[k].at[shard, bits >> (k + 1)],
                flip(me, steps[k]),
            )

        def parts_of(k):
            return [high << (k + 1) for high in reversed(range(1 << (count - 1 - k)))]

        def send_first(shard, amount):
            for bits in parts_of(0):
                copy(0, shard, bits | 1).start()

        def own_first(shard, amount):
            for bits in parts_of(0):
                own_copy(shard, bits).start()

        def take_step(k, shard, amount, parts=None):
            for bits in parts or parts_of(k):
                copy(k, shard, bits | 1 << k).wait_recv()
                arrived = store(k, shard, bits)
                if k == 0:
                    own_copy(shard, bits).wait()
                    mine = own.at[shard, bits >> 1]
                else:
                    mine = store(k - 1, shard, bits)
                add_blocks(arrived, rows_of(mine), rows_of(arrived), rows)
                if k + 1 < count and bits >> (k + 1) & 1:
                    copy(k + 1, shard, bits).start()

        def line_inside(amount):
            there = my_line + amount
            return (there >= 0) & (there < lines)

        def line_copy(amount, shard):
            way = (amount + 1) // 2
            return remote(
                on_line.at[way, shard],
                on_line.at[way, shard],
                line_send.at[way, shard],
                line_recv.at[way, shard],
                along(me, amount),
            )

        def each(distance, work):
            if distance == 0:
                work(my_line, 0)
                return
            for amount in (1, -1):
                shard = my_line + amount * distance
                pl.when((shard >= 0) & (shard < lines))(functools.partial(work, shard, amount))

        def line_step(shard, amount):
            done = held[last].at[shard, 0]
            moving = on_line.at[(amount + 1) // 2, shard]

            @pl.when(line_inside(-amount))
            def _():
                line_copy(amount, shard).wait_recv()
                add_blocks(moving, rows_of(moving), rows_of(done), rows)

            @pl.when(jnp.logical_not(line_inside(-amount)))
            def _():
                add_blocks(moving, rows_of(done), None, rows)

            line_copy(amount, shard).start()

        order = list(reversed(range(lines)))

        def begin():
            for distance in order:
                each(distance, send_first)
            for distance in order:
                each(distance, own_first)

        def tick(number):
            for k in reversed(range(count)):
                index = number - k
                if 0 <= index < lines:
                    each(order[index], functools.partial(take_step, k))
            index = number - count
            if 0 <= index < lines and order[index] > 0:
                each(order[index], line_step)

        def end():
            final = held[last].at[my_line, 0]
            add_blocks(out_ref, rows_of(final), None, rows)
            if lines > 1:
                for amount in (1, -1):

                    @pl.when(line_inside(-amount))
                    def _():
                        line_copy(amount, my_line).wait_recv()
                        moving = on_line.at[(amount + 1) // 2, my_line]
                        add_blocks(out_ref, rows_of(out_ref), rows_of(moving), rows)

                for amount in (1, -1):
                    for distance in range(1, lines):
                        shard = my_line + amount * distance
                        pl.when((shard >= 0) & (shard < lines))(
                            lambda amount=amount, shard=shard: line_copy(amount, shard).wait_send()
                        )
            if self.shared:
                share = remote(
                    whole_ref.at[:, self.columns - self.shared : self.columns],
                    whole_ref.at[:, self.columns :],
                    share_sem.at[0],
                    share_sem.at[1],
                    flip(me, "tp"),
                )
                share.start()
                share.wait()
            for k in range(count):
                for shard in range(lines):
                    for bits in parts_of(k):
                        copy(k, shard, bits | 1 << k).wait_send()

        if lines == 1:
            ticks = [
                functools.partial(take_step, k, 0, 0, [bits]) for k in range(count) for bits in parts_of(k)
            ]
        else:
            ticks = [functools.partial(tick, number) for number in range(lines + count)]
        return [begin] + ticks + [end]


DIRECT = (("pair",), ("fsdp",), ("pair", "fsdp"))


def move(me, names):
    place = me
    for name in names:
        place = flip(place, name)
    return place


def quarter_of(place):
    return place["fsdp"] * 2 + place["pair"]


class Exchange:
    steps, lines = ("pair", "fsdp"), 1

    def __init__(self, moves, shape, kind):
        self.moves = moves
        self.out = jax.ShapeDtypeStruct(shape, kind)
        self.in_spec = self.out_spec = pl.BlockSpec(memory_space=pl.ANY)

    def scratch(self):
        count = len(self.moves)
        return [
            pltpu.SemaphoreType.DMA((count,)),
            pltpu.SemaphoreType.DMA((count, 3)),
            pltpu.SemaphoreType.DMA((count, 3)),
        ]

    def stages(self, me, x_refs, out_ref, own_sem, send, recv):
        copies = []
        for n, (source, target) in enumerate(self.moves):
            there_ref = target(out_ref, quarter_of(me))
            for k, names in reversed(list(enumerate(DIRECT))):
                there = move(me, names)
                copies.append(
                    remote(
                        source(x_refs, quarter_of(there)), there_ref, send.at[n, k], recv.at[n, k], there
                    )
                )
            copies.append(
                pltpu.make_async_copy(source(x_refs, quarter_of(me)), there_ref, own_sem.at[n])
            )

        def begin():
            for one in copies:
                one.start()

        def end():
            for one in copies:
                one.wait()

        return [begin, end]


def half_quarter(ref, quarter, half, rows=None):
    columns = ref.shape[1] // 8
    cut = pl.ds(pl.multiple_of((quarter * 2 + half) * columns, columns), columns)
    return ref.at[:, cut] if rows is None else ref.at[rows, cut]


def spread_halves(pieces, columns, kind):
    moves, start = [], 0
    for index, rows, half in pieces:
        count = rows.stop - rows.start
        moves.append(
            (
                lambda refs, quarter, index=index, rows=rows, half=half: half_quarter(
                    refs[index], quarter, half, rows
                ),
                lambda ref, quarter, start=start, count=count: ref.at[quarter, start : start + count],
            )
        )
        start += count
    return Exchange(moves, (4, start, columns // 8), kind)


def join_halves(rows, columns, kind):
    moves = [
        (
            lambda refs, quarter, half=half: refs[half].at[quarter],
            lambda ref, quarter, half=half: half_quarter(ref, quarter, half),
        )
        for half in range(2)
    ]
    return Exchange(moves, (rows, columns), kind)


class Work:
    steps, lines = (), 1

    def __init__(self, work, shape, kind):
        self.work, self.out = work, jax.ShapeDtypeStruct(shape, kind)
        self.in_spec = self.out_spec = pl.BlockSpec(memory_space=pltpu.VMEM)

    def scratch(self):
        return []

    def stages(self, me, x_refs, out_ref):
        return [functools.partial(self.work, me, x_refs, out_ref), lambda: None]


class Total:
    steps = ("tp", "pair", "fsdp")

    def __init__(self, values, lines):
        self.lines, self.out = lines, jax.ShapeDtypeStruct(values.shape, F32)
        self.in_spec = self.out_spec = pl.BlockSpec(memory_space=pltpu.VMEM)

    def scratch(self):
        shape, lines = self.out.shape, self.lines
        return [
            pltpu.VMEM((3, 2) + shape, F32),
            pltpu.VMEM((lines,) + shape, F32),
            pltpu.SemaphoreType.DMA((3,)),
            pltpu.SemaphoreType.DMA((3,)),
            pltpu.SemaphoreType.DMA((2, lines)),
            pltpu.SemaphoreType.DMA((lines,)),
        ]

    def stages(self, me, x_ref, out_ref, moved, on_line, send, recv, line_send, line_recv):
        lines = self.lines

        def swap(k):
            return remote(
                moved.at[k, 0], moved.at[k, 1], send.at[k], recv.at[k], flip(me, self.steps[k])
            )

        def copy(amount, shard):
            return remote(
                on_line.at[shard],
                on_line.at[shard],
                line_send.at[(amount + 1) // 2, shard],
                line_recv.at[shard],
                along(me, amount),
            )

        def inside(amount):
            there = me["line"] + amount
            return (there >= 0) & (there < lines)

        def begin():
            moved[0, 0] = x_ref[...]
            swap(0).start()

        def after(k):
            swap(k).wait()
            if k < 2:
                moved[k + 1, 0] = moved[k, 0] + moved[k, 1]
                swap(k + 1).start()
                return
            on_line[me["line"]] = moved[k, 0] + moved[k, 1]
            for amount in (1, -1):
                pl.when(inside(amount))(lambda amount=amount: copy(amount, me["line"]).start())

        def hop(distance):
            for amount in (1, -1):
                shard = me["line"] - amount * distance

                @pl.when((shard >= 0) & (shard < lines))
                def _():
                    copy(amount, shard).wait_recv()
                    pl.when(inside(amount))(lambda: copy(amount, shard).start())

        def end():
            total = on_line[0]
            for shard in range(1, lines):
                total = total + on_line[shard]
            out_ref[...] = total
            for amount in (1, -1):
                for distance in range(lines):
                    shard = me["line"] - amount * distance
                    pl.when((shard >= 0) & (shard < lines) & inside(amount))(
                        lambda amount=amount, shard=shard: copy(amount, shard).wait_send()
                    )

        return (
            [begin]
            + [functools.partial(after, k) for k in range(3)]
            + [functools.partial(hop, distance) for distance in range(1, lines)]
            + [end]
        )


def greet(me, programs, partners=()):
    barrier = pltpu.get_barrier_semaphore()
    lines = max(one.lines for one in programs)
    steps = list(dict.fromkeys([step for one in programs for step in one.steps] + list(partners)))
    if SIDE in steps or FRONT in steps:
        steps = [SIDE, FRONT] + [step for step in steps if step not in (SIDE, FRONT)]
        steps = [step for step in steps if step not in ("pair", "fsdp")]
    places = [flip(me, step) for step in steps]
    if any(isinstance(one, Exchange) for one in programs):
        places.append(move(me, ("pair", "fsdp")))
    for place in places:
        pl.semaphore_signal(barrier, inc=1, device_id=place, device_id_type=MESH_ID)
    count = len(places)
    if lines > 1:
        for amount in (-1, 1):
            there = me["line"] + amount
            inside = (there >= 0) & (there < lines)

            @pl.when(inside)
            def _():
                pl.semaphore_signal(
                    barrier, inc=1, device_id=along(me, amount), device_id_type=MESH_ID
                )

            count = count + inside.astype(jnp.int32)
    pl.semaphore_wait(barrier, count)


def split_scratch(programs, refs):
    parts, start = [], 0
    for one in programs:
        size = len(one.scratch())
        parts.append(refs[start : start + size])
        start += size
    return parts


def schedule(programs, x_refs, out_refs, scratch, partners=()):
    me = here()
    works = [(0.0, functools.partial(greet, me, programs, partners))]
    for one, x_ref, out_ref, held in zip(programs, x_refs, out_refs, split_scratch(programs, scratch)):
        stages = one.stages(me, x_ref, out_ref, *held)
        places = getattr(one, "places", (0.0, 1.0))
        if len(places) == 2:
            places = spaced(places[0], places[1], len(stages))
        last = len(places) - 2
        works += [
            (places[-1] if k == len(stages) - 1 else places[min(k, last)], stage)
            for k, stage in enumerate(stages)
        ]
    return sorted(works, key=lambda work: work[0])


def placed(program, *places):
    program.places = list(places)
    return program


def spaced(start, stop, count):
    return [start + (stop - start) * k / (count - 1) for k in range(count)]


def run_programs(programs, arrays, number, near=(), far=()):
    count = len(programs)
    given = [k for k, array in enumerate(arrays) if not callable(array)]
    others = len(near) + len(far)

    def kernel(*refs):
        (more, refs) = refs[:others], refs[others:]
        plain, out_refs = refs[: len(given)], refs[len(given) : len(given) + count]
        in_refs = [
            array(more, out_refs) if callable(array) else plain[given.index(k)]
            for k, array in enumerate(arrays)
        ]
        for _, work in schedule(programs, in_refs, out_refs, refs[len(given) + count :]):
            work()

    return pl.pallas_call(
        kernel,
        out_shape=[one.out for one in programs],
        in_specs=[pl.BlockSpec(memory_space=pltpu.VMEM)] * len(near)
        + [pl.BlockSpec(memory_space=pl.ANY)] * len(far)
        + [programs[k].in_spec for k in given],
        out_specs=[one.out_spec for one in programs],
        scratch_shapes=[held for one in programs for held in one.scratch()],
        compiler_params=pltpu.CompilerParams(
            collective_id=number, has_side_effects=True, vmem_limit_bytes=VMEM_BYTES
        ),
        cost_estimate=SMALL,
    )(*near, *far, *[arrays[k] for k in given])


def by_rows_slot(ref, at):
    return ref.at[at["fsdp"], at["line"], at["pair"]]


def by_plane_slot(ref, at):
    return ref.at[at["fsdp"], at["pair"], at["tp"]]


def by_ctx_slot(ref, at):
    return ref.at[at["tp"], at["line"], at["pair"]]


def rows_gather(values):
    lines = lax.axis_size("line")
    return Gather(values, (SIDE, FRONT), lines, (2, lines, 2) + values.shape, by_rows_slot)


def line_gather(shape, kind):
    lines = lax.axis_size("line")
    like = jax.ShapeDtypeStruct(shape, kind)
    return Gather(like, (), lines, (lines,) + shape, lambda ref, at: ref.at[at["line"]])


def columns_gather(values):
    lines, rows, columns = values.shape
    return Gather(
        values, (SIDE, FRONT), 1, (2, lines, 2, rows, columns), lambda ref, at: ref.at[at["fsdp"], :, at["pair"]]
    )


def rows_sum(values, shared=0):
    lines, (total, columns) = lax.axis_size("line"), values.shape
    rows = total // (4 * lines)
    parts = values.astype(BF16).reshape(2, lines, 2, rows, columns)
    return Sum((FRONT, SIDE), lines, rows, columns, by_rows_slot, shared), parts


def plane_gather(values):
    return Gather(values, (SIDE, FRONT, "tp"), 1, (2, 2, 2) + values.shape, by_plane_slot)


def plane_sum(values):
    rows, columns = values.shape[0] // 8, values.shape[1]
    parts = values.astype(BF16).reshape(2, 2, 2, rows, columns)
    return Sum(("tp", FRONT, SIDE), 1, rows, columns, by_plane_slot), parts


def flat(values):
    return values.reshape(-1, values.shape[-1])


def ctx_gather(shape, kind):
    lines = lax.axis_size("line")
    like = jax.ShapeDtypeStruct(shape, kind)
    return Gather(like, ("pair", "tp"), lines, (2, lines, 2) + shape, by_ctx_slot)


def ctx_sum(values):
    _, lines, _, rows, columns = values.shape
    return Sum(("tp", "pair"), lines, rows, columns, by_ctx_slot)


LOG2E = 1.4426950408889634


def visible_bias(bias_ref, position, chunks):
    prompt = position < PBLK
    row = lax.broadcasted_iota(jnp.int32, (BLK, BLK), 0)
    column = lax.broadcasted_iota(jnp.int32, (BLK, BLK), 1)
    limit = jnp.where(prompt, position * BLK + column, PBLK * BLK)
    for chunk in range(chunks - 1):
        bias_ref[chunk] = jnp.where(row + chunk * BLK <= limit, 0.0, MASKED)
    own_limit = jnp.where(prompt, -1, column)
    bias_ref[chunks - 1] = jnp.where(row <= own_limit, 0.0, MASKED)


def rows_by_rows(left, right):
    return lax.dot_general(left, right, (((1,), (1,)), ((), ())), preferred_element_type=F32)


def beside(programs, in_refs, out_refs, scratch, step, steps):
    late = []
    for place, work in schedule(programs, in_refs, out_refs, scratch):
        if place < 1:
            pl.when(step == int(place * steps))(work)
        else:
            late.append(work)

    def finish():
        @pl.when(step == steps - 1)
        def _():
            for work in late:
                work()

    return finish


def attend_kernel(programs, steps, *refs):
    count = len(programs)
    (position_ref, slot_ref, query_ref, table_ref), refs = refs[:4], refs[4:]
    others, refs = refs[:count], refs[count:]
    (mixed_ref, logsum_ref), refs = refs[:2], refs[2:]
    other_outs, refs = refs[:count], refs[count:]
    (bias_ref, score_ref, value_t_ref), scratch = refs[:3], refs[3:]
    chunks = PBLK + 1
    block = pl.program_id(0)
    factor = HD**-0.5 * LOG2E
    step = pl.program_id(0) * pl.num_programs(1) + pl.program_id(1)
    finish = beside(programs, others, other_outs, scratch, step, steps)

    @pl.when(pl.program_id(1) == 0)
    def _():
        visible_bias(bias_ref, position_ref[block], chunks)
        for chunk in range(chunks):
            value_t_ref[chunk] = table_ref[1, slot_ref[block, chunk]].astype(F32).T.astype(BF16)

    query = query_ref[...]
    largest = None
    for chunk in range(chunks):
        keys = table_ref[0, slot_ref[block, chunk]]
        score = rows_by_rows(keys, query) + bias_ref[chunk]
        score_ref[chunk] = score
        top = jnp.max(score.reshape(BLK // 8, 8, BLK), axis=0)
        largest = top if largest is None else jnp.maximum(largest, top)
    largest = jnp.max(largest, axis=0, keepdims=True)
    total = jnp.zeros((8, BLK), F32)
    mixed = jnp.zeros((HD, BLK), F32)
    for chunk in range(chunks):
        weight = jnp.exp2((score_ref[chunk] - largest) * factor)
        total = total + jnp.sum(weight.reshape(BLK // 8, 8, BLK), axis=0)
        mixed = mixed + jnp.dot(
            value_t_ref[chunk], weight.astype(BF16), preferred_element_type=F32
        )
    total = jnp.sum(total, axis=0, keepdims=True)
    mixed_ref[...] = (mixed / total).T.astype(BF16)
    logsum_ref[0, 0] = largest * factor + jnp.log2(total)
    finish()


def attend(queries, table, positions, key_slots, programs, arrays, number):
    rows, width = queries.shape
    blocks, heads = rows // BLK, width // HD
    count = (PBLK + 1) * BLK
    out = pl.pallas_call(
        functools.partial(attend_kernel, programs, blocks * heads),
        grid=(blocks, heads),
        out_shape=[
            jax.ShapeDtypeStruct((rows, width), BF16),
            jax.ShapeDtypeStruct((blocks, heads, 1, BLK), F32),
        ]
        + [one.out for one in programs],
        in_specs=[
            pl.BlockSpec(memory_space=pltpu.SMEM),
            pl.BlockSpec(memory_space=pltpu.SMEM),
            pl.BlockSpec((BLK, HD), lambda b, h: (b, h)),
            pl.BlockSpec(memory_space=pltpu.VMEM),
        ]
        + [one.in_spec for one in programs],
        out_specs=[
            pl.BlockSpec((BLK, HD), lambda b, h: (b, h)),
            pl.BlockSpec((1, 1, 1, BLK), lambda b, h: (b, h, 0, 0)),
        ]
        + [one.out_spec for one in programs],
        scratch_shapes=[
            pltpu.VMEM((PBLK + 1, BLK, BLK), F32),
            pltpu.VMEM((PBLK + 1, BLK, BLK), F32),
            pltpu.VMEM((PBLK + 1, HD, BLK), BF16),
        ]
        + [held for one in programs for held in one.scratch()],
        compiler_params=pltpu.CompilerParams(
            collective_id=number, has_side_effects=True, vmem_limit_bytes=VMEM_BYTES
        ),
        cost_estimate=SMALL,
    )(positions, key_slots, queries, table, *arrays)
    return out[0], out[1], out[2:]


def attend_back_kernel(programs, steps, *refs):
    count = len(programs)
    (position_ref, slot_ref, query_ref, grad_ref, mixed_ref), refs = refs[:5], refs[5:]
    (logsum_ref, table_ref), refs = refs[:2], refs[2:]
    others, refs = refs[:count], refs[count:]
    (grad_query_ref, set_ref), refs = refs[:2], refs[2:]
    other_outs, refs = refs[:count], refs[count:]
    (bias_ref, key_t_ref), scratch = refs[:2], refs[2:]
    chunks = PBLK + 1
    scale = HD**-0.5
    block, head = pl.program_id(0), pl.program_id(1)
    step = pl.program_id(0) * pl.num_programs(1) + pl.program_id(1)
    finish = beside(programs, others, other_outs, scratch, step, steps)

    @pl.when(head == 0)
    def _():
        visible_bias(bias_ref, position_ref[block], chunks)
        set_ref[...] = jnp.zeros_like(set_ref)
        for chunk in range(chunks):
            key_t_ref[chunk] = table_ref[0, slot_ref[block, chunk]].astype(F32).T.astype(BF16)

    query, grad = query_ref[...], grad_ref[...]
    inner = jnp.sum(grad.astype(F32) * mixed_ref[...].astype(F32), axis=1, keepdims=True)
    inner = jnp.broadcast_to(inner, (BLK, HD)).T[:1, :]
    logsum = logsum_ref[0, 0]
    grad_query = jnp.zeros((HD, BLK), F32)
    for chunk in range(chunks):
        cut = slice(chunk * BLK, (chunk + 1) * BLK)
        slot = slot_ref[block, chunk]
        score = rows_by_rows(table_ref[0, slot], query)
        weight = jnp.exp2(score * (scale * LOG2E) + bias_ref[chunk] - logsum)
        grad_weight = rows_by_rows(table_ref[1, slot], grad)
        grad_score = (weight * (grad_weight - inner)).astype(BF16)
        set_ref[0, cut, :HD] += jnp.dot(grad_score, query, preferred_element_type=F32)
        set_ref[0, cut, HD:] += jnp.dot(weight.astype(BF16), grad, preferred_element_type=F32)
        grad_query = grad_query + jnp.dot(
            key_t_ref[chunk], grad_score, preferred_element_type=F32
        )
    grad_query_ref[...] = (grad_query * scale).T.astype(BF16)

    @pl.when(head == pl.num_programs(1) - 1)
    def _():
        set_ref[0, :, :HD] = set_ref[0, :, :HD] * scale

    finish()


def attend_back(
    queries, grads, mixed, logsums, table, positions, key_slots, programs, arrays, number
):
    rows, width = queries.shape
    blocks, heads = rows // BLK, width // HD
    count = (PBLK + 1) * BLK
    by_head = pl.BlockSpec((BLK, HD), lambda b, h: (b, h))
    out = pl.pallas_call(
        functools.partial(attend_back_kernel, programs, blocks * heads),
        grid=(blocks, heads),
        out_shape=[
            jax.ShapeDtypeStruct((rows, width), BF16),
            jax.ShapeDtypeStruct((blocks, count, 2 * HD), F32),
        ]
        + [one.out for one in programs],
        in_specs=[
            pl.BlockSpec(memory_space=pltpu.SMEM),
            pl.BlockSpec(memory_space=pltpu.SMEM),
            by_head,
            by_head,
            by_head,
            pl.BlockSpec((1, 1, 1, BLK), lambda b, h: (b, h, 0, 0)),
            pl.BlockSpec(memory_space=pltpu.VMEM),
        ]
        + [one.in_spec for one in programs],
        out_specs=[by_head, pl.BlockSpec((1, count, 2 * HD), lambda b, h: (b, 0, 0))]
        + [one.out_spec for one in programs],
        scratch_shapes=[
            pltpu.VMEM((PBLK + 1, BLK, BLK), F32),
            pltpu.VMEM((PBLK + 1, HD, BLK), BF16),
        ]
        + [held for one in programs for held in one.scratch()],
        compiler_params=pltpu.CompilerParams(
            collective_id=number, has_side_effects=True, vmem_limit_bytes=VMEM_BYTES
        ),
        cost_estimate=SMALL,
    )(positions, key_slots, queries, grads, mixed, logsums, table, *arrays)
    return out[0], out[1], out[2:]


def by_slot_kernel(slot_ref, set_ref, out_ref, table_ref):
    blocks, chunks = slot_ref.shape

    def clear(index, carry):
        table_ref[index] = jnp.zeros(table_ref.shape[1:], F32)
        return carry

    def give(index, carry):
        out_ref[0, index] = table_ref[index, :, :HD].astype(BF16)
        out_ref[1, index] = table_ref[index, :, HD:].astype(BF16)
        return carry

    lax.fori_loop(0, table_ref.shape[0], clear, 0)
    for block in range(blocks):
        for chunk in range(chunks):
            cut = slice(chunk * BLK, (chunk + 1) * BLK)
            table_ref[slot_ref[block, chunk]] += set_ref[block, cut, :]
    lax.fori_loop(0, table_ref.shape[0], give, 0)


def by_slot(sets, key_slots, slot_count):
    return pl.pallas_call(
        by_slot_kernel,
        out_shape=jax.ShapeDtypeStruct((2, slot_count, BLK, HD), BF16),
        in_specs=[
            pl.BlockSpec(memory_space=pltpu.SMEM),
            pl.BlockSpec(memory_space=pltpu.VMEM),
        ],
        out_specs=pl.BlockSpec(memory_space=pltpu.VMEM),
        scratch_shapes=[pltpu.VMEM((slot_count, BLK, 2 * HD), F32)],
        compiler_params=pltpu.CompilerParams(vmem_limit_bytes=VMEM_BYTES),
        cost_estimate=SMALL,
    )(key_slots, sets)


GELU_OUTER = 0.7978845608028654
GELU_INNER = 0.044715


def weight_copies(parts, target, sems):
    copies, start = [], 0
    for number, (ref, rows) in enumerate(parts):
        count = rows.stop - rows.start
        copies.append(
            pltpu.make_async_copy(
                ref.at[:, :, rows], target.at[:, :, start : start + count], sems.at[number]
            )
        )
        start += count
    return copies


def first_half(rows, first, refs):
    piece, early = refs[0], refs[1]
    down = [(piece, slice(0, first)), (early, slice(0, rows - first))]
    return down, [(early, slice(rows - first, 2 * rows - first))]


def second_half(rows, first, refs):
    early, late = refs[1], refs[2]
    start = 2 * rows - first
    there = early.shape[2] - start
    down = [(early, slice(start, start + there)), (late, slice(0, rows - there))]
    return down, [(late, slice(rows - there, 2 * rows - there))]


def gelu_both(value, grad_act):
    square = value * value
    bend = jnp.tanh(GELU_OUTER * value * (1.0 + GELU_INNER * square))
    slope = 0.5 * (1.0 + bend) + 0.5 * GELU_OUTER * value * (1.0 - bend * bend) * (
        1.0 + 3.0 * GELU_INNER * square
    )
    return 0.5 * value * (1.0 + bend), grad_act * slope


def forward_kernel(
    x_ref,
    cotangent_ref,
    piece_ref,
    early_ref,
    shift_ref,
    all_ref,
    act_ref,
    pre_ref,
    part_ref,
    bias_ref,
    up_own,
    down_own,
    rows_own,
    cotangent_own,
    act_own,
    pre_own,
    part_own,
    weight_sem,
    load_sem,
    store_sem,
    own_sem,
    send,
    recv,
):
    me = here()
    steps = (SIDE, FRONT, "tp")
    half, width = x_ref.shape
    hidden = early_ref.shape[3]

    def place(bits):
        at = me
        for k in (2, 1, 0):
            if bits >> k & 1:
                at = flip(at, steps[k])
        return at

    def block(bits):
        return by_plane_slot(all_ref, place(bits))

    def to_step(k, bits):
        source = block(bits) if bits else x_ref
        return remote(
            source, block(bits), send.at[k, bits], recv.at[bits | 1 << k], flip(me, steps[k])
        )

    def arrived(bits):
        remote(block(bits), block(bits), send.at[0, 0], recv.at[bits], me).wait_recv()

    def loads(number):
        slot, copies = number % 2, []
        for side, bits in enumerate((number, number + 4)):
            rows = pl.ds(side * half, half)
            copies.append(
                pltpu.make_async_copy(
                    by_plane_slot(cotangent_ref, place(bits)),
                    cotangent_own.at[slot, rows],
                    load_sem.at[slot, 0, side],
                )
            )
            copies.append(
                pltpu.make_async_copy(
                    block(bits) if bits else x_ref,
                    rows_own.at[slot, rows],
                    load_sem.at[slot, 1, side],
                )
            )
        return copies

    def stores(number, kind):
        slot = number % 2
        source, target = ((act_own, act_ref), (pre_own, pre_ref), (part_own, part_ref))[kind]
        return [
            pltpu.make_async_copy(
                source.at[slot, pl.ds(side * half, half)],
                by_plane_slot(target, place(bits)),
                store_sem.at[slot, kind, side],
            )
            for side, bits in enumerate((number, number + 4))
        ]

    def products(number):
        slot = number % 2
        tile = 256

        def one(index, carry):
            cut = pl.ds(pl.multiple_of(index * tile, tile), tile)
            down = down_own[:, :, :, cut].reshape(width, tile)
            up = up_own[:, :, :, cut].reshape(width, tile)
            grad_act = jnp.dot(cotangent_own[slot], down, preferred_element_type=F32)
            value = jnp.dot(rows_own[slot], up, preferred_element_type=F32)
            value = value + shift_ref[:, cut]
            act, grad_pre = gelu_both(value, grad_act)
            act_own[slot, :, cut] = act.astype(BF16)
            grad_pre = grad_pre.astype(BF16)
            pre_own[slot, :, cut] = grad_pre
            bias_ref[:, cut] += jnp.sum(
                grad_pre.astype(F32).reshape(2 * half // 8, 8, tile), axis=0
            )
            return carry

        lax.fori_loop(0, hidden // tile, one, 0)

    def back(number):
        slot = number % 2
        tile = up_own.shape[1] * up_own.shape[2]

        def one(index, carry):
            cut = pl.ds(pl.multiple_of(index * tile, tile), tile)
            up = up_own[index].reshape(tile, hidden)
            part_own[slot, :, cut] = rows_by_rows(pre_own[slot], up).astype(BF16)
            return carry

        lax.fori_loop(0, width // tile, one, 0)

    def pass_on(bits, *ways):
        arrived(bits)
        for k in ways:
            to_step(k, bits).start()

    def second():
        to_step(0, 0).wait_send()
        to_step(1, 0).start()

    between = [
        second,
        functools.partial(pass_on, 2, 2),
        functools.partial(pass_on, 3, 2),
        lambda: None,
    ]
    barrier = pltpu.get_barrier_semaphore()
    for step in steps:
        pl.semaphore_signal(barrier, inc=1, device_id=flip(me, step), device_id_type=MESH_ID)
    pl.semaphore_wait(barrier, 3)
    to_step(0, 0).start()
    to_step(2, 0).start()
    own = pltpu.make_async_copy(x_ref, block(0), own_sem)
    own.start()
    down_parts, up_parts = first_half(up_own.shape[2], piece_ref.shape[2], (piece_ref, early_ref))
    weights = weight_copies(down_parts, down_own, weight_sem)
    weights += weight_copies(up_parts, up_own, weight_sem.at[2:])
    for one in weights:
        one.start()
    bias_ref[...] = jnp.zeros_like(bias_ref)
    for number in range(4):
        if number == 1:
            pass_on(1, 1, 2)
        arrived(4 + number)
        copies = loads(number)
        for one in copies:
            one.start()
        if number == 0:
            for one in weights:
                one.wait()
        if number >= 2:
            for kind in range(3):
                for one in stores(number - 2, kind):
                    one.wait()
        for one in copies:
            one.wait()
        products(number)
        between[number]()
        for kind in range(2):
            for one in stores(number, kind):
                one.start()
        back(number)
        for one in stores(number, 2):
            one.start()
    for number in (2, 3):
        for kind in range(3):
            for one in stores(number, kind):
                one.wait()
    own.wait()
    for k, bits in ((1, 0), (2, 0), (1, 1), (2, 1), (2, 2), (2, 3)):
        to_step(k, bits).wait_send()


def forward_products(rows, cotangent_all, piece, early, shift, number):
    half, width = rows.shape
    lines, quarters, _, hidden = early.shape
    weights = (lines, quarters, width // (lines * quarters), hidden)
    anywhere = pl.BlockSpec(memory_space=pl.ANY)
    inside = pl.BlockSpec(memory_space=pltpu.VMEM)
    lead = (2, 2, 2, half)
    return pl.pallas_call(
        forward_kernel,
        out_shape=[
            jax.ShapeDtypeStruct(lead + (width,), BF16),
            jax.ShapeDtypeStruct(lead + (hidden,), BF16),
            jax.ShapeDtypeStruct(lead + (hidden,), BF16),
            jax.ShapeDtypeStruct(lead + (width,), BF16),
            jax.ShapeDtypeStruct((8, hidden), F32),
        ],
        in_specs=[anywhere] * 4 + [inside],
        out_specs=[anywhere] * 4 + [inside],
        scratch_shapes=[
            pltpu.VMEM(weights, BF16),
            pltpu.VMEM(weights, BF16),
            pltpu.VMEM((2, 2 * half, width), BF16),
            pltpu.VMEM((2, 2 * half, width), BF16),
            pltpu.VMEM((2, 2 * half, hidden), BF16),
            pltpu.VMEM((2, 2 * half, hidden), BF16),
            pltpu.VMEM((2, 2 * half, width), BF16),
            pltpu.SemaphoreType.DMA((3,)),
            pltpu.SemaphoreType.DMA((2, 2, 2)),
            pltpu.SemaphoreType.DMA((2, 3, 2)),
            pltpu.SemaphoreType.DMA(()),
            pltpu.SemaphoreType.DMA((3, 4)),
            pltpu.SemaphoreType.DMA((8,)),
        ],
        compiler_params=pltpu.CompilerParams(
            collective_id=number, has_side_effects=True, vmem_limit_bytes=VMEM_BYTES
        ),
        cost_estimate=SMALL,
    )(rows, cotangent_all, piece, early, shift)


def second_kernel(
    rows_ref,
    cotangent_ref,
    before_ref,
    piece_ref,
    early_ref,
    late_ref,
    shift_ref,
    act_ref,
    pre_ref,
    part_ref,
    bias_ref,
    up_own,
    down_own,
    weight_sem,
):
    step = pl.program_id(0)
    width, hidden = rows_ref.shape[1], act_ref.shape[1]

    @pl.when(step == 0)
    def _():
        down_parts, up_parts = second_half(
            up_own.shape[2], piece_ref.shape[2], (piece_ref, early_ref, late_ref)
        )
        weights = weight_copies(down_parts, down_own, weight_sem)
        weights += weight_copies(up_parts, up_own, weight_sem.at[2:])
        for one in weights:
            one.start()
        bias_ref[...] = jnp.zeros_like(bias_ref)
        for one in weights:
            one.wait()

    tile = 256

    def one(index, carry):
        cut = pl.ds(pl.multiple_of(index * tile, tile), tile)
        down = down_own[:, :, :, cut].reshape(width, tile)
        up = up_own[:, :, :, cut].reshape(width, tile)
        grad_act = jnp.dot(cotangent_ref[...], down, preferred_element_type=F32)
        value = jnp.dot(rows_ref[...], up, preferred_element_type=F32) + shift_ref[:, cut]
        act, grad_pre = gelu_both(value, grad_act)
        act_ref[:, cut] = act.astype(BF16)
        grad_pre = grad_pre.astype(BF16)
        pre_ref[:, cut] = grad_pre
        bias_ref[:, cut] += fold_rows(grad_pre.astype(F32))
        return carry

    lax.fori_loop(0, hidden // tile, one, 0)
    tile_back = up_own.shape[1] * up_own.shape[2]

    def back(index, carry):
        cut = pl.ds(pl.multiple_of(index * tile_back, tile_back), tile_back)
        up = up_own[index].reshape(tile_back, hidden)
        part = before_ref[:, cut].astype(F32) + rows_by_rows(pre_ref[...], up)
        part_ref[:, cut] = part.astype(BF16)
        return carry

    lax.fori_loop(0, width // tile_back, back, 0)


def second_products(rows_all, cotangent_all, before, piece, early, late, shift):
    rows, width = rows_all.shape
    lines, quarters, _, hidden = late.shape
    weights = (lines, quarters, width // (lines * quarters), hidden)
    steps = 4
    wide = pl.BlockSpec((rows // steps, width), lambda i: (i, 0))
    narrow = pl.BlockSpec((rows // steps, hidden), lambda i: (i, 0))
    anywhere = pl.BlockSpec(memory_space=pl.ANY)
    return pl.pallas_call(
        second_kernel,
        grid=(steps,),
        out_shape=[
            jax.ShapeDtypeStruct((rows, hidden), BF16),
            jax.ShapeDtypeStruct((rows, hidden), BF16),
            jax.ShapeDtypeStruct((rows, width), BF16),
            jax.ShapeDtypeStruct((8, hidden), F32),
        ],
        in_specs=[wide] * 3 + [anywhere] * 3 + [pl.BlockSpec((1, hidden), lambda i: (0, 0))],
        out_specs=[narrow, narrow, wide, pl.BlockSpec((8, hidden), lambda i: (0, 0))],
        scratch_shapes=[
            pltpu.VMEM(weights, BF16),
            pltpu.VMEM(weights, BF16),
            pltpu.SemaphoreType.DMA((3,)),
        ],
        compiler_params=pltpu.CompilerParams(vmem_limit_bytes=VMEM_BYTES),
        cost_estimate=SMALL,
    )(rows_all, cotangent_all, before, piece, early, late, shift)


def by_columns(left, right):
    return lax.dot_general(left, right, (((0,), (0,)), ((), ())), preferred_element_type=F32)


def weight_kernel(cotangent_ref, rows_ref, act_ref, pre_ref, out_ref):
    shards, _, shard_rows, hidden = out_ref.shape
    for kind, (left, right) in enumerate(((cotangent_ref, act_ref), (rows_ref, pre_ref))):
        grad = by_columns(left[...], right[...]).astype(BF16)
        out_ref[:, kind] = grad.reshape(shards, shard_rows, hidden)


def weight_products(cotangent_all, rows_all, act, pre, shards):
    rows, width = rows_all.shape
    hidden, steps = act.shape[1], 8
    columns = pl.BlockSpec((rows, width // steps), lambda i: (0, i))
    whole = pl.BlockSpec((rows, hidden), lambda i: (0, 0))
    return pl.pallas_call(
        weight_kernel,
        grid=(steps,),
        out_shape=jax.ShapeDtypeStruct((shards, 2, width // shards, hidden), BF16),
        in_specs=[columns, columns, whole, whole],
        out_specs=pl.BlockSpec((shards // steps, 2, width // shards, hidden), lambda i: (i, 0, 0, 0)),
        compiler_params=pltpu.CompilerParams(vmem_limit_bytes=VMEM_BYTES),
        cost_estimate=SMALL,
    )(cotangent_all, rows_all, act, pre)


def grads_kernel(programs, steps, *refs):
    count = len(programs)
    (cotangent_ref, rows_ref, act_a_ref, act_b_ref, pre_ref), refs = refs[:5], refs[5:]
    (piece_ref, early_ref, late_ref), refs = refs[:3], refs[3:]
    others, refs = refs[:count], refs[count:]
    (down_part_ref, weight_grad_ref), refs = refs[:2], refs[2:]
    other_outs, refs = refs[:count], refs[count:]
    (acts, pre_own, downs, load_sem, weight_sem), scratch = refs[:5], refs[5:]
    step = pl.program_id(0)
    finish = beside(programs, others, other_outs, scratch, step, steps)

    @pl.when(step == 0)
    def _():
        rows, first = downs.shape[3], piece_ref.shape[2]
        places = (piece_ref, early_ref, late_ref)
        copies = [
            pltpu.make_async_copy(act_a_ref, acts.at[0], load_sem.at[0]),
            pltpu.make_async_copy(act_b_ref, acts.at[1], load_sem.at[1]),
            pltpu.make_async_copy(pre_ref, pre_own, load_sem.at[2]),
        ]
        copies += weight_copies(first_half(rows, first, places)[0], downs.at[0], weight_sem.at[0])
        copies += weight_copies(second_half(rows, first, places)[0], downs.at[1], weight_sem.at[1])
        for one in copies:
            one.start()
        for one in copies:
            one.wait()

    tile, width = down_part_ref.shape
    rows = pl.ds(pl.multiple_of(step * tile, tile), tile)
    shards, _, shard_rows, hidden = weight_grad_ref.shape
    for kind, (left, right) in enumerate(((cotangent_ref, acts.at[1]), (rows_ref, pre_own))):
        grad = by_columns(left[...], right[...]).astype(BF16)
        weight_grad_ref[:, kind] = grad.reshape(shards, shard_rows, hidden)
    part = rows_by_rows(acts[0, rows, :], downs[0].reshape(width, hidden))
    part = part + rows_by_rows(acts[1, rows, :], downs[1].reshape(width, hidden))
    down_part_ref[...] = part.astype(BF16)
    finish()


def grad_products(
    cotangent_all, rows_all, act_a, act_b, pre, piece, early, late, programs, arrays, number
):
    rows, width = rows_all.shape
    lines, quarters, _, hidden = late.shape
    shards, shard_rows = lines * quarters, width // (lines * quarters)
    steps = 8
    columns = pl.BlockSpec((rows, width // steps), lambda i: (0, i))
    anywhere = pl.BlockSpec(memory_space=pl.ANY)
    grads = pl.BlockSpec((shards // steps, 2, shard_rows, hidden), lambda i: (i, 0, 0, 0))
    out = pl.pallas_call(
        functools.partial(grads_kernel, programs, steps),
        grid=(steps,),
        out_shape=[
            jax.ShapeDtypeStruct((rows, width), BF16),
            jax.ShapeDtypeStruct((shards, 2, shard_rows, hidden), BF16),
        ]
        + [one.out for one in programs],
        in_specs=[columns, columns] + [anywhere] * 6 + [one.in_spec for one in programs],
        out_specs=[pl.BlockSpec((rows // steps, width), lambda i: (i, 0)), grads]
        + [one.out_spec for one in programs],
        scratch_shapes=[
            pltpu.VMEM((2, rows, hidden), BF16),
            pltpu.VMEM((rows, hidden), BF16),
            pltpu.VMEM((2, lines, quarters, shard_rows, hidden), BF16),
            pltpu.SemaphoreType.DMA((3,)),
            pltpu.SemaphoreType.DMA((2, 2)),
        ]
        + [held for one in programs for held in one.scratch()],
        compiler_params=pltpu.CompilerParams(
            collective_id=number, has_side_effects=True, vmem_limit_bytes=VMEM_BYTES
        ),
        cost_estimate=SMALL,
    )(cotangent_all, rows_all, act_a, act_b, pre, piece, early, late, *arrays)
    return out[0], out[1], out[2:]


def reorder_kernel(cuts, size, x_ref, out_ref):
    for index, cut in enumerate(cuts):
        out_ref[:, index * size : (index + 1) * size] = x_ref[:, cut : cut + size]


def reorder(values, cuts):
    size = values.shape[1] // len(cuts)
    if size % 128:
        return jnp.concatenate([values[:, cut : cut + size] for cut in cuts], axis=1)
    return pl.pallas_call(
        functools.partial(reorder_kernel, cuts, size),
        out_shape=jax.ShapeDtypeStruct(values.shape, values.dtype),
        compiler_params=pltpu.CompilerParams(vmem_limit_bytes=VMEM_BYTES),
        cost_estimate=SMALL,
    )(values)


def to_line_order(values):
    lines = lax.axis_size("line")
    size = values.shape[1] // (2 * lines)
    return reorder(
        values, [(half * lines + shard) * size for shard in range(lines) for half in range(2)]
    )


def from_line_order(values):
    lines = lax.axis_size("line")
    size = values.shape[1] // (2 * lines)
    return reorder(
        values, [(shard * 2 + half) * size for half in range(2) for shard in range(lines)]
    )


def meet_sibling(me):
    barrier = pltpu.get_barrier_semaphore()
    pl.semaphore_signal(barrier, inc=1, device_id=flip(me, "tp"), device_id_type=MESH_ID)
    pl.semaphore_wait(barrier, 1)


def half_rows_of(core, rows):
    return pl.ds(pl.multiple_of(core * rows, rows), rows)


def each_rows(total, tile, work):
    def one(index, carry):
        work(pl.ds(pl.multiple_of(index * tile, tile), tile))
        return carry

    lax.fori_loop(0, total // tile, one, 0)


def each_columns(total, tile, work):
    each_rows(total, tile, work)


def moments(values):
    centered = values - jnp.mean(values, axis=1, keepdims=True)
    spread = jnp.mean(centered * centered, axis=1, keepdims=True)
    return centered, lax.rsqrt(spread + EPSILON)


def norm_back(values, gain, grad):
    centered, rstd = moments(values)
    xhat = centered * rstd
    scaled = grad * gain
    inner = jnp.mean(scaled * xhat, axis=1, keepdims=True)
    return xhat, rstd * (scaled - jnp.mean(scaled, axis=1, keepdims=True) - xhat * inner)


def fold_rows(values):
    return jnp.sum(values.reshape(values.shape[0] // 8, 8, values.shape[1]), axis=0)


def shuffled(cuts, ref, rows):
    if cuts is None:
        return ref[rows, :]
    size = ref.shape[1] // len(cuts)
    return jnp.concatenate([ref[rows, cut : cut + size] for cut in cuts], axis=1)


def norm_work(me, refs, out_ref):
    stream_ref, gain_ref, shift_ref = refs
    gain, shift = gain_ref[...].astype(F32), shift_ref[...].astype(F32)

    def work(rows):
        centered, rstd = moments(stream_ref[rows, :].astype(F32))
        out_ref[rows, :] = (centered * rstd * gain + shift).astype(BF16)

    each_rows(out_ref.shape[0], 32, work)


def reorder_work(cuts, me, x_ref, out_ref):
    half, size = out_ref.shape[0], out_ref.shape[1] // len(cuts)
    few = 64

    def work(rows):
        start = pl.multiple_of(me["tp"] * half + rows.start, few)
        for index, cut in enumerate(cuts):
            out_ref[rows, index * size : (index + 1) * size] = x_ref[
                pl.ds(start, few), cut : cut + size
            ]

    each_rows(half, few, work)


def part_work(me, refs, out_ref):
    normed_ref, weight_ref, shift_ref = refs
    heads = weight_ref.shape[1] - out_ref.shape[1]
    part = jnp.dot(normed_ref[...], weight_ref[:, heads:], preferred_element_type=F32)
    out_ref[...] = (part + shift_ref[:, heads:]).astype(BF16)


def query_work(me, refs, out_ref):
    normed_ref, weight_ref, shift_ref = refs

    def work(cut):
        query = jnp.dot(normed_ref[...], weight_ref[:, cut], preferred_element_type=F32)
        out_ref[:, cut] = (query + shift_ref[:, cut]).astype(BF16)

    each_columns(out_ref.shape[1], 256, work)


def project_kernel(
    cuts,
    mixed_ref,
    proj_ref,
    stream_ref,
    bias_ref,
    gain_ref,
    shift_ref,
    middle_ref,
    normed_ref,
    sent_ref,
    got_ref,
    sems,
):
    me = here()
    half, width = middle_ref.shape
    mine, other = half_rows_of(me["tp"], half), half_rows_of(1 - me["tp"], half)
    tile = 512
    meet_sibling(me)
    copy = remote(sent_ref, got_ref, sems.at[0], sems.at[1], flip(me, "tp"))

    def part(rows, target):
        def work(cut):
            target[:, cut] = rows_by_rows(mixed_ref[rows, :], proj_ref[cut, :])

        each_columns(width, tile, work)

    part(other, sent_ref)
    copy.start()
    part(mine, middle_ref)
    copy.wait_recv()
    bias, gain = bias_ref[...].astype(F32), gain_ref[...].astype(F32)
    shift = shift_ref[...].astype(F32)
    few = 32

    def finish(rows):
        start = pl.multiple_of(me["tp"] * half + rows.start, few)
        stream = stream_ref[pl.ds(start, few), :].astype(F32)
        middle = stream + (middle_ref[rows, :] + got_ref[rows, :] + bias)
        middle_ref[rows, :] = middle
        centered, rstd = moments(middle)
        normed = (centered * rstd * gain + shift).astype(BF16)
        if cuts is None:
            normed_ref[rows, :] = normed
            return
        size = width // len(cuts)
        for index, cut in enumerate(cuts):
            normed_ref[rows, index * size : (index + 1) * size] = normed[:, cut : cut + size]

    each_rows(half, few, finish)
    copy.wait_send()


def in_vmem(count):
    return [pl.BlockSpec(memory_space=pltpu.VMEM)] * count


def kernel_params(number):
    return pltpu.CompilerParams(
        collective_id=number, has_side_effects=True, vmem_limit_bytes=VMEM_BYTES
    )


def line_cuts(width, back):
    lines = lax.axis_size("line")
    size = width // (2 * lines)
    if size % 128:
        return None
    if back:
        return [(shard * 2 + half) * size for half in range(2) for shard in range(lines)]
    return [(half * lines + shard) * size for shard in range(lines) for half in range(2)]


def project(mixed, proj_all, stream, bias, gain, shift, number):
    rows, width = stream.shape
    half = rows // 2
    cuts = line_cuts(width, False)
    middle, normed = pl.pallas_call(
        functools.partial(project_kernel, cuts),
        out_shape=[
            jax.ShapeDtypeStruct((half, width), F32),
            jax.ShapeDtypeStruct((half, width), BF16),
        ],
        in_specs=in_vmem(6),
        out_specs=in_vmem(2),
        scratch_shapes=[
            pltpu.VMEM((half, width), F32),
            pltpu.VMEM((half, width), F32),
            pltpu.SemaphoreType.DMA((2,)),
        ],
        compiler_params=kernel_params(number),
        cost_estimate=SMALL,
    )(mixed, proj_all, stream, bias[None], gain[None], shift[None])
    return middle, normed if cuts else to_line_order(normed)


def middle_back_kernel(
    cuts,
    sum_ref,
    middle_ref,
    cotangent_ref,
    mixed_ref,
    proj_ref,
    gain_ref,
    grad_middle_ref,
    grad_mixed_ref,
    proj_grad_ref,
    sums_ref,
    attn_ref,
    sums_own,
    sems,
):
    me = here()
    half, width = middle_ref.shape
    mine, other = half_rows_of(me["tp"], half), half_rows_of(1 - me["tp"], half)
    few = 32
    gain = gain_ref[...].astype(F32)
    meet_sibling(me)
    sums_own[...] = jnp.zeros_like(sums_own)

    def norm(rows):
        start = pl.multiple_of(me["tp"] * half + rows.start, few)
        cotangent = cotangent_ref[pl.ds(start, few), :].astype(F32)
        grad = shuffled(cuts, sum_ref, rows)
        xhat, back = norm_back(middle_ref[rows, :], gain, grad)
        grad_middle = cotangent + back
        grad_middle_ref[rows, :] = grad_middle
        attn = grad_middle.astype(BF16)
        attn_ref[pl.ds(start, few), :] = attn
        sums_own[0] += fold_rows(grad * xhat)
        sums_own[1] += fold_rows(grad)
        sums_own[2] += fold_rows(attn.astype(F32))
        sums_own[3] += fold_rows(cotangent)

    each_rows(half, few, norm)
    copy = remote(attn_ref.at[mine], attn_ref.at[mine], sems.at[0], sems.at[1], flip(me, "tp"))
    copy.start()

    def to_heads(rows):
        def work(cut):
            grad = jnp.dot(attn_ref[rows, :], proj_ref[:, cut], preferred_element_type=F32)
            grad_mixed_ref[rows, cut] = grad.astype(BF16)

        each_columns(proj_ref.shape[1], 256, work)

    to_heads(mine)
    for kind in range(4):
        sums_ref[kind : kind + 1, :] = jnp.sum(sums_own[kind], axis=0, keepdims=True)
    sums_ref[4:8, :] = jnp.zeros((4, width), F32)
    copy.wait_recv()
    to_heads(other)

    def weight(cut):
        grad = lax.dot_general(
            attn_ref[:, cut], mixed_ref[...], (((0,), (0,)), ((), ())), preferred_element_type=F32
        )
        proj_grad_ref[cut, :] = grad.astype(BF16)

    each_columns(width, 256, weight)
    copy.wait_send()


def middle_back(grad_sum, middle, cotangent, mixed, proj_all, gain, number):
    rows, width = cotangent.shape
    half, heads = rows // 2, mixed.shape[1]
    cuts = line_cuts(width, True)
    return pl.pallas_call(
        functools.partial(middle_back_kernel, cuts),
        out_shape=[
            jax.ShapeDtypeStruct((half, width), F32),
            jax.ShapeDtypeStruct((rows, heads), BF16),
            jax.ShapeDtypeStruct((width, heads), BF16),
            jax.ShapeDtypeStruct((8, width), F32),
        ],
        in_specs=in_vmem(6),
        out_specs=in_vmem(4),
        scratch_shapes=[
            pltpu.VMEM((rows, width), BF16),
            pltpu.VMEM((4, 8, width), F32),
            pltpu.SemaphoreType.DMA((2,)),
        ],
        compiler_params=kernel_params(number),
        cost_estimate=SMALL,
    )(grad_sum if cuts else from_line_order(grad_sum), middle, cotangent, mixed, proj_all, gain[None])


def first_back_kernel(cuts, programs, *refs):
    (
        grad_query_ref,
        grad_part_ref,
        first_ref,
        stream_ref,
        normed_ref,
        gain_ref,
        grad_middle_ref,
        mlp_ref,
        middle_ref,
        bias_ref,
        middle_sums_ref,
        hidden_sums_ref,
        cut_a_ref,
        cut_b_ref,
    ), refs = refs[:14], refs[14:]
    (input_ref, layer_ref, down_out, up_out, part_out, total_out), refs = refs[:6], refs[6:]
    (weight_ref, vector_ref, sent_ref, got_ref, grad_first_ref, held_ref, sems), scratch = refs[:7], refs[7:]
    me = here()
    rows, width = stream_ref.shape
    half, heads = rows // 2, grad_query_ref.shape[1]
    shard_rows = part_out.shape[0]
    mine, other = half_rows_of(me["tp"], half), half_rows_of(1 - me["tp"], half)
    few = 32
    sibling = flip(me, "tp")
    works = schedule(
        programs,
        (
            (cut_a_ref.at[:, :shard_rows], cut_b_ref.at[:, :shard_rows]),
            (cut_a_ref.at[:, shard_rows:], cut_b_ref.at[:, shard_rows:]),
            weight_ref.reshape(2, -1, 2, shard_rows, weight_ref.shape[1]),
            vector_ref,
        ),
        (down_out, up_out, part_out, total_out),
        scratch,
        ("tp",),
    )

    def run_until(stop):
        while works and works[0][0] < stop:
            works.pop(0)[1]()

    run_until(0.1)
    grad_first_ref[:, :heads] = grad_query_ref[...]
    grad_first_ref[:, heads:] = grad_part_ref[...].astype(BF16)

    def weight(cut):
        grad = lax.dot_general(
            normed_ref[:, cut],
            grad_first_ref[:, heads:],
            (((0,), (0,)), ((), ())),
            preferred_element_type=F32,
        )
        weight_ref[cut, :] = grad.astype(BF16)

    each_columns(width, 512, weight)
    run_until(0.2)

    def part(at, target):
        def work(cut):
            target[:, cut] = rows_by_rows(grad_first_ref[at, :], first_ref[cut, :])

        each_columns(width, 512, work)

    part(other, sent_ref)
    sums_copy = remote(sent_ref, got_ref, sems.at[0], sems.at[1], sibling)
    sums_copy.start()
    run_until(0.3)
    bias = bias_ref[...].astype(F32)

    def layer(at):
        start = pl.multiple_of(me["tp"] * half + at.start, few)
        out = middle_ref[at, :] + (shuffled(cuts, mlp_ref, at) + bias)
        layer_ref[pl.ds(start, few), :] = out.astype(BF16)

    each_rows(half, few, layer)
    layer_copy = remote(layer_ref.at[mine], layer_ref.at[mine], sems.at[2], sems.at[3], sibling)
    layer_copy.start()
    run_until(0.4)
    grad_own, folded = held_ref.at[0], held_ref.at[1]
    part(mine, grad_own)
    run_until(0.5)
    sums_copy.wait_recv()
    gain = gain_ref[...].astype(F32)
    folded[0:16, :] = jnp.zeros((16, width), F32)

    def norm(at):
        start = pl.multiple_of(me["tp"] * half + at.start, few)
        grad = grad_own[at, :] + got_ref[at, :]
        xhat, back = norm_back(stream_ref[pl.ds(start, few), :].astype(F32), gain, grad)
        input_ref[pl.ds(start, few), :] = (grad_middle_ref[at, :] + back).astype(BF16)
        folded[0:8, :] += fold_rows(grad * xhat)
        folded[8:16, :] += fold_rows(grad)

    each_rows(half, few, norm)
    input_copy = remote(input_ref.at[mine], input_ref.at[mine], sems.at[4], sems.at[5], sibling)
    input_copy.start()
    vector_ref[...] = jnp.zeros_like(vector_ref)
    vector_ref[0:1, :width] = jnp.sum(folded[0:8, :], axis=0, keepdims=True)
    vector_ref[0:1, width : 2 * width] = jnp.sum(folded[8:16, :], axis=0, keepdims=True)
    for kind in range(4):
        at = slice(kind % 2 * width, (kind % 2 + 1) * width)
        vector_ref[1 + kind // 2 : 2 + kind // 2, at] = middle_sums_ref[kind : kind + 1, :]
    query_sums = jnp.sum(fold_rows(grad_query_ref[...].astype(F32)), axis=0, keepdims=True)
    part_sums = jnp.sum(
        fold_rows(grad_first_ref[:, heads:].astype(F32)), axis=0, keepdims=True
    )
    hidden_sums = jnp.sum(hidden_sums_ref[...], axis=0, keepdims=True)
    hidden, part_width = hidden_sums.shape[1], part_sums.shape[1]
    for core in range(2):
        own = me["tp"] == core
        vector_ref[3:4, core * heads : (core + 1) * heads] = jnp.where(own, query_sums, 0.0)
        for quarter in range(4):
            here_too = own & (quarter_of(me) == quarter)
            vector_ref[4 + core : 5 + core, quarter * hidden : (quarter + 1) * hidden] = jnp.where(
                here_too, hidden_sums, 0.0
            )
    vector_ref[3:4, 2 * heads : 2 * heads + part_width] = jnp.where(me["tp"] == 1, part_sums, 0.0)
    run_until(2.0)
    layer_copy.wait()
    input_copy.wait()
    sums_copy.wait_send()


def first_back(
    grad_query,
    grad_part,
    first_all,
    stream,
    normed,
    gain,
    grad_middle,
    mlp_sum,
    middle,
    bias,
    middle_sums,
    hidden_sums,
    cut_a,
    cut_b,
    number,
):
    rows, width = stream.shape
    half, heads, part = rows // 2, grad_query.shape[1], grad_part.shape[1]
    lines, hidden = lax.axis_size("line"), hidden_sums.shape[1]
    cuts = line_cuts(width, True)
    shard_rows = width // (4 * lines)
    vector = (8, max(2 * width, 4 * hidden, 2 * heads + part))
    programs = [
        placed(join_halves(shard_rows, 8 * cut_a.shape[2], BF16), 0.0, 1.0),
        placed(join_halves(shard_rows, 8 * cut_a.shape[2], BF16), 0.0, 1.0),
        placed(
            Sum((FRONT, SIDE), lines, shard_rows, part, by_rows_slot, part),
            0.1, *spaced(0.9, 0.99, lines + 3),
        ),
        placed(Total(jax.ShapeDtypeStruct(vector, F32), lines), 0.9, 0.99),
    ]
    anywhere = [pl.BlockSpec(memory_space=pl.ANY)] * 2
    return pl.pallas_call(
        functools.partial(first_back_kernel, cuts, programs),
        out_shape=[
            jax.ShapeDtypeStruct((rows, width), BF16),
            jax.ShapeDtypeStruct((rows, width), BF16),
        ]
        + [one.out for one in programs],
        in_specs=in_vmem(12) + anywhere,
        out_specs=in_vmem(2) + [one.out_spec for one in programs],
        scratch_shapes=[
            pltpu.VMEM((width, part), BF16),
            pltpu.VMEM(vector, F32),
            pltpu.VMEM((half, width), F32),
            pltpu.VMEM((half, width), F32),
            pltpu.VMEM((rows, heads + part), BF16),
            pltpu.VMEM((2, half, width), F32),
            pltpu.SemaphoreType.DMA((6,)),
        ]
        + [held for one in programs for held in one.scratch()],
        compiler_params=kernel_params(number),
        cost_estimate=SMALL,
    )(
        grad_query,
        grad_part,
        first_all,
        stream,
        normed,
        gain[None],
        grad_middle,
        mlp_sum if cuts else from_line_order(mlp_sum),
        middle,
        bias[None],
        middle_sums,
        hidden_sums,
        cut_a,
        cut_b,
    )


def body(
    hidden_in,
    block_order,
    attn_norm_gain,
    attn_norm_bias,
    query_weight,
    query_bias,
    keyval_weight,
    value_bias,
    proj_weight,
    proj_bias,
    mlp_norm_gain,
    mlp_norm_bias,
    up_weight,
    up_bias,
    down_weight,
    down_bias,
    out_cotangent,
):
    rows_dev = hidden_in.shape[0]
    half_rows = rows_dev // 2
    width = hidden_in.shape[1]
    blocks_dev = rows_dev // BLK
    slot_count = block_order.shape[1]
    group_blocks = PBLK + CONTS
    heads_dev = query_bias.shape[0] // HD
    head_width = heads_dev * HD
    core = lax.axis_index("tp")
    quarter = lax.axis_index("fsdp") * lax.axis_size("pair") + lax.axis_index("pair")
    quarters = lax.axis_size("fsdp") * lax.axis_size("pair")
    hidden_dev = up_weight.shape[1] // quarters

    def own_half(values):
        return lax.dynamic_slice_in_dim(values, core * half_rows, half_rows, axis=0)

    def in_order(mine, other, axis=0):
        first = jnp.where(core == 0, mine, other)
        second = jnp.where(core == 0, other, mine)
        return jnp.concatenate([first, second], axis=axis)


    slot_ids = jnp.arange(slot_count, dtype=jnp.int32)
    ordering = block_order[0]
    inverse = jnp.sum(
        jnp.where(ordering[None, :] == slot_ids[:, None], slot_ids[None, :], 0), axis=1
    )
    ctx_index = lax.axis_index("line") * lax.axis_size("pair") + lax.axis_index("pair")
    first_slot = ctx_index * blocks_dev
    my_slots = first_slot + jnp.arange(blocks_dev, dtype=jnp.int32)
    my_blocks = lax.dynamic_slice_in_dim(ordering, first_slot, blocks_dev)
    positions = my_blocks % group_blocks
    group_base = my_blocks // group_blocks * group_blocks
    prompt_slots = jnp.take(
        inverse, group_base[:, None] + jnp.arange(PBLK, dtype=jnp.int32)[None, :]
    )
    key_slots = jnp.concatenate([prompt_slots, my_slots[:, None]], axis=1)

    keyval_cut = lax.dynamic_slice_in_dim(keyval_weight, core * HD, HD, axis=1)
    first_cut = jnp.concatenate([query_weight, keyval_cut], axis=1)
    shard_rows = down_weight.shape[0]
    hidden_half = hidden_dev // 2
    columns = down_weight.shape[1]
    first_rows = shard_rows * 3 // 4 // 16 * 16
    early_rows = shard_rows // 2
    cuts = line_cuts(width, False)
    lines = lax.axis_size("line")
    first_pieces = [(0, slice(0, first_rows), 0)]
    early_pieces = [
        (0, slice(first_rows, shard_rows), 0),
        (1, slice(0, shard_rows), 0),
        (0, slice(0, early_rows), 1),
    ]
    late_pieces = [(0, slice(early_rows, shard_rows), 1), (1, slice(0, shard_rows), 1)]
    hops = [0.1 * k for k in range(1, 4)] if lines == 4 else spaced(0.1, 0.3, lines - 1)
    levels = spaced(0.4, 0.98, 2 * lines)
    piece_hops = spaced(0.35, 0.75, lines - 1)
    _, first_all, early_cut, late_cut, mlp_piece, normed_one, cotangent_line = run_programs(
        [
            placed(spread_halves(first_pieces, columns, BF16), 0.0, 0.05),
            placed(rows_gather(first_cut), 0.01, *hops, *levels, 1.0),
            placed(spread_halves(early_pieces, columns, BF16), 0.06, 1.0),
            placed(spread_halves(late_pieces, columns, BF16), 0.061, 1.0),
            placed(line_gather((quarters, first_rows, hidden_half), BF16), 0.07, *piece_hops, 1.0),
            placed(Work(norm_work, hidden_in.shape, BF16), 0.31, 0.31),
            placed(Work(functools.partial(reorder_work, cuts or [0]), (half_rows, width), BF16), 0.32, 0.32),
        ],
        [
            lambda more, outs: more[4:6],
            lambda more, outs: more[6],
            lambda more, outs: more[4:6],
            lambda more, outs: more[4:6],
            lambda more, outs: outs[0],
            lambda more, outs: more[:3],
            lambda more, outs: more[3],
        ],
        1,
        near=[hidden_in, attn_norm_gain[None], attn_norm_bias[None], out_cotangent],
        far=[down_weight, up_weight, first_cut],
    )
    if cuts is None:
        cotangent_line = to_line_order(own_half(out_cotangent))
    first_all = flat(first_all)

    value_shift = jnp.where(core == 1, value_bias.astype(F32), 0.0)
    first_shift = jnp.concatenate([query_bias.astype(F32), value_shift])
    part_like = (rows_dev, HD)
    _, query_low, keyval_every, proj_line = run_programs(
        [
            placed(Work(part_work, part_like, BF16), 0.0, 0.0),
            placed(Work(query_work, (rows_dev, head_width), BF16), 0.2, 0.2),
            placed(ctx_gather(part_like, BF16), 0.1, 1.0),
            placed(line_gather(proj_weight.shape, BF16), 0.11, 1.0),
        ],
        [
            lambda more, outs: more[:3],
            lambda more, outs: more[:3],
            lambda more, outs: outs[0],
            lambda more, outs: more[3],
        ],
        4,
        near=[normed_one, first_all, first_shift[None]],
        far=[proj_weight],
    )
    keyval_every, early_cut = lax.optimization_barrier((keyval_every, early_cut))
    mlp_early = lax.all_gather(early_cut, "line", axis=0, tiled=False)
    table = keyval_every.reshape(2, slot_count, BLK, HD)
    mixed_low, logsums, (proj_all, cotangent_all) = attend(
        query_low,
        table,
        positions,
        key_slots,
        [
            placed(columns_gather(proj_line), 0.0, 0.9, 1.0, 1.0),
            placed(plane_gather(cotangent_line), 0.0, 0.9, 1.0, 1.0),
        ],
        [proj_line, cotangent_line],
        2,
    )
    proj_all = flat(proj_all)
    mixed_low, mlp_early, late_cut = lax.optimization_barrier((mixed_low, mlp_early, late_cut))
    mlp_late = lax.all_gather(late_cut, "line", axis=0, tiled=False)
    middle, normed_two_line = project(
        mixed_low, proj_all, hidden_in, proj_bias, mlp_norm_gain, mlp_norm_bias, 5
    )

    up_shift = lax.dynamic_slice_in_dim(up_bias, quarter * hidden_dev, hidden_dev).astype(F32)
    up_shift = up_shift[None]
    shards = lines * quarters
    rows_all, act_a, pre_a, back_a, bias_a = forward_products(
        normed_two_line, cotangent_all, mlp_piece, mlp_early, up_shift[:, :hidden_half], 6
    )
    rows_all, act_a, pre_a, back_a = flat(rows_all), flat(act_a), flat(pre_a), flat(back_a)
    cotangent_all = flat(cotangent_all)
    weight_grad_a = weight_products(cotangent_all, rows_all, act_a, pre_a, shards)
    cut_a = lax.psum_scatter(weight_grad_a, "line", scatter_dimension=0, tiled=True)
    rows_all, weight_grad_a = lax.optimization_barrier((rows_all, weight_grad_a))
    act_b, pre_b, back_both, bias_b = second_products(
        rows_all,
        cotangent_all,
        back_a,
        mlp_piece,
        mlp_early,
        mlp_late,
        up_shift[:, hidden_half:],
    )
    plane_two, plane_parts = plane_sum(back_both)
    placed(plane_two, 0.0, 0.13, 0.13, 0.13, 0.13, 0.51, 0.9, 1.0, 1.0)
    down_part, weight_grad_b, (grad_normed_two,) = grad_products(
        cotangent_all,
        rows_all,
        act_a,
        act_b,
        pre_b,
        mlp_piece,
        mlp_early,
        mlp_late,
        [plane_two],
        [plane_parts],
        7,
    )
    cut_b = lax.psum_scatter(weight_grad_b, "line", scatter_dimension=0, tiled=True)
    cut_a = cut_a.reshape(quarters, 2 * shard_rows, hidden_half)
    cut_b = cut_b.reshape(quarters, 2 * shard_rows, hidden_half)
    up_bias_parts = jnp.concatenate([bias_a, bias_b], axis=1)

    grad_middle, grad_mixed, proj_weight_grad, middle_sums = middle_back(
        grad_normed_two, middle, out_cotangent, mixed_low, proj_all, mlp_norm_gain, 8
    )
    grad_mixed, cut_a = lax.optimization_barrier((grad_mixed, cut_a))
    sum_proj, proj_parts = rows_sum(proj_weight_grad)
    sum_down, down_parts = plane_sum(down_part)
    grad_query, grad_sets, (grad_proj_weight, mlp_out) = attend_back(
        query_low,
        grad_mixed,
        mixed_low,
        logsums,
        table,
        positions,
        key_slots,
        [
            placed(sum_proj, 0.0, 0.13, 0.26, 0.38, 0.51, 0.63, 0.7, 0.9),
            placed(sum_down, 0.0, 0.45, 0.45, 0.45, 0.45, 0.76, 0.95, 1.0, 1.0),
        ],
        [proj_parts, down_parts],
        3,
    )
    grad_table = by_slot(grad_sets, key_slots, slot_count)
    grad_parts = grad_table.reshape(
        2, lax.axis_size("line"), lax.axis_size("pair"), rows_dev, HD
    )
    query_weight_grad = jnp.einsum("rd,rk->dk", normed_one, grad_query, preferred_element_type=F32)
    sum_query, query_parts = rows_sum(query_weight_grad)
    grad_part, grad_query_weight = run_programs(
        [ctx_sum(grad_parts), sum_query], [grad_parts, query_parts], 12
    )
    input_grad, layer_out, down_wide, up_wide, grad_part_weight, summed = first_back(
        grad_query,
        grad_part,
        first_all,
        hidden_in,
        normed_one,
        attn_norm_gain,
        grad_middle,
        mlp_out,
        middle,
        down_bias,
        middle_sums,
        up_bias_parts,
        cut_a,
        cut_b,
        9,
    )
    grad_down_weight, grad_up_weight = down_wide.astype(F32), up_wide.astype(F32)
    grad_keyval_weight = in_order(grad_part_weight[:, :HD], grad_part_weight[:, HD:], axis=1)
    sum_query = lax.dynamic_slice_in_dim(summed[3], core * head_width, head_width)
    sum_up = jnp.where(core == 0, summed[4], summed[5])[: quarters * hidden_dev]
    return (
        layer_out,
        input_grad,
        summed[0, :width],
        summed[0, width : 2 * width],
        grad_query_weight,
        sum_query,
        grad_keyval_weight,
        summed[3, 2 * head_width : 2 * head_width + HD],
        grad_proj_weight,
        summed[2, :width],
        summed[1, :width],
        summed[1, width : 2 * width],
        grad_up_weight,
        sum_up,
        grad_down_weight,
        summed[2, width : 2 * width],
    )


def solution(mesh):
    fsdp, ctx, tp = mesh.devices.shape
    grid = Mesh(mesh.devices.reshape(fsdp, ctx // 2, 2, tp), EVERY)
    by_rows = P(ROWS, None)
    by_both = P(ROWS, "tp")
    return jax.shard_map(
        body,
        mesh=grid,
        in_specs=(
            by_rows,
            P("fsdp", None),
            P(),
            P(),
            by_both,
            P("tp"),
            by_rows,
            P(),
            by_both,
            P(),
            P(),
            P(),
            by_both,
            P("tp"),
            by_both,
            P(),
            by_rows,
        ),
        out_specs=(
            by_rows,
            by_rows,
            P(),
            P(),
            by_both,
            P("tp"),
            by_rows,
            P(),
            by_both,
            P(),
            P(),
            P(),
            by_both,
            P("tp"),
            by_both,
            P(),
        ),
        check_vma=False,
    )
```

```python
import functools

import jax
import jax.numpy as jnp
from jax import lax
from jax.experimental import pallas as pl
from jax.experimental.pallas import tpu as pltpu
from jax.sharding import Mesh, PartitionSpec as P

HD = 128
BLK = 256
PBLK = 8
CONTS = 8
EPSILON = 1e-05
MASKED = -1e30
F32 = jnp.float32
BF16 = jnp.bfloat16
ROWS = ("fsdp", "line", "pair")
EVERY = ("fsdp", "line", "pair", "tp")


MESH_ID = pl.DeviceIdType.MESH
VMEM_BYTES = 60 * 1024 * 1024
SMALL = pl.CostEstimate(flops=1, bytes_accessed=1, transcendentals=0)
SIDE = ("pair", "fsdp")
FRONT = ("fsdp", "pair")


def here():
    return {name: lax.axis_index(name) for name in EVERY}


def flip(place, step):
    place = dict(place)
    if isinstance(step, str):
        place[step] = 1 - place[step]
    else:
        core = place["tp"]
        for name, used in ((step[0], 1 - core), (step[1], core)):
            place[name] = place[name] + (1 - 2 * place[name]) * used
    return place


def along(place, amount):
    return dict(place, line=place["line"] + amount)


def remote(source, target, send_sem, recv_sem, place):
    return pltpu.make_async_remote_copy(
        src_ref=source,
        dst_ref=target,
        send_sem=send_sem,
        recv_sem=recv_sem,
        device_id=place,
        device_id_type=MESH_ID,
    )


def top_bit(bits):
    return bits.bit_length() - 1


def add_blocks(target, first, second, rows):
    tile = min(rows, 64)

    def one(index, carry):
        cut = pl.ds(pl.multiple_of(index * tile, tile), tile)
        total = first(cut).astype(F32)
        if second is not None:
            total = total + second(cut).astype(F32)
        target[cut, :] = total.astype(target.dtype)
        return carry

    lax.fori_loop(0, rows // tile, one, 0)


def rows_of(ref):
    return lambda cut: ref[cut, :]


class Gather:
    def __init__(self, values, steps, lines, shape, slot):
        self.steps, self.lines, self.slot = steps, lines, slot
        self.out = jax.ShapeDtypeStruct(shape, values.dtype)
        self.in_spec = self.out_spec = pl.BlockSpec(memory_space=pl.ANY)

    def scratch(self):
        parts = 1 << len(self.steps)
        return [
            pltpu.SemaphoreType.DMA(()),
            pltpu.SemaphoreType.DMA((2, self.lines)),
            pltpu.SemaphoreType.DMA((self.lines,)),
            pltpu.SemaphoreType.DMA((self.lines, max(1, len(self.steps)) * parts)),
            pltpu.SemaphoreType.DMA((self.lines, parts)),
        ]

    def stages(self, me, x_ref, out_ref, own_sem, line_send, line_recv, send, recv):
        steps, lines, slot = self.steps, self.lines, self.slot
        count = len(steps)
        my_line = me["line"] if lines > 1 else 0

        def block(bits, shard):
            place = me
            for k in reversed(range(count)):
                if bits >> k & 1:
                    place = flip(place, steps[k])
            return slot(out_ref, dict(place, line=shard))

        def to_step(k, bits, shard, source):
            return remote(
                source,
                block(bits, shard),
                send.at[shard, k * (1 << count) + bits],
                recv.at[shard, bits | 1 << k],
                flip(me, steps[k]),
            )

        def to_line(amount, shard, source):
            return remote(
                source,
                block(0, shard),
                line_send.at[(amount + 1) // 2, shard],
                line_recv.at[shard],
                along(me, amount),
            )

        def send_on(bits, shard, source):
            for k in range(top_bit(bits) + 1, count):
                to_step(k, bits, shard, source).start()

        def at_distance(distance, work):
            if distance == 0:
                work(my_line, 0)
                return
            for amount in (1, -1):
                shard = my_line - amount * distance
                pl.when((shard >= 0) & (shard < lines))(functools.partial(work, shard, amount))

        def line_inside(amount):
            there = my_line + amount
            return (there >= 0) & (there < lines)

        own = pltpu.make_async_copy(x_ref, block(0, my_line), own_sem)

        def begin():
            if lines > 1:
                for amount in (1, -1):
                    pl.when(line_inside(amount))(
                        lambda amount=amount: to_line(amount, my_line, x_ref).start()
                    )
            send_on(0, my_line, x_ref)
            own.start()

        def line_arrival(shard, amount):
            remote(
                block(0, shard), block(0, shard), line_send.at[0, shard], line_recv.at[shard], me
            ).wait_recv()
            pl.when(line_inside(amount))(lambda: to_line(amount, shard, block(0, shard)).start())
            send_on(0, shard, block(0, shard))

        def level_arrival(level, shard, amount):
            for bits in range(1 << level, 2 << level):
                remote(
                    block(bits, shard),
                    block(bits, shard),
                    send.at[shard, 0],
                    recv.at[shard, bits],
                    me,
                ).wait_recv()
                send_on(bits, shard, block(bits, shard))

        def end():
            own.wait()
            if lines > 1:
                for amount in (1, -1):
                    for distance in range(lines):
                        shard = my_line - amount * distance
                        pl.when((shard >= 0) & (shard < lines) & line_inside(amount))(
                            lambda amount=amount, shard=shard: to_line(
                                amount, shard, block(0, shard)
                            ).wait_send()
                        )
            for shard in range(lines):
                for bits in range(1 << count):
                    for k in range(top_bit(bits) + 1, count):
                        to_step(k, bits, shard, block(bits, shard)).wait_send()

        line = [functools.partial(at_distance, number, line_arrival) for number in range(1, lines)]
        levels = [
            functools.partial(at_distance, number - level, functools.partial(level_arrival, level))
            for number in range(lines + count - 1)
            for level in range(count)
            if 0 <= number - level < lines
        ]
        return [begin] + line + levels + [end]


class Sum:
    def __init__(self, steps, lines, rows, columns, slot, kind=F32):
        self.steps, self.lines, self.rows, self.columns = steps, lines, rows, columns
        self.slot = slot
        self.out = jax.ShapeDtypeStruct((rows, columns), kind)
        self.in_spec = pl.BlockSpec(memory_space=pl.ANY)
        self.out_spec = pl.BlockSpec(memory_space=pltpu.VMEM)

    def scratch(self):
        count, lines = len(self.steps), self.lines
        sizes = [1 << (count - 1 - k) for k in range(count)]
        block = (self.rows, self.columns)
        return (
            [pltpu.VMEM((lines, sizes[0]) + block, BF16)]
            + [pltpu.VMEM((lines, size) + block, BF16) for size in sizes]
            + [pltpu.VMEM((2, lines) + (block if lines > 1 else (16, 128)), BF16)]
            + [pltpu.SemaphoreType.DMA((lines, sizes[0]))]
            + [pltpu.SemaphoreType.DMA((lines, size)) for size in sizes] * 2
            + [pltpu.SemaphoreType.DMA((2, lines))] * 2
        )

    def stages(self, me, x_ref, out_ref, own, *rest):
        steps, lines, rows, slot = self.steps, self.lines, self.rows, self.slot
        count = len(steps)
        held, rest = rest[:count], rest[count:]
        on_line, own_sem, rest = rest[0], rest[1], rest[2:]
        send, recv = rest[:count], rest[count : 2 * count]
        line_send, line_recv = rest[2 * count :]
        my_line = me["line"] if lines > 1 else 0
        last = count - 1

        def target_of(bits, shard):
            place = me
            for k in range(count):
                if bits >> k & 1:
                    place = flip(place, steps[k])
            return dict(place, line=shard)

        def store(k, shard, bits):
            return held[k].at[shard, bits >> (k + 1)]

        def own_copy(shard, bits):
            return pltpu.make_async_copy(
                slot(x_ref, target_of(bits, shard)),
                own.at[shard, bits >> 1],
                own_sem.at[shard, bits >> 1],
            )

        def copy(k, shard, bits):
            source = slot(x_ref, target_of(bits, shard)) if k == 0 else store(k - 1, shard, bits)
            return remote(
                source,
                store(k, shard, bits ^ (1 << k)),
                send[k].at[shard, bits >> (k + 1)],
                recv[k].at[shard, bits >> (k + 1)],
                flip(me, steps[k]),
            )

        def parts_of(k):
            return [high << (k + 1) for high in reversed(range(1 << (count - 1 - k)))]

        def send_first(shard, amount):
            for bits in parts_of(0):
                copy(0, shard, bits | 1).start()

        def own_first(shard, amount):
            for bits in parts_of(0):
                own_copy(shard, bits).start()

        def take_step(k, shard, amount, parts=None):
            for bits in parts or parts_of(k):
                copy(k, shard, bits | 1 << k).wait_recv()
                arrived = store(k, shard, bits)
                if k == 0:
                    own_copy(shard, bits).wait()
                    mine = own.at[shard, bits >> 1]
                else:
                    mine = store(k - 1, shard, bits)
                add_blocks(arrived, rows_of(mine), rows_of(arrived), rows)
                if k + 1 < count and bits >> (k + 1) & 1:
                    copy(k + 1, shard, bits).start()

        def line_inside(amount):
            there = my_line + amount
            return (there >= 0) & (there < lines)

        def line_copy(amount, shard):
            way = (amount + 1) // 2
            return remote(
                on_line.at[way, shard],
                on_line.at[way, shard],
                line_send.at[way, shard],
                line_recv.at[way, shard],
                along(me, amount),
            )

        def each(distance, work):
            if distance == 0:
                work(my_line, 0)
                return
            for amount in (1, -1):
                shard = my_line + amount * distance
                pl.when((shard >= 0) & (shard < lines))(functools.partial(work, shard, amount))

        def line_step(shard, amount):
            done = held[last].at[shard, 0]
            moving = on_line.at[(amount + 1) // 2, shard]

            @pl.when(line_inside(-amount))
            def _():
                line_copy(amount, shard).wait_recv()
                add_blocks(moving, rows_of(moving), rows_of(done), rows)

            @pl.when(jnp.logical_not(line_inside(-amount)))
            def _():
                add_blocks(moving, rows_of(done), None, rows)

            line_copy(amount, shard).start()

        order = list(reversed(range(lines)))

        def begin():
            for distance in order:
                each(distance, send_first)
            for distance in order:
                each(distance, own_first)

        def tick(number):
            for k in reversed(range(count)):
                index = number - k
                if 0 <= index < lines:
                    each(order[index], functools.partial(take_step, k))
            index = number - count
            if 0 <= index < lines and order[index] > 0:
                each(order[index], line_step)

        def end():
            final = held[last].at[my_line, 0]
            if lines == 1:
                add_blocks(out_ref, rows_of(final), None, rows)
            else:
                for way, amount in enumerate((-1, 1)):

                    @pl.when(line_inside(-amount))
                    def _():
                        line_copy(amount, my_line).wait_recv()

                    @pl.when(jnp.logical_not(line_inside(-amount)))
                    def _():
                        add_blocks(on_line.at[way, my_line], lambda cut: jnp.zeros_like(final[cut, :]), None, rows)

                left, right = on_line.at[0, my_line], on_line.at[1, my_line]
                add_blocks(
                    out_ref,
                    lambda cut: final[cut, :].astype(F32) + left[cut, :].astype(F32),
                    rows_of(right),
                    rows,
                )

                for amount in (1, -1):
                    for distance in range(1, lines):
                        shard = my_line + amount * distance
                        pl.when((shard >= 0) & (shard < lines))(
                            lambda amount=amount, shard=shard: line_copy(amount, shard).wait_send()
                        )
            for k in range(count):
                for shard in range(lines):
                    for bits in parts_of(k):
                        copy(k, shard, bits | 1 << k).wait_send()

        if lines == 1:
            ticks = [
                functools.partial(take_step, k, 0, 0, [bits]) for k in range(count) for bits in parts_of(k)
            ]
        else:
            ticks = [functools.partial(tick, number) for number in range(lines + count)]
        return [begin] + ticks + [end]


DIRECT = (("pair",), ("fsdp",), ("pair", "fsdp"))


def move(me, names):
    place = me
    for name in names:
        place = flip(place, name)
    return place


def quarter_of(place):
    return place["fsdp"] * 2 + place["pair"]


class Exchange:
    steps, lines = ("pair", "fsdp"), 1

    def __init__(self, moves, shape, kind):
        self.moves = moves
        self.out = jax.ShapeDtypeStruct(shape, kind)
        self.in_spec = self.out_spec = pl.BlockSpec(memory_space=pl.ANY)

    def scratch(self):
        count = len(self.moves)
        return [
            pltpu.SemaphoreType.DMA((count,)),
            pltpu.SemaphoreType.DMA((count, 3)),
            pltpu.SemaphoreType.DMA((count, 3)),
        ]

    def stages(self, me, x_refs, out_ref, own_sem, send, recv):
        copies = []
        for n, (source, target) in enumerate(self.moves):
            there_ref = target(out_ref, quarter_of(me))
            for k, names in reversed(list(enumerate(DIRECT))):
                there = move(me, names)
                copies.append(
                    remote(
                        source(x_refs, quarter_of(there)), there_ref, send.at[n, k], recv.at[n, k], there
                    )
                )
            copies.append(
                pltpu.make_async_copy(source(x_refs, quarter_of(me)), there_ref, own_sem.at[n])
            )

        def begin():
            for one in copies:
                one.start()

        def end():
            for one in copies:
                one.wait()

        return [begin, end]


def half_quarter(ref, quarter, half, rows=None):
    columns = ref.shape[1] // 8
    cut = pl.ds(pl.multiple_of((quarter * 2 + half) * columns, columns), columns)
    return ref.at[:, cut] if rows is None else ref.at[rows, cut]


def spread_halves(pieces, columns, kind):
    moves, start = [], 0
    for index, rows, half in pieces:
        count = rows.stop - rows.start
        moves.append(
            (
                lambda refs, quarter, index=index, rows=rows, half=half: half_quarter(
                    refs[index], quarter, half, rows
                ),
                lambda ref, quarter, start=start, count=count: ref.at[quarter, start : start + count],
            )
        )
        start += count
    return Exchange(moves, (4, start, columns // 8), kind)


def join_halves(rows, columns, kind):
    moves = [
        (
            lambda refs, quarter, half=half: refs[half].at[quarter],
            lambda ref, quarter, half=half: half_quarter(ref, quarter, half),
        )
        for half in range(2)
    ]
    return Exchange(moves, (rows, columns), kind)


class Work:
    steps, lines = (), 1

    def __init__(self, work, shape, kind):
        self.work, self.out = work, jax.ShapeDtypeStruct(shape, kind)
        self.in_spec = self.out_spec = pl.BlockSpec(memory_space=pltpu.VMEM)

    def scratch(self):
        return []

    def stages(self, me, x_refs, out_ref):
        return [functools.partial(self.work, me, x_refs, out_ref), lambda: None]


class Direct:
    steps, rows_too = ("tp",), True

    def __init__(self, lines, rows, columns, shared):
        self.lines, self.rows, self.columns, self.shared = lines, rows, columns, shared
        self.out = jax.ShapeDtypeStruct((rows, columns + shared), F32)
        self.in_spec = self.out_spec = pl.BlockSpec(memory_space=pltpu.VMEM)

    def scratch(self):
        lines = self.lines
        return [
            pltpu.VMEM((2, lines, 2, self.rows, self.columns), BF16),
            pltpu.SemaphoreType.DMA((4, 2, lines)),
            pltpu.SemaphoreType.DMA((2, lines, 2)),
            pltpu.SemaphoreType.DMA((2,)),
        ]

    def stages(self, me, x_ref, out_ref, held, send, recv, share_sem):
        def on_others(work):
            for side in range(4):
                for distance in range(self.lines):
                    for way, amount in enumerate((1, -1) if distance else (1,)):
                        if side or distance:
                            place = along(plane_partner(me, side * 2), amount * distance)
                            inside = (place["line"] >= 0) & (place["line"] < self.lines)
                            pl.when(inside)(
                                functools.partial(work, place, send.at[side, way, distance])
                            )

        def copy(place, sem):
            return remote(
                by_rows_slot(x_ref, place),
                by_rows_slot(held, me),
                sem,
                by_rows_slot(recv, me),
                place,
            )

        def arrived(place, sem):
            slot = by_rows_slot(held, place)
            remote(slot, slot, sem, by_rows_slot(recv, place), me).wait_recv()

        def begin():
            on_others(lambda place, sem: copy(place, sem).start())
            held[me["fsdp"], me["line"], me["pair"]] = x_ref[me["fsdp"], me["line"], me["pair"]]

        def end():
            on_others(arrived)
            total = jnp.zeros((self.rows, self.columns), F32)
            for half in range(2):
                for shard in range(self.lines):
                    for side in range(2):
                        total = total + held[half, shard, side].astype(F32)
            out_ref[:, : self.columns] = total
            share = remote(
                out_ref.at[:, : self.columns],
                out_ref.at[:, self.columns :],
                share_sem.at[0],
                share_sem.at[1],
                flip(me, "tp"),
            )
            share.start()
            share.wait()
            on_others(lambda place, sem: copy(place, sem).wait_send())

        return [begin, end]


class Total:
    steps, everyone = (), True

    def __init__(self, shape, lines, special, heads):
        self.lines, self.shape, self.special, self.heads = lines, shape, special, heads
        self.out = jax.ShapeDtypeStruct((shape[0], 2 * shape[1]), F32)
        self.in_spec = self.out_spec = pl.BlockSpec(memory_space=pltpu.VMEM)

    def scratch(self):
        shape, lines = self.shape, self.lines
        return [
            pltpu.VMEM((lines,) + shape, F32),
            pltpu.VMEM((8,) + shape, F32),
            pltpu.SemaphoreType.DMA((2, lines)),
            pltpu.SemaphoreType.DMA((lines,)),
            pltpu.SemaphoreType.DMA((8,)),
            pltpu.SemaphoreType.DMA((8,)),
        ]

    def stages(self, me, x_ref, out_ref, on_line, on_plane, line_send, line_recv, send, recv):
        lines, mine = self.lines, me["line"]
        number = plane_number(me)

        def on_others(work):
            for distance in range(1, lines):
                for way, amount in enumerate((1, -1)):
                    there = mine + amount * distance
                    pl.when((there >= 0) & (there < lines))(
                        functools.partial(work, way, amount, distance, there)
                    )

        def to_line(way, amount, distance):
            return remote(
                on_line.at[mine],
                on_line.at[mine],
                line_send.at[way, distance],
                line_recv.at[mine],
                along(me, amount * distance),
            )

        def to_plane(bits):
            return remote(
                on_plane.at[number],
                on_plane.at[number],
                send.at[bits],
                recv.at[number],
                plane_partner(me, bits),
            )

        def begin():
            on_line[mine] = x_ref[...]
            on_others(lambda way, amount, distance, there: to_line(way, amount, distance).start())

        def arrived(way, amount, distance, there):
            remote(
                on_line.at[there], on_line.at[there], line_send.at[0, 0], line_recv.at[there], me
            ).wait_recv()

        def middle():
            on_others(arrived)
            total = on_line[0]
            for shard in range(1, lines):
                total = total + on_line[shard]
            on_plane[number] = total
            for bits in range(1, 8):
                to_plane(bits).start()

        def end():
            for bits in range(1, 8):
                there = plane_number(plane_partner(me, bits))
                remote(
                    on_plane.at[there], on_plane.at[there], send.at[0], recv.at[there], me
                ).wait_recv()
            total = on_plane[0]
            for other in range(1, 8):
                total = total + on_plane[other]
            width, row, heads = self.shape[1], slice(self.special, self.special + 1), self.heads
            out_ref[...] = jnp.zeros_like(out_ref)
            out_ref[:, :width] = total
            same = [on_plane[quarter * 2 + me["tp"], row, :] for quarter in range(4)]
            out_ref[row, :heads] = sum(part[:, :heads] for part in same)
            for quarter, part in enumerate(same):
                out_ref[quarter : quarter + 1, width : 2 * width - heads] = part[:, heads:]
            for bits in range(1, 8):
                to_plane(bits).wait_send()
            on_others(lambda way, amount, distance, there: to_line(way, amount, distance).wait_send())

        return [begin, middle, end]


def plane_number(place):
    return (place["fsdp"] * 2 + place["pair"]) * 2 + place["tp"]


def plane_partner(me, bits):
    place = me
    for bit, name in ((1, "tp"), (2, "pair"), (4, "fsdp")):
        if bits & bit:
            place = flip(place, name)
    return place


def greet(me, programs, partners=()):
    barrier = pltpu.get_barrier_semaphore()
    plane, reach, lines, corners = set(), 0, 1, False
    for one in programs:
        lines = max(lines, one.lines)
        if one.lines > 1:
            reach = max(reach, one.lines - 1 if hasattr(one, "everyone") else 1)
        if hasattr(one, "everyone"):
            plane |= set(range(1, 8))
        if isinstance(one, Exchange) or hasattr(one, "rows_too"):
            plane |= {2, 4, 6}
        if hasattr(one, "rows_too"):
            reach, corners = one.lines - 1, True
    for step in [step for one in programs for step in one.steps] + list(partners):
        plane |= {"tp": {1}, "pair": {2}, "fsdp": {4}}.get(step, {2, 4})
    for bits in sorted(plane):
        pl.semaphore_signal(
            barrier, inc=1, device_id=plane_partner(me, bits), device_id_type=MESH_ID
        )
    count = len(plane)
    for distance in range(1, reach + 1):
        for amount in (-distance, distance):
            there = me["line"] + amount
            inside = (there >= 0) & (there < lines)

            for bits in (0, 2, 4, 6) if corners else (0,):

                @pl.when(inside)
                def _():
                    pl.semaphore_signal(
                        barrier,
                        inc=1,
                        device_id=along(plane_partner(me, bits), amount),
                        device_id_type=MESH_ID,
                    )

                count = count + inside.astype(jnp.int32)
    pl.semaphore_wait(barrier, count)


def split_scratch(programs, refs):
    parts, start = [], 0
    for one in programs:
        size = len(one.scratch())
        parts.append(refs[start : start + size])
        start += size
    return parts


def schedule(programs, x_refs, out_refs, scratch, partners=()):
    me = here()
    works = [(0.0, functools.partial(greet, me, programs, partners))]
    for one, x_ref, out_ref, held in zip(programs, x_refs, out_refs, split_scratch(programs, scratch)):
        stages = one.stages(me, x_ref, out_ref, *held)
        places = getattr(one, "places", (0.0, 1.0))
        if len(places) == 2:
            places = spaced(places[0], places[1], len(stages))
        last = len(places) - 2
        works += [
            (places[-1] if k == len(stages) - 1 else places[min(k, last)], stage)
            for k, stage in enumerate(stages)
        ]
    return sorted(works, key=lambda work: work[0])


def placed(program, *places):
    program.places = list(places)
    return program


def spaced(start, stop, count):
    return [start + (stop - start) * k / (count - 1) for k in range(count)]


def run_programs(programs, arrays, number, near=(), far=()):
    count = len(programs)
    given = [k for k, array in enumerate(arrays) if not callable(array)]
    others = len(near) + len(far)

    def kernel(*refs):
        (more, refs) = refs[:others], refs[others:]
        plain, out_refs = refs[: len(given)], refs[len(given) : len(given) + count]
        in_refs = [
            array(more, out_refs) if callable(array) else plain[given.index(k)]
            for k, array in enumerate(arrays)
        ]
        for _, work in schedule(programs, in_refs, out_refs, refs[len(given) + count :]):
            work()

    return pl.pallas_call(
        kernel,
        out_shape=[one.out for one in programs],
        in_specs=[pl.BlockSpec(memory_space=pltpu.VMEM)] * len(near)
        + [pl.BlockSpec(memory_space=pl.ANY)] * len(far)
        + [programs[k].in_spec for k in given],
        out_specs=[one.out_spec for one in programs],
        scratch_shapes=[held for one in programs for held in one.scratch()],
        compiler_params=pltpu.CompilerParams(
            collective_id=number, has_side_effects=True, vmem_limit_bytes=VMEM_BYTES
        ),
        cost_estimate=SMALL,
    )(*near, *far, *[arrays[k] for k in given])


def by_rows_slot(ref, at):
    return ref.at[at["fsdp"], at["line"], at["pair"]]


def by_plane_slot(ref, at):
    return ref.at[at["fsdp"], at["pair"], at["tp"]]


def by_ctx_slot(ref, at):
    return ref.at[at["tp"], at["line"], at["pair"]]


def rows_gather(values):
    lines = lax.axis_size("line")
    return Gather(values, (SIDE, FRONT), lines, (2, lines, 2) + values.shape, by_rows_slot)


def line_gather(shape, kind):
    lines = lax.axis_size("line")
    like = jax.ShapeDtypeStruct(shape, kind)
    return Gather(like, (), lines, (lines,) + shape, lambda ref, at: ref.at[at["line"]])


def columns_gather(values):
    lines, rows, columns = values.shape
    return Gather(
        values, (SIDE, FRONT), 1, (2, lines, 2, rows, columns), lambda ref, at: ref.at[at["fsdp"], :, at["pair"]]
    )


def rows_sum(values):
    lines, (total, columns) = lax.axis_size("line"), values.shape
    rows = total // (4 * lines)
    parts = values.astype(BF16).reshape(2, lines, 2, rows, columns)
    return Sum((FRONT, SIDE), lines, rows, columns, by_rows_slot), parts


def plane_gather(values):
    return Gather(values, (SIDE, FRONT, "tp"), 1, (2, 2, 2) + values.shape, by_plane_slot)


def plane_sum(values):
    rows, columns = values.shape[0] // 8, values.shape[1]
    parts = values.astype(BF16).reshape(2, 2, 2, rows, columns)
    return Sum(("tp", FRONT, SIDE), 1, rows, columns, by_plane_slot), parts


def flat(values):
    return values.reshape(-1, values.shape[-1])


def ctx_gather(shape, kind):
    lines = lax.axis_size("line")
    like = jax.ShapeDtypeStruct(shape, kind)
    return Gather(like, ("pair", "tp"), lines, (2, lines, 2) + shape, by_ctx_slot)


def ctx_sums(values):
    _, lines, rows, columns = values.shape
    along_line = Sum(
        ("tp",), lines, rows, columns, lambda ref, at: ref.at[at["tp"], at["line"]], BF16
    )
    over_pair = Sum(("pair",), 1, rows // 2, columns, lambda ref, at: ref.at[at["pair"]])
    return along_line, over_pair


LOG2E = 1.4426950408889634


def visible_bias(bias_ref, position, chunks):
    prompt = position < PBLK
    row = lax.broadcasted_iota(jnp.int32, (BLK, BLK), 0)
    column = lax.broadcasted_iota(jnp.int32, (BLK, BLK), 1)
    limit = jnp.where(prompt, position * BLK + column, PBLK * BLK)
    for chunk in range(chunks - 1):
        bias_ref[chunk] = jnp.where(row + chunk * BLK <= limit, 0.0, MASKED)
    own_limit = jnp.where(prompt, -1, column)
    bias_ref[chunks - 1] = jnp.where(row <= own_limit, 0.0, MASKED)


def rows_by_rows(left, right):
    return lax.dot_general(left, right, (((1,), (1,)), ((), ())), preferred_element_type=F32)


def beside(programs, in_refs, out_refs, scratch, step, steps):
    late = []
    for place, work in schedule(programs, in_refs, out_refs, scratch):
        if place < 1:
            pl.when(step == int(place * steps))(work)
        else:
            late.append(work)

    def finish():
        @pl.when(step == steps - 1)
        def _():
            for work in late:
                work()

    return finish


def attend_kernel(programs, steps, *refs):
    count = len(programs)
    (position_ref, slot_ref, query_ref, table_ref), refs = refs[:4], refs[4:]
    others, refs = refs[:count], refs[count:]
    (mixed_ref, logsum_ref), refs = refs[:2], refs[2:]
    other_outs, refs = refs[:count], refs[count:]
    (bias_ref, score_ref, value_t_ref), scratch = refs[:3], refs[3:]
    chunks = PBLK + 1
    block = pl.program_id(0)
    factor = HD**-0.5 * LOG2E
    step = pl.program_id(0) * pl.num_programs(1) + pl.program_id(1)
    finish = beside(programs, others, other_outs, scratch, step, steps)

    @pl.when(pl.program_id(1) == 0)
    def _():
        visible_bias(bias_ref, position_ref[block], chunks)
        for chunk in range(chunks):
            value_t_ref[chunk] = table_ref[1, slot_ref[block, chunk]].astype(F32).T.astype(BF16)

    query = query_ref[...]
    largest = None
    for chunk in range(chunks):
        keys = table_ref[0, slot_ref[block, chunk]]
        score = rows_by_rows(keys, query) + bias_ref[chunk]
        score_ref[chunk] = score
        top = jnp.max(score.reshape(BLK // 8, 8, BLK), axis=0)
        largest = top if largest is None else jnp.maximum(largest, top)
    largest = jnp.max(largest, axis=0, keepdims=True)
    total = jnp.zeros((8, BLK), F32)
    mixed = jnp.zeros((HD, BLK), F32)
    for chunk in range(chunks):
        weight = jnp.exp2((score_ref[chunk] - largest) * factor)
        total = total + jnp.sum(weight.reshape(BLK // 8, 8, BLK), axis=0)
        mixed = mixed + jnp.dot(
            value_t_ref[chunk], weight.astype(BF16), preferred_element_type=F32
        )
    total = jnp.sum(total, axis=0, keepdims=True)
    mixed_ref[...] = (mixed / total).T.astype(BF16)
    logsum_ref[0, 0] = largest * factor + jnp.log2(total)
    finish()


def attend(queries, table, positions, key_slots, programs, arrays, number):
    rows, width = queries.shape
    blocks, heads = rows // BLK, width // HD
    count = (PBLK + 1) * BLK
    out = pl.pallas_call(
        functools.partial(attend_kernel, programs, blocks * heads),
        grid=(blocks, heads),
        out_shape=[
            jax.ShapeDtypeStruct((rows, width), BF16),
            jax.ShapeDtypeStruct((blocks, heads, 1, BLK), F32),
        ]
        + [one.out for one in programs],
        in_specs=[
            pl.BlockSpec(memory_space=pltpu.SMEM),
            pl.BlockSpec(memory_space=pltpu.SMEM),
            pl.BlockSpec((BLK, HD), lambda b, h: (b, h)),
            pl.BlockSpec(memory_space=pltpu.VMEM),
        ]
        + [one.in_spec for one in programs],
        out_specs=[
            pl.BlockSpec((BLK, HD), lambda b, h: (b, h)),
            pl.BlockSpec((1, 1, 1, BLK), lambda b, h: (b, h, 0, 0)),
        ]
        + [one.out_spec for one in programs],
        scratch_shapes=[
            pltpu.VMEM((PBLK + 1, BLK, BLK), F32),
            pltpu.VMEM((PBLK + 1, BLK, BLK), F32),
            pltpu.VMEM((PBLK + 1, HD, BLK), BF16),
        ]
        + [held for one in programs for held in one.scratch()],
        compiler_params=pltpu.CompilerParams(
            collective_id=number, has_side_effects=True, vmem_limit_bytes=VMEM_BYTES
        ),
        cost_estimate=SMALL,
    )(positions, key_slots, queries, table, *arrays)
    return out[0], out[1], out[2:]


def attend_back_kernel(programs, steps, *refs):
    count = len(programs)
    (position_ref, slot_ref, query_ref, grad_ref, mixed_ref), refs = refs[:5], refs[5:]
    (logsum_ref, table_ref), refs = refs[:2], refs[2:]
    others, refs = refs[:count], refs[count:]
    (grad_query_ref, set_ref), refs = refs[:2], refs[2:]
    other_outs, refs = refs[:count], refs[count:]
    (bias_ref, key_t_ref), scratch = refs[:2], refs[2:]
    chunks = PBLK + 1
    scale = HD**-0.5
    block, head = pl.program_id(0), pl.program_id(1)
    step = pl.program_id(0) * pl.num_programs(1) + pl.program_id(1)
    finish = beside(programs, others, other_outs, scratch, step, steps)

    @pl.when(head == 0)
    def _():
        visible_bias(bias_ref, position_ref[block], chunks)
        set_ref[...] = jnp.zeros_like(set_ref)
        for chunk in range(chunks):
            key_t_ref[chunk] = table_ref[0, slot_ref[block, chunk]].astype(F32).T.astype(BF16)

    query, grad = query_ref[...], grad_ref[...]
    inner = jnp.sum(grad.astype(F32) * mixed_ref[...].astype(F32), axis=1, keepdims=True)
    inner = jnp.broadcast_to(inner, (BLK, HD)).T[:1, :]
    logsum = logsum_ref[0, 0]
    grad_query = jnp.zeros((HD, BLK), F32)
    for chunk in range(chunks):
        cut = slice(chunk * BLK, (chunk + 1) * BLK)
        slot = slot_ref[block, chunk]
        score = rows_by_rows(table_ref[0, slot], query)
        weight = jnp.exp2(score * (scale * LOG2E) + bias_ref[chunk] - logsum)
        grad_weight = rows_by_rows(table_ref[1, slot], grad)
        grad_score = (weight * (grad_weight - inner)).astype(BF16)
        set_ref[0, cut, :HD] += jnp.dot(grad_score, query, preferred_element_type=F32)
        set_ref[0, cut, HD:] += jnp.dot(weight.astype(BF16), grad, preferred_element_type=F32)
        grad_query = grad_query + jnp.dot(
            key_t_ref[chunk], grad_score, preferred_element_type=F32
        )
    grad_query_ref[...] = (grad_query * scale).T.astype(BF16)

    @pl.when(head == pl.num_programs(1) - 1)
    def _():
        set_ref[0, :, :HD] = set_ref[0, :, :HD] * scale

    finish()


def attend_back(
    queries, grads, mixed, logsums, table, positions, key_slots, programs, arrays, number
):
    rows, width = queries.shape
    blocks, heads = rows // BLK, width // HD
    count = (PBLK + 1) * BLK
    by_head = pl.BlockSpec((BLK, HD), lambda b, h: (b, h))
    out = pl.pallas_call(
        functools.partial(attend_back_kernel, programs, blocks * heads),
        grid=(blocks, heads),
        out_shape=[
            jax.ShapeDtypeStruct((rows, width), BF16),
            jax.ShapeDtypeStruct((blocks, count, 2 * HD), F32),
        ]
        + [one.out for one in programs],
        in_specs=[
            pl.BlockSpec(memory_space=pltpu.SMEM),
            pl.BlockSpec(memory_space=pltpu.SMEM),
            by_head,
            by_head,
            by_head,
            pl.BlockSpec((1, 1, 1, BLK), lambda b, h: (b, h, 0, 0)),
            pl.BlockSpec(memory_space=pltpu.VMEM),
        ]
        + [one.in_spec for one in programs],
        out_specs=[by_head, pl.BlockSpec((1, count, 2 * HD), lambda b, h: (b, 0, 0))]
        + [one.out_spec for one in programs],
        scratch_shapes=[
            pltpu.VMEM((PBLK + 1, BLK, BLK), F32),
            pltpu.VMEM((PBLK + 1, HD, BLK), BF16),
        ]
        + [held for one in programs for held in one.scratch()],
        compiler_params=pltpu.CompilerParams(
            collective_id=number, has_side_effects=True, vmem_limit_bytes=VMEM_BYTES
        ),
        cost_estimate=SMALL,
    )(positions, key_slots, queries, grads, mixed, logsums, table, *arrays)
    return out[0], out[1], out[2:]


def by_slot_kernel(slot_ref, set_ref, out_ref, table_ref):
    blocks, chunks = slot_ref.shape

    def clear(index, carry):
        table_ref[index] = jnp.zeros(table_ref.shape[1:], F32)
        return carry

    def give(index, carry):
        out_ref[0, index] = table_ref[index, :, :HD].astype(BF16)
        out_ref[1, index] = table_ref[index, :, HD:].astype(BF16)
        return carry

    lax.fori_loop(0, table_ref.shape[0], clear, 0)
    for block in range(blocks):
        for chunk in range(chunks):
            cut = slice(chunk * BLK, (chunk + 1) * BLK)
            table_ref[slot_ref[block, chunk]] += set_ref[block, cut, :]
    lax.fori_loop(0, table_ref.shape[0], give, 0)


def by_slot(sets, key_slots, slot_count):
    return pl.pallas_call(
        by_slot_kernel,
        out_shape=jax.ShapeDtypeStruct((2, slot_count, BLK, HD), BF16),
        in_specs=[
            pl.BlockSpec(memory_space=pltpu.SMEM),
            pl.BlockSpec(memory_space=pltpu.VMEM),
        ],
        out_specs=pl.BlockSpec(memory_space=pltpu.VMEM),
        scratch_shapes=[pltpu.VMEM((slot_count, BLK, 2 * HD), F32)],
        compiler_params=pltpu.CompilerParams(vmem_limit_bytes=VMEM_BYTES),
        cost_estimate=SMALL,
    )(key_slots, sets)


GELU_OUTER = 0.7978845608028654
GELU_INNER = 0.044715


def weight_copies(parts, target, sems):
    copies, start = [], 0
    for number, (ref, rows) in enumerate(parts):
        count = rows.stop - rows.start
        copies.append(
            pltpu.make_async_copy(
                ref.at[:, :, rows], target.at[:, :, start : start + count], sems.at[number]
            )
        )
        start += count
    return copies


def first_half(rows, first, refs):
    piece, early = refs[0], refs[1]
    down = [(piece, slice(0, first)), (early, slice(0, rows - first))]
    return down, [(early, slice(rows - first, 2 * rows - first))]


def second_half(rows, first, refs):
    early, late = refs[1], refs[2]
    start = 2 * rows - first
    there = early.shape[2] - start
    down = [(early, slice(start, start + there)), (late, slice(0, rows - there))]
    return down, [(late, slice(rows - there, 2 * rows - there))]


def gelu_both(value, grad_act):
    square = value * value
    bend = jnp.tanh(GELU_OUTER * value * (1.0 + GELU_INNER * square))
    slope = 0.5 * (1.0 + bend) + 0.5 * GELU_OUTER * value * (1.0 - bend * bend) * (
        1.0 + 3.0 * GELU_INNER * square
    )
    return 0.5 * value * (1.0 + bend), grad_act * slope


def forward_kernel(
    x_ref,
    cotangent_ref,
    piece_ref,
    early_ref,
    shift_ref,
    all_ref,
    act_ref,
    pre_ref,
    part_ref,
    bias_ref,
    weight_grad_ref,
    up_own,
    down_own,
    grads_own,
    rows_own,
    cotangent_own,
    act_own,
    pre_own,
    part_own,
    weight_sem,
    load_sem,
    store_sem,
    own_sem,
    send,
    recv,
):
    me = here()
    steps = (SIDE, FRONT, "tp")
    half, width = x_ref.shape
    hidden = early_ref.shape[3]

    def place(bits):
        at = me
        for k in (2, 1, 0):
            if bits >> k & 1:
                at = flip(at, steps[k])
        return at

    def block(bits):
        return by_plane_slot(all_ref, place(bits))

    def to_step(k, bits):
        source = block(bits) if bits else x_ref
        return remote(
            source, block(bits), send.at[k, bits], recv.at[bits | 1 << k], flip(me, steps[k])
        )

    def arrived(bits):
        remote(block(bits), block(bits), send.at[0, 0], recv.at[bits], me).wait_recv()

    def loads(number):
        slot, copies = number % 2, []
        for side, bits in enumerate((number, number + 4)):
            rows = pl.ds(side * half, half)
            copies.append(
                pltpu.make_async_copy(
                    by_plane_slot(cotangent_ref, place(bits)),
                    cotangent_own.at[slot, rows],
                    load_sem.at[slot, 0, side],
                )
            )
            copies.append(
                pltpu.make_async_copy(
                    block(bits) if bits else x_ref,
                    rows_own.at[slot, rows],
                    load_sem.at[slot, 1, side],
                )
            )
        return copies

    def stores(number, kind):
        slot = number % 2
        source, target = ((act_own, act_ref), (pre_own, pre_ref), (part_own, part_ref))[kind]
        return [
            pltpu.make_async_copy(
                source.at[slot, pl.ds(side * half, half)],
                by_plane_slot(target, place(bits)),
                store_sem.at[slot, kind, side],
            )
            for side, bits in enumerate((number, number + 4))
        ]

    def products(number):
        slot = number % 2
        tile = 256

        def one(index, carry):
            cut = pl.ds(pl.multiple_of(index * tile, tile), tile)
            down = down_own[:, :, :, cut].reshape(width, tile)
            up = up_own[:, :, :, cut].reshape(width, tile)
            grad_act = jnp.dot(cotangent_own[slot], down, preferred_element_type=F32)
            value = jnp.dot(rows_own[slot], up, preferred_element_type=F32)
            value = value + shift_ref[:, cut]
            act, grad_pre = gelu_both(value, grad_act)
            act_own[slot, :, cut] = act.astype(BF16)
            grad_pre = grad_pre.astype(BF16)
            pre_own[slot, :, cut] = grad_pre
            bias_ref[:, cut] += jnp.sum(
                grad_pre.astype(F32).reshape(2 * half // 8, 8, tile), axis=0
            )
            return carry

        lax.fori_loop(0, hidden // tile, one, 0)

    def back(number):
        slot = number % 2
        tile = up_own.shape[1] * up_own.shape[2]

        def one(index, carry):
            cut = pl.ds(pl.multiple_of(index * tile, tile), tile)
            up = up_own[index].reshape(tile, hidden)
            part_own[slot, :, cut] = rows_by_rows(pre_own[slot], up).astype(BF16)
            return carry

        lax.fori_loop(0, width // tile, one, 0)

    def grads(number):
        slot = number % 2
        tile = 256
        shard_rows = weight_grad_ref.shape[2]

        def one(index, carry):
            cut = pl.ds(pl.multiple_of(index * tile, tile), tile)
            for kind, (left, right) in enumerate(((cotangent_own, act_own), (rows_own, pre_own))):
                grad = by_columns(left[slot, :, cut], right[slot])
                if number > 0:
                    grad = grads_own[kind, cut, :] + grad
                if number < 3:
                    grads_own[kind, cut, :] = grad
                else:
                    count = tile // shard_rows
                    shards = pl.ds(pl.multiple_of(index * count, count), count)
                    grad = grad.astype(BF16).reshape(count, shard_rows, hidden)
                    weight_grad_ref[shards, kind] = grad
            return carry

        lax.fori_loop(0, width // tile, one, 0)

    def pass_on(bits, *ways):
        arrived(bits)
        for k in ways:
            to_step(k, bits).start()

    def second():
        to_step(0, 0).wait_send()
        to_step(1, 0).start()

    def third():
        to_step(1, 0).wait_send()
        to_step(1, 1).start()
        pass_on(2, 2)

    between = [second, third, functools.partial(pass_on, 3, 2), lambda: None]
    barrier = pltpu.get_barrier_semaphore()
    for step in steps:
        pl.semaphore_signal(barrier, inc=1, device_id=flip(me, step), device_id_type=MESH_ID)
    pl.semaphore_wait(barrier, 3)
    to_step(0, 0).start()
    to_step(2, 0).start()
    own = pltpu.make_async_copy(x_ref, block(0), own_sem)
    own.start()
    down_parts, up_parts = first_half(up_own.shape[2], piece_ref.shape[2], (piece_ref, early_ref))
    weights = weight_copies(down_parts, down_own, weight_sem)
    weights += weight_copies(up_parts, up_own, weight_sem.at[2:])
    for one in weights:
        one.start()
    bias_ref[...] = jnp.zeros_like(bias_ref)
    for number in range(4):
        if number == 1:
            pass_on(1, 2)
        arrived(4 + number)
        copies = loads(number)
        for one in copies:
            one.start()
        if number == 0:
            for one in weights:
                one.wait()
        if number >= 2:
            for kind in range(3):
                for one in stores(number - 2, kind):
                    one.wait()
        for one in copies:
            one.wait()
        products(number)
        between[number]()
        for kind in range(2):
            for one in stores(number, kind):
                one.start()
        back(number)
        for one in stores(number, 2):
            one.start()
        grads(number)
    for number in (2, 3):
        for kind in range(3):
            for one in stores(number, kind):
                one.wait()
    own.wait()
    for k, bits in ((2, 0), (1, 1), (2, 1), (2, 2), (2, 3)):
        to_step(k, bits).wait_send()


def forward_products(rows, cotangent_all, piece, early, shift, number):
    half, width = rows.shape
    lines, quarters, _, hidden = early.shape
    weights = (lines, quarters, width // (lines * quarters), hidden)
    anywhere = pl.BlockSpec(memory_space=pl.ANY)
    inside = pl.BlockSpec(memory_space=pltpu.VMEM)
    lead = (2, 2, 2, half)
    return pl.pallas_call(
        forward_kernel,
        out_shape=[
            jax.ShapeDtypeStruct(lead + (width,), BF16),
            jax.ShapeDtypeStruct(lead + (hidden,), BF16),
            jax.ShapeDtypeStruct(lead + (hidden,), BF16),
            jax.ShapeDtypeStruct(lead + (width,), BF16),
            jax.ShapeDtypeStruct((8, hidden), F32),
            jax.ShapeDtypeStruct((lines * quarters, 2, weights[2], hidden), BF16),
        ],
        in_specs=[anywhere] * 4 + [inside],
        out_specs=[anywhere] * 4 + [inside] * 2,
        scratch_shapes=[
            pltpu.VMEM(weights, BF16),
            pltpu.VMEM(weights, BF16),
            pltpu.VMEM((2, width, hidden), F32),
            pltpu.VMEM((2, 2 * half, width), BF16),
            pltpu.VMEM((2, 2 * half, width), BF16),
            pltpu.VMEM((2, 2 * half, hidden), BF16),
            pltpu.VMEM((2, 2 * half, hidden), BF16),
            pltpu.VMEM((2, 2 * half, width), BF16),
            pltpu.SemaphoreType.DMA((3,)),
            pltpu.SemaphoreType.DMA((2, 2, 2)),
            pltpu.SemaphoreType.DMA((2, 3, 2)),
            pltpu.SemaphoreType.DMA(()),
            pltpu.SemaphoreType.DMA((3, 4)),
            pltpu.SemaphoreType.DMA((8,)),
        ],
        compiler_params=pltpu.CompilerParams(
            collective_id=number, has_side_effects=True, vmem_limit_bytes=VMEM_BYTES
        ),
        cost_estimate=SMALL,
    )(rows, cotangent_all, piece, early, shift)


def second_kernel(
    rows_ref,
    cotangent_ref,
    before_ref,
    piece_ref,
    early_ref,
    late_ref,
    shift_ref,
    act_ref,
    pre_ref,
    part_ref,
    bias_ref,
    up_own,
    down_own,
    weight_sem,
):
    step = pl.program_id(0)
    width, hidden = rows_ref.shape[1], act_ref.shape[1]

    @pl.when(step == 0)
    def _():
        down_parts, up_parts = second_half(
            up_own.shape[2], piece_ref.shape[2], (piece_ref, early_ref, late_ref)
        )
        weights = weight_copies(down_parts, down_own, weight_sem)
        weights += weight_copies(up_parts, up_own, weight_sem.at[2:])
        for one in weights:
            one.start()
        bias_ref[...] = jnp.zeros_like(bias_ref)
        for one in weights:
            one.wait()

    tile = 256

    def one(index, carry):
        cut = pl.ds(pl.multiple_of(index * tile, tile), tile)
        down = down_own[:, :, :, cut].reshape(width, tile)
        up = up_own[:, :, :, cut].reshape(width, tile)
        grad_act = jnp.dot(cotangent_ref[...], down, preferred_element_type=F32)
        value = jnp.dot(rows_ref[...], up, preferred_element_type=F32) + shift_ref[:, cut]
        act, grad_pre = gelu_both(value, grad_act)
        act_ref[:, cut] = act.astype(BF16)
        grad_pre = grad_pre.astype(BF16)
        pre_ref[:, cut] = grad_pre
        bias_ref[:, cut] += fold_rows(grad_pre.astype(F32))
        return carry

    lax.fori_loop(0, hidden // tile, one, 0)
    tile_back = up_own.shape[1] * up_own.shape[2]

    def back(index, carry):
        cut = pl.ds(pl.multiple_of(index * tile_back, tile_back), tile_back)
        up = up_own[index].reshape(tile_back, hidden)
        part = before_ref[:, cut].astype(F32) + rows_by_rows(pre_ref[...], up)
        part_ref[:, cut] = part.astype(BF16)
        return carry

    lax.fori_loop(0, width // tile_back, back, 0)


def second_products(rows_all, cotangent_all, before, piece, early, late, shift):
    rows, width = rows_all.shape
    lines, quarters, _, hidden = late.shape
    weights = (lines, quarters, width // (lines * quarters), hidden)
    steps = 4
    wide = pl.BlockSpec((rows // steps, width), lambda i: (i, 0))
    narrow = pl.BlockSpec((rows // steps, hidden), lambda i: (i, 0))
    anywhere = pl.BlockSpec(memory_space=pl.ANY)
    return pl.pallas_call(
        second_kernel,
        grid=(steps,),
        out_shape=[
            jax.ShapeDtypeStruct((rows, hidden), BF16),
            jax.ShapeDtypeStruct((rows, hidden), BF16),
            jax.ShapeDtypeStruct((rows, width), BF16),
            jax.ShapeDtypeStruct((8, hidden), F32),
        ],
        in_specs=[wide] * 3 + [anywhere] * 3 + [pl.BlockSpec((1, hidden), lambda i: (0, 0))],
        out_specs=[narrow, narrow, wide, pl.BlockSpec((8, hidden), lambda i: (0, 0))],
        scratch_shapes=[
            pltpu.VMEM(weights, BF16),
            pltpu.VMEM(weights, BF16),
            pltpu.SemaphoreType.DMA((3,)),
        ],
        compiler_params=pltpu.CompilerParams(vmem_limit_bytes=VMEM_BYTES),
        cost_estimate=SMALL,
    )(rows_all, cotangent_all, before, piece, early, late, shift)


def by_columns(left, right):
    return lax.dot_general(left, right, (((0,), (0,)), ((), ())), preferred_element_type=F32)


def grads_kernel(programs, steps, *refs):
    count = len(programs)
    (cotangent_ref, rows_ref, act_a_ref, act_b_ref, pre_ref), refs = refs[:5], refs[5:]
    (piece_ref, early_ref, late_ref), refs = refs[:3], refs[3:]
    others, refs = refs[:count], refs[count:]
    (down_part_ref, weight_grad_ref), refs = refs[:2], refs[2:]
    other_outs, refs = refs[:count], refs[count:]
    (acts, pre_own, downs, load_sem, weight_sem), scratch = refs[:5], refs[5:]
    step = pl.program_id(0)
    finish = beside(programs, others, other_outs, scratch, step, steps)

    @pl.when(step == 0)
    def _():
        rows, first = downs.shape[3], piece_ref.shape[2]
        places = (piece_ref, early_ref, late_ref)
        copies = [
            pltpu.make_async_copy(act_a_ref, acts.at[0], load_sem.at[0]),
            pltpu.make_async_copy(act_b_ref, acts.at[1], load_sem.at[1]),
            pltpu.make_async_copy(pre_ref, pre_own, load_sem.at[2]),
        ]
        copies += weight_copies(first_half(rows, first, places)[0], downs.at[0], weight_sem.at[0])
        copies += weight_copies(second_half(rows, first, places)[0], downs.at[1], weight_sem.at[1])
        for one in copies:
            one.start()
        for one in copies:
            one.wait()

    tile, width = down_part_ref.shape
    rows = pl.ds(pl.multiple_of(step * tile, tile), tile)
    shards, _, shard_rows, hidden = weight_grad_ref.shape
    for kind, (left, right) in enumerate(((cotangent_ref, acts.at[1]), (rows_ref, pre_own))):
        grad = by_columns(left[...], right[...]).astype(BF16)
        weight_grad_ref[:, kind] = grad.reshape(shards, shard_rows, hidden)
    part = rows_by_rows(acts[0, rows, :], downs[0].reshape(width, hidden))
    part = part + rows_by_rows(acts[1, rows, :], downs[1].reshape(width, hidden))
    down_part_ref[...] = part.astype(BF16)
    finish()


def grad_products(
    cotangent_all, rows_all, act_a, act_b, pre, piece, early, late, programs, arrays, number
):
    rows, width = rows_all.shape
    lines, quarters, _, hidden = late.shape
    shards, shard_rows = lines * quarters, width // (lines * quarters)
    steps = 8
    columns = pl.BlockSpec((rows, width // steps), lambda i: (0, i))
    anywhere = pl.BlockSpec(memory_space=pl.ANY)
    grads = pl.BlockSpec((shards // steps, 2, shard_rows, hidden), lambda i: (i, 0, 0, 0))
    out = pl.pallas_call(
        functools.partial(grads_kernel, programs, steps),
        grid=(steps,),
        out_shape=[
            jax.ShapeDtypeStruct((rows, width), BF16),
            jax.ShapeDtypeStruct((shards, 2, shard_rows, hidden), BF16),
        ]
        + [one.out for one in programs],
        in_specs=[columns, columns] + [anywhere] * 6 + [one.in_spec for one in programs],
        out_specs=[pl.BlockSpec((rows // steps, width), lambda i: (i, 0)), grads]
        + [one.out_spec for one in programs],
        scratch_shapes=[
            pltpu.VMEM((2, rows, hidden), BF16),
            pltpu.VMEM((rows, hidden), BF16),
            pltpu.VMEM((2, lines, quarters, shard_rows, hidden), BF16),
            pltpu.SemaphoreType.DMA((3,)),
            pltpu.SemaphoreType.DMA((2, 2)),
        ]
        + [held for one in programs for held in one.scratch()],
        compiler_params=pltpu.CompilerParams(
            collective_id=number, has_side_effects=True, vmem_limit_bytes=VMEM_BYTES
        ),
        cost_estimate=SMALL,
    )(cotangent_all, rows_all, act_a, act_b, pre, piece, early, late, *arrays)
    return out[0], out[1], out[2:]


def reorder_kernel(cuts, size, x_ref, out_ref):
    for index, cut in enumerate(cuts):
        out_ref[:, index * size : (index + 1) * size] = x_ref[:, cut : cut + size]


def reorder(values, cuts):
    size = values.shape[1] // len(cuts)
    if size % 128:
        return jnp.concatenate([values[:, cut : cut + size] for cut in cuts], axis=1)
    return pl.pallas_call(
        functools.partial(reorder_kernel, cuts, size),
        out_shape=jax.ShapeDtypeStruct(values.shape, values.dtype),
        compiler_params=pltpu.CompilerParams(vmem_limit_bytes=VMEM_BYTES),
        cost_estimate=SMALL,
    )(values)


def to_line_order(values):
    lines = lax.axis_size("line")
    size = values.shape[1] // (2 * lines)
    return reorder(
        values, [(half * lines + shard) * size for shard in range(lines) for half in range(2)]
    )


def from_line_order(values):
    lines = lax.axis_size("line")
    size = values.shape[1] // (2 * lines)
    return reorder(
        values, [(shard * 2 + half) * size for half in range(2) for shard in range(lines)]
    )


def meet_sibling(me):
    barrier = pltpu.get_barrier_semaphore()
    pl.semaphore_signal(barrier, inc=1, device_id=flip(me, "tp"), device_id_type=MESH_ID)
    pl.semaphore_wait(barrier, 1)


def half_rows_of(core, rows):
    return pl.ds(pl.multiple_of(core * rows, rows), rows)


def each_rows(total, tile, work):
    def one(index, carry):
        work(pl.ds(pl.multiple_of(index * tile, tile), tile))
        return carry

    lax.fori_loop(0, total // tile, one, 0)


def each_columns(total, tile, work):
    each_rows(total, tile, work)


def moments(values):
    centered = values - jnp.mean(values, axis=1, keepdims=True)
    spread = jnp.mean(centered * centered, axis=1, keepdims=True)
    return centered, lax.rsqrt(spread + EPSILON)


def norm_back(values, gain, grad):
    centered, rstd = moments(values)
    xhat = centered * rstd
    scaled = grad * gain
    inner = jnp.mean(scaled * xhat, axis=1, keepdims=True)
    return xhat, rstd * (scaled - jnp.mean(scaled, axis=1, keepdims=True) - xhat * inner)


def fold_rows(values):
    return jnp.sum(values.reshape(values.shape[0] // 8, 8, values.shape[1]), axis=0)


def shuffled(cuts, ref, rows):
    if cuts is None:
        return ref[rows, :]
    size = ref.shape[1] // len(cuts)
    return jnp.concatenate([ref[rows, cut : cut + size] for cut in cuts], axis=1)


def norm_work(me, refs, out_ref):
    stream_ref, gain_ref, shift_ref = refs
    gain, shift = gain_ref[...].astype(F32), shift_ref[...].astype(F32)

    def work(rows):
        centered, rstd = moments(stream_ref[rows, :].astype(F32))
        out_ref[rows, :] = (centered * rstd * gain + shift).astype(BF16)

    each_rows(out_ref.shape[0], 32, work)


def reorder_work(cuts, me, x_ref, out_ref):
    half, size = out_ref.shape[0], out_ref.shape[1] // len(cuts)
    few = 64

    def work(rows):
        start = pl.multiple_of(me["tp"] * half + rows.start, few)
        for index, cut in enumerate(cuts):
            out_ref[rows, index * size : (index + 1) * size] = x_ref[
                pl.ds(start, few), cut : cut + size
            ]

    each_rows(half, few, work)


def part_work(me, refs, out_ref):
    normed_ref, weight_ref, shift_ref = refs
    heads = weight_ref.shape[1] - out_ref.shape[1]
    part = jnp.dot(normed_ref[...], weight_ref[:, heads:], preferred_element_type=F32)
    out_ref[...] = (part + shift_ref[:, heads:]).astype(BF16)


def query_work(me, refs, out_ref):
    normed_ref, weight_ref, shift_ref = refs

    def work(cut):
        query = jnp.dot(normed_ref[...], weight_ref[:, cut], preferred_element_type=F32)
        out_ref[:, cut] = (query + shift_ref[:, cut]).astype(BF16)

    each_columns(out_ref.shape[1], 256, work)


def project_kernel(
    cuts,
    mixed_ref,
    proj_ref,
    stream_ref,
    bias_ref,
    gain_ref,
    shift_ref,
    middle_ref,
    normed_ref,
    sent_ref,
    got_ref,
    sems,
):
    me = here()
    half, width = middle_ref.shape
    mine, other = half_rows_of(me["tp"], half), half_rows_of(1 - me["tp"], half)
    tile = 512
    meet_sibling(me)
    copy = remote(sent_ref, got_ref, sems.at[0], sems.at[1], flip(me, "tp"))

    def part(rows, target):
        def work(cut):
            target[:, cut] = rows_by_rows(mixed_ref[rows, :], proj_ref[cut, :])

        each_columns(width, tile, work)

    part(other, sent_ref)
    copy.start()
    part(mine, middle_ref)
    copy.wait_recv()
    bias, gain = bias_ref[...].astype(F32), gain_ref[...].astype(F32)
    shift = shift_ref[...].astype(F32)
    few = 32

    def finish(rows):
        start = pl.multiple_of(me["tp"] * half + rows.start, few)
        stream = stream_ref[pl.ds(start, few), :].astype(F32)
        middle = stream + (middle_ref[rows, :] + got_ref[rows, :] + bias)
        middle_ref[rows, :] = middle
        centered, rstd = moments(middle)
        normed = (centered * rstd * gain + shift).astype(BF16)
        if cuts is None:
            normed_ref[rows, :] = normed
            return
        size = width // len(cuts)
        for index, cut in enumerate(cuts):
            normed_ref[rows, index * size : (index + 1) * size] = normed[:, cut : cut + size]

    each_rows(half, few, finish)
    copy.wait_send()


def in_vmem(count):
    return [pl.BlockSpec(memory_space=pltpu.VMEM)] * count


def kernel_params(number):
    return pltpu.CompilerParams(
        collective_id=number, has_side_effects=True, vmem_limit_bytes=VMEM_BYTES
    )


def line_cuts(width, back):
    lines = lax.axis_size("line")
    size = width // (2 * lines)
    if size % 128:
        return None
    if back:
        return [(shard * 2 + half) * size for half in range(2) for shard in range(lines)]
    return [(half * lines + shard) * size for shard in range(lines) for half in range(2)]


def project(mixed, proj_all, stream, bias, gain, shift, number):
    rows, width = stream.shape
    half = rows // 2
    cuts = line_cuts(width, False)
    middle, normed = pl.pallas_call(
        functools.partial(project_kernel, cuts),
        out_shape=[
            jax.ShapeDtypeStruct((half, width), F32),
            jax.ShapeDtypeStruct((half, width), BF16),
        ],
        in_specs=in_vmem(6),
        out_specs=in_vmem(2),
        scratch_shapes=[
            pltpu.VMEM((half, width), F32),
            pltpu.VMEM((half, width), F32),
            pltpu.SemaphoreType.DMA((2,)),
        ],
        compiler_params=kernel_params(number),
        cost_estimate=SMALL,
    )(mixed, proj_all, stream, bias[None], gain[None], shift[None])
    return middle, normed if cuts else to_line_order(normed)


def middle_back_kernel(
    cuts,
    sum_ref,
    middle_ref,
    cotangent_ref,
    mixed_ref,
    proj_ref,
    gain_ref,
    hidden_a_ref,
    hidden_b_ref,
    grad_middle_ref,
    grad_mixed_ref,
    proj_grad_ref,
    vector_ref,
    attn_ref,
    sums_own,
    sems,
):
    me = here()
    half, width = middle_ref.shape
    mine, other = half_rows_of(me["tp"], half), half_rows_of(1 - me["tp"], half)
    few = 32
    gain = gain_ref[...].astype(F32)
    meet_sibling(me)
    sums_own[...] = jnp.zeros_like(sums_own)

    def norm(rows):
        start = pl.multiple_of(me["tp"] * half + rows.start, few)
        cotangent = cotangent_ref[pl.ds(start, few), :].astype(F32)
        grad = shuffled(cuts, sum_ref, rows)
        xhat, back = norm_back(middle_ref[rows, :], gain, grad)
        grad_middle = cotangent + back
        grad_middle_ref[rows, :] = grad_middle
        attn = grad_middle.astype(BF16)
        attn_ref[pl.ds(start, few), :] = attn
        sums_own[0] += fold_rows(grad * xhat)
        sums_own[1] += fold_rows(grad)
        sums_own[2] += fold_rows(attn.astype(F32))
        sums_own[3] += fold_rows(cotangent)

    each_rows(half, few, norm)
    copy = remote(attn_ref.at[mine], attn_ref.at[mine], sems.at[0], sems.at[1], flip(me, "tp"))
    copy.start()

    def to_heads(rows):
        def work(cut):
            grad = jnp.dot(attn_ref[rows, :], proj_ref[:, cut], preferred_element_type=F32)
            grad_mixed_ref[rows, cut] = grad.astype(BF16)

        each_columns(proj_ref.shape[1], 256, work)

    to_heads(mine)
    vector_ref[...] = jnp.zeros_like(vector_ref)
    for kind in range(4):
        vector_ref[2 + kind : 3 + kind, :] = jnp.sum(sums_own[kind], axis=0, keepdims=True)
    size = hidden_a_ref.shape[1]
    for number, hidden_ref in enumerate((hidden_a_ref, hidden_b_ref)):
        start = width - (2 - number) * size
        vector_ref[6:7, start : start + size] = jnp.sum(hidden_ref[...], axis=0, keepdims=True)
    copy.wait_recv()
    to_heads(other)

    def weight(cut):
        grad = lax.dot_general(
            attn_ref[:, cut], mixed_ref[...], (((0,), (0,)), ((), ())), preferred_element_type=F32
        )
        proj_grad_ref[cut, :] = grad.astype(BF16)

    each_columns(width, 256, weight)
    copy.wait_send()


def middle_back(grad_sum, middle, cotangent, mixed, proj_all, gain, hidden_a, hidden_b, number):
    rows, width = cotangent.shape
    half, heads = rows // 2, mixed.shape[1]
    cuts = line_cuts(width, True)
    return pl.pallas_call(
        functools.partial(middle_back_kernel, cuts),
        out_shape=[
            jax.ShapeDtypeStruct((half, width), F32),
            jax.ShapeDtypeStruct((rows, heads), BF16),
            jax.ShapeDtypeStruct((width, heads), BF16),
            jax.ShapeDtypeStruct((8, width), F32),
        ],
        in_specs=in_vmem(8),
        out_specs=in_vmem(4),
        scratch_shapes=[
            pltpu.VMEM((rows, width), BF16),
            pltpu.VMEM((4, 8, width), F32),
            pltpu.SemaphoreType.DMA((2,)),
        ],
        compiler_params=kernel_params(number),
        cost_estimate=SMALL,
    )(
        grad_sum if cuts else from_line_order(grad_sum),
        middle,
        cotangent,
        mixed,
        proj_all,
        gain[None],
        hidden_a,
        hidden_b,
    )


def first_back_kernel(cuts, programs, *refs):
    (
        grad_query_ref,
        grad_part_ref,
        first_ref,
        stream_ref,
        normed_ref,
        gain_ref,
        grad_middle_ref,
        mlp_ref,
        middle_ref,
        bias_ref,
        early_ref,
        cut_a_ref,
        cut_b_ref,
    ), refs = refs[:13], refs[13:]
    (input_ref, layer_ref, down_out, up_out, part_out, total_out), refs = refs[:6], refs[6:]
    (weight_ref, vector_ref, sent_ref, got_ref, grad_first_ref, held_ref, sems), scratch = refs[:7], refs[7:]
    me = here()
    rows, width = stream_ref.shape
    half, heads = rows // 2, grad_query_ref.shape[1]
    shard_rows = part_out.shape[0]
    mine, other = half_rows_of(me["tp"], half), half_rows_of(1 - me["tp"], half)
    few = 32
    sibling = flip(me, "tp")
    works = schedule(
        programs,
        (
            (cut_a_ref.at[:, :shard_rows], cut_b_ref.at[:, :shard_rows]),
            (cut_a_ref.at[:, shard_rows:], cut_b_ref.at[:, shard_rows:]),
            weight_ref.reshape(2, -1, 2, shard_rows, weight_ref.shape[1]),
            vector_ref,
        ),
        (down_out, up_out, part_out, total_out),
        scratch,
        ("tp",),
    )

    def run_until(stop):
        while works and works[0][0] < stop:
            works.pop(0)[1]()

    run_until(0.1)
    grad_first_ref[:, :heads] = grad_query_ref[...]
    grad_first_ref[:, heads:] = grad_part_ref[...].astype(BF16)

    def weight(cut):
        grad = lax.dot_general(
            normed_ref[:, cut],
            grad_first_ref[:, heads:],
            (((0,), (0,)), ((), ())),
            preferred_element_type=F32,
        )
        weight_ref[cut, :] = grad.astype(BF16)

    each_columns(width, 512, weight)
    run_until(0.2)

    def part(at, target):
        def work(cut):
            target[:, cut] = rows_by_rows(grad_first_ref[at, :], first_ref[cut, :])

        each_columns(width, 512, work)

    part(other, sent_ref)
    sums_copy = remote(sent_ref, got_ref, sems.at[0], sems.at[1], sibling)
    sums_copy.start()
    run_until(0.3)
    bias = bias_ref[...].astype(F32)

    def layer(at):
        start = pl.multiple_of(me["tp"] * half + at.start, few)
        out = middle_ref[at, :] + (shuffled(cuts, mlp_ref, at) + bias)
        layer_ref[pl.ds(start, few), :] = out.astype(BF16)

    each_rows(half, few, layer)
    layer_copy = remote(layer_ref.at[mine], layer_ref.at[mine], sems.at[2], sems.at[3], sibling)
    layer_copy.start()
    run_until(0.4)
    grad_own, folded = held_ref.at[0], held_ref.at[1]
    part(mine, grad_own)
    run_until(0.5)
    sums_copy.wait_recv()
    gain = gain_ref[...].astype(F32)
    folded[0:16, :] = jnp.zeros((16, width), F32)

    def norm(at):
        start = pl.multiple_of(me["tp"] * half + at.start, few)
        grad = grad_own[at, :] + got_ref[at, :]
        xhat, back = norm_back(stream_ref[pl.ds(start, few), :].astype(F32), gain, grad)
        input_ref[pl.ds(start, few), :] = (grad_middle_ref[at, :] + back).astype(BF16)
        folded[0:8, :] += fold_rows(grad * xhat)
        folded[8:16, :] += fold_rows(grad)

    each_rows(half, few, norm)
    input_copy = remote(input_ref.at[mine], input_ref.at[mine], sems.at[4], sems.at[5], sibling)
    input_copy.start()
    vector_ref[...] = early_ref[...]
    for kind in range(2):
        total = jnp.sum(folded[kind * 8 : kind * 8 + 8, :], axis=0, keepdims=True)
        vector_ref[kind : kind + 1, :] = total
    vector_ref[6:7, :heads] = jnp.sum(
        fold_rows(grad_query_ref[...].astype(F32)), axis=0, keepdims=True
    )
    part_sums = jnp.sum(
        fold_rows(grad_first_ref[:, heads:].astype(F32)), axis=0, keepdims=True
    )
    vector_ref[7:8, : part_sums.shape[1]] = jnp.where(me["tp"] == 1, part_sums, 0.0)
    run_until(2.0)
    layer_copy.wait()
    input_copy.wait()
    sums_copy.wait_send()


def first_back(
    grad_query,
    grad_part,
    first_all,
    stream,
    normed,
    gain,
    grad_middle,
    mlp_sum,
    middle,
    bias,
    early,
    cut_a,
    cut_b,
    number,
):
    rows, width = stream.shape
    half, heads, part = rows // 2, grad_query.shape[1], grad_part.shape[1]
    lines = lax.axis_size("line")
    cuts = line_cuts(width, True)
    shard_rows = width // (4 * lines)
    vector = early.shape
    programs = [
        placed(join_halves(shard_rows, 8 * cut_a.shape[2], BF16), 0.0, 1.0),
        placed(join_halves(shard_rows, 8 * cut_a.shape[2], BF16), 0.0, 1.0),
        placed(Direct(lines, shard_rows, part, part), 0.1, 0.95),
        placed(Total(vector, lines, 6, heads), 0.9, 0.93, 0.97),
    ]
    anywhere = [pl.BlockSpec(memory_space=pl.ANY)] * 2
    return pl.pallas_call(
        functools.partial(first_back_kernel, cuts, programs),
        out_shape=[
            jax.ShapeDtypeStruct((rows, width), BF16),
            jax.ShapeDtypeStruct((rows, width), BF16),
        ]
        + [one.out for one in programs],
        in_specs=in_vmem(11) + anywhere,
        out_specs=in_vmem(2) + [one.out_spec for one in programs],
        scratch_shapes=[
            pltpu.VMEM((width, part), BF16),
            pltpu.VMEM(vector, F32),
            pltpu.VMEM((half, width), F32),
            pltpu.VMEM((half, width), F32),
            pltpu.VMEM((rows, heads + part), BF16),
            pltpu.VMEM((2, half, width), F32),
            pltpu.SemaphoreType.DMA((6,)),
        ]
        + [held for one in programs for held in one.scratch()],
        compiler_params=kernel_params(number),
        cost_estimate=SMALL,
    )(
        grad_query,
        grad_part,
        first_all,
        stream,
        normed,
        gain[None],
        grad_middle,
        mlp_sum if cuts else from_line_order(mlp_sum),
        middle,
        bias[None],
        early,
        cut_a,
        cut_b,
    )


def body(
    hidden_in,
    block_order,
    attn_norm_gain,
    attn_norm_bias,
    query_weight,
    query_bias,
    keyval_weight,
    value_bias,
    proj_weight,
    proj_bias,
    mlp_norm_gain,
    mlp_norm_bias,
    up_weight,
    up_bias,
    down_weight,
    down_bias,
    out_cotangent,
):
    rows_dev = hidden_in.shape[0]
    half_rows = rows_dev // 2
    width = hidden_in.shape[1]
    blocks_dev = rows_dev // BLK
    slot_count = block_order.shape[1]
    group_blocks = PBLK + CONTS
    heads_dev = query_bias.shape[0] // HD
    head_width = heads_dev * HD
    core = lax.axis_index("tp")
    quarter = lax.axis_index("fsdp") * lax.axis_size("pair") + lax.axis_index("pair")
    quarters = lax.axis_size("fsdp") * lax.axis_size("pair")
    hidden_dev = up_weight.shape[1] // quarters

    def own_half(values):
        return lax.dynamic_slice_in_dim(values, core * half_rows, half_rows, axis=0)

    def in_order(mine, other, axis=0):
        first = jnp.where(core == 0, mine, other)
        second = jnp.where(core == 0, other, mine)
        return jnp.concatenate([first, second], axis=axis)


    slot_ids = jnp.arange(slot_count, dtype=jnp.int32)
    ordering = block_order[0]
    inverse = jnp.sum(
        jnp.where(ordering[None, :] == slot_ids[:, None], slot_ids[None, :], 0), axis=1
    )
    ctx_index = lax.axis_index("line") * lax.axis_size("pair") + lax.axis_index("pair")
    first_slot = ctx_index * blocks_dev
    my_slots = first_slot + jnp.arange(blocks_dev, dtype=jnp.int32)
    my_blocks = lax.dynamic_slice_in_dim(ordering, first_slot, blocks_dev)
    positions = my_blocks % group_blocks
    group_base = my_blocks // group_blocks * group_blocks
    prompt_slots = jnp.take(
        inverse, group_base[:, None] + jnp.arange(PBLK, dtype=jnp.int32)[None, :]
    )
    key_slots = jnp.concatenate([prompt_slots, my_slots[:, None]], axis=1)

    keyval_cut = lax.dynamic_slice_in_dim(keyval_weight, core * HD, HD, axis=1)
    first_cut = jnp.concatenate([query_weight, keyval_cut], axis=1)
    shard_rows = down_weight.shape[0]
    hidden_half = hidden_dev // 2
    columns = down_weight.shape[1]
    first_rows = shard_rows // 2
    early_rows = shard_rows // 2
    cuts = line_cuts(width, False)
    lines = lax.axis_size("line")
    first_pieces = [(0, slice(0, first_rows), 0)]
    early_pieces = [
        (0, slice(first_rows, shard_rows), 0),
        (1, slice(0, shard_rows), 0),
        (0, slice(0, early_rows), 1),
    ]
    late_pieces = [(0, slice(early_rows, shard_rows), 1), (1, slice(0, shard_rows), 1)]
    hops = [0.1 * k for k in range(1, 4)] if lines == 4 else spaced(0.1, 0.3, lines - 1)
    levels = spaced(0.4, 0.98, 2 * lines)
    piece_hops = spaced(0.35, 0.75, lines - 1)
    _, first_all, early_cut, late_cut, mlp_piece, normed_one, cotangent_line, proj_line = run_programs(
        [
            placed(spread_halves(first_pieces, columns, BF16), 0.0, 0.05),
            placed(rows_gather(first_cut), 0.01, *hops, *levels, 1.0),
            placed(spread_halves(early_pieces, columns, BF16), 0.06, 1.0),
            placed(spread_halves(late_pieces, columns, BF16), 0.061, 1.0),
            placed(line_gather((quarters, first_rows, hidden_half), BF16), 0.07, *piece_hops, 1.0),
            placed(Work(norm_work, hidden_in.shape, BF16), 0.31, 0.31),
            placed(Work(functools.partial(reorder_work, cuts or [0]), (half_rows, width), BF16), 0.32, 0.32),
            placed(line_gather(proj_weight.shape, BF16), 0.305, *spaced(0.48, 0.88, lines - 1), 1.0),
        ],
        [
            lambda more, outs: more[4:6],
            lambda more, outs: more[6],
            lambda more, outs: more[4:6],
            lambda more, outs: more[4:6],
            lambda more, outs: outs[0],
            lambda more, outs: more[:3],
            lambda more, outs: more[3],
            lambda more, outs: more[7],
        ],
        1,
        near=[hidden_in, attn_norm_gain[None], attn_norm_bias[None], out_cotangent],
        far=[down_weight, up_weight, first_cut, proj_weight],
    )
    if cuts is None:
        cotangent_line = to_line_order(own_half(out_cotangent))
    first_all = flat(first_all)

    value_shift = jnp.where(core == 1, value_bias.astype(F32), 0.0)
    first_shift = jnp.concatenate([query_bias.astype(F32), value_shift])
    part_like = (rows_dev, HD)
    _, query_low, keyval_every = run_programs(
        [
            placed(Work(part_work, part_like, BF16), 0.0, 0.0),
            placed(Work(query_work, (rows_dev, head_width), BF16), 0.2, 0.2),
            placed(ctx_gather(part_like, BF16), 0.1, 1.0),
        ],
        [
            lambda more, outs: more[:3],
            lambda more, outs: more[:3],
            lambda more, outs: outs[0],
        ],
        4,
        near=[normed_one, first_all, first_shift[None]],
    )
    keyval_every, early_cut = lax.optimization_barrier((keyval_every, early_cut))
    mlp_early = lax.all_gather(early_cut, "line", axis=0, tiled=False)
    table = keyval_every.reshape(2, slot_count, BLK, HD)
    mixed_low, logsums, (proj_all, cotangent_all) = attend(
        query_low,
        table,
        positions,
        key_slots,
        [
            placed(columns_gather(proj_line), 0.0, 0.9, 1.0, 1.0),
            placed(plane_gather(cotangent_line), 0.0, 0.9, 1.0, 1.0),
        ],
        [proj_line, cotangent_line],
        2,
    )
    proj_all = flat(proj_all)
    mixed_low, mlp_early, late_cut = lax.optimization_barrier((mixed_low, mlp_early, late_cut))
    mlp_late = lax.all_gather(late_cut, "line", axis=0, tiled=False)
    middle, normed_two_line = project(
        mixed_low, proj_all, hidden_in, proj_bias, mlp_norm_gain, mlp_norm_bias, 5
    )

    up_shift = lax.dynamic_slice_in_dim(up_bias, quarter * hidden_dev, hidden_dev).astype(F32)
    up_shift = up_shift[None]
    rows_all, act_a, pre_a, back_a, bias_a, weight_grad_a = forward_products(
        normed_two_line, cotangent_all, mlp_piece, mlp_early, up_shift[:, :hidden_half], 6
    )
    rows_all, act_a, pre_a, back_a = flat(rows_all), flat(act_a), flat(pre_a), flat(back_a)
    cotangent_all = flat(cotangent_all)
    cut_a = lax.psum_scatter(weight_grad_a, "line", scatter_dimension=0, tiled=True)
    rows_all, weight_grad_a = lax.optimization_barrier((rows_all, weight_grad_a))
    act_b, pre_b, back_both, bias_b = second_products(
        rows_all,
        cotangent_all,
        back_a,
        mlp_piece,
        mlp_early,
        mlp_late,
        up_shift[:, hidden_half:],
    )
    plane_two, plane_parts = plane_sum(back_both)
    placed(plane_two, 0.0, 0.13, 0.13, 0.13, 0.13, 0.51, 0.9, 1.0, 1.0)
    down_part, weight_grad_b, (grad_normed_two,) = grad_products(
        cotangent_all,
        rows_all,
        act_a,
        act_b,
        pre_b,
        mlp_piece,
        mlp_early,
        mlp_late,
        [plane_two],
        [plane_parts],
        7,
    )
    cut_b = lax.psum_scatter(weight_grad_b, "line", scatter_dimension=0, tiled=True)
    cut_a = cut_a.reshape(quarters, 2 * shard_rows, hidden_half)
    cut_b = cut_b.reshape(quarters, 2 * shard_rows, hidden_half)

    grad_middle, grad_mixed, proj_weight_grad, vector = middle_back(
        grad_normed_two, middle, out_cotangent, mixed_low, proj_all, mlp_norm_gain, bias_a, bias_b, 8
    )
    grad_mixed, cut_a = lax.optimization_barrier((grad_mixed, cut_a))
    sum_proj, proj_parts = rows_sum(proj_weight_grad)
    sum_down, down_parts = plane_sum(down_part)
    grad_query, grad_sets, (grad_proj_weight, mlp_out) = attend_back(
        query_low,
        grad_mixed,
        mixed_low,
        logsums,
        table,
        positions,
        key_slots,
        [
            placed(sum_proj, 0.0, 0.13, 0.26, 0.38, 0.51, 0.63, 0.7, 0.9),
            placed(sum_down, 0.0, 0.45, 0.45, 0.45, 0.45, 0.76, 0.95, 1.0, 1.0),
        ],
        [proj_parts, down_parts],
        3,
    )
    grad_table = by_slot(grad_sets, key_slots, slot_count)
    grad_parts = grad_table.reshape(2, lines, 2 * rows_dev, HD)
    along_line, over_pair = ctx_sums(grad_parts)
    query_weight_grad = jnp.einsum("rd,rk->dk", normed_one, grad_query, preferred_element_type=F32)
    sum_query, query_parts = rows_sum(query_weight_grad)
    _, grad_part, grad_query_weight = run_programs(
        [
            placed(along_line, 0.01, 0.75),
            placed(over_pair, 0.76, 0.86, 0.97),
            placed(sum_query, 0.0, 1.0),
        ],
        [
            grad_parts,
            lambda more, outs: outs[0].reshape(2, rows_dev, HD),
            query_parts,
        ],
        12,
    )
    input_grad, layer_out, down_wide, up_wide, grad_part_weight, summed = first_back(
        grad_query,
        grad_part,
        first_all,
        hidden_in,
        normed_one,
        attn_norm_gain,
        grad_middle,
        mlp_out,
        middle,
        down_bias,
        vector,
        cut_a,
        cut_b,
        9,
    )
    grad_down_weight, grad_up_weight = down_wide.astype(F32), up_wide.astype(F32)
    grad_keyval_weight = in_order(grad_part_weight[:, :HD], grad_part_weight[:, HD:], axis=1)
    sum_up = summed[:quarters, width : 2 * width - head_width].reshape(quarters * hidden_dev)
    return (
        layer_out,
        input_grad,
        summed[0, :width],
        summed[1, :width],
        grad_query_weight,
        summed[6, :head_width],
        grad_keyval_weight,
        summed[7, :HD],
        grad_proj_weight,
        summed[4, :width],
        summed[2, :width],
        summed[3, :width],
        grad_up_weight,
        sum_up,
        grad_down_weight,
        summed[5, :width],
    )


def solution(mesh):
    fsdp, ctx, tp = mesh.devices.shape
    grid = Mesh(mesh.devices.reshape(fsdp, ctx // 2, 2, tp), EVERY)
    by_rows = P(ROWS, None)
    by_both = P(ROWS, "tp")
    return jax.shard_map(
        body,
        mesh=grid,
        in_specs=(
            by_rows,
            P("fsdp", None),
            P(),
            P(),
            by_both,
            P("tp"),
            by_rows,
            P(),
            by_both,
            P(),
            P(),
            P(),
            by_both,
            P("tp"),
            by_both,
            P(),
            by_rows,
        ),
        out_specs=(
            by_rows,
            by_rows,
            P(),
            P(),
            by_both,
            P("tp"),
            by_rows,
            P(),
            by_both,
            P(),
            P(),
            P(),
            by_both,
            P("tp"),
            by_both,
            P(),
        ),
        check_vma=False,
    )
```

```python
import functools

import jax
import jax.numpy as jnp
from jax import lax
from jax.experimental import pallas as pl
from jax.experimental.pallas import tpu as pltpu
from jax.sharding import Mesh, PartitionSpec as P

HD = 128
BLK = 256
PBLK = 8
CONTS = 8
EPSILON = 1e-05
MASKED = -1e30
F32 = jnp.float32
BF16 = jnp.bfloat16
ROWS = ("fsdp", "line", "pair")
EVERY = ("fsdp", "line", "pair", "tp")


MESH_ID = pl.DeviceIdType.MESH
VMEM_BYTES = 60 * 1024 * 1024
SMALL = pl.CostEstimate(flops=1, bytes_accessed=1, transcendentals=0)
SIDE = ("pair", "fsdp")
FRONT = ("fsdp", "pair")


def here():
    return {name: lax.axis_index(name) for name in EVERY}


def flip(place, step):
    place = dict(place)
    if isinstance(step, str):
        place[step] = 1 - place[step]
    else:
        core = place["tp"]
        for name, used in ((step[0], 1 - core), (step[1], core)):
            place[name] = place[name] + (1 - 2 * place[name]) * used
    return place


def along(place, amount):
    return dict(place, line=place["line"] + amount)


def remote(source, target, send_sem, recv_sem, place):
    return pltpu.make_async_remote_copy(
        src_ref=source,
        dst_ref=target,
        send_sem=send_sem,
        recv_sem=recv_sem,
        device_id=place,
        device_id_type=MESH_ID,
    )


def top_bit(bits):
    return bits.bit_length() - 1


def add_blocks(target, first, second, rows):
    tile = min(rows, 64)

    def one(index, carry):
        cut = pl.ds(pl.multiple_of(index * tile, tile), tile)
        total = first(cut).astype(F32)
        if second is not None:
            total = total + second(cut).astype(F32)
        target[cut, :] = total.astype(target.dtype)
        return carry

    lax.fori_loop(0, rows // tile, one, 0)


def rows_of(ref):
    return lambda cut: ref[cut, :]


class Gather:
    def __init__(self, values, steps, lines, shape, slot):
        self.steps, self.lines, self.slot = steps, lines, slot
        self.out = jax.ShapeDtypeStruct(shape, values.dtype)
        self.in_spec = self.out_spec = pl.BlockSpec(memory_space=pl.ANY)

    def scratch(self):
        parts = 1 << len(self.steps)
        return [
            pltpu.SemaphoreType.DMA(()),
            pltpu.SemaphoreType.DMA((2, self.lines)),
            pltpu.SemaphoreType.DMA((self.lines,)),
            pltpu.SemaphoreType.DMA((self.lines, max(1, len(self.steps)) * parts)),
            pltpu.SemaphoreType.DMA((self.lines, parts)),
        ]

    def stages(self, me, x_ref, out_ref, own_sem, line_send, line_recv, send, recv):
        steps, lines, slot = self.steps, self.lines, self.slot
        count = len(steps)
        my_line = me["line"] if lines > 1 else 0

        def block(bits, shard):
            place = me
            for k in reversed(range(count)):
                if bits >> k & 1:
                    place = flip(place, steps[k])
            return slot(out_ref, dict(place, line=shard))

        def to_step(k, bits, shard, source):
            return remote(
                source,
                block(bits, shard),
                send.at[shard, k * (1 << count) + bits],
                recv.at[shard, bits | 1 << k],
                flip(me, steps[k]),
            )

        def to_line(amount, shard, source):
            return remote(
                source,
                block(0, shard),
                line_send.at[(amount + 1) // 2, shard],
                line_recv.at[shard],
                along(me, amount),
            )

        def send_on(bits, shard, source):
            for k in range(top_bit(bits) + 1, count):
                to_step(k, bits, shard, source).start()

        def at_distance(distance, work):
            if distance == 0:
                work(my_line, 0)
                return
            for amount in (1, -1):
                shard = my_line - amount * distance
                pl.when((shard >= 0) & (shard < lines))(functools.partial(work, shard, amount))

        def line_inside(amount):
            there = my_line + amount
            return (there >= 0) & (there < lines)

        own = pltpu.make_async_copy(x_ref, block(0, my_line), own_sem)

        def begin():
            if lines > 1:
                for amount in (1, -1):
                    pl.when(line_inside(amount))(
                        lambda amount=amount: to_line(amount, my_line, x_ref).start()
                    )
            send_on(0, my_line, x_ref)
            own.start()

        def line_arrival(shard, amount):
            remote(
                block(0, shard), block(0, shard), line_send.at[0, shard], line_recv.at[shard], me
            ).wait_recv()
            pl.when(line_inside(amount))(lambda: to_line(amount, shard, block(0, shard)).start())
            send_on(0, shard, block(0, shard))

        def level_arrival(level, shard, amount):
            for bits in range(1 << level, 2 << level):
                remote(
                    block(bits, shard),
                    block(bits, shard),
                    send.at[shard, 0],
                    recv.at[shard, bits],
                    me,
                ).wait_recv()
                send_on(bits, shard, block(bits, shard))

        def end():
            own.wait()
            if lines > 1:
                for amount in (1, -1):
                    for distance in range(lines):
                        shard = my_line - amount * distance
                        pl.when((shard >= 0) & (shard < lines) & line_inside(amount))(
                            lambda amount=amount, shard=shard: to_line(
                                amount, shard, block(0, shard)
                            ).wait_send()
                        )
            for shard in range(lines):
                for bits in range(1 << count):
                    for k in range(top_bit(bits) + 1, count):
                        to_step(k, bits, shard, block(bits, shard)).wait_send()

        line = [functools.partial(at_distance, number, line_arrival) for number in range(1, lines)]
        levels = [
            functools.partial(at_distance, number - level, functools.partial(level_arrival, level))
            for number in range(lines + count - 1)
            for level in range(count)
            if 0 <= number - level < lines
        ]
        return [begin] + line + levels + [end]


class Sum:
    far_line = True

    def __init__(self, steps, lines, rows, columns, slot, kind=F32):
        self.steps, self.lines, self.rows, self.columns = steps, lines, rows, columns
        self.slot = slot
        self.out = jax.ShapeDtypeStruct((rows, columns), kind)
        self.in_spec = pl.BlockSpec(memory_space=pl.ANY)
        self.out_spec = pl.BlockSpec(memory_space=pltpu.VMEM)

    def scratch(self):
        count, lines = len(self.steps), self.lines
        sizes = [1 << (count - 1 - k) for k in range(count)]
        block = (self.rows, self.columns)
        return (
            [pltpu.VMEM((lines, sizes[0]) + block, BF16)]
            + [pltpu.VMEM((lines, size) + block, BF16) for size in sizes]
            + [pltpu.VMEM((lines,) + (block if lines > 1 else (16, 128)), BF16)]
            + [pltpu.SemaphoreType.DMA((lines, sizes[0]))]
            + [pltpu.SemaphoreType.DMA((lines, size)) for size in sizes] * 2
            + [pltpu.SemaphoreType.DMA((lines,))] * 2
        )

    def stages(self, me, x_ref, out_ref, own, *rest):
        steps, lines, rows, slot = self.steps, self.lines, self.rows, self.slot
        count = len(steps)
        held, rest = rest[:count], rest[count:]
        on_line, own_sem, rest = rest[0], rest[1], rest[2:]
        send, recv = rest[:count], rest[count : 2 * count]
        line_send, line_recv = rest[2 * count :]
        my_line = me["line"] if lines > 1 else 0
        last = count - 1

        def target_of(bits, shard):
            place = me
            for k in range(count):
                if bits >> k & 1:
                    place = flip(place, steps[k])
            return dict(place, line=shard)

        def store(k, shard, bits):
            return held[k].at[shard, bits >> (k + 1)]

        def own_copy(shard, bits):
            return pltpu.make_async_copy(
                slot(x_ref, target_of(bits, shard)),
                own.at[shard, bits >> 1],
                own_sem.at[shard, bits >> 1],
            )

        def copy(k, shard, bits):
            source = slot(x_ref, target_of(bits, shard)) if k == 0 else store(k - 1, shard, bits)
            return remote(
                source,
                store(k, shard, bits ^ (1 << k)),
                send[k].at[shard, bits >> (k + 1)],
                recv[k].at[shard, bits >> (k + 1)],
                flip(me, steps[k]),
            )

        def parts_of(k):
            return [high << (k + 1) for high in reversed(range(1 << (count - 1 - k)))]

        def send_first(shard, amount):
            for bits in parts_of(0):
                copy(0, shard, bits | 1).start()

        def own_first(shard, amount):
            for bits in parts_of(0):
                own_copy(shard, bits).start()

        def take_step(k, shard, amount, parts=None):
            for bits in parts or parts_of(k):
                copy(k, shard, bits | 1 << k).wait_recv()
                arrived = store(k, shard, bits)
                if k == 0:
                    own_copy(shard, bits).wait()
                    mine = own.at[shard, bits >> 1]
                else:
                    mine = store(k - 1, shard, bits)
                add_blocks(arrived, rows_of(mine), rows_of(arrived), rows)
                if k + 1 < count and bits >> (k + 1) & 1:
                    copy(k + 1, shard, bits).start()

        def line_copy(shard):
            return remote(
                held[last].at[shard, 0],
                on_line.at[my_line],
                line_send.at[shard],
                line_recv.at[my_line],
                along(me, shard - my_line),
            )

        def each(distance, work):
            if distance == 0:
                work(my_line, 0)
                return
            for amount in (1, -1):
                shard = my_line + amount * distance
                pl.when((shard >= 0) & (shard < lines))(functools.partial(work, shard, amount))

        order = list(reversed(range(lines)))

        def begin():
            for distance in order:
                each(distance, send_first)
            for distance in order:
                each(distance, own_first)

        def tick(number):
            for k in reversed(range(count)):
                index = number - k
                if 0 <= index < lines:
                    each(order[index], functools.partial(take_step, k))
                    if k == last and order[index] > 0:
                        each(order[index], lambda shard, amount: line_copy(shard).start())

        def end():
            final = held[last].at[my_line, 0]
            if lines == 1:
                add_blocks(out_ref, rows_of(final), None, rows)
            else:
                add_blocks(on_line.at[my_line], rows_of(final), None, rows)

                def arrived(shard, amount):
                    remote(
                        on_line.at[shard], on_line.at[shard], line_send.at[0], line_recv.at[shard], me
                    ).wait_recv()

                for distance in range(1, lines):
                    each(distance, arrived)
                add_blocks(
                    out_ref,
                    lambda cut: sum(on_line[shard, cut, :].astype(F32) for shard in range(lines)),
                    None,
                    rows,
                )
                for distance in range(1, lines):
                    each(distance, lambda shard, amount: line_copy(shard).wait_send())
            for k in range(count):
                for shard in range(lines):
                    for bits in parts_of(k):
                        copy(k, shard, bits | 1 << k).wait_send()

        if lines == 1:
            ticks = [
                functools.partial(take_step, k, 0, 0, [bits]) for k in range(count) for bits in parts_of(k)
            ]
        else:
            ticks = [functools.partial(tick, number) for number in range(lines + count - 1)]
        return [begin] + ticks + [end]


DIRECT = (("pair",), ("fsdp",), ("pair", "fsdp"))


def move(me, names):
    place = me
    for name in names:
        place = flip(place, name)
    return place


def quarter_of(place):
    return place["fsdp"] * 2 + place["pair"]


class Exchange:
    steps, lines = ("pair", "fsdp"), 1

    def __init__(self, moves, shape, kind):
        self.moves = moves
        self.out = jax.ShapeDtypeStruct(shape, kind)
        self.in_spec = self.out_spec = pl.BlockSpec(memory_space=pl.ANY)

    def scratch(self):
        count = len(self.moves)
        return [
            pltpu.SemaphoreType.DMA((count,)),
            pltpu.SemaphoreType.DMA((count, 3)),
            pltpu.SemaphoreType.DMA((count, 3)),
        ]

    def stages(self, me, x_refs, out_ref, own_sem, send, recv):
        copies = []
        for n, (source, target) in enumerate(self.moves):
            there_ref = target(out_ref, quarter_of(me))
            for k, names in reversed(list(enumerate(DIRECT))):
                there = move(me, names)
                copies.append(
                    remote(
                        source(x_refs, quarter_of(there)), there_ref, send.at[n, k], recv.at[n, k], there
                    )
                )
            copies.append(
                pltpu.make_async_copy(source(x_refs, quarter_of(me)), there_ref, own_sem.at[n])
            )

        def begin():
            for one in copies:
                one.start()

        def end():
            for one in copies:
                one.wait()

        return [begin, end]


def half_quarter(ref, quarter, half, rows=None):
    columns = ref.shape[1] // 8
    cut = pl.ds(pl.multiple_of((quarter * 2 + half) * columns, columns), columns)
    return ref.at[:, cut] if rows is None else ref.at[rows, cut]


def spread_halves(pieces, columns, kind):
    moves, start = [], 0
    for index, rows, half in pieces:
        count = rows.stop - rows.start
        moves.append(
            (
                lambda refs, quarter, index=index, rows=rows, half=half: half_quarter(
                    refs[index], quarter, half, rows
                ),
                lambda ref, quarter, start=start, count=count: ref.at[quarter, start : start + count],
            )
        )
        start += count
    return Exchange(moves, (4, start, columns // 8), kind)


def join_halves(rows, columns, kind):
    moves = [
        (
            lambda refs, quarter, half=half: refs[half].at[quarter],
            lambda ref, quarter, half=half: half_quarter(ref, quarter, half),
        )
        for half in range(2)
    ]
    return Exchange(moves, (rows, columns), kind)


class Work:
    steps, lines = (), 1

    def __init__(self, work, shape, kind):
        self.work, self.out = work, jax.ShapeDtypeStruct(shape, kind)
        self.in_spec = self.out_spec = pl.BlockSpec(memory_space=pltpu.VMEM)

    def scratch(self):
        return []

    def stages(self, me, x_refs, out_ref):
        return [functools.partial(self.work, me, x_refs, out_ref), lambda: None]


class Direct:
    steps, rows_too = ("tp",), True

    def __init__(self, lines, rows, columns, shared):
        self.lines, self.rows, self.columns, self.shared = lines, rows, columns, shared
        self.out = jax.ShapeDtypeStruct((rows, columns + shared), F32)
        self.in_spec = self.out_spec = pl.BlockSpec(memory_space=pltpu.VMEM)

    def scratch(self):
        lines = self.lines
        return [
            pltpu.VMEM((2, lines, 2, self.rows, self.columns), BF16),
            pltpu.SemaphoreType.DMA((4, 2, lines)),
            pltpu.SemaphoreType.DMA((2, lines, 2)),
            pltpu.SemaphoreType.DMA((2,)),
        ]

    def stages(self, me, x_ref, out_ref, held, send, recv, share_sem):
        def on_others(work):
            for side in range(4):
                for distance in range(self.lines):
                    for way, amount in enumerate((1, -1) if distance else (1,)):
                        if side or distance:
                            place = along(plane_partner(me, side * 2), amount * distance)
                            inside = (place["line"] >= 0) & (place["line"] < self.lines)
                            pl.when(inside)(
                                functools.partial(work, place, send.at[side, way, distance])
                            )

        def copy(place, sem):
            return remote(
                by_rows_slot(x_ref, place),
                by_rows_slot(held, me),
                sem,
                by_rows_slot(recv, me),
                place,
            )

        def arrived(place, sem):
            slot = by_rows_slot(held, place)
            remote(slot, slot, sem, by_rows_slot(recv, place), me).wait_recv()

        def begin():
            on_others(lambda place, sem: copy(place, sem).start())
            held[me["fsdp"], me["line"], me["pair"]] = x_ref[me["fsdp"], me["line"], me["pair"]]

        def end():
            on_others(arrived)
            total = jnp.zeros((self.rows, self.columns), F32)
            for half in range(2):
                for shard in range(self.lines):
                    for side in range(2):
                        total = total + held[half, shard, side].astype(F32)
            out_ref[:, : self.columns] = total
            share = remote(
                out_ref.at[:, : self.columns],
                out_ref.at[:, self.columns :],
                share_sem.at[0],
                share_sem.at[1],
                flip(me, "tp"),
            )
            share.start()
            share.wait()
            on_others(lambda place, sem: copy(place, sem).wait_send())

        return [begin, end]


class Total:
    steps, everyone = (), True

    def __init__(self, shape, lines, special, heads):
        self.lines, self.shape, self.special, self.heads = lines, shape, special, heads
        self.out = jax.ShapeDtypeStruct((shape[0], 2 * shape[1]), F32)
        self.in_spec = self.out_spec = pl.BlockSpec(memory_space=pltpu.VMEM)

    def scratch(self):
        shape, lines = self.shape, self.lines
        return [
            pltpu.VMEM((lines,) + shape, F32),
            pltpu.VMEM((8,) + shape, F32),
            pltpu.SemaphoreType.DMA((2, lines)),
            pltpu.SemaphoreType.DMA((lines,)),
            pltpu.SemaphoreType.DMA((8,)),
            pltpu.SemaphoreType.DMA((8,)),
        ]

    def stages(self, me, x_ref, out_ref, on_line, on_plane, line_send, line_recv, send, recv):
        lines, mine = self.lines, me["line"]
        number = plane_number(me)

        def on_others(work):
            for distance in range(1, lines):
                for way, amount in enumerate((1, -1)):
                    there = mine + amount * distance
                    pl.when((there >= 0) & (there < lines))(
                        functools.partial(work, way, amount, distance, there)
                    )

        def to_line(way, amount, distance):
            return remote(
                on_line.at[mine],
                on_line.at[mine],
                line_send.at[way, distance],
                line_recv.at[mine],
                along(me, amount * distance),
            )

        def to_plane(bits):
            return remote(
                on_plane.at[number],
                on_plane.at[number],
                send.at[bits],
                recv.at[number],
                plane_partner(me, bits),
            )

        def begin():
            on_line[mine] = x_ref[...]
            on_others(lambda way, amount, distance, there: to_line(way, amount, distance).start())

        def arrived(way, amount, distance, there):
            remote(
                on_line.at[there], on_line.at[there], line_send.at[0, 0], line_recv.at[there], me
            ).wait_recv()

        def middle():
            on_others(arrived)
            total = on_line[0]
            for shard in range(1, lines):
                total = total + on_line[shard]
            on_plane[number] = total
            for bits in range(1, 8):
                to_plane(bits).start()

        def end():
            for bits in range(1, 8):
                there = plane_number(plane_partner(me, bits))
                remote(
                    on_plane.at[there], on_plane.at[there], send.at[0], recv.at[there], me
                ).wait_recv()
            total = on_plane[0]
            for other in range(1, 8):
                total = total + on_plane[other]
            width, row, heads = self.shape[1], slice(self.special, self.special + 1), self.heads
            out_ref[...] = jnp.zeros_like(out_ref)
            out_ref[:, :width] = total
            same = [on_plane[quarter * 2 + me["tp"], row, :] for quarter in range(4)]
            out_ref[row, :heads] = sum(part[:, :heads] for part in same)
            for quarter, part in enumerate(same):
                out_ref[quarter : quarter + 1, width : 2 * width - heads] = part[:, heads:]
            for bits in range(1, 8):
                to_plane(bits).wait_send()
            on_others(lambda way, amount, distance, there: to_line(way, amount, distance).wait_send())

        return [begin, middle, end]


def plane_number(place):
    return (place["fsdp"] * 2 + place["pair"]) * 2 + place["tp"]


def plane_partner(me, bits):
    place = me
    for bit, name in ((1, "tp"), (2, "pair"), (4, "fsdp")):
        if bits & bit:
            place = flip(place, name)
    return place


def greet(me, programs, partners=()):
    barrier = pltpu.get_barrier_semaphore()
    plane, reach, lines, corners = set(), 0, 1, False
    for one in programs:
        lines = max(lines, one.lines)
        if one.lines > 1:
            far = hasattr(one, "everyone") or hasattr(one, "far_line")
            reach = max(reach, one.lines - 1 if far else 1)
        if hasattr(one, "everyone"):
            plane |= set(range(1, 8))
        if isinstance(one, Exchange) or hasattr(one, "rows_too"):
            plane |= {2, 4, 6}
        if hasattr(one, "rows_too"):
            reach, corners = one.lines - 1, True
    for step in [step for one in programs for step in one.steps] + list(partners):
        plane |= {"tp": {1}, "pair": {2}, "fsdp": {4}}.get(step, {2, 4})
    for bits in sorted(plane):
        pl.semaphore_signal(
            barrier, inc=1, device_id=plane_partner(me, bits), device_id_type=MESH_ID
        )
    count = len(plane)
    for distance in range(1, reach + 1):
        for amount in (-distance, distance):
            there = me["line"] + amount
            inside = (there >= 0) & (there < lines)

            for bits in (0, 2, 4, 6) if corners else (0,):

                @pl.when(inside)
                def _():
                    pl.semaphore_signal(
                        barrier,
                        inc=1,
                        device_id=along(plane_partner(me, bits), amount),
                        device_id_type=MESH_ID,
                    )

                count = count + inside.astype(jnp.int32)
    pl.semaphore_wait(barrier, count)


def split_scratch(programs, refs):
    parts, start = [], 0
    for one in programs:
        size = len(one.scratch())
        parts.append(refs[start : start + size])
        start += size
    return parts


def schedule(programs, x_refs, out_refs, scratch, partners=()):
    me = here()
    works = [(0.0, functools.partial(greet, me, programs, partners))]
    for one, x_ref, out_ref, held in zip(programs, x_refs, out_refs, split_scratch(programs, scratch)):
        stages = one.stages(me, x_ref, out_ref, *held)
        places = getattr(one, "places", (0.0, 1.0))
        if len(places) == 2:
            places = spaced(places[0], places[1], len(stages))
        last = len(places) - 2
        works += [
            (places[-1] if k == len(stages) - 1 else places[min(k, last)], stage)
            for k, stage in enumerate(stages)
        ]
    return sorted(works, key=lambda work: work[0])


def placed(program, *places):
    program.places = list(places)
    return program


def spaced(start, stop, count):
    return [start + (stop - start) * k / (count - 1) for k in range(count)]


def run_programs(programs, arrays, number, near=(), far=()):
    count = len(programs)
    given = [k for k, array in enumerate(arrays) if not callable(array)]
    others = len(near) + len(far)

    def kernel(*refs):
        (more, refs) = refs[:others], refs[others:]
        plain, out_refs = refs[: len(given)], refs[len(given) : len(given) + count]
        in_refs = [
            array(more, out_refs) if callable(array) else plain[given.index(k)]
            for k, array in enumerate(arrays)
        ]
        for _, work in schedule(programs, in_refs, out_refs, refs[len(given) + count :]):
            work()

    return pl.pallas_call(
        kernel,
        out_shape=[one.out for one in programs],
        in_specs=[pl.BlockSpec(memory_space=pltpu.VMEM)] * len(near)
        + [pl.BlockSpec(memory_space=pl.ANY)] * len(far)
        + [programs[k].in_spec for k in given],
        out_specs=[one.out_spec for one in programs],
        scratch_shapes=[held for one in programs for held in one.scratch()],
        compiler_params=pltpu.CompilerParams(
            collective_id=number, has_side_effects=True, vmem_limit_bytes=VMEM_BYTES
        ),
        cost_estimate=SMALL,
    )(*near, *far, *[arrays[k] for k in given])


def by_rows_slot(ref, at):
    return ref.at[at["fsdp"], at["line"], at["pair"]]


def by_plane_slot(ref, at):
    return ref.at[at["fsdp"], at["pair"], at["tp"]]


def by_ctx_slot(ref, at):
    return ref.at[at["tp"], at["line"], at["pair"]]


def rows_gather(values):
    lines = lax.axis_size("line")
    return Gather(values, (SIDE, FRONT), lines, (2, lines, 2) + values.shape, by_rows_slot)


def line_gather(shape, kind):
    lines = lax.axis_size("line")
    like = jax.ShapeDtypeStruct(shape, kind)
    return Gather(like, (), lines, (lines,) + shape, lambda ref, at: ref.at[at["line"]])


def columns_gather(values):
    lines, rows, columns = values.shape
    return Gather(
        values, (SIDE, FRONT), 1, (2, lines, 2, rows, columns), lambda ref, at: ref.at[at["fsdp"], :, at["pair"]]
    )


def rows_sum(values):
    lines, (total, columns) = lax.axis_size("line"), values.shape
    rows = total // (4 * lines)
    parts = values.astype(BF16).reshape(2, lines, 2, rows, columns)
    return Sum((FRONT, SIDE), lines, rows, columns, by_rows_slot), parts


def plane_gather(values):
    return Gather(values, (SIDE, FRONT, "tp"), 1, (2, 2, 2) + values.shape, by_plane_slot)


def plane_sum(values):
    rows, columns = values.shape[0] // 8, values.shape[1]
    parts = values.astype(BF16).reshape(2, 2, 2, rows, columns)
    return Sum(("tp", FRONT, SIDE), 1, rows, columns, by_plane_slot), parts


def flat(values):
    return values.reshape(-1, values.shape[-1])


def ctx_gather(shape, kind):
    lines = lax.axis_size("line")
    like = jax.ShapeDtypeStruct(shape, kind)
    return Gather(like, ("pair", "tp"), lines, (2, lines, 2) + shape, by_ctx_slot)


def ctx_sums(values):
    _, lines, rows, columns = values.shape
    along_line = Sum(
        ("tp",), lines, rows, columns, lambda ref, at: ref.at[at["tp"], at["line"]], BF16
    )
    over_pair = Sum(("pair",), 1, rows // 2, columns, lambda ref, at: ref.at[at["pair"]])
    return along_line, over_pair


LOG2E = 1.4426950408889634


def visible_bias(bias_ref, position, chunks):
    prompt = position < PBLK
    row = lax.broadcasted_iota(jnp.int32, (BLK, BLK), 0)
    column = lax.broadcasted_iota(jnp.int32, (BLK, BLK), 1)
    limit = jnp.where(prompt, position * BLK + column, PBLK * BLK)
    for chunk in range(chunks - 1):
        bias_ref[chunk] = jnp.where(row + chunk * BLK <= limit, 0.0, MASKED)
    own_limit = jnp.where(prompt, -1, column)
    bias_ref[chunks - 1] = jnp.where(row <= own_limit, 0.0, MASKED)


def rows_by_rows(left, right):
    return lax.dot_general(left, right, (((1,), (1,)), ((), ())), preferred_element_type=F32)


def beside(programs, in_refs, out_refs, scratch, step, steps):
    late = []
    for place, work in schedule(programs, in_refs, out_refs, scratch):
        if place < 1:
            pl.when(step == int(place * steps))(work)
        else:
            late.append((place, work))

    def finish(own=None):
        @pl.when(step == steps - 1)
        def _():
            early = [work for place, work in late if place < 1.05]
            rest = [work for place, work in late if place >= 1.05]
            for work in early + ([own] if own else []) + rest:
                work()

    return finish


def attend_kernel(programs, steps, *refs):
    count = len(programs)
    (position_ref, slot_ref, query_ref, table_ref), refs = refs[:4], refs[4:]
    others, refs = refs[:count], refs[count:]
    (mixed_ref, logsum_ref), refs = refs[:2], refs[2:]
    other_outs, refs = refs[:count], refs[count:]
    (bias_ref, score_ref, value_t_ref), scratch = refs[:3], refs[3:]
    chunks = PBLK + 1
    block = pl.program_id(0)
    factor = HD**-0.5 * LOG2E
    step = pl.program_id(0) * pl.num_programs(1) + pl.program_id(1)
    finish = beside(programs, others, other_outs, scratch, step, steps)

    @pl.when(pl.program_id(1) == 0)
    def _():
        visible_bias(bias_ref, position_ref[block], chunks)
        for chunk in range(chunks):
            value_t_ref[chunk] = table_ref[1, slot_ref[block, chunk]].astype(F32).T.astype(BF16)

    query = query_ref[...]
    largest = None
    for chunk in range(chunks):
        keys = table_ref[0, slot_ref[block, chunk]]
        score = rows_by_rows(keys, query) + bias_ref[chunk]
        score_ref[chunk] = score
        top = jnp.max(score.reshape(BLK // 8, 8, BLK), axis=0)
        largest = top if largest is None else jnp.maximum(largest, top)
    largest = jnp.max(largest, axis=0, keepdims=True)
    total = jnp.zeros((8, BLK), F32)
    mixed = jnp.zeros((HD, BLK), F32)
    for chunk in range(chunks):
        weight = jnp.exp2((score_ref[chunk] - largest) * factor)
        total = total + jnp.sum(weight.reshape(BLK // 8, 8, BLK), axis=0)
        mixed = mixed + jnp.dot(
            value_t_ref[chunk], weight.astype(BF16), preferred_element_type=F32
        )
    total = jnp.sum(total, axis=0, keepdims=True)
    mixed_ref[...] = (mixed / total).T.astype(BF16)
    logsum_ref[0, 0] = largest * factor + jnp.log2(total)
    finish()


def attend(queries, table, positions, key_slots, programs, arrays, number):
    rows, width = queries.shape
    blocks, heads = rows // BLK, width // HD
    count = (PBLK + 1) * BLK
    out = pl.pallas_call(
        functools.partial(attend_kernel, programs, blocks * heads),
        grid=(blocks, heads),
        out_shape=[
            jax.ShapeDtypeStruct((rows, width), BF16),
            jax.ShapeDtypeStruct((blocks, heads, 1, BLK), F32),
        ]
        + [one.out for one in programs],
        in_specs=[
            pl.BlockSpec(memory_space=pltpu.SMEM),
            pl.BlockSpec(memory_space=pltpu.SMEM),
            pl.BlockSpec((BLK, HD), lambda b, h: (b, h)),
            pl.BlockSpec(memory_space=pltpu.VMEM),
        ]
        + [one.in_spec for one in programs],
        out_specs=[
            pl.BlockSpec((BLK, HD), lambda b, h: (b, h)),
            pl.BlockSpec((1, 1, 1, BLK), lambda b, h: (b, h, 0, 0)),
        ]
        + [one.out_spec for one in programs],
        scratch_shapes=[
            pltpu.VMEM((PBLK + 1, BLK, BLK), F32),
            pltpu.VMEM((PBLK + 1, BLK, BLK), F32),
            pltpu.VMEM((PBLK + 1, HD, BLK), BF16),
        ]
        + [held for one in programs for held in one.scratch()],
        compiler_params=pltpu.CompilerParams(
            collective_id=number, has_side_effects=True, vmem_limit_bytes=VMEM_BYTES
        ),
        cost_estimate=SMALL,
    )(positions, key_slots, queries, table, *arrays)
    return out[0], out[1], out[2:]


def attend_back_kernel(programs, steps, *refs):
    count = len(programs)
    (position_ref, slot_ref, query_ref, grad_ref, mixed_ref), refs = refs[:5], refs[5:]
    (logsum_ref, table_ref, normed_ref), refs = refs[:3], refs[3:]
    others, refs = refs[:count], refs[count:]
    (grad_query_ref, set_ref, weight_ref), refs = refs[:3], refs[3:]
    other_outs, refs = refs[:count], refs[count:]
    (bias_ref, key_t_ref, kept_ref), scratch = refs[:3], refs[3:]
    chunks = PBLK + 1
    scale = HD**-0.5
    block, head = pl.program_id(0), pl.program_id(1)
    step = pl.program_id(0) * pl.num_programs(1) + pl.program_id(1)
    finish = beside(programs, others, other_outs, scratch, step, steps)

    @pl.when(head == 0)
    def _():
        visible_bias(bias_ref, position_ref[block], chunks)
        set_ref[...] = jnp.zeros_like(set_ref)
        for chunk in range(chunks):
            key_t_ref[chunk] = table_ref[0, slot_ref[block, chunk]].astype(F32).T.astype(BF16)

    query, grad = query_ref[...], grad_ref[...]
    inner = jnp.sum(grad.astype(F32) * mixed_ref[...].astype(F32), axis=1, keepdims=True)
    inner = jnp.broadcast_to(inner, (BLK, HD)).T[:1, :]
    logsum = logsum_ref[0, 0]
    grad_query = jnp.zeros((HD, BLK), F32)
    for chunk in range(chunks):
        cut = slice(chunk * BLK, (chunk + 1) * BLK)
        slot = slot_ref[block, chunk]
        score = rows_by_rows(table_ref[0, slot], query)
        weight = jnp.exp2(score * (scale * LOG2E) + bias_ref[chunk] - logsum)
        grad_weight = rows_by_rows(table_ref[1, slot], grad)
        grad_score = (weight * (grad_weight - inner)).astype(BF16)
        set_ref[0, cut, :HD] += jnp.dot(grad_score, query, preferred_element_type=F32)
        set_ref[0, cut, HD:] += jnp.dot(weight.astype(BF16), grad, preferred_element_type=F32)
        grad_query = grad_query + jnp.dot(
            key_t_ref[chunk], grad_score, preferred_element_type=F32
        )
    grad_query = (grad_query * scale).T.astype(BF16)
    grad_query_ref[...] = grad_query
    kept_ref[block, head] = grad_query

    @pl.when(head == pl.num_programs(1) - 1)
    def _():
        set_ref[0, :, :HD] = set_ref[0, :, :HD] * scale

    def weights():
        blocks, heads = kept_ref.shape[:2]
        kept = [
            jnp.concatenate([kept_ref[b, h] for h in range(heads)], axis=1) for b in range(blocks)
        ]
        kept = jnp.concatenate(kept, axis=0)

        def work(cut):
            weight_ref[cut, :] = by_columns(normed_ref[:, cut], kept).astype(BF16)

        each_columns(weight_ref.shape[0], 256, work)

    finish(weights)


def attend_back(
    queries, grads, mixed, logsums, table, normed, positions, key_slots, programs, arrays, number
):
    rows, width = queries.shape
    blocks, heads = rows // BLK, width // HD
    count = (PBLK + 1) * BLK
    by_head = pl.BlockSpec((BLK, HD), lambda b, h: (b, h))
    out = pl.pallas_call(
        functools.partial(attend_back_kernel, programs, blocks * heads),
        grid=(blocks, heads),
        out_shape=[
            jax.ShapeDtypeStruct((rows, width), BF16),
            jax.ShapeDtypeStruct((blocks, count, 2 * HD), F32),
            jax.ShapeDtypeStruct((normed.shape[1], width), BF16),
        ]
        + [one.out for one in programs],
        in_specs=[
            pl.BlockSpec(memory_space=pltpu.SMEM),
            pl.BlockSpec(memory_space=pltpu.SMEM),
            by_head,
            by_head,
            by_head,
            pl.BlockSpec((1, 1, 1, BLK), lambda b, h: (b, h, 0, 0)),
            pl.BlockSpec(memory_space=pltpu.VMEM),
            pl.BlockSpec(memory_space=pltpu.VMEM),
        ]
        + [one.in_spec for one in programs],
        out_specs=[
            by_head,
            pl.BlockSpec((1, count, 2 * HD), lambda b, h: (b, 0, 0)),
            pl.BlockSpec(memory_space=pltpu.VMEM),
        ]
        + [one.out_spec for one in programs],
        scratch_shapes=[
            pltpu.VMEM((PBLK + 1, BLK, BLK), F32),
            pltpu.VMEM((PBLK + 1, HD, BLK), BF16),
            pltpu.VMEM((blocks, heads, BLK, HD), BF16),
        ]
        + [held for one in programs for held in one.scratch()],
        compiler_params=pltpu.CompilerParams(
            collective_id=number, has_side_effects=True, vmem_limit_bytes=VMEM_BYTES
        ),
        cost_estimate=SMALL,
    )(positions, key_slots, queries, grads, mixed, logsums, table, normed, *arrays)
    return out[0], out[1], out[2], out[3:]


def by_slot_kernel(slot_ref, set_ref, out_ref, table_ref):
    blocks, chunks = slot_ref.shape

    def clear(index, carry):
        table_ref[index] = jnp.zeros(table_ref.shape[1:], F32)
        return carry

    def give(index, carry):
        out_ref[0, index] = table_ref[index, :, :HD].astype(BF16)
        out_ref[1, index] = table_ref[index, :, HD:].astype(BF16)
        return carry

    lax.fori_loop(0, table_ref.shape[0], clear, 0)
    for block in range(blocks):
        for chunk in range(chunks):
            cut = slice(chunk * BLK, (chunk + 1) * BLK)
            table_ref[slot_ref[block, chunk]] += set_ref[block, cut, :]
    lax.fori_loop(0, table_ref.shape[0], give, 0)


def by_slot(sets, key_slots, slot_count):
    return pl.pallas_call(
        by_slot_kernel,
        out_shape=jax.ShapeDtypeStruct((2, slot_count, BLK, HD), BF16),
        in_specs=[
            pl.BlockSpec(memory_space=pltpu.SMEM),
            pl.BlockSpec(memory_space=pltpu.VMEM),
        ],
        out_specs=pl.BlockSpec(memory_space=pltpu.VMEM),
        scratch_shapes=[pltpu.VMEM((slot_count, BLK, 2 * HD), F32)],
        compiler_params=pltpu.CompilerParams(vmem_limit_bytes=VMEM_BYTES),
        cost_estimate=SMALL,
    )(key_slots, sets)


GELU_OUTER = 0.7978845608028654
GELU_INNER = 0.044715


def weight_copies(parts, target, sems):
    copies, start = [], 0
    for number, (ref, rows) in enumerate(parts):
        count = rows.stop - rows.start
        copies.append(
            pltpu.make_async_copy(
                ref.at[:, :, rows], target.at[:, :, start : start + count], sems.at[number]
            )
        )
        start += count
    return copies


def first_half(rows, first, refs):
    piece, early = refs[0], refs[1]
    down = [(piece, slice(0, first)), (early, slice(0, rows - first))]
    return down, [(early, slice(rows - first, 2 * rows - first))]


def second_half(rows, first, refs):
    early, late = refs[1], refs[2]
    start = 2 * rows - first
    there = early.shape[2] - start
    down = [(early, slice(start, start + there)), (late, slice(0, rows - there))]
    return down, [(late, slice(rows - there, 2 * rows - there))]


def gelu_both(value, grad_act):
    square = value * value
    bend = jnp.tanh(GELU_OUTER * value * (1.0 + GELU_INNER * square))
    slope = 0.5 * (1.0 + bend) + 0.5 * GELU_OUTER * value * (1.0 - bend * bend) * (
        1.0 + 3.0 * GELU_INNER * square
    )
    return 0.5 * value * (1.0 + bend), grad_act * slope


def forward_kernel(
    x_ref,
    cotangent_ref,
    piece_ref,
    early_ref,
    shift_ref,
    all_ref,
    act_ref,
    pre_ref,
    part_ref,
    bias_ref,
    weight_grad_ref,
    up_own,
    down_own,
    grads_own,
    rows_own,
    cotangent_own,
    act_own,
    pre_own,
    part_own,
    weight_sem,
    load_sem,
    store_sem,
    own_sem,
    send,
    recv,
):
    me = here()
    steps = (SIDE, FRONT, "tp")
    half, width = x_ref.shape
    hidden = early_ref.shape[3]

    def place(bits):
        at = me
        for k in (2, 1, 0):
            if bits >> k & 1:
                at = flip(at, steps[k])
        return at

    def block(bits):
        return by_plane_slot(all_ref, place(bits))

    def to_step(k, bits):
        source = block(bits) if bits else x_ref
        return remote(
            source, block(bits), send.at[k, bits], recv.at[bits | 1 << k], flip(me, steps[k])
        )

    def arrived(bits):
        remote(block(bits), block(bits), send.at[0, 0], recv.at[bits], me).wait_recv()

    def loads(number):
        slot, copies = number % 2, []
        for side, bits in enumerate((number, number + 4)):
            rows = pl.ds(side * half, half)
            copies.append(
                pltpu.make_async_copy(
                    by_plane_slot(cotangent_ref, place(bits)),
                    cotangent_own.at[slot, rows],
                    load_sem.at[slot, 0, side],
                )
            )
            copies.append(
                pltpu.make_async_copy(
                    block(bits) if bits else x_ref,
                    rows_own.at[slot, rows],
                    load_sem.at[slot, 1, side],
                )
            )
        return copies

    def stores(number, kind):
        slot = number % 2
        source, target = ((act_own, act_ref), (pre_own, pre_ref), (part_own, part_ref))[kind]
        return [
            pltpu.make_async_copy(
                source.at[slot, pl.ds(side * half, half)],
                by_plane_slot(target, place(bits)),
                store_sem.at[slot, kind, side],
            )
            for side, bits in enumerate((number, number + 4))
        ]

    def products(number):
        slot = number % 2
        tile = 256

        def one(index, carry):
            cut = pl.ds(pl.multiple_of(index * tile, tile), tile)
            down = down_own[:, :, :, cut].reshape(width, tile)
            up = up_own[:, :, :, cut].reshape(width, tile)
            grad_act = jnp.dot(cotangent_own[slot], down, preferred_element_type=F32)
            value = jnp.dot(rows_own[slot], up, preferred_element_type=F32)
            value = value + shift_ref[:, cut]
            act, grad_pre = gelu_both(value, grad_act)
            act_own[slot, :, cut] = act.astype(BF16)
            grad_pre = grad_pre.astype(BF16)
            pre_own[slot, :, cut] = grad_pre
            bias_ref[:, cut] += jnp.sum(
                grad_pre.astype(F32).reshape(2 * half // 8, 8, tile), axis=0
            )
            return carry

        lax.fori_loop(0, hidden // tile, one, 0, unroll=True)

    def back(number):
        slot = number % 2
        tile = up_own.shape[1] * up_own.shape[2]

        def one(index, carry):
            cut = pl.ds(pl.multiple_of(index * tile, tile), tile)
            up = up_own[index].reshape(tile, hidden)
            part_own[slot, :, cut] = rows_by_rows(pre_own[slot], up).astype(BF16)
            return carry

        lax.fori_loop(0, width // tile, one, 0, unroll=2)

    def grads(number):
        slot = number % 2
        tile = 256
        shard_rows = weight_grad_ref.shape[2]

        def one(index, carry):
            cut = pl.ds(pl.multiple_of(index * tile, tile), tile)
            for kind, (left, right) in enumerate(((cotangent_own, act_own), (rows_own, pre_own))):
                grad = by_columns(left[slot, :, cut], right[slot])
                if number > 0:
                    grad = grads_own[kind, cut, :] + grad
                if number < 3:
                    grads_own[kind, cut, :] = grad
                else:
                    count = tile // shard_rows
                    shards = pl.ds(pl.multiple_of(index * count, count), count)
                    grad = grad.astype(BF16).reshape(count, shard_rows, hidden)
                    weight_grad_ref[shards, kind] = grad
            return carry

        lax.fori_loop(0, width // tile, one, 0, unroll=2)

    def pass_on(bits, *ways):
        arrived(bits)
        for k in ways:
            to_step(k, bits).start()

    def second():
        to_step(0, 0).wait_send()
        to_step(1, 0).start()

    def third():
        to_step(1, 0).wait_send()
        to_step(1, 1).start()
        pass_on(2, 2)

    between = [second, third, functools.partial(pass_on, 3, 2), lambda: None]
    barrier = pltpu.get_barrier_semaphore()
    for step in steps:
        pl.semaphore_signal(barrier, inc=1, device_id=flip(me, step), device_id_type=MESH_ID)
    pl.semaphore_wait(barrier, 3)
    to_step(0, 0).start()
    to_step(2, 0).start()
    own = pltpu.make_async_copy(x_ref, block(0), own_sem)
    own.start()
    down_parts, up_parts = first_half(up_own.shape[2], piece_ref.shape[2], (piece_ref, early_ref))
    weights = weight_copies(down_parts, down_own, weight_sem)
    weights += weight_copies(up_parts, up_own, weight_sem.at[2:])
    for one in weights:
        one.start()
    bias_ref[...] = jnp.zeros_like(bias_ref)
    for number in range(4):
        if number == 1:
            pass_on(1, 2)
        arrived(4 + number)
        copies = loads(number)
        for one in copies:
            one.start()
        if number == 0:
            for one in weights:
                one.wait()
        if number >= 2:
            for kind in range(3):
                for one in stores(number - 2, kind):
                    one.wait()
        for one in copies:
            one.wait()
        products(number)
        between[number]()
        for kind in range(2):
            for one in stores(number, kind):
                one.start()
        back(number)
        for one in stores(number, 2):
            one.start()
        grads(number)
    for number in (2, 3):
        for kind in range(3):
            for one in stores(number, kind):
                one.wait()
    own.wait()
    for k, bits in ((2, 0), (1, 1), (2, 1), (2, 2), (2, 3)):
        to_step(k, bits).wait_send()


def forward_products(rows, cotangent_all, piece, early, shift, number):
    half, width = rows.shape
    lines, quarters, _, hidden = early.shape
    weights = (lines, quarters, width // (lines * quarters), hidden)
    anywhere = pl.BlockSpec(memory_space=pl.ANY)
    inside = pl.BlockSpec(memory_space=pltpu.VMEM)
    lead = (2, 2, 2, half)
    return pl.pallas_call(
        forward_kernel,
        out_shape=[
            jax.ShapeDtypeStruct(lead + (width,), BF16),
            jax.ShapeDtypeStruct(lead + (hidden,), BF16),
            jax.ShapeDtypeStruct(lead + (hidden,), BF16),
            jax.ShapeDtypeStruct(lead + (width,), BF16),
            jax.ShapeDtypeStruct((8, hidden), F32),
            jax.ShapeDtypeStruct((lines * quarters, 2, weights[2], hidden), BF16),
        ],
        in_specs=[anywhere] * 4 + [inside],
        out_specs=[anywhere] * 4 + [inside] * 2,
        scratch_shapes=[
            pltpu.VMEM(weights, BF16),
            pltpu.VMEM(weights, BF16),
            pltpu.VMEM((2, width, hidden), F32),
            pltpu.VMEM((2, 2 * half, width), BF16),
            pltpu.VMEM((2, 2 * half, width), BF16),
            pltpu.VMEM((2, 2 * half, hidden), BF16),
            pltpu.VMEM((2, 2 * half, hidden), BF16),
            pltpu.VMEM((2, 2 * half, width), BF16),
            pltpu.SemaphoreType.DMA((3,)),
            pltpu.SemaphoreType.DMA((2, 2, 2)),
            pltpu.SemaphoreType.DMA((2, 3, 2)),
            pltpu.SemaphoreType.DMA(()),
            pltpu.SemaphoreType.DMA((3, 4)),
            pltpu.SemaphoreType.DMA((8,)),
        ],
        compiler_params=pltpu.CompilerParams(
            collective_id=number, has_side_effects=True, vmem_limit_bytes=VMEM_BYTES
        ),
        cost_estimate=SMALL,
    )(rows, cotangent_all, piece, early, shift)


CHIPS = ((1, 1), (1, 0), (0, 1), (0, 0))


def second_kernel(
    rows_ref,
    cotangent_ref,
    before_ref,
    rows_columns_ref,
    cotangent_columns_ref,
    act_a_ref,
    piece_ref,
    early_ref,
    late_ref,
    shift_ref,
    down_part_ref,
    weight_grad_ref,
    bias_ref,
    sum_ref,
    up_own,
    downs,
    acts,
    pre_own,
    rows_own,
    cotangent_own,
    before_own,
    part_own,
    over_core,
    over_front,
    over_side,
    weight_sem,
    load_sem,
    core_send,
    core_recv,
    front_send,
    front_recv,
    side_sem,
):
    step = pl.program_id(0)
    me = here()
    core = me["tp"]
    width, hidden = rows_ref.shape[1], pre_own.shape[1]
    count = rows_ref.shape[0] // 4
    half = count // 2
    tile = 256
    places = (piece_ref, early_ref, late_ref)
    shard_rows, first = up_own.shape[2], piece_ref.shape[2]

    def chip(number):
        up, side = CHIPS[number]
        fsdp = me["fsdp"] + up * (1 - 2 * me["fsdp"])
        return fsdp, me["pair"] + side * (1 - 2 * me["pair"])

    def rows_of_chip(number):
        fsdp, pair = chip(number)
        return pl.ds(pl.multiple_of((fsdp * 2 + pair) * count, count), count)

    def loads(number):
        slot, rows = number % 2, rows_of_chip(number)
        pairs = ((rows_ref, rows_own), (cotangent_ref, cotangent_own), (before_ref, before_own))
        return [
            pltpu.make_async_copy(source.at[rows], target.at[slot], load_sem.at[slot, kind])
            for kind, (source, target) in enumerate(pairs)
        ]

    def second_weights():
        down_parts, up_parts = second_half(shard_rows, first, places)
        copies = weight_copies(down_parts, downs.at[1], weight_sem.at[0])
        return copies + weight_copies(up_parts, up_own, weight_sem.at[1])

    def first_weights():
        copies = weight_copies(first_half(shard_rows, first, places)[0], downs.at[0], weight_sem.at[2])
        return copies + [pltpu.make_async_copy(act_a_ref, acts.at[0], weight_sem.at[1, 1])]

    def to_core(number):
        fsdp, pair = chip(number)
        up, side = CHIPS[number]
        return remote(
            part_own.at[fsdp, pair, 1 - core],
            over_core.at[up, side],
            core_send.at[up, side],
            core_recv.at[up, side],
            flip(me, "tp"),
        )

    def take_core(number):
        fsdp, pair = chip(number)
        to_core(number).wait_recv()
        held = over_core.at[CHIPS[number]]
        add_blocks(held, rows_of(part_own.at[fsdp, pair, core]), rows_of(held), half)

    def to_front(corner):
        source = over_core.at[1, 1] if corner else over_core.at[1 - core, core]
        return remote(
            source, over_front.at[corner], front_send.at[corner], front_recv.at[corner], flip(me, FRONT)
        )

    def to_side():
        return remote(over_front.at[1], over_side, side_sem.at[0], side_sem.at[1], flip(me, SIDE))

    def take_front(corner):
        to_front(corner).wait_recv()
        held = over_front.at[corner]
        mine = over_core.at[core, 1 - core] if corner else over_core.at[0, 0]
        add_blocks(held, rows_of(mine), rows_of(held), half)

    def products(number):
        slot, rows = number % 2, rows_of_chip(number)

        def one(index, carry):
            cut = pl.ds(pl.multiple_of(index * tile, tile), tile)
            down = downs[1, :, :, :, cut].reshape(width, tile)
            up = up_own[:, :, :, cut].reshape(width, tile)
            grad_act = jnp.dot(cotangent_own[slot], down, preferred_element_type=F32)
            value = jnp.dot(rows_own[slot], up, preferred_element_type=F32) + shift_ref[:, cut]
            act, grad_pre = gelu_both(value, grad_act)
            acts[1, rows, cut] = act.astype(BF16)
            grad_pre = grad_pre.astype(BF16)
            pre_own[rows, cut] = grad_pre
            bias_ref[:, cut] += fold_rows(grad_pre.astype(F32))
            return carry

        lax.fori_loop(0, hidden // tile, one, 0, unroll=True)
        tile_back = up_own.shape[1] * shard_rows
        fsdp, pair = chip(number)

        def back(index, carry):
            cut = pl.ds(pl.multiple_of(index * tile_back, tile_back), tile_back)
            up = up_own[index].reshape(tile_back, hidden)
            part = before_own[slot, :, cut].astype(F32) + rows_by_rows(pre_own[rows, :], up)
            part_own[fsdp, pair, :, :, cut] = part.astype(BF16).reshape(2, half, tile_back)
            return carry

        lax.fori_loop(0, width // tile_back, back, 0, unroll=2)

    def chunk_step(number):
        if number == 0:
            barrier = pltpu.get_barrier_semaphore()
            for bits in (1, 2, 4):
                pl.semaphore_signal(
                    barrier, inc=1, device_id=plane_partner(me, bits), device_id_type=MESH_ID
                )
            for one in loads(0) + second_weights() + first_weights():
                one.start()
            bias_ref[...] = jnp.zeros_like(bias_ref)
            for one in second_weights():
                one.wait()
            pl.semaphore_wait(barrier, 3)
        for one in loads(number):
            one.wait()
        if number < 3:
            for one in loads(number + 1):
                one.start()
        products(number)
        to_core(number).start()
        if number > 0:
            take_core(number - 1)
        if number == 1:
            to_front(1).start()
        if number == 2:
            pl.when(core == 0)(lambda: to_front(0).start())
        if number == 3:
            pl.when(core == 1)(lambda: to_front(0).start())
            for one in first_weights():
                one.wait()

    for number in range(4):
        pl.when(step == number)(functools.partial(chunk_step, number))

    @pl.when(step == 4)
    def _():
        take_core(3)

    @pl.when(step == 5)
    def _():
        take_front(1)
        to_side().start()

    @pl.when(step == 9)
    def _():
        take_front(0)

    @pl.when(step >= 4)
    def _():
        rows_here = down_part_ref.shape[0]
        rows = pl.ds(pl.multiple_of((step - 4) * rows_here, rows_here), rows_here)
        shards = weight_grad_ref.shape[0]
        for kind, (left, right) in enumerate(
            ((cotangent_columns_ref, acts.at[1]), (rows_columns_ref, pre_own))
        ):
            grad = by_columns(left[...], right[...]).astype(BF16)
            weight_grad_ref[:, kind] = grad.reshape(shards, shard_rows, hidden)
        part = rows_by_rows(acts[0, rows, :], downs[0].reshape(width, hidden))
        part = part + rows_by_rows(acts[1, rows, :], downs[1].reshape(width, hidden))
        down_part_ref[...] = part.astype(BF16)

    @pl.when(step == pl.num_programs(0) - 1)
    def _():
        to_side().wait_recv()
        final = over_front.at[0]
        add_blocks(sum_ref, rows_of(final), rows_of(over_side), half)
        for number in range(4):
            to_core(number).wait_send()
        for corner in range(2):
            to_front(corner).wait_send()
        to_side().wait_send()


def second_products(rows_all, cotangent_all, before, act_a, piece, early, late, shift, number):
    rows, width = rows_all.shape
    lines, quarters, _, hidden = late.shape
    shards, shard_rows = lines * quarters, width // (lines * quarters)
    weights = (lines, quarters, shard_rows, hidden)
    steps, tiles, half = 12, 8, rows // 8

    def tile(i):
        return jnp.maximum(i - 4, 0)

    columns = pl.BlockSpec((rows, width // tiles), lambda i: (0, tile(i)))
    anywhere = pl.BlockSpec(memory_space=pl.ANY)
    fixed = lambda shape: pl.BlockSpec(shape, lambda i: (0,) * len(shape))
    return pl.pallas_call(
        second_kernel,
        grid=(steps,),
        out_shape=[
            jax.ShapeDtypeStruct((rows, width), BF16),
            jax.ShapeDtypeStruct((shards, 2, shard_rows, hidden), BF16),
            jax.ShapeDtypeStruct((8, hidden), F32),
            jax.ShapeDtypeStruct((half, width), F32),
        ],
        in_specs=[anywhere] * 3 + [columns] * 2 + [anywhere] * 4 + [fixed((1, hidden))],
        out_specs=[
            pl.BlockSpec((rows // tiles, width), lambda i: (tile(i), 0)),
            pl.BlockSpec((shards // tiles, 2, shard_rows, hidden), lambda i: (tile(i), 0, 0, 0)),
            fixed((8, hidden)),
            fixed((half, width)),
        ],
        scratch_shapes=[
            pltpu.VMEM(weights, BF16),
            pltpu.VMEM((2,) + weights, BF16),
            pltpu.VMEM((2, rows, hidden), BF16),
            pltpu.VMEM((rows, hidden), BF16),
            pltpu.VMEM((2, 2 * half, width), BF16),
            pltpu.VMEM((2, 2 * half, width), BF16),
            pltpu.VMEM((2, 2 * half, width), BF16),
            pltpu.VMEM((2, 2, 2, half, width), BF16),
            pltpu.VMEM((2, 2, half, width), BF16),
            pltpu.VMEM((2, half, width), BF16),
            pltpu.VMEM((half, width), BF16),
            pltpu.SemaphoreType.DMA((3, 2)),
            pltpu.SemaphoreType.DMA((2, 3)),
            pltpu.SemaphoreType.DMA((2, 2)),
            pltpu.SemaphoreType.DMA((2, 2)),
            pltpu.SemaphoreType.DMA((2,)),
            pltpu.SemaphoreType.DMA((2,)),
            pltpu.SemaphoreType.DMA((2,)),
        ],
        compiler_params=kernel_params(number),
        cost_estimate=SMALL,
    )(rows_all, cotangent_all, before, rows_all, cotangent_all, act_a, piece, early, late, shift)


def by_columns(left, right):
    return lax.dot_general(left, right, (((0,), (0,)), ((), ())), preferred_element_type=F32)


def reorder_kernel(cuts, size, x_ref, out_ref):
    for index, cut in enumerate(cuts):
        out_ref[:, index * size : (index + 1) * size] = x_ref[:, cut : cut + size]


def reorder(values, cuts):
    size = values.shape[1] // len(cuts)
    if size % 128:
        return jnp.concatenate([values[:, cut : cut + size] for cut in cuts], axis=1)
    return pl.pallas_call(
        functools.partial(reorder_kernel, cuts, size),
        out_shape=jax.ShapeDtypeStruct(values.shape, values.dtype),
        compiler_params=pltpu.CompilerParams(vmem_limit_bytes=VMEM_BYTES),
        cost_estimate=SMALL,
    )(values)


def to_line_order(values):
    lines = lax.axis_size("line")
    size = values.shape[1] // (2 * lines)
    return reorder(
        values, [(half * lines + shard) * size for shard in range(lines) for half in range(2)]
    )


def from_line_order(values):
    lines = lax.axis_size("line")
    size = values.shape[1] // (2 * lines)
    return reorder(
        values, [(shard * 2 + half) * size for half in range(2) for shard in range(lines)]
    )


def meet_sibling(me):
    barrier = pltpu.get_barrier_semaphore()
    pl.semaphore_signal(barrier, inc=1, device_id=flip(me, "tp"), device_id_type=MESH_ID)
    pl.semaphore_wait(barrier, 1)


def half_rows_of(core, rows):
    return pl.ds(pl.multiple_of(core * rows, rows), rows)


def each_rows(total, tile, work):
    def one(index, carry):
        work(pl.ds(pl.multiple_of(index * tile, tile), tile))
        return carry

    lax.fori_loop(0, total // tile, one, 0)


def each_columns(total, tile, work):
    each_rows(total, tile, work)


def moments(values):
    centered = values - jnp.mean(values, axis=1, keepdims=True)
    spread = jnp.mean(centered * centered, axis=1, keepdims=True)
    return centered, lax.rsqrt(spread + EPSILON)


def norm_back(values, gain, grad):
    centered, rstd = moments(values)
    xhat = centered * rstd
    scaled = grad * gain
    inner = jnp.mean(scaled * xhat, axis=1, keepdims=True)
    return xhat, rstd * (scaled - jnp.mean(scaled, axis=1, keepdims=True) - xhat * inner)


def fold_rows(values):
    return jnp.sum(values.reshape(values.shape[0] // 8, 8, values.shape[1]), axis=0)


def shuffled(cuts, ref, rows):
    if cuts is None:
        return ref[rows, :]
    size = ref.shape[1] // len(cuts)
    return jnp.concatenate([ref[rows, cut : cut + size] for cut in cuts], axis=1)


def norm_work(me, refs, out_ref):
    stream_ref, vectors_ref = refs
    gain, shift = vectors_ref[0:1, :], vectors_ref[1:2, :]

    def work(rows):
        centered, rstd = moments(stream_ref[rows, :].astype(F32))
        out_ref[rows, :] = (centered * rstd * gain + shift).astype(BF16)

    each_rows(out_ref.shape[0], 32, work)


def reorder_work(cuts, me, x_ref, out_ref):
    half, size = out_ref.shape[0], out_ref.shape[1] // len(cuts)
    few = 64

    def work(rows):
        start = pl.multiple_of(me["tp"] * half + rows.start, few)
        for index, cut in enumerate(cuts):
            out_ref[rows, index * size : (index + 1) * size] = x_ref[
                pl.ds(start, few), cut : cut + size
            ]

    each_rows(half, few, work)


def part_work(me, refs, out_ref):
    normed_ref, weight_ref, shift_ref = refs
    heads = weight_ref.shape[1] - out_ref.shape[1]
    part = jnp.dot(normed_ref[...], weight_ref[:, heads:], preferred_element_type=F32)
    out_ref[...] = (part + shift_ref[:, heads:]).astype(BF16)


def query_work(me, refs, out_ref):
    normed_ref, weight_ref, shift_ref = refs

    def work(cut):
        query = jnp.dot(normed_ref[...], weight_ref[:, cut], preferred_element_type=F32)
        out_ref[:, cut] = (query + shift_ref[:, cut]).astype(BF16)

    each_columns(out_ref.shape[1], 256, work)


def project_kernel(
    cuts,
    mixed_ref,
    proj_ref,
    stream_ref,
    vectors_ref,
    middle_ref,
    normed_ref,
    sent_ref,
    got_ref,
    sems,
):
    me = here()
    half, width = middle_ref.shape
    mine, other = half_rows_of(me["tp"], half), half_rows_of(1 - me["tp"], half)
    tile = 512
    meet_sibling(me)
    copy = remote(sent_ref, got_ref, sems.at[0], sems.at[1], flip(me, "tp"))

    def part(rows, target):
        def work(cut):
            target[:, cut] = rows_by_rows(mixed_ref[rows, :], proj_ref[cut, :])

        each_columns(width, tile, work)

    part(other, sent_ref)
    copy.start()
    part(mine, middle_ref)
    copy.wait_recv()
    bias, gain, shift = vectors_ref[2:3, :], vectors_ref[3:4, :], vectors_ref[4:5, :]
    few = 32

    def finish(rows):
        start = pl.multiple_of(me["tp"] * half + rows.start, few)
        stream = stream_ref[pl.ds(start, few), :].astype(F32)
        middle = stream + (middle_ref[rows, :] + got_ref[rows, :] + bias)
        middle_ref[rows, :] = middle
        centered, rstd = moments(middle)
        normed = (centered * rstd * gain + shift).astype(BF16)
        if cuts is None:
            normed_ref[rows, :] = normed
            return
        size = width // len(cuts)
        for index, cut in enumerate(cuts):
            normed_ref[rows, index * size : (index + 1) * size] = normed[:, cut : cut + size]

    each_rows(half, few, finish)
    copy.wait_send()


def in_vmem(count):
    return [pl.BlockSpec(memory_space=pltpu.VMEM)] * count


def kernel_params(number):
    return pltpu.CompilerParams(
        collective_id=number, has_side_effects=True, vmem_limit_bytes=VMEM_BYTES
    )


def line_cuts(width, back):
    lines = lax.axis_size("line")
    size = width // (2 * lines)
    if size % 128:
        return None
    if back:
        return [(shard * 2 + half) * size for half in range(2) for shard in range(lines)]
    return [(half * lines + shard) * size for shard in range(lines) for half in range(2)]


def project(mixed, proj_all, stream, vectors, number):
    rows, width = stream.shape
    half = rows // 2
    cuts = line_cuts(width, False)
    middle, normed = pl.pallas_call(
        functools.partial(project_kernel, cuts),
        out_shape=[
            jax.ShapeDtypeStruct((half, width), F32),
            jax.ShapeDtypeStruct((half, width), BF16),
        ],
        in_specs=in_vmem(4),
        out_specs=in_vmem(2),
        scratch_shapes=[
            pltpu.VMEM((half, width), F32),
            pltpu.VMEM((half, width), F32),
            pltpu.SemaphoreType.DMA((2,)),
        ],
        compiler_params=kernel_params(number),
        cost_estimate=SMALL,
    )(mixed, proj_all, stream, vectors)
    return middle, normed if cuts else to_line_order(normed)


def middle_back_kernel(
    cuts,
    sum_ref,
    middle_ref,
    cotangent_ref,
    mixed_ref,
    proj_ref,
    vectors_ref,
    hidden_a_ref,
    hidden_b_ref,
    grad_middle_ref,
    grad_mixed_ref,
    proj_grad_ref,
    vector_ref,
    attn_ref,
    sums_own,
    sems,
):
    me = here()
    half, width = middle_ref.shape
    mine, other = half_rows_of(me["tp"], half), half_rows_of(1 - me["tp"], half)
    few = 32
    gain = vectors_ref[3:4, :]
    meet_sibling(me)
    sums_own[...] = jnp.zeros_like(sums_own)

    def norm(rows):
        start = pl.multiple_of(me["tp"] * half + rows.start, few)
        cotangent = cotangent_ref[pl.ds(start, few), :].astype(F32)
        grad = shuffled(cuts, sum_ref, rows)
        xhat, back = norm_back(middle_ref[rows, :], gain, grad)
        grad_middle = cotangent + back
        grad_middle_ref[rows, :] = grad_middle
        attn = grad_middle.astype(BF16)
        attn_ref[pl.ds(start, few), :] = attn
        sums_own[0] += fold_rows(grad * xhat)
        sums_own[1] += fold_rows(grad)
        sums_own[2] += fold_rows(attn.astype(F32))
        sums_own[3] += fold_rows(cotangent)

    each_rows(half, few, norm)
    copy = remote(attn_ref.at[mine], attn_ref.at[mine], sems.at[0], sems.at[1], flip(me, "tp"))
    copy.start()

    def to_heads(rows):
        def work(cut):
            grad = jnp.dot(attn_ref[rows, :], proj_ref[:, cut], preferred_element_type=F32)
            grad_mixed_ref[rows, cut] = grad.astype(BF16)

        each_columns(proj_ref.shape[1], 256, work)

    to_heads(mine)
    vector_ref[...] = jnp.zeros_like(vector_ref)
    for kind in range(4):
        vector_ref[2 + kind : 3 + kind, :] = jnp.sum(sums_own[kind], axis=0, keepdims=True)
    size = hidden_a_ref.shape[1]
    for number, hidden_ref in enumerate((hidden_a_ref, hidden_b_ref)):
        start = width - (2 - number) * size
        vector_ref[6:7, start : start + size] = jnp.sum(hidden_ref[...], axis=0, keepdims=True)
    copy.wait_recv()
    to_heads(other)

    def weight(cut):
        grad = lax.dot_general(
            attn_ref[:, cut], mixed_ref[...], (((0,), (0,)), ((), ())), preferred_element_type=F32
        )
        proj_grad_ref[cut, :] = grad.astype(BF16)

    each_columns(width, 256, weight)
    copy.wait_send()


def middle_back(grad_sum, middle, cotangent, mixed, proj_all, vectors, hidden_a, hidden_b, number):
    rows, width = cotangent.shape
    half, heads = rows // 2, mixed.shape[1]
    cuts = line_cuts(width, True)
    return pl.pallas_call(
        functools.partial(middle_back_kernel, cuts),
        out_shape=[
            jax.ShapeDtypeStruct((half, width), F32),
            jax.ShapeDtypeStruct((rows, heads), BF16),
            jax.ShapeDtypeStruct((width, heads), BF16),
            jax.ShapeDtypeStruct((8, width), F32),
        ],
        in_specs=in_vmem(8),
        out_specs=in_vmem(4),
        scratch_shapes=[
            pltpu.VMEM((rows, width), BF16),
            pltpu.VMEM((4, 8, width), F32),
            pltpu.SemaphoreType.DMA((2,)),
        ],
        compiler_params=kernel_params(number),
        cost_estimate=SMALL,
    )(
        grad_sum if cuts else from_line_order(grad_sum),
        middle,
        cotangent,
        mixed,
        proj_all,
        vectors,
        hidden_a,
        hidden_b,
    )


def first_back_kernel(cuts, programs, *refs):
    (
        grad_query_ref,
        grad_part_ref,
        first_ref,
        stream_ref,
        normed_ref,
        vectors_ref,
        grad_middle_ref,
        mlp_ref,
        middle_ref,
        early_ref,
        cut_a_ref,
        cut_b_ref,
    ), refs = refs[:12], refs[12:]
    (input_ref, layer_ref, down_out, up_out, part_out, total_out), refs = refs[:6], refs[6:]
    (weight_ref, vector_ref, sent_ref, got_ref, grad_first_ref, held_ref, sems), scratch = refs[:7], refs[7:]
    me = here()
    rows, width = stream_ref.shape
    half, heads = rows // 2, grad_query_ref.shape[1]
    shard_rows = part_out.shape[0]
    mine, other = half_rows_of(me["tp"], half), half_rows_of(1 - me["tp"], half)
    few = 32
    sibling = flip(me, "tp")
    works = schedule(
        programs,
        (
            (cut_a_ref.at[:, :shard_rows], cut_b_ref.at[:, :shard_rows]),
            (cut_a_ref.at[:, shard_rows:], cut_b_ref.at[:, shard_rows:]),
            weight_ref.reshape(2, -1, 2, shard_rows, weight_ref.shape[1]),
            vector_ref,
        ),
        (down_out, up_out, part_out, total_out),
        scratch,
        ("tp",),
    )

    def run_until(stop):
        while works and works[0][0] < stop:
            works.pop(0)[1]()

    run_until(0.1)
    grad_first_ref[:, :heads] = grad_query_ref[...]
    grad_first_ref[:, heads:] = grad_part_ref[...].astype(BF16)

    def weight(cut):
        grad = lax.dot_general(
            normed_ref[:, cut],
            grad_first_ref[:, heads:],
            (((0,), (0,)), ((), ())),
            preferred_element_type=F32,
        )
        weight_ref[cut, :] = grad.astype(BF16)

    each_columns(width, 512, weight)
    run_until(0.2)

    def part(at, target):
        def work(cut):
            target[:, cut] = rows_by_rows(grad_first_ref[at, :], first_ref[cut, :])

        each_columns(width, 512, work)

    part(other, sent_ref)
    sums_copy = remote(sent_ref, got_ref, sems.at[0], sems.at[1], sibling)
    sums_copy.start()
    run_until(0.3)
    bias = vectors_ref[5:6, :]

    def layer(at):
        start = pl.multiple_of(me["tp"] * half + at.start, few)
        out = middle_ref[at, :] + (shuffled(cuts, mlp_ref, at) + bias)
        layer_ref[pl.ds(start, few), :] = out.astype(BF16)

    each_rows(half, few, layer)
    layer_copy = remote(layer_ref.at[mine], layer_ref.at[mine], sems.at[2], sems.at[3], sibling)
    layer_copy.start()
    run_until(0.4)
    grad_own, folded = held_ref.at[0], held_ref.at[1]
    part(mine, grad_own)
    run_until(0.5)
    sums_copy.wait_recv()
    gain = vectors_ref[0:1, :]
    folded[0:16, :] = jnp.zeros((16, width), F32)

    def norm(at):
        start = pl.multiple_of(me["tp"] * half + at.start, few)
        grad = grad_own[at, :] + got_ref[at, :]
        xhat, back = norm_back(stream_ref[pl.ds(start, few), :].astype(F32), gain, grad)
        input_ref[pl.ds(start, few), :] = (grad_middle_ref[at, :] + back).astype(BF16)
        folded[0:8, :] += fold_rows(grad * xhat)
        folded[8:16, :] += fold_rows(grad)

    each_rows(half, few, norm)
    input_copy = remote(input_ref.at[mine], input_ref.at[mine], sems.at[4], sems.at[5], sibling)
    input_copy.start()
    vector_ref[...] = early_ref[...]
    for kind in range(2):
        total = jnp.sum(folded[kind * 8 : kind * 8 + 8, :], axis=0, keepdims=True)
        vector_ref[kind : kind + 1, :] = total
    vector_ref[6:7, :heads] = jnp.sum(
        fold_rows(grad_query_ref[...].astype(F32)), axis=0, keepdims=True
    )
    part_sums = jnp.sum(
        fold_rows(grad_first_ref[:, heads:].astype(F32)), axis=0, keepdims=True
    )
    vector_ref[7:8, : part_sums.shape[1]] = jnp.where(me["tp"] == 1, part_sums, 0.0)
    run_until(2.0)
    layer_copy.wait()
    input_copy.wait()
    sums_copy.wait_send()


def first_back(
    grad_query,
    grad_part,
    first_all,
    stream,
    normed,
    vectors,
    grad_middle,
    mlp_sum,
    middle,
    early,
    cut_a,
    cut_b,
    number,
):
    rows, width = stream.shape
    half, heads, part = rows // 2, grad_query.shape[1], grad_part.shape[1]
    lines = lax.axis_size("line")
    cuts = line_cuts(width, True)
    shard_rows = width // (4 * lines)
    vector = early.shape
    programs = [
        placed(join_halves(shard_rows, 8 * cut_a.shape[2], BF16), 0.0, 1.0),
        placed(join_halves(shard_rows, 8 * cut_a.shape[2], BF16), 0.0, 1.0),
        placed(Direct(lines, shard_rows, part, part), 0.1, 0.95),
        placed(Total(vector, lines, 6, heads), 0.9, 0.93, 0.97),
    ]
    anywhere = [pl.BlockSpec(memory_space=pl.ANY)] * 2
    return pl.pallas_call(
        functools.partial(first_back_kernel, cuts, programs),
        out_shape=[
            jax.ShapeDtypeStruct((rows, width), BF16),
            jax.ShapeDtypeStruct((rows, width), BF16),
        ]
        + [one.out for one in programs],
        in_specs=in_vmem(10) + anywhere,
        out_specs=in_vmem(2) + [one.out_spec for one in programs],
        scratch_shapes=[
            pltpu.VMEM((width, part), BF16),
            pltpu.VMEM(vector, F32),
            pltpu.VMEM((half, width), F32),
            pltpu.VMEM((half, width), F32),
            pltpu.VMEM((rows, heads + part), BF16),
            pltpu.VMEM((2, half, width), F32),
            pltpu.SemaphoreType.DMA((6,)),
        ]
        + [held for one in programs for held in one.scratch()],
        compiler_params=kernel_params(number),
        cost_estimate=SMALL,
    )(
        grad_query,
        grad_part,
        first_all,
        stream,
        normed,
        vectors,
        grad_middle,
        mlp_sum if cuts else from_line_order(mlp_sum),
        middle,
        early,
        cut_a,
        cut_b,
    )


def body(
    hidden_in,
    block_order,
    attn_norm_gain,
    attn_norm_bias,
    query_weight,
    query_bias,
    keyval_weight,
    value_bias,
    proj_weight,
    proj_bias,
    mlp_norm_gain,
    mlp_norm_bias,
    up_weight,
    up_bias,
    down_weight,
    down_bias,
    out_cotangent,
):
    rows_dev = hidden_in.shape[0]
    half_rows = rows_dev // 2
    width = hidden_in.shape[1]
    blocks_dev = rows_dev // BLK
    slot_count = block_order.shape[1]
    group_blocks = PBLK + CONTS
    heads_dev = query_bias.shape[0] // HD
    head_width = heads_dev * HD
    core = lax.axis_index("tp")
    quarter = lax.axis_index("fsdp") * lax.axis_size("pair") + lax.axis_index("pair")
    quarters = lax.axis_size("fsdp") * lax.axis_size("pair")
    hidden_dev = up_weight.shape[1] // quarters

    def own_half(values):
        return lax.dynamic_slice_in_dim(values, core * half_rows, half_rows, axis=0)

    def in_order(mine, other, axis=0):
        first = jnp.where(core == 0, mine, other)
        second = jnp.where(core == 0, other, mine)
        return jnp.concatenate([first, second], axis=axis)


    slot_ids = jnp.arange(slot_count, dtype=jnp.int32)
    ordering = block_order[0]
    inverse = jnp.sum(
        jnp.where(ordering[None, :] == slot_ids[:, None], slot_ids[None, :], 0), axis=1
    )
    ctx_index = lax.axis_index("line") * lax.axis_size("pair") + lax.axis_index("pair")
    first_slot = ctx_index * blocks_dev
    my_slots = first_slot + jnp.arange(blocks_dev, dtype=jnp.int32)
    my_blocks = lax.dynamic_slice_in_dim(ordering, first_slot, blocks_dev)
    positions = my_blocks % group_blocks
    group_base = my_blocks // group_blocks * group_blocks
    prompt_slots = jnp.take(
        inverse, group_base[:, None] + jnp.arange(PBLK, dtype=jnp.int32)[None, :]
    )
    key_slots = jnp.concatenate([prompt_slots, my_slots[:, None]], axis=1)

    vectors = [
        attn_norm_gain,
        attn_norm_bias,
        proj_bias,
        mlp_norm_gain,
        mlp_norm_bias,
        down_bias,
    ]
    vectors = jnp.stack(vectors + [jnp.zeros_like(down_bias)] * 2).astype(F32)

    keyval_cut = lax.dynamic_slice_in_dim(keyval_weight, core * HD, HD, axis=1)
    first_cut = jnp.concatenate([query_weight, keyval_cut], axis=1)
    shard_rows = down_weight.shape[0]
    hidden_half = hidden_dev // 2
    columns = down_weight.shape[1]
    first_rows = shard_rows // 2
    early_rows = shard_rows // 2
    cuts = line_cuts(width, False)
    lines = lax.axis_size("line")
    first_pieces = [(0, slice(0, first_rows), 0)]
    early_pieces = [
        (0, slice(first_rows, shard_rows), 0),
        (1, slice(0, shard_rows), 0),
        (0, slice(0, early_rows), 1),
    ]
    late_pieces = [(0, slice(early_rows, shard_rows), 1), (1, slice(0, shard_rows), 1)]
    hops = [0.1 * k for k in range(1, 4)] if lines == 4 else spaced(0.1, 0.3, lines - 1)
    levels = spaced(0.4, 0.98, 2 * lines)
    piece_hops = spaced(0.35, 0.75, lines - 1)
    _, first_all, early_cut, late_cut, mlp_piece, normed_one, cotangent_line, proj_line = run_programs(
        [
            placed(spread_halves(first_pieces, columns, BF16), 0.0, 0.05),
            placed(rows_gather(first_cut), 0.01, *hops, *levels, 1.0),
            placed(spread_halves(early_pieces, columns, BF16), 0.06, 1.0),
            placed(spread_halves(late_pieces, columns, BF16), 0.061, 1.0),
            placed(line_gather((quarters, first_rows, hidden_half), BF16), 0.07, *piece_hops, 1.0),
            placed(Work(norm_work, hidden_in.shape, BF16), 0.31, 0.31),
            placed(Work(functools.partial(reorder_work, cuts or [0]), (half_rows, width), BF16), 0.32, 0.32),
            placed(line_gather(proj_weight.shape, BF16), 0.305, *spaced(0.48, 0.88, lines - 1), 1.0),
        ],
        [
            lambda more, outs: more[3:5],
            lambda more, outs: more[5],
            lambda more, outs: more[3:5],
            lambda more, outs: more[3:5],
            lambda more, outs: outs[0],
            lambda more, outs: more[:2],
            lambda more, outs: more[2],
            lambda more, outs: more[6],
        ],
        1,
        near=[hidden_in, vectors, out_cotangent],
        far=[down_weight, up_weight, first_cut, proj_weight],
    )
    if cuts is None:
        cotangent_line = to_line_order(own_half(out_cotangent))
    first_all = flat(first_all)

    value_shift = jnp.where(core == 1, value_bias.astype(F32), 0.0)
    first_shift = jnp.concatenate([query_bias.astype(F32), value_shift])
    part_like = (rows_dev, HD)
    _, query_low, keyval_every = run_programs(
        [
            placed(Work(part_work, part_like, BF16), 0.0, 0.0),
            placed(Work(query_work, (rows_dev, head_width), BF16), 0.2, 0.2),
            placed(ctx_gather(part_like, BF16), 0.1, 1.0),
        ],
        [
            lambda more, outs: more[:3],
            lambda more, outs: more[:3],
            lambda more, outs: outs[0],
        ],
        4,
        near=[normed_one, first_all, first_shift[None]],
    )
    keyval_every, early_cut = lax.optimization_barrier((keyval_every, early_cut))
    mlp_early = lax.all_gather(early_cut, "line", axis=0, tiled=False)
    table = keyval_every.reshape(2, slot_count, BLK, HD)
    mixed_low, logsums, (proj_all, cotangent_all) = attend(
        query_low,
        table,
        positions,
        key_slots,
        [
            placed(columns_gather(proj_line), 0.0, 0.9, 1.0, 1.0),
            placed(plane_gather(cotangent_line), 0.0, 0.9, 1.0, 1.0),
        ],
        [proj_line, cotangent_line],
        2,
    )
    proj_all = flat(proj_all)
    mixed_low, mlp_early, late_cut = lax.optimization_barrier((mixed_low, mlp_early, late_cut))
    mlp_late = lax.all_gather(late_cut, "line", axis=0, tiled=False)
    middle, normed_two_line = project(
        mixed_low, proj_all, hidden_in, vectors, 5
    )

    up_shift = lax.dynamic_slice_in_dim(up_bias, quarter * hidden_dev, hidden_dev).astype(F32)
    up_shift = up_shift[None]
    rows_all, act_a, pre_a, back_a, bias_a, weight_grad_a = forward_products(
        normed_two_line, cotangent_all, mlp_piece, mlp_early, up_shift[:, :hidden_half], 6
    )
    rows_all, act_a, pre_a, back_a = flat(rows_all), flat(act_a), flat(pre_a), flat(back_a)
    cotangent_all = flat(cotangent_all)
    cut_a = lax.psum_scatter(weight_grad_a, "line", scatter_dimension=0, tiled=True)
    rows_all, weight_grad_a = lax.optimization_barrier((rows_all, weight_grad_a))
    down_part, weight_grad_b, bias_b, grad_normed_two = second_products(
        rows_all,
        cotangent_all,
        back_a,
        act_a,
        mlp_piece,
        mlp_early,
        mlp_late,
        up_shift[:, hidden_half:],
        7,
    )
    cut_b = lax.psum_scatter(weight_grad_b, "line", scatter_dimension=0, tiled=True)
    cut_a = cut_a.reshape(quarters, 2 * shard_rows, hidden_half)
    cut_b = cut_b.reshape(quarters, 2 * shard_rows, hidden_half)

    grad_middle, grad_mixed, proj_weight_grad, vector = middle_back(
        grad_normed_two, middle, out_cotangent, mixed_low, proj_all, vectors, bias_a, bias_b, 8
    )
    grad_mixed, cut_a = lax.optimization_barrier((grad_mixed, cut_a))
    sum_proj, proj_parts = rows_sum(proj_weight_grad)
    sum_down, down_parts = plane_sum(down_part)
    grad_query, grad_sets, query_weight_grad, (grad_proj_weight, mlp_out) = attend_back(
        query_low,
        grad_mixed,
        mixed_low,
        logsums,
        table,
        normed_one,
        positions,
        key_slots,
        [
            placed(sum_proj, 0.0, *spaced(0.13, 0.51, lines), 0.63, 1.06),
            placed(sum_down, 0.0, 0.45, 0.45, 0.45, 0.45, 0.76, 0.95, 1.1, 1.2),
        ],
        [proj_parts, down_parts],
        3,
    )
    grad_table = by_slot(grad_sets, key_slots, slot_count)
    grad_parts = grad_table.reshape(2, lines, 2 * rows_dev, HD)
    along_line, over_pair = ctx_sums(grad_parts)
    sum_query, query_parts = rows_sum(query_weight_grad)
    _, grad_part, grad_query_weight = run_programs(
        [
            placed(along_line, 0.01, 0.75),
            placed(over_pair, 0.76, 0.86, 0.97),
            placed(sum_query, 0.0, 1.0),
        ],
        [
            grad_parts,
            lambda more, outs: outs[0].reshape(2, rows_dev, HD),
            query_parts,
        ],
        12,
    )
    input_grad, layer_out, down_wide, up_wide, grad_part_weight, summed = first_back(
        grad_query,
        grad_part,
        first_all,
        hidden_in,
        normed_one,
        vectors,
        grad_middle,
        mlp_out,
        middle,
        vector,
        cut_a,
        cut_b,
        9,
    )
    grad_down_weight, grad_up_weight = down_wide.astype(F32), up_wide.astype(F32)
    grad_keyval_weight = in_order(grad_part_weight[:, :HD], grad_part_weight[:, HD:], axis=1)
    sum_up = summed[:quarters, width : 2 * width - head_width].reshape(quarters * hidden_dev)
    return (
        layer_out,
        input_grad,
        summed[0, :width],
        summed[1, :width],
        grad_query_weight,
        summed[6, :head_width],
        grad_keyval_weight,
        summed[7, :HD],
        grad_proj_weight,
        summed[4, :width],
        summed[2, :width],
        summed[3, :width],
        grad_up_weight,
        sum_up,
        grad_down_weight,
        summed[5, :width],
    )


def solution(mesh):
    fsdp, ctx, tp = mesh.devices.shape
    grid = Mesh(mesh.devices.reshape(fsdp, ctx // 2, 2, tp), EVERY)
    by_rows = P(ROWS, None)
    by_both = P(ROWS, "tp")
    return jax.shard_map(
        body,
        mesh=grid,
        in_specs=(
            by_rows,
            P("fsdp", None),
            P(),
            P(),
            by_both,
            P("tp"),
            by_rows,
            P(),
            by_both,
            P(),
            P(),
            P(),
            by_both,
            P("tp"),
            by_both,
            P(),
            by_rows,
        ),
        out_specs=(
            by_rows,
            by_rows,
            P(),
            P(),
            by_both,
            P("tp"),
            by_rows,
            P(),
            by_both,
            P(),
            P(),
            P(),
            by_both,
            P("tp"),
            by_both,
            P(),
        ),
        check_vma=False,
    )
```

```python
import functools

import jax
import jax.numpy as jnp
from jax import lax
from jax.experimental import pallas as pl
from jax.experimental.pallas import tpu as pltpu
from jax.sharding import Mesh, PartitionSpec as P

HD = 128
BLK = 256
PBLK = 8
CONTS = 8
EPSILON = 1e-05
MASKED = -1e30
F32 = jnp.float32
BF16 = jnp.bfloat16
ROWS = ("fsdp", "line", "pair")
EVERY = ("fsdp", "line", "pair", "tp")


MESH_ID = pl.DeviceIdType.MESH
VMEM_BYTES = 60 * 1024 * 1024
SMALL = pl.CostEstimate(flops=1, bytes_accessed=1, transcendentals=0)
SIDE = ("pair", "fsdp")
FRONT = ("fsdp", "pair")


def here():
    return {name: lax.axis_index(name) for name in EVERY}


def flip(place, step):
    place = dict(place)
    if isinstance(step, str):
        place[step] = 1 - place[step]
    else:
        core = place["tp"]
        for name, used in ((step[0], 1 - core), (step[1], core)):
            place[name] = place[name] + (1 - 2 * place[name]) * used
    return place


def along(place, amount):
    return dict(place, line=place["line"] + amount)


def remote(source, target, send_sem, recv_sem, place):
    return pltpu.make_async_remote_copy(
        src_ref=source,
        dst_ref=target,
        send_sem=send_sem,
        recv_sem=recv_sem,
        device_id=place,
        device_id_type=MESH_ID,
    )


def top_bit(bits):
    return bits.bit_length() - 1


def add_blocks(target, first, second, rows):
    tile = min(rows, 64)

    def one(index, carry):
        cut = pl.ds(pl.multiple_of(index * tile, tile), tile)
        total = first(cut).astype(F32)
        if second is not None:
            total = total + second(cut).astype(F32)
        target[cut, :] = total.astype(target.dtype)
        return carry

    lax.fori_loop(0, rows // tile, one, 0)


def rows_of(ref):
    return lambda cut: ref[cut, :]


class Gather:
    def __init__(self, values, steps, lines, shape, slot):
        self.steps, self.lines, self.slot = steps, lines, slot
        self.out = jax.ShapeDtypeStruct(shape, values.dtype)
        self.in_spec = self.out_spec = pl.BlockSpec(memory_space=pl.ANY)

    def scratch(self):
        parts = 1 << len(self.steps)
        return [
            pltpu.SemaphoreType.DMA(()),
            pltpu.SemaphoreType.DMA((2, self.lines)),
            pltpu.SemaphoreType.DMA((self.lines,)),
            pltpu.SemaphoreType.DMA((self.lines, max(1, len(self.steps)) * parts)),
            pltpu.SemaphoreType.DMA((self.lines, parts)),
        ]

    def stages(self, me, x_ref, out_ref, own_sem, line_send, line_recv, send, recv):
        steps, lines, slot = self.steps, self.lines, self.slot
        count = len(steps)
        my_line = me["line"] if lines > 1 else 0

        def block(bits, shard):
            place = me
            for k in reversed(range(count)):
                if bits >> k & 1:
                    place = flip(place, steps[k])
            return slot(out_ref, dict(place, line=shard))

        def to_step(k, bits, shard, source):
            return remote(
                source,
                block(bits, shard),
                send.at[shard, k * (1 << count) + bits],
                recv.at[shard, bits | 1 << k],
                flip(me, steps[k]),
            )

        def to_line(amount, shard, source):
            return remote(
                source,
                block(0, shard),
                line_send.at[(amount + 1) // 2, shard],
                line_recv.at[shard],
                along(me, amount),
            )

        def send_on(bits, shard, source):
            for k in range(top_bit(bits) + 1, count):
                to_step(k, bits, shard, source).start()

        def at_distance(distance, work):
            if distance == 0:
                work(my_line, 0)
                return
            for amount in (1, -1):
                shard = my_line - amount * distance
                pl.when((shard >= 0) & (shard < lines))(functools.partial(work, shard, amount))

        def line_inside(amount):
            there = my_line + amount
            return (there >= 0) & (there < lines)

        own = pltpu.make_async_copy(x_ref, block(0, my_line), own_sem)

        def begin():
            if lines > 1:
                for amount in (1, -1):
                    pl.when(line_inside(amount))(
                        lambda amount=amount: to_line(amount, my_line, x_ref).start()
                    )
            send_on(0, my_line, x_ref)
            own.start()

        def line_arrival(shard, amount):
            remote(
                block(0, shard), block(0, shard), line_send.at[0, shard], line_recv.at[shard], me
            ).wait_recv()
            pl.when(line_inside(amount))(lambda: to_line(amount, shard, block(0, shard)).start())
            send_on(0, shard, block(0, shard))

        def level_arrival(level, shard, amount):
            for bits in range(1 << level, 2 << level):
                remote(
                    block(bits, shard),
                    block(bits, shard),
                    send.at[shard, 0],
                    recv.at[shard, bits],
                    me,
                ).wait_recv()
                send_on(bits, shard, block(bits, shard))

        def end():
            own.wait()
            if lines > 1:
                for amount in (1, -1):
                    for distance in range(lines):
                        shard = my_line - amount * distance
                        pl.when((shard >= 0) & (shard < lines) & line_inside(amount))(
                            lambda amount=amount, shard=shard: to_line(
                                amount, shard, block(0, shard)
                            ).wait_send()
                        )
            for shard in range(lines):
                for bits in range(1 << count):
                    for k in range(top_bit(bits) + 1, count):
                        to_step(k, bits, shard, block(bits, shard)).wait_send()

        line = [functools.partial(at_distance, number, line_arrival) for number in range(1, lines)]
        levels = [
            functools.partial(at_distance, number - level, functools.partial(level_arrival, level))
            for number in range(lines + count - 1)
            for level in range(count)
            if 0 <= number - level < lines
        ]
        return [begin] + line + levels + [end]


class Sum:
    far_line = True

    def __init__(self, steps, lines, rows, columns, slot, kind=F32):
        self.steps, self.lines, self.rows, self.columns = steps, lines, rows, columns
        self.slot = slot
        self.out = jax.ShapeDtypeStruct((rows, columns), kind)
        self.in_spec = pl.BlockSpec(memory_space=pl.ANY)
        self.out_spec = pl.BlockSpec(memory_space=pltpu.VMEM)

    def scratch(self):
        count, lines = len(self.steps), self.lines
        sizes = [1 << (count - 1 - k) for k in range(count)]
        block = (self.rows, self.columns)
        return (
            [pltpu.VMEM((lines, sizes[0]) + block, BF16)]
            + [pltpu.VMEM((lines, size) + block, BF16) for size in sizes]
            + [pltpu.VMEM((lines,) + (block if lines > 1 else (16, 128)), BF16)]
            + [pltpu.SemaphoreType.DMA((lines, sizes[0]))]
            + [pltpu.SemaphoreType.DMA((lines, size)) for size in sizes] * 2
            + [pltpu.SemaphoreType.DMA((lines,))] * 2
        )

    def stages(self, me, x_ref, out_ref, own, *rest):
        steps, lines, rows, slot = self.steps, self.lines, self.rows, self.slot
        count = len(steps)
        held, rest = rest[:count], rest[count:]
        on_line, own_sem, rest = rest[0], rest[1], rest[2:]
        send, recv = rest[:count], rest[count : 2 * count]
        line_send, line_recv = rest[2 * count :]
        my_line = me["line"] if lines > 1 else 0
        last = count - 1

        def target_of(bits, shard):
            place = me
            for k in range(count):
                if bits >> k & 1:
                    place = flip(place, steps[k])
            return dict(place, line=shard)

        def store(k, shard, bits):
            return held[k].at[shard, bits >> (k + 1)]

        def own_copy(shard, bits):
            return pltpu.make_async_copy(
                slot(x_ref, target_of(bits, shard)),
                own.at[shard, bits >> 1],
                own_sem.at[shard, bits >> 1],
            )

        def copy(k, shard, bits):
            source = slot(x_ref, target_of(bits, shard)) if k == 0 else store(k - 1, shard, bits)
            return remote(
                source,
                store(k, shard, bits ^ (1 << k)),
                send[k].at[shard, bits >> (k + 1)],
                recv[k].at[shard, bits >> (k + 1)],
                flip(me, steps[k]),
            )

        def parts_of(k):
            return [high << (k + 1) for high in reversed(range(1 << (count - 1 - k)))]

        def send_first(shard, amount):
            for bits in parts_of(0):
                copy(0, shard, bits | 1).start()

        def own_first(shard, amount):
            for bits in parts_of(0):
                own_copy(shard, bits).start()

        def take_step(k, shard, amount, parts=None):
            for bits in parts or parts_of(k):
                copy(k, shard, bits | 1 << k).wait_recv()
                arrived = store(k, shard, bits)
                if k == 0:
                    own_copy(shard, bits).wait()
                    mine = own.at[shard, bits >> 1]
                else:
                    mine = store(k - 1, shard, bits)
                add_blocks(arrived, rows_of(mine), rows_of(arrived), rows)
                if k + 1 < count and bits >> (k + 1) & 1:
                    copy(k + 1, shard, bits).start()

        def line_copy(shard):
            return remote(
                held[last].at[shard, 0],
                on_line.at[my_line],
                line_send.at[shard],
                line_recv.at[my_line],
                along(me, shard - my_line),
            )

        def each(distance, work):
            if distance == 0:
                work(my_line, 0)
                return
            for amount in (1, -1):
                shard = my_line + amount * distance
                pl.when((shard >= 0) & (shard < lines))(functools.partial(work, shard, amount))

        order = list(reversed(range(lines)))

        def begin():
            for distance in order:
                each(distance, send_first)
            for distance in order:
                each(distance, own_first)

        def tick(number):
            for k in reversed(range(count)):
                index = number - k
                if 0 <= index < lines:
                    each(order[index], functools.partial(take_step, k))
                    if k == last and order[index] > 0:
                        each(order[index], lambda shard, amount: line_copy(shard).start())

        def end():
            final = held[last].at[my_line, 0]
            if lines == 1:
                add_blocks(out_ref, rows_of(final), None, rows)
            else:
                add_blocks(on_line.at[my_line], rows_of(final), None, rows)

                def arrived(shard, amount):
                    remote(
                        on_line.at[shard], on_line.at[shard], line_send.at[0], line_recv.at[shard], me
                    ).wait_recv()

                for distance in range(1, lines):
                    each(distance, arrived)
                add_blocks(
                    out_ref,
                    lambda cut: sum(on_line[shard, cut, :].astype(F32) for shard in range(lines)),
                    None,
                    rows,
                )
                for distance in range(1, lines):
                    each(distance, lambda shard, amount: line_copy(shard).wait_send())
            for k in range(count):
                for shard in range(lines):
                    for bits in parts_of(k):
                        copy(k, shard, bits | 1 << k).wait_send()

        if lines == 1:
            ticks = [
                functools.partial(take_step, k, 0, 0, [bits]) for k in range(count) for bits in parts_of(k)
            ]
        else:
            ticks = [functools.partial(tick, number) for number in range(lines + count - 1)]
        return [begin] + ticks + [end]


DIRECT = (("pair",), ("fsdp",), ("pair", "fsdp"))


def move(me, names):
    place = me
    for name in names:
        place = flip(place, name)
    return place


def quarter_of(place):
    return place["fsdp"] * 2 + place["pair"]


class Exchange:
    steps, lines = ("pair", "fsdp"), 1

    def __init__(self, moves, shape, kind):
        self.moves = moves
        self.out = jax.ShapeDtypeStruct(shape, kind)
        self.in_spec = self.out_spec = pl.BlockSpec(memory_space=pl.ANY)

    def scratch(self):
        count = len(self.moves)
        return [
            pltpu.SemaphoreType.DMA((count,)),
            pltpu.SemaphoreType.DMA((count, 3)),
            pltpu.SemaphoreType.DMA((count, 3)),
        ]

    def stages(self, me, x_refs, out_ref, own_sem, send, recv):
        copies = []
        for n, (source, target) in enumerate(self.moves):
            there_ref = target(out_ref, quarter_of(me))
            for k, names in reversed(list(enumerate(DIRECT))):
                there = move(me, names)
                copies.append(
                    remote(
                        source(x_refs, quarter_of(there)), there_ref, send.at[n, k], recv.at[n, k], there
                    )
                )
            copies.append(
                pltpu.make_async_copy(source(x_refs, quarter_of(me)), there_ref, own_sem.at[n])
            )

        def begin():
            for one in copies:
                one.start()

        def end():
            for one in copies:
                one.wait()

        return [begin, end]


def half_quarter(ref, quarter, half, rows=None):
    columns = ref.shape[1] // 8
    cut = pl.ds(pl.multiple_of((quarter * 2 + half) * columns, columns), columns)
    return ref.at[:, cut] if rows is None else ref.at[rows, cut]


def spread_halves(pieces, columns, kind):
    moves, start = [], 0
    for index, rows, half in pieces:
        count = rows.stop - rows.start
        moves.append(
            (
                lambda refs, quarter, index=index, rows=rows, half=half: half_quarter(
                    refs[index], quarter, half, rows
                ),
                lambda ref, quarter, start=start, count=count: ref.at[quarter, start : start + count],
            )
        )
        start += count
    return Exchange(moves, (4, start, columns // 8), kind)


def return_half(cut, kind):
    quarters, rows, columns = cut.shape

    def place(ref, quarter):
        return ref.at[:, pl.ds(pl.multiple_of(quarter * columns, columns), columns)]

    return Exchange(
        [(lambda ref, quarter: ref.at[quarter], place)], (rows, quarters * columns), kind
    )


def widen_kernel(a_ref, b_ref, down_ref, up_ref):
    rows, columns = down_ref.shape[0], a_ref.shape[1] // 4
    for start, out_ref in ((0, down_ref), (rows, up_ref)):
        for quarter in range(4):
            for half, ref in enumerate((a_ref, b_ref)):
                at = (quarter * 2 + half) * columns
                cut = slice(quarter * columns, (quarter + 1) * columns)
                out_ref[:, at : at + columns] = ref[start : start + rows, cut].astype(F32)


def widen(half_a, half_b):
    rows, columns = half_a.shape
    shape = jax.ShapeDtypeStruct((rows // 2, 2 * columns), F32)
    return pl.pallas_call(
        widen_kernel,
        out_shape=[shape, shape],
        compiler_params=pltpu.CompilerParams(vmem_limit_bytes=VMEM_BYTES),
        cost_estimate=SMALL,
    )(half_a, half_b)


class Work:
    steps, lines = (), 1

    def __init__(self, work, shape, kind):
        self.work, self.out = work, jax.ShapeDtypeStruct(shape, kind)
        self.in_spec = self.out_spec = pl.BlockSpec(memory_space=pltpu.VMEM)

    def scratch(self):
        return []

    def stages(self, me, x_refs, out_ref):
        return [functools.partial(self.work, me, x_refs, out_ref), lambda: None]


class Direct:
    steps, rows_too = ("tp",), True

    def __init__(self, lines, rows, columns, shared):
        self.lines, self.rows, self.columns, self.shared = lines, rows, columns, shared
        self.out = jax.ShapeDtypeStruct((rows, columns + shared), F32)
        self.in_spec = self.out_spec = pl.BlockSpec(memory_space=pltpu.VMEM)

    def scratch(self):
        lines = self.lines
        return [
            pltpu.VMEM((2, lines, 2, self.rows, self.columns), BF16),
            pltpu.SemaphoreType.DMA((4, 2, lines)),
            pltpu.SemaphoreType.DMA((2, lines, 2)),
            pltpu.SemaphoreType.DMA((2,)),
        ]

    def stages(self, me, x_ref, out_ref, held, send, recv, share_sem):
        def on_others(work):
            for side in range(4):
                for distance in range(self.lines):
                    for way, amount in enumerate((1, -1) if distance else (1,)):
                        if side or distance:
                            place = along(plane_partner(me, side * 2), amount * distance)
                            inside = (place["line"] >= 0) & (place["line"] < self.lines)
                            pl.when(inside)(
                                functools.partial(work, place, send.at[side, way, distance])
                            )

        def copy(place, sem):
            return remote(
                by_rows_slot(x_ref, place),
                by_rows_slot(held, me),
                sem,
                by_rows_slot(recv, me),
                place,
            )

        def arrived(place, sem):
            slot = by_rows_slot(held, place)
            remote(slot, slot, sem, by_rows_slot(recv, place), me).wait_recv()

        def begin():
            on_others(lambda place, sem: copy(place, sem).start())
            held[me["fsdp"], me["line"], me["pair"]] = x_ref[me["fsdp"], me["line"], me["pair"]]

        def end():
            on_others(arrived)
            total = jnp.zeros((self.rows, self.columns), F32)
            for half in range(2):
                for shard in range(self.lines):
                    for side in range(2):
                        total = total + held[half, shard, side].astype(F32)
            out_ref[:, : self.columns] = total
            share = remote(
                out_ref.at[:, : self.columns],
                out_ref.at[:, self.columns :],
                share_sem.at[0],
                share_sem.at[1],
                flip(me, "tp"),
            )
            share.start()
            share.wait()
            on_others(lambda place, sem: copy(place, sem).wait_send())

        return [begin, end]


class Total:
    steps, everyone = (), True

    def __init__(self, shape, lines, special, heads):
        self.lines, self.shape, self.special, self.heads = lines, shape, special, heads
        self.out = jax.ShapeDtypeStruct((shape[0], 2 * shape[1]), F32)
        self.in_spec = self.out_spec = pl.BlockSpec(memory_space=pltpu.VMEM)

    def scratch(self):
        shape, lines = self.shape, self.lines
        return [
            pltpu.VMEM((lines,) + shape, F32),
            pltpu.VMEM((8,) + shape, F32),
            pltpu.SemaphoreType.DMA((2, lines)),
            pltpu.SemaphoreType.DMA((lines,)),
            pltpu.SemaphoreType.DMA((8,)),
            pltpu.SemaphoreType.DMA((8,)),
        ]

    def stages(self, me, x_ref, out_ref, on_line, on_plane, line_send, line_recv, send, recv):
        lines, mine = self.lines, me["line"]
        number = plane_number(me)

        def on_others(work):
            for distance in range(1, lines):
                for way, amount in enumerate((1, -1)):
                    there = mine + amount * distance
                    pl.when((there >= 0) & (there < lines))(
                        functools.partial(work, way, amount, distance, there)
                    )

        def to_line(way, amount, distance):
            return remote(
                on_line.at[mine],
                on_line.at[mine],
                line_send.at[way, distance],
                line_recv.at[mine],
                along(me, amount * distance),
            )

        def to_plane(bits):
            return remote(
                on_plane.at[number],
                on_plane.at[number],
                send.at[bits],
                recv.at[number],
                plane_partner(me, bits),
            )

        def begin():
            on_line[mine] = x_ref[...]
            on_others(lambda way, amount, distance, there: to_line(way, amount, distance).start())

        def arrived(way, amount, distance, there):
            remote(
                on_line.at[there], on_line.at[there], line_send.at[0, 0], line_recv.at[there], me
            ).wait_recv()

        def middle():
            on_others(arrived)
            total = on_line[0]
            for shard in range(1, lines):
                total = total + on_line[shard]
            on_plane[number] = total
            for bits in range(1, 8):
                to_plane(bits).start()

        def end():
            for bits in range(1, 8):
                there = plane_number(plane_partner(me, bits))
                remote(
                    on_plane.at[there], on_plane.at[there], send.at[0], recv.at[there], me
                ).wait_recv()
            total = on_plane[0]
            for other in range(1, 8):
                total = total + on_plane[other]
            width, row, heads = self.shape[1], slice(self.special, self.special + 1), self.heads
            out_ref[...] = jnp.zeros_like(out_ref)
            out_ref[:, :width] = total
            same = [on_plane[quarter * 2 + me["tp"], row, :] for quarter in range(4)]
            out_ref[row, :heads] = sum(part[:, :heads] for part in same)
            for quarter, part in enumerate(same):
                out_ref[quarter : quarter + 1, width : 2 * width - heads] = part[:, heads:]
            for bits in range(1, 8):
                to_plane(bits).wait_send()
            on_others(lambda way, amount, distance, there: to_line(way, amount, distance).wait_send())

        return [begin, middle, end]


def plane_number(place):
    return (place["fsdp"] * 2 + place["pair"]) * 2 + place["tp"]


def plane_partner(me, bits):
    place = me
    for bit, name in ((1, "tp"), (2, "pair"), (4, "fsdp")):
        if bits & bit:
            place = flip(place, name)
    return place


def greet(me, programs, partners=()):
    barrier = pltpu.get_barrier_semaphore()
    plane, reach, lines, corners = set(), 0, 1, False
    for one in programs:
        lines = max(lines, one.lines)
        if one.lines > 1:
            far = hasattr(one, "everyone") or hasattr(one, "far_line")
            reach = max(reach, one.lines - 1 if far else 1)
        if hasattr(one, "everyone"):
            plane |= set(range(1, 8))
        if isinstance(one, Exchange) or hasattr(one, "rows_too"):
            plane |= {2, 4, 6}
        if hasattr(one, "rows_too"):
            reach, corners = one.lines - 1, True
    for step in [step for one in programs for step in one.steps] + list(partners):
        plane |= {"tp": {1}, "pair": {2}, "fsdp": {4}}.get(step, {2, 4})
    for bits in sorted(plane):
        pl.semaphore_signal(
            barrier, inc=1, device_id=plane_partner(me, bits), device_id_type=MESH_ID
        )
    count = len(plane)
    for distance in range(1, reach + 1):
        for amount in (-distance, distance):
            there = me["line"] + amount
            inside = (there >= 0) & (there < lines)

            for bits in (0, 2, 4, 6) if corners else (0,):

                @pl.when(inside)
                def _():
                    pl.semaphore_signal(
                        barrier,
                        inc=1,
                        device_id=along(plane_partner(me, bits), amount),
                        device_id_type=MESH_ID,
                    )

                count = count + inside.astype(jnp.int32)
    pl.semaphore_wait(barrier, count)


def split_scratch(programs, refs):
    parts, start = [], 0
    for one in programs:
        size = len(one.scratch())
        parts.append(refs[start : start + size])
        start += size
    return parts


def schedule(programs, x_refs, out_refs, scratch, partners=()):
    me = here()
    works = [(0.0, functools.partial(greet, me, programs, partners))]
    for one, x_ref, out_ref, held in zip(programs, x_refs, out_refs, split_scratch(programs, scratch)):
        stages = one.stages(me, x_ref, out_ref, *held)
        places = getattr(one, "places", (0.0, 1.0))
        if len(places) == 2:
            places = spaced(places[0], places[1], len(stages))
        last = len(places) - 2
        works += [
            (places[-1] if k == len(stages) - 1 else places[min(k, last)], stage)
            for k, stage in enumerate(stages)
        ]
    return sorted(works, key=lambda work: work[0])


def placed(program, *places):
    program.places = list(places)
    return program


def spaced(start, stop, count):
    return [start + (stop - start) * k / (count - 1) for k in range(count)]


def run_programs(programs, arrays, number, near=(), far=()):
    count = len(programs)
    given = [k for k, array in enumerate(arrays) if not callable(array)]
    others = len(near) + len(far)

    def kernel(*refs):
        (more, refs) = refs[:others], refs[others:]
        plain, out_refs = refs[: len(given)], refs[len(given) : len(given) + count]
        in_refs = [
            array(more, out_refs) if callable(array) else plain[given.index(k)]
            for k, array in enumerate(arrays)
        ]
        for _, work in schedule(programs, in_refs, out_refs, refs[len(given) + count :]):
            work()

    return pl.pallas_call(
        kernel,
        out_shape=[one.out for one in programs],
        in_specs=[pl.BlockSpec(memory_space=pltpu.VMEM)] * len(near)
        + [pl.BlockSpec(memory_space=pl.ANY)] * len(far)
        + [programs[k].in_spec for k in given],
        out_specs=[one.out_spec for one in programs],
        scratch_shapes=[held for one in programs for held in one.scratch()],
        compiler_params=pltpu.CompilerParams(
            collective_id=number, has_side_effects=True, vmem_limit_bytes=VMEM_BYTES
        ),
        cost_estimate=SMALL,
    )(*near, *far, *[arrays[k] for k in given])


def by_rows_slot(ref, at):
    return ref.at[at["fsdp"], at["line"], at["pair"]]


def by_plane_slot(ref, at):
    return ref.at[at["fsdp"], at["pair"], at["tp"]]


def by_ctx_slot(ref, at):
    return ref.at[at["tp"], at["line"], at["pair"]]


def rows_gather(values):
    lines = lax.axis_size("line")
    return Gather(values, (SIDE, FRONT), lines, (2, lines, 2) + values.shape, by_rows_slot)


def line_gather(shape, kind):
    lines = lax.axis_size("line")
    like = jax.ShapeDtypeStruct(shape, kind)
    return Gather(like, (), lines, (lines,) + shape, lambda ref, at: ref.at[at["line"]])


def columns_gather(values):
    lines, rows, columns = values.shape
    return Gather(
        values, (SIDE, FRONT), 1, (2, lines, 2, rows, columns), lambda ref, at: ref.at[at["fsdp"], :, at["pair"]]
    )


def rows_sum(values):
    lines, (total, columns) = lax.axis_size("line"), values.shape
    rows = total // (4 * lines)
    parts = values.astype(BF16).reshape(2, lines, 2, rows, columns)
    return Sum((FRONT, SIDE), lines, rows, columns, by_rows_slot), parts


def plane_gather(values):
    return Gather(values, (SIDE, FRONT, "tp"), 1, (2, 2, 2) + values.shape, by_plane_slot)


def plane_sum(values):
    rows, columns = values.shape[0] // 8, values.shape[1]
    parts = values.astype(BF16).reshape(2, 2, 2, rows, columns)
    return Sum(("tp", FRONT, SIDE), 1, rows, columns, by_plane_slot), parts


def flat(values):
    return values.reshape(-1, values.shape[-1])


def ctx_gather(shape, kind):
    lines = lax.axis_size("line")
    like = jax.ShapeDtypeStruct(shape, kind)
    return Gather(like, ("pair", "tp"), lines, (2, lines, 2) + shape, by_ctx_slot)


def ctx_sums(values):
    _, lines, rows, columns = values.shape
    along_line = Sum(
        ("tp",), lines, rows, columns, lambda ref, at: ref.at[at["tp"], at["line"]], BF16
    )
    over_pair = Sum(("pair",), 1, rows // 2, columns, lambda ref, at: ref.at[at["pair"]])
    return along_line, over_pair


LOG2E = 1.4426950408889634


def visible_bias(bias_ref, position, chunks):
    prompt = position < PBLK
    row = lax.broadcasted_iota(jnp.int32, (BLK, BLK), 0)
    column = lax.broadcasted_iota(jnp.int32, (BLK, BLK), 1)
    limit = jnp.where(prompt, position * BLK + column, PBLK * BLK)
    for chunk in range(chunks - 1):
        bias_ref[chunk] = jnp.where(row + chunk * BLK <= limit, 0.0, MASKED)
    own_limit = jnp.where(prompt, -1, column)
    bias_ref[chunks - 1] = jnp.where(row <= own_limit, 0.0, MASKED)


def rows_by_rows(left, right):
    return lax.dot_general(left, right, (((1,), (1,)), ((), ())), preferred_element_type=F32)


def beside(programs, in_refs, out_refs, scratch, step, steps):
    late = []
    for place, work in schedule(programs, in_refs, out_refs, scratch):
        if place < 1:
            pl.when(step == int(place * steps))(work)
        else:
            late.append((place, work))

    def finish(own=None):
        @pl.when(step == steps - 1)
        def _():
            early = [work for place, work in late if place < 1.05]
            rest = [work for place, work in late if place >= 1.05]
            for work in early + ([own] if own else []) + rest:
                work()

    return finish


def attend_kernel(programs, steps, *refs):
    count = len(programs)
    (position_ref, slot_ref, query_ref, table_ref), refs = refs[:4], refs[4:]
    others, refs = refs[:count], refs[count:]
    (mixed_ref, logsum_ref), refs = refs[:2], refs[2:]
    other_outs, refs = refs[:count], refs[count:]
    (bias_ref, score_ref, value_t_ref), scratch = refs[:3], refs[3:]
    chunks = PBLK + 1
    block = pl.program_id(0)
    factor = HD**-0.5 * LOG2E
    step = pl.program_id(0) * pl.num_programs(1) + pl.program_id(1)
    finish = beside(programs, others, other_outs, scratch, step, steps)

    @pl.when(pl.program_id(1) == 0)
    def _():
        visible_bias(bias_ref, position_ref[block], chunks)
        for chunk in range(chunks):
            value_t_ref[chunk] = table_ref[1, slot_ref[block, chunk]].astype(F32).T.astype(BF16)

    query = query_ref[...]
    largest = None
    for chunk in range(chunks):
        keys = table_ref[0, slot_ref[block, chunk]]
        score = rows_by_rows(keys, query) + bias_ref[chunk]
        score_ref[chunk] = score
        top = jnp.max(score.reshape(BLK // 8, 8, BLK), axis=0)
        largest = top if largest is None else jnp.maximum(largest, top)
    largest = jnp.max(largest, axis=0, keepdims=True)
    total = jnp.zeros((8, BLK), F32)
    mixed = jnp.zeros((HD, BLK), F32)
    for chunk in range(chunks):
        weight = jnp.exp2((score_ref[chunk] - largest) * factor)
        total = total + jnp.sum(weight.reshape(BLK // 8, 8, BLK), axis=0)
        mixed = mixed + jnp.dot(
            value_t_ref[chunk], weight.astype(BF16), preferred_element_type=F32
        )
    total = jnp.sum(total, axis=0, keepdims=True)
    mixed_ref[...] = (mixed / total).T.astype(BF16)
    logsum_ref[0, 0] = largest * factor + jnp.log2(total)
    finish()


def attend(queries, table, positions, key_slots, programs, arrays, number):
    rows, width = queries.shape
    blocks, heads = rows // BLK, width // HD
    count = (PBLK + 1) * BLK
    out = pl.pallas_call(
        functools.partial(attend_kernel, programs, blocks * heads),
        grid=(blocks, heads),
        out_shape=[
            jax.ShapeDtypeStruct((rows, width), BF16),
            jax.ShapeDtypeStruct((blocks, heads, 1, BLK), F32),
        ]
        + [one.out for one in programs],
        in_specs=[
            pl.BlockSpec(memory_space=pltpu.SMEM),
            pl.BlockSpec(memory_space=pltpu.SMEM),
            pl.BlockSpec((BLK, HD), lambda b, h: (b, h)),
            pl.BlockSpec(memory_space=pltpu.VMEM),
        ]
        + [one.in_spec for one in programs],
        out_specs=[
            pl.BlockSpec((BLK, HD), lambda b, h: (b, h)),
            pl.BlockSpec((1, 1, 1, BLK), lambda b, h: (b, h, 0, 0)),
        ]
        + [one.out_spec for one in programs],
        scratch_shapes=[
            pltpu.VMEM((PBLK + 1, BLK, BLK), F32),
            pltpu.VMEM((PBLK + 1, BLK, BLK), F32),
            pltpu.VMEM((PBLK + 1, HD, BLK), BF16),
        ]
        + [held for one in programs for held in one.scratch()],
        compiler_params=pltpu.CompilerParams(
            collective_id=number, has_side_effects=True, vmem_limit_bytes=VMEM_BYTES
        ),
        cost_estimate=SMALL,
    )(positions, key_slots, queries, table, *arrays)
    return out[0], out[1], out[2:]


def attend_back_kernel(programs, steps, *refs):
    count = len(programs)
    (position_ref, slot_ref, query_ref, grad_ref, mixed_ref), refs = refs[:5], refs[5:]
    (logsum_ref, table_ref, normed_ref), refs = refs[:3], refs[3:]
    others, refs = refs[:count], refs[count:]
    (grad_query_ref, set_ref, weight_ref), refs = refs[:3], refs[3:]
    other_outs, refs = refs[:count], refs[count:]
    (bias_ref, key_t_ref, kept_ref), scratch = refs[:3], refs[3:]
    chunks = PBLK + 1
    scale = HD**-0.5
    block, head = pl.program_id(0), pl.program_id(1)
    step = pl.program_id(0) * pl.num_programs(1) + pl.program_id(1)
    finish = beside(programs, others, other_outs, scratch, step, steps)

    @pl.when(head == 0)
    def _():
        visible_bias(bias_ref, position_ref[block], chunks)
        set_ref[...] = jnp.zeros_like(set_ref)
        for chunk in range(chunks):
            key_t_ref[chunk] = table_ref[0, slot_ref[block, chunk]].astype(F32).T.astype(BF16)

    query, grad = query_ref[...], grad_ref[...]
    inner = jnp.sum(grad.astype(F32) * mixed_ref[...].astype(F32), axis=1, keepdims=True)
    inner = jnp.broadcast_to(inner, (BLK, HD)).T[:1, :]
    logsum = logsum_ref[0, 0]
    grad_query = jnp.zeros((HD, BLK), F32)
    for chunk in range(chunks):
        cut = slice(chunk * BLK, (chunk + 1) * BLK)
        slot = slot_ref[block, chunk]
        score = rows_by_rows(table_ref[0, slot], query)
        weight = jnp.exp2(score * (scale * LOG2E) + bias_ref[chunk] - logsum)
        grad_weight = rows_by_rows(table_ref[1, slot], grad)
        grad_score = (weight * (grad_weight - inner)).astype(BF16)
        set_ref[0, cut, :HD] += jnp.dot(grad_score, query, preferred_element_type=F32)
        set_ref[0, cut, HD:] += jnp.dot(weight.astype(BF16), grad, preferred_element_type=F32)
        grad_query = grad_query + jnp.dot(
            key_t_ref[chunk], grad_score, preferred_element_type=F32
        )
    grad_query = (grad_query * scale).T.astype(BF16)
    grad_query_ref[...] = grad_query
    kept_ref[block, head] = grad_query

    @pl.when(head == pl.num_programs(1) - 1)
    def _():
        set_ref[0, :, :HD] = set_ref[0, :, :HD] * scale

    def weights():
        blocks, heads = kept_ref.shape[:2]
        kept = [
            jnp.concatenate([kept_ref[b, h] for h in range(heads)], axis=1) for b in range(blocks)
        ]
        kept = jnp.concatenate(kept, axis=0)

        def work(cut):
            weight_ref[cut, :] = by_columns(normed_ref[:, cut], kept).astype(BF16)

        each_columns(weight_ref.shape[0], 256, work)

    finish(weights)


def attend_back(
    queries, grads, mixed, logsums, table, normed, positions, key_slots, programs, arrays, number
):
    rows, width = queries.shape
    blocks, heads = rows // BLK, width // HD
    count = (PBLK + 1) * BLK
    by_head = pl.BlockSpec((BLK, HD), lambda b, h: (b, h))
    out = pl.pallas_call(
        functools.partial(attend_back_kernel, programs, blocks * heads),
        grid=(blocks, heads),
        out_shape=[
            jax.ShapeDtypeStruct((rows, width), BF16),
            jax.ShapeDtypeStruct((blocks, count, 2 * HD), F32),
            jax.ShapeDtypeStruct((normed.shape[1], width), BF16),
        ]
        + [one.out for one in programs],
        in_specs=[
            pl.BlockSpec(memory_space=pltpu.SMEM),
            pl.BlockSpec(memory_space=pltpu.SMEM),
            by_head,
            by_head,
            by_head,
            pl.BlockSpec((1, 1, 1, BLK), lambda b, h: (b, h, 0, 0)),
            pl.BlockSpec(memory_space=pltpu.VMEM),
            pl.BlockSpec(memory_space=pltpu.VMEM),
        ]
        + [one.in_spec for one in programs],
        out_specs=[
            by_head,
            pl.BlockSpec((1, count, 2 * HD), lambda b, h: (b, 0, 0)),
            pl.BlockSpec(memory_space=pltpu.VMEM),
        ]
        + [one.out_spec for one in programs],
        scratch_shapes=[
            pltpu.VMEM((PBLK + 1, BLK, BLK), F32),
            pltpu.VMEM((PBLK + 1, HD, BLK), BF16),
            pltpu.VMEM((blocks, heads, BLK, HD), BF16),
        ]
        + [held for one in programs for held in one.scratch()],
        compiler_params=pltpu.CompilerParams(
            collective_id=number, has_side_effects=True, vmem_limit_bytes=VMEM_BYTES
        ),
        cost_estimate=SMALL,
    )(positions, key_slots, queries, grads, mixed, logsums, table, normed, *arrays)
    return out[0], out[1], out[2], out[3:]


def by_slot_kernel(slot_ref, set_ref, out_ref, table_ref):
    blocks, chunks = slot_ref.shape

    def clear(index, carry):
        table_ref[index] = jnp.zeros(table_ref.shape[1:], F32)
        return carry

    def give(index, carry):
        out_ref[0, index] = table_ref[index, :, :HD].astype(BF16)
        out_ref[1, index] = table_ref[index, :, HD:].astype(BF16)
        return carry

    lax.fori_loop(0, table_ref.shape[0], clear, 0)
    for block in range(blocks):
        for chunk in range(chunks):
            cut = slice(chunk * BLK, (chunk + 1) * BLK)
            table_ref[slot_ref[block, chunk]] += set_ref[block, cut, :]
    lax.fori_loop(0, table_ref.shape[0], give, 0)


def by_slot(sets, key_slots, slot_count):
    return pl.pallas_call(
        by_slot_kernel,
        out_shape=jax.ShapeDtypeStruct((2, slot_count, BLK, HD), BF16),
        in_specs=[
            pl.BlockSpec(memory_space=pltpu.SMEM),
            pl.BlockSpec(memory_space=pltpu.VMEM),
        ],
        out_specs=pl.BlockSpec(memory_space=pltpu.VMEM),
        scratch_shapes=[pltpu.VMEM((slot_count, BLK, 2 * HD), F32)],
        compiler_params=pltpu.CompilerParams(vmem_limit_bytes=VMEM_BYTES),
        cost_estimate=SMALL,
    )(key_slots, sets)


GELU_OUTER = 0.7978845608028654
GELU_INNER = 0.044715


def weight_copies(parts, target, sems):
    copies, start = [], 0
    for number, (ref, rows) in enumerate(parts):
        count = rows.stop - rows.start
        copies.append(
            pltpu.make_async_copy(
                ref.at[:, :, rows], target.at[:, :, start : start + count], sems.at[number]
            )
        )
        start += count
    return copies


def first_half(rows, refs):
    piece, other, early = refs[:3]
    first = piece.shape[2]
    return [(piece, slice(0, first)), (other, slice(0, rows - first))], [(early, slice(0, rows))]


def second_half(rows, refs):
    early, late = refs[2:]
    there = early.shape[2] - rows
    down = [(early, slice(rows, rows + there)), (late, slice(0, rows - there))]
    return down, [(late, slice(rows - there, 2 * rows - there))]


def gelu_both(value, grad_act):
    square = value * value
    bend = jnp.tanh(GELU_OUTER * value * (1.0 + GELU_INNER * square))
    slope = 0.5 * (1.0 + bend) + 0.5 * GELU_OUTER * value * (1.0 - bend * bend) * (
        1.0 + 3.0 * GELU_INNER * square
    )
    return 0.5 * value * (1.0 + bend), grad_act * slope


def forward_kernel(
    x_ref,
    cotangent_ref,
    piece_ref,
    other_ref,
    early_ref,
    shift_ref,
    all_ref,
    act_ref,
    pre_ref,
    part_ref,
    bias_ref,
    weight_grad_ref,
    up_own,
    down_own,
    grads_own,
    rows_own,
    cotangent_own,
    act_own,
    pre_own,
    part_own,
    weight_sem,
    load_sem,
    store_sem,
    own_sem,
    send,
    recv,
):
    me = here()
    steps = (SIDE, FRONT, "tp")
    half, width = x_ref.shape
    hidden = early_ref.shape[3]

    def place(bits):
        at = me
        for k in (2, 1, 0):
            if bits >> k & 1:
                at = flip(at, steps[k])
        return at

    def block(bits):
        return by_plane_slot(all_ref, place(bits))

    def to_step(k, bits):
        source = block(bits) if bits else x_ref
        return remote(
            source, block(bits), send.at[k, bits], recv.at[bits | 1 << k], flip(me, steps[k])
        )

    def arrived(bits):
        remote(block(bits), block(bits), send.at[0, 0], recv.at[bits], me).wait_recv()

    def loads(number):
        slot, copies = number % 2, []
        for side, bits in enumerate((number, number + 4)):
            rows = pl.ds(side * half, half)
            copies.append(
                pltpu.make_async_copy(
                    by_plane_slot(cotangent_ref, place(bits)),
                    cotangent_own.at[slot, rows],
                    load_sem.at[slot, 0, side],
                )
            )
            copies.append(
                pltpu.make_async_copy(
                    block(bits) if bits else x_ref,
                    rows_own.at[slot, rows],
                    load_sem.at[slot, 1, side],
                )
            )
        return copies

    def stores(number, kind):
        slot = number % 2
        source, target = ((act_own, act_ref), (pre_own, pre_ref), (part_own, part_ref))[kind]
        return [
            pltpu.make_async_copy(
                source.at[slot, pl.ds(side * half, half)],
                by_plane_slot(target, place(bits)),
                store_sem.at[slot, kind, side],
            )
            for side, bits in enumerate((number, number + 4))
        ]

    def products(number):
        slot = number % 2
        tile = 256

        def one(index, carry):
            cut = pl.ds(pl.multiple_of(index * tile, tile), tile)
            down = down_own[:, :, :, cut].reshape(width, tile)
            up = up_own[:, :, :, cut].reshape(width, tile)
            grad_act = jnp.dot(cotangent_own[slot], down, preferred_element_type=F32)
            value = jnp.dot(rows_own[slot], up, preferred_element_type=F32)
            value = value + shift_ref[:, cut]
            act, grad_pre = gelu_both(value, grad_act)
            act_own[slot, :, cut] = act.astype(BF16)
            grad_pre = grad_pre.astype(BF16)
            pre_own[slot, :, cut] = grad_pre
            bias_ref[:, cut] += jnp.sum(
                grad_pre.astype(F32).reshape(2 * half // 8, 8, tile), axis=0
            )
            return carry

        lax.fori_loop(0, hidden // tile, one, 0, unroll=True)

    def back(number):
        slot = number % 2
        tile = up_own.shape[1] * up_own.shape[2]

        def one(index, carry):
            cut = pl.ds(pl.multiple_of(index * tile, tile), tile)
            up = up_own[index].reshape(tile, hidden)
            part_own[slot, :, cut] = rows_by_rows(pre_own[slot], up).astype(BF16)
            return carry

        lax.fori_loop(0, width // tile, one, 0, unroll=2)

    def grads(number):
        tile = 256
        shard_rows = weight_grad_ref.shape[2]
        rows = 4 * half

        def one(index, carry):
            cut = pl.ds(pl.multiple_of(index * tile, tile), tile)
            for kind, (left, right) in enumerate(((cotangent_own, act_own), (rows_own, pre_own))):
                grad = by_columns(
                    left[:, :, cut].reshape(rows, tile), right[...].reshape(rows, hidden)
                )
                if number == 1:
                    grads_own[kind, cut, :] = grad
                else:
                    count = tile // shard_rows
                    shards = pl.ds(pl.multiple_of(index * count, count), count)
                    grad = (grads_own[kind, cut, :] + grad).astype(BF16)
                    weight_grad_ref[shards, kind] = grad.reshape(count, shard_rows, hidden)
            return carry

        lax.fori_loop(0, width // tile, one, 0, unroll=2)

    def pass_on(bits, *ways):
        arrived(bits)
        for k in ways:
            to_step(k, bits).start()

    def second():
        to_step(0, 0).wait_send()
        to_step(1, 0).start()

    def third():
        to_step(1, 0).wait_send()
        to_step(1, 1).start()
        pass_on(2, 2)

    between = [second, third, functools.partial(pass_on, 3, 2), lambda: None]
    barrier = pltpu.get_barrier_semaphore()
    for step in steps:
        pl.semaphore_signal(barrier, inc=1, device_id=flip(me, step), device_id_type=MESH_ID)
    pl.semaphore_wait(barrier, 3)
    to_step(0, 0).start()
    to_step(2, 0).start()
    own = pltpu.make_async_copy(x_ref, block(0), own_sem)
    own.start()
    down_parts, up_parts = first_half(up_own.shape[2], (piece_ref, other_ref, early_ref))
    weights = weight_copies(down_parts, down_own, weight_sem)
    weights += weight_copies(up_parts, up_own, weight_sem.at[2:])
    for one in weights:
        one.start()
    bias_ref[...] = jnp.zeros_like(bias_ref)
    for number in range(4):
        if number == 1:
            pass_on(1, 2)
        arrived(4 + number)
        copies = loads(number)
        for one in copies:
            one.start()
        if number == 0:
            for one in weights:
                one.wait()
        if number >= 2:
            for kind in range(3):
                for one in stores(number - 2, kind):
                    one.wait()
        for one in copies:
            one.wait()
        products(number)
        between[number]()
        for kind in range(2):
            for one in stores(number, kind):
                one.start()
        back(number)
        for one in stores(number, 2):
            one.start()
        if number % 2:
            grads(number)
    for number in (2, 3):
        for kind in range(3):
            for one in stores(number, kind):
                one.wait()
    own.wait()
    for k, bits in ((2, 0), (1, 1), (2, 1), (2, 2), (2, 3)):
        to_step(k, bits).wait_send()


def forward_products(rows, cotangent_all, piece, other, early, shift, number):
    half, width = rows.shape
    lines, quarters, _, hidden = early.shape
    weights = (lines, quarters, width // (lines * quarters), hidden)
    anywhere = pl.BlockSpec(memory_space=pl.ANY)
    inside = pl.BlockSpec(memory_space=pltpu.VMEM)
    lead = (2, 2, 2, half)
    return pl.pallas_call(
        forward_kernel,
        out_shape=[
            jax.ShapeDtypeStruct(lead + (width,), BF16),
            jax.ShapeDtypeStruct(lead + (hidden,), BF16),
            jax.ShapeDtypeStruct(lead + (hidden,), BF16),
            jax.ShapeDtypeStruct(lead + (width,), BF16),
            jax.ShapeDtypeStruct((8, hidden), F32),
            jax.ShapeDtypeStruct((lines * quarters, 2, weights[2], hidden), BF16),
        ],
        in_specs=[anywhere] * 5 + [inside],
        out_specs=[anywhere] * 4 + [inside] * 2,
        scratch_shapes=[
            pltpu.VMEM(weights, BF16),
            pltpu.VMEM(weights, BF16),
            pltpu.VMEM((2, width, hidden), F32),
            pltpu.VMEM((2, 2 * half, width), BF16),
            pltpu.VMEM((2, 2 * half, width), BF16),
            pltpu.VMEM((2, 2 * half, hidden), BF16),
            pltpu.VMEM((2, 2 * half, hidden), BF16),
            pltpu.VMEM((2, 2 * half, width), BF16),
            pltpu.SemaphoreType.DMA((3,)),
            pltpu.SemaphoreType.DMA((2, 2, 2)),
            pltpu.SemaphoreType.DMA((2, 3, 2)),
            pltpu.SemaphoreType.DMA(()),
            pltpu.SemaphoreType.DMA((3, 4)),
            pltpu.SemaphoreType.DMA((8,)),
        ],
        compiler_params=pltpu.CompilerParams(
            collective_id=number, has_side_effects=True, vmem_limit_bytes=VMEM_BYTES
        ),
        cost_estimate=SMALL,
    )(rows, cotangent_all, piece, other, early, shift)


CHIPS = ((1, 1), (1, 0), (0, 1), (0, 0))


def second_kernel(
    rows_ref,
    cotangent_ref,
    before_ref,
    rows_columns_ref,
    cotangent_columns_ref,
    act_a_ref,
    piece_ref,
    other_ref,
    early_ref,
    late_ref,
    shift_ref,
    down_part_ref,
    weight_grad_ref,
    bias_ref,
    sum_ref,
    up_own,
    downs,
    acts,
    pre_own,
    rows_own,
    cotangent_own,
    before_own,
    part_own,
    over_core,
    over_front,
    over_side,
    weight_sem,
    load_sem,
    core_send,
    core_recv,
    front_send,
    front_recv,
    side_sem,
):
    step = pl.program_id(0)
    me = here()
    core = me["tp"]
    width, hidden = rows_ref.shape[1], pre_own.shape[1]
    count = rows_ref.shape[0] // 4
    half = count // 2
    tile = 256
    places = (piece_ref, other_ref, early_ref, late_ref)
    shard_rows = up_own.shape[2]

    def chip(number):
        up, side = CHIPS[number]
        fsdp = me["fsdp"] + up * (1 - 2 * me["fsdp"])
        return fsdp, me["pair"] + side * (1 - 2 * me["pair"])

    def rows_of_chip(number):
        fsdp, pair = chip(number)
        return pl.ds(pl.multiple_of((fsdp * 2 + pair) * count, count), count)

    def loads(number):
        slot, rows = number % 2, rows_of_chip(number)
        pairs = ((rows_ref, rows_own), (cotangent_ref, cotangent_own), (before_ref, before_own))
        return [
            pltpu.make_async_copy(source.at[rows], target.at[slot], load_sem.at[slot, kind])
            for kind, (source, target) in enumerate(pairs)
        ]

    def second_weights():
        down_parts, up_parts = second_half(shard_rows, places)
        copies = weight_copies(down_parts, downs.at[1], weight_sem.at[0])
        return copies + weight_copies(up_parts, up_own, weight_sem.at[1])

    def first_weights():
        copies = weight_copies(first_half(shard_rows, places)[0], downs.at[0], weight_sem.at[2])
        return copies + [pltpu.make_async_copy(act_a_ref, acts.at[0], weight_sem.at[1, 1])]

    def to_core(number):
        fsdp, pair = chip(number)
        up, side = CHIPS[number]
        return remote(
            part_own.at[fsdp, pair, 1 - core],
            over_core.at[up, side],
            core_send.at[up, side],
            core_recv.at[up, side],
            flip(me, "tp"),
        )

    def take_core(number):
        fsdp, pair = chip(number)
        to_core(number).wait_recv()
        held = over_core.at[CHIPS[number]]
        add_blocks(held, rows_of(part_own.at[fsdp, pair, core]), rows_of(held), half)

    def to_front(corner):
        source = over_core.at[1, 1] if corner else over_core.at[1 - core, core]
        return remote(
            source, over_front.at[corner], front_send.at[corner], front_recv.at[corner], flip(me, FRONT)
        )

    def to_side():
        return remote(over_front.at[1], over_side, side_sem.at[0], side_sem.at[1], flip(me, SIDE))

    def take_front(corner):
        to_front(corner).wait_recv()
        held = over_front.at[corner]
        mine = over_core.at[core, 1 - core] if corner else over_core.at[0, 0]
        add_blocks(held, rows_of(mine), rows_of(held), half)

    def products(number):
        slot, rows = number % 2, rows_of_chip(number)

        def one(index, carry):
            cut = pl.ds(pl.multiple_of(index * tile, tile), tile)
            down = downs[1, :, :, :, cut].reshape(width, tile)
            up = up_own[:, :, :, cut].reshape(width, tile)
            grad_act = jnp.dot(cotangent_own[slot], down, preferred_element_type=F32)
            value = jnp.dot(rows_own[slot], up, preferred_element_type=F32) + shift_ref[:, cut]
            act, grad_pre = gelu_both(value, grad_act)
            acts[1, rows, cut] = act.astype(BF16)
            grad_pre = grad_pre.astype(BF16)
            pre_own[rows, cut] = grad_pre
            bias_ref[:, cut] += fold_rows(grad_pre.astype(F32))
            return carry

        lax.fori_loop(0, hidden // tile, one, 0, unroll=True)
        tile_back = up_own.shape[1] * shard_rows
        fsdp, pair = chip(number)

        def back(index, carry):
            cut = pl.ds(pl.multiple_of(index * tile_back, tile_back), tile_back)
            up = up_own[index].reshape(tile_back, hidden)
            part = before_own[slot, :, cut].astype(F32) + rows_by_rows(pre_own[rows, :], up)
            part_own[fsdp, pair, :, :, cut] = part.astype(BF16).reshape(2, half, tile_back)
            return carry

        lax.fori_loop(0, width // tile_back, back, 0, unroll=2)

    def chunk_step(number):
        if number == 0:
            barrier = pltpu.get_barrier_semaphore()
            for bits in (1, 2, 4):
                pl.semaphore_signal(
                    barrier, inc=1, device_id=plane_partner(me, bits), device_id_type=MESH_ID
                )
            for one in loads(0) + second_weights() + first_weights():
                one.start()
            bias_ref[...] = jnp.zeros_like(bias_ref)
            for one in second_weights():
                one.wait()
            pl.semaphore_wait(barrier, 3)
        for one in loads(number):
            one.wait()
        if number < 3:
            for one in loads(number + 1):
                one.start()
        products(number)
        to_core(number).start()
        if number > 0:
            take_core(number - 1)
        if number == 1:
            to_front(1).start()
        if number == 2:
            pl.when(core == 0)(lambda: to_front(0).start())
        if number == 3:
            pl.when(core == 1)(lambda: to_front(0).start())
            for one in first_weights():
                one.wait()

    for number in range(4):
        pl.when(step == number)(functools.partial(chunk_step, number))

    @pl.when(step == 4)
    def _():
        take_core(3)

    @pl.when(step == 5)
    def _():
        take_front(1)
        to_side().start()

    @pl.when(step == 9)
    def _():
        take_front(0)

    @pl.when(step >= 4)
    def _():
        rows_here = down_part_ref.shape[0]
        rows = pl.ds(pl.multiple_of((step - 4) * rows_here, rows_here), rows_here)
        shards = weight_grad_ref.shape[0]
        for kind, (left, right) in enumerate(
            ((cotangent_columns_ref, acts.at[1]), (rows_columns_ref, pre_own))
        ):
            grad = by_columns(left[...], right[...]).astype(BF16)
            weight_grad_ref[:, kind] = grad.reshape(shards, shard_rows, hidden)
        part = rows_by_rows(acts[0, rows, :], downs[0].reshape(width, hidden))
        part = part + rows_by_rows(acts[1, rows, :], downs[1].reshape(width, hidden))
        down_part_ref[...] = part.astype(BF16)

    @pl.when(step == pl.num_programs(0) - 1)
    def _():
        to_side().wait_recv()
        final = over_front.at[0]
        add_blocks(sum_ref, rows_of(final), rows_of(over_side), half)
        for number in range(4):
            to_core(number).wait_send()
        for corner in range(2):
            to_front(corner).wait_send()
        to_side().wait_send()


def second_products(rows_all, cotangent_all, before, act_a, pieces, shift, number):
    rows, width = rows_all.shape
    lines, quarters, _, hidden = pieces[-1].shape
    shards, shard_rows = lines * quarters, width // (lines * quarters)
    weights = (lines, quarters, shard_rows, hidden)
    steps, tiles, half = 12, 8, rows // 8

    def tile(i):
        return jnp.maximum(i - 4, 0)

    columns = pl.BlockSpec((rows, width // tiles), lambda i: (0, tile(i)))
    anywhere = pl.BlockSpec(memory_space=pl.ANY)
    fixed = lambda shape: pl.BlockSpec(shape, lambda i: (0,) * len(shape))
    return pl.pallas_call(
        second_kernel,
        grid=(steps,),
        out_shape=[
            jax.ShapeDtypeStruct((rows, width), BF16),
            jax.ShapeDtypeStruct((shards, 2, shard_rows, hidden), BF16),
            jax.ShapeDtypeStruct((8, hidden), F32),
            jax.ShapeDtypeStruct((half, width), F32),
        ],
        in_specs=[anywhere] * 3 + [columns] * 2 + [anywhere] * 5 + [fixed((1, hidden))],
        out_specs=[
            pl.BlockSpec((rows // tiles, width), lambda i: (tile(i), 0)),
            pl.BlockSpec((shards // tiles, 2, shard_rows, hidden), lambda i: (tile(i), 0, 0, 0)),
            fixed((8, hidden)),
            fixed((half, width)),
        ],
        scratch_shapes=[
            pltpu.VMEM(weights, BF16),
            pltpu.VMEM((2,) + weights, BF16),
            pltpu.VMEM((2, rows, hidden), BF16),
            pltpu.VMEM((rows, hidden), BF16),
            pltpu.VMEM((2, 2 * half, width), BF16),
            pltpu.VMEM((2, 2 * half, width), BF16),
            pltpu.VMEM((2, 2 * half, width), BF16),
            pltpu.VMEM((2, 2, 2, half, width), BF16),
            pltpu.VMEM((2, 2, half, width), BF16),
            pltpu.VMEM((2, half, width), BF16),
            pltpu.VMEM((half, width), BF16),
            pltpu.SemaphoreType.DMA((3, 2)),
            pltpu.SemaphoreType.DMA((2, 3)),
            pltpu.SemaphoreType.DMA((2, 2)),
            pltpu.SemaphoreType.DMA((2, 2)),
            pltpu.SemaphoreType.DMA((2,)),
            pltpu.SemaphoreType.DMA((2,)),
            pltpu.SemaphoreType.DMA((2,)),
        ],
        compiler_params=kernel_params(number),
        cost_estimate=SMALL,
    )(rows_all, cotangent_all, before, rows_all, cotangent_all, act_a, *pieces, shift)


def by_columns(left, right):
    return lax.dot_general(left, right, (((0,), (0,)), ((), ())), preferred_element_type=F32)


def reorder_kernel(cuts, size, x_ref, out_ref):
    for index, cut in enumerate(cuts):
        out_ref[:, index * size : (index + 1) * size] = x_ref[:, cut : cut + size]


def reorder(values, cuts):
    size = values.shape[1] // len(cuts)
    if size % 128:
        return jnp.concatenate([values[:, cut : cut + size] for cut in cuts], axis=1)
    return pl.pallas_call(
        functools.partial(reorder_kernel, cuts, size),
        out_shape=jax.ShapeDtypeStruct(values.shape, values.dtype),
        compiler_params=pltpu.CompilerParams(vmem_limit_bytes=VMEM_BYTES),
        cost_estimate=SMALL,
    )(values)


def to_line_order(values):
    lines = lax.axis_size("line")
    size = values.shape[1] // (2 * lines)
    return reorder(
        values, [(half * lines + shard) * size for shard in range(lines) for half in range(2)]
    )


def from_line_order(values):
    lines = lax.axis_size("line")
    size = values.shape[1] // (2 * lines)
    return reorder(
        values, [(shard * 2 + half) * size for half in range(2) for shard in range(lines)]
    )


def meet_sibling(me):
    barrier = pltpu.get_barrier_semaphore()
    pl.semaphore_signal(barrier, inc=1, device_id=flip(me, "tp"), device_id_type=MESH_ID)
    pl.semaphore_wait(barrier, 1)


def half_rows_of(core, rows):
    return pl.ds(pl.multiple_of(core * rows, rows), rows)


def each_rows(total, tile, work):
    def one(index, carry):
        work(pl.ds(pl.multiple_of(index * tile, tile), tile))
        return carry

    lax.fori_loop(0, total // tile, one, 0)


def each_columns(total, tile, work):
    each_rows(total, tile, work)


def moments(values):
    centered = values - jnp.mean(values, axis=1, keepdims=True)
    spread = jnp.mean(centered * centered, axis=1, keepdims=True)
    return centered, lax.rsqrt(spread + EPSILON)


def norm_back(values, gain, grad):
    centered, rstd = moments(values)
    xhat = centered * rstd
    scaled = grad * gain
    inner = jnp.mean(scaled * xhat, axis=1, keepdims=True)
    return xhat, rstd * (scaled - jnp.mean(scaled, axis=1, keepdims=True) - xhat * inner)


def fold_rows(values):
    return jnp.sum(values.reshape(values.shape[0] // 8, 8, values.shape[1]), axis=0)


def shuffled(cuts, ref, rows):
    if cuts is None:
        return ref[rows, :]
    size = ref.shape[1] // len(cuts)
    return jnp.concatenate([ref[rows, cut : cut + size] for cut in cuts], axis=1)


def norm_work(me, refs, out_ref):
    stream_ref, vectors_ref = refs
    gain, shift = vectors_ref[0:1, :], vectors_ref[1:2, :]

    def work(rows):
        centered, rstd = moments(stream_ref[rows, :].astype(F32))
        out_ref[rows, :] = (centered * rstd * gain + shift).astype(BF16)

    each_rows(out_ref.shape[0], 32, work)


def reorder_work(cuts, me, x_ref, out_ref):
    half, size = out_ref.shape[0], out_ref.shape[1] // len(cuts)
    few = 64

    def work(rows):
        start = pl.multiple_of(me["tp"] * half + rows.start, few)
        for index, cut in enumerate(cuts):
            out_ref[rows, index * size : (index + 1) * size] = x_ref[
                pl.ds(start, few), cut : cut + size
            ]

    each_rows(half, few, work)


def part_work(me, refs, out_ref):
    normed_ref, weight_ref, shift_ref = refs
    heads = weight_ref.shape[1] - out_ref.shape[1]
    part = jnp.dot(normed_ref[...], weight_ref[:, heads:], preferred_element_type=F32)
    out_ref[...] = (part + shift_ref[:, heads:]).astype(BF16)


def query_work(me, refs, out_ref):
    normed_ref, weight_ref, shift_ref = refs

    def work(cut):
        query = jnp.dot(normed_ref[...], weight_ref[:, cut], preferred_element_type=F32)
        out_ref[:, cut] = (query + shift_ref[:, cut]).astype(BF16)

    each_columns(out_ref.shape[1], 256, work)


def project_kernel(
    cuts,
    mixed_ref,
    proj_a_ref,
    proj_b_ref,
    stream_ref,
    vectors_ref,
    middle_ref,
    normed_ref,
    sent_ref,
    got_ref,
    sems,
):
    me = here()
    half, width = middle_ref.shape
    mine, other = half_rows_of(me["tp"], half), half_rows_of(1 - me["tp"], half)
    tile = 512
    meet_sibling(me)
    copy = remote(sent_ref, got_ref, sems.at[0], sems.at[1], flip(me, "tp"))

    def part(rows, target):
        def work(cut):
            heads = proj_a_ref.shape[1]
            part = rows_by_rows(mixed_ref[rows, :heads], proj_a_ref[cut, :])
            target[:, cut] = part + rows_by_rows(mixed_ref[rows, heads:], proj_b_ref[cut, :])

        each_columns(width, tile, work)

    part(other, sent_ref)
    copy.start()
    part(mine, middle_ref)
    copy.wait_recv()
    bias, gain, shift = vectors_ref[2:3, :], vectors_ref[3:4, :], vectors_ref[4:5, :]
    few = 32

    def finish(rows):
        start = pl.multiple_of(me["tp"] * half + rows.start, few)
        stream = stream_ref[pl.ds(start, few), :].astype(F32)
        middle = stream + (middle_ref[rows, :] + got_ref[rows, :] + bias)
        middle_ref[rows, :] = middle
        centered, rstd = moments(middle)
        normed = (centered * rstd * gain + shift).astype(BF16)
        if cuts is None:
            normed_ref[rows, :] = normed
            return
        size = width // len(cuts)
        for index, cut in enumerate(cuts):
            normed_ref[rows, index * size : (index + 1) * size] = normed[:, cut : cut + size]

    each_rows(half, few, finish)
    copy.wait_send()


def in_vmem(count):
    return [pl.BlockSpec(memory_space=pltpu.VMEM)] * count


def kernel_params(number):
    return pltpu.CompilerParams(
        collective_id=number, has_side_effects=True, vmem_limit_bytes=VMEM_BYTES
    )


def line_cuts(width, back):
    lines = lax.axis_size("line")
    size = width // (2 * lines)
    if size % 128:
        return None
    if back:
        return [(shard * 2 + half) * size for half in range(2) for shard in range(lines)]
    return [(half * lines + shard) * size for shard in range(lines) for half in range(2)]


def project(mixed, proj_a, proj_b, stream, vectors, number):
    rows, width = stream.shape
    half = rows // 2
    cuts = line_cuts(width, False)
    middle, normed = pl.pallas_call(
        functools.partial(project_kernel, cuts),
        out_shape=[
            jax.ShapeDtypeStruct((half, width), F32),
            jax.ShapeDtypeStruct((half, width), BF16),
        ],
        in_specs=in_vmem(5),
        out_specs=in_vmem(2),
        scratch_shapes=[
            pltpu.VMEM((half, width), F32),
            pltpu.VMEM((half, width), F32),
            pltpu.SemaphoreType.DMA((2,)),
        ],
        compiler_params=kernel_params(number),
        cost_estimate=SMALL,
    )(mixed, proj_a, proj_b, stream, vectors)
    return middle, normed if cuts else to_line_order(normed)


def middle_back_kernel(
    cuts,
    sum_ref,
    middle_ref,
    cotangent_ref,
    mixed_ref,
    proj_a_ref,
    proj_b_ref,
    vectors_ref,
    hidden_a_ref,
    hidden_b_ref,
    grad_middle_ref,
    grad_mixed_ref,
    proj_grad_ref,
    vector_ref,
    attn_ref,
    sums_own,
    sems,
):
    me = here()
    half, width = middle_ref.shape
    mine, other = half_rows_of(me["tp"], half), half_rows_of(1 - me["tp"], half)
    few = 32
    gain = vectors_ref[3:4, :]
    meet_sibling(me)
    sums_own[...] = jnp.zeros_like(sums_own)

    def norm(rows):
        start = pl.multiple_of(me["tp"] * half + rows.start, few)
        cotangent = cotangent_ref[pl.ds(start, few), :].astype(F32)
        grad = shuffled(cuts, sum_ref, rows)
        xhat, back = norm_back(middle_ref[rows, :], gain, grad)
        grad_middle = cotangent + back
        grad_middle_ref[rows, :] = grad_middle
        attn = grad_middle.astype(BF16)
        attn_ref[pl.ds(start, few), :] = attn
        sums_own[0] += fold_rows(grad * xhat)
        sums_own[1] += fold_rows(grad)
        sums_own[2] += fold_rows(attn.astype(F32))
        sums_own[3] += fold_rows(cotangent)

    each_rows(half, few, norm)
    copy = remote(attn_ref.at[mine], attn_ref.at[mine], sems.at[0], sems.at[1], flip(me, "tp"))
    copy.start()

    def to_heads(rows):
        for number, proj_ref in enumerate((proj_a_ref, proj_b_ref)):
            heads = proj_ref.shape[1]
            grad_ref = grad_mixed_ref.at[:, number * heads : (number + 1) * heads]

            def work(cut):
                grad = jnp.dot(attn_ref[rows, :], proj_ref[:, cut], preferred_element_type=F32)
                grad_ref[rows, cut] = grad.astype(BF16)

            each_columns(heads, 256, work)

    to_heads(mine)
    vector_ref[...] = jnp.zeros_like(vector_ref)
    for kind in range(4):
        vector_ref[2 + kind : 3 + kind, :] = jnp.sum(sums_own[kind], axis=0, keepdims=True)
    size = hidden_a_ref.shape[1]
    for number, hidden_ref in enumerate((hidden_a_ref, hidden_b_ref)):
        start = width - (2 - number) * size
        vector_ref[6:7, start : start + size] = jnp.sum(hidden_ref[...], axis=0, keepdims=True)
    copy.wait_recv()
    to_heads(other)

    def weight(cut):
        grad = lax.dot_general(
            attn_ref[:, cut], mixed_ref[...], (((0,), (0,)), ((), ())), preferred_element_type=F32
        )
        proj_grad_ref[cut, :] = grad.astype(BF16)

    each_columns(width, 256, weight)
    copy.wait_send()


def middle_back(grad_sum, middle, cotangent, mixed, proj_a, proj_b, vectors, hidden_a, hidden_b, number):
    rows, width = cotangent.shape
    half, heads = rows // 2, mixed.shape[1]
    cuts = line_cuts(width, True)
    return pl.pallas_call(
        functools.partial(middle_back_kernel, cuts),
        out_shape=[
            jax.ShapeDtypeStruct((half, width), F32),
            jax.ShapeDtypeStruct((rows, heads), BF16),
            jax.ShapeDtypeStruct((width, heads), BF16),
            jax.ShapeDtypeStruct((8, width), F32),
        ],
        in_specs=in_vmem(9),
        out_specs=in_vmem(4),
        scratch_shapes=[
            pltpu.VMEM((rows, width), BF16),
            pltpu.VMEM((4, 8, width), F32),
            pltpu.SemaphoreType.DMA((2,)),
        ],
        compiler_params=kernel_params(number),
        cost_estimate=SMALL,
    )(
        grad_sum if cuts else from_line_order(grad_sum),
        middle,
        cotangent,
        mixed,
        proj_a,
        proj_b,
        vectors,
        hidden_a,
        hidden_b,
    )


def first_back_kernel(cuts, programs, *refs):
    (
        grad_query_ref,
        grad_part_ref,
        first_ref,
        stream_ref,
        normed_ref,
        vectors_ref,
        grad_middle_ref,
        mlp_ref,
        middle_ref,
        early_ref,
        cut_b_ref,
    ), refs = refs[:11], refs[11:]
    (input_ref, layer_ref, mlp_out, part_out, total_out), refs = refs[:5], refs[5:]
    (weight_ref, vector_ref, sent_ref, got_ref, grad_first_ref, held_ref, sems), scratch = refs[:7], refs[7:]
    me = here()
    rows, width = stream_ref.shape
    half, heads = rows // 2, grad_query_ref.shape[1]
    shard_rows = part_out.shape[0]
    mine, other = half_rows_of(me["tp"], half), half_rows_of(1 - me["tp"], half)
    few = 32
    sibling = flip(me, "tp")
    works = schedule(
        programs,
        (
            cut_b_ref,
            weight_ref.reshape(2, -1, 2, shard_rows, weight_ref.shape[1]),
            vector_ref,
        ),
        (mlp_out, part_out, total_out),
        scratch,
        ("tp",),
    )

    def run_until(stop):
        while works and works[0][0] < stop:
            works.pop(0)[1]()

    run_until(0.1)
    grad_first_ref[:, :heads] = grad_query_ref[...]
    grad_first_ref[:, heads:] = grad_part_ref[...].astype(BF16)

    def weight(cut):
        grad = lax.dot_general(
            normed_ref[:, cut],
            grad_first_ref[:, heads:],
            (((0,), (0,)), ((), ())),
            preferred_element_type=F32,
        )
        weight_ref[cut, :] = grad.astype(BF16)

    each_columns(width, 512, weight)
    run_until(0.2)

    def part(at, target):
        def work(cut):
            target[:, cut] = rows_by_rows(grad_first_ref[at, :], first_ref[cut, :])

        each_columns(width, 512, work)

    part(other, sent_ref)
    sums_copy = remote(sent_ref, got_ref, sems.at[0], sems.at[1], sibling)
    sums_copy.start()
    run_until(0.3)
    bias = vectors_ref[5:6, :]

    def layer(at):
        start = pl.multiple_of(me["tp"] * half + at.start, few)
        out = middle_ref[at, :] + (shuffled(cuts, mlp_ref, at) + bias)
        layer_ref[pl.ds(start, few), :] = out.astype(BF16)

    each_rows(half, few, layer)
    layer_copy = remote(layer_ref.at[mine], layer_ref.at[mine], sems.at[2], sems.at[3], sibling)
    layer_copy.start()
    run_until(0.4)
    grad_own, folded = held_ref.at[0], held_ref.at[1]
    part(mine, grad_own)
    run_until(0.5)
    sums_copy.wait_recv()
    gain = vectors_ref[0:1, :]
    folded[0:16, :] = jnp.zeros((16, width), F32)

    def norm(at):
        start = pl.multiple_of(me["tp"] * half + at.start, few)
        grad = grad_own[at, :] + got_ref[at, :]
        xhat, back = norm_back(stream_ref[pl.ds(start, few), :].astype(F32), gain, grad)
        input_ref[pl.ds(start, few), :] = (grad_middle_ref[at, :] + back).astype(BF16)
        folded[0:8, :] += fold_rows(grad * xhat)
        folded[8:16, :] += fold_rows(grad)

    each_rows(half, few, norm)
    input_copy = remote(input_ref.at[mine], input_ref.at[mine], sems.at[4], sems.at[5], sibling)
    input_copy.start()
    vector_ref[...] = early_ref[...]
    for kind in range(2):
        total = jnp.sum(folded[kind * 8 : kind * 8 + 8, :], axis=0, keepdims=True)
        vector_ref[kind : kind + 1, :] = total
    vector_ref[6:7, :heads] = jnp.sum(
        fold_rows(grad_query_ref[...].astype(F32)), axis=0, keepdims=True
    )
    part_sums = jnp.sum(
        fold_rows(grad_first_ref[:, heads:].astype(F32)), axis=0, keepdims=True
    )
    vector_ref[7:8, : part_sums.shape[1]] = jnp.where(me["tp"] == 1, part_sums, 0.0)
    run_until(2.0)
    layer_copy.wait()
    input_copy.wait()
    sums_copy.wait_send()


def first_back(
    grad_query,
    grad_part,
    first_all,
    stream,
    normed,
    vectors,
    grad_middle,
    mlp_sum,
    middle,
    early,
    cut_b,
    number,
):
    rows, width = stream.shape
    half, heads, part = rows // 2, grad_query.shape[1], grad_part.shape[1]
    lines = lax.axis_size("line")
    cuts = line_cuts(width, True)
    shard_rows = width // (4 * lines)
    vector = early.shape
    programs = [
        placed(return_half(cut_b, BF16), 0.0, 1.0),
        placed(Direct(lines, shard_rows, part, part), 0.1, 0.95),
        placed(Total(vector, lines, 6, heads), 0.9, 0.93, 0.97),
    ]
    anywhere = [pl.BlockSpec(memory_space=pl.ANY)]
    return pl.pallas_call(
        functools.partial(first_back_kernel, cuts, programs),
        out_shape=[
            jax.ShapeDtypeStruct((rows, width), BF16),
            jax.ShapeDtypeStruct((rows, width), BF16),
        ]
        + [one.out for one in programs],
        in_specs=in_vmem(10) + anywhere,
        out_specs=in_vmem(2) + [one.out_spec for one in programs],
        scratch_shapes=[
            pltpu.VMEM((width, part), BF16),
            pltpu.VMEM(vector, F32),
            pltpu.VMEM((half, width), F32),
            pltpu.VMEM((half, width), F32),
            pltpu.VMEM((rows, heads + part), BF16),
            pltpu.VMEM((2, half, width), F32),
            pltpu.SemaphoreType.DMA((6,)),
        ]
        + [held for one in programs for held in one.scratch()],
        compiler_params=kernel_params(number),
        cost_estimate=SMALL,
    )(
        grad_query,
        grad_part,
        first_all,
        stream,
        normed,
        vectors,
        grad_middle,
        mlp_sum if cuts else from_line_order(mlp_sum),
        middle,
        early,
        cut_b,
    )


def body(
    hidden_in,
    block_order,
    attn_norm_gain,
    attn_norm_bias,
    query_weight,
    query_bias,
    keyval_weight,
    value_bias,
    proj_weight,
    proj_bias,
    mlp_norm_gain,
    mlp_norm_bias,
    up_weight,
    up_bias,
    down_weight,
    down_bias,
    out_cotangent,
):
    rows_dev = hidden_in.shape[0]
    half_rows = rows_dev // 2
    width = hidden_in.shape[1]
    blocks_dev = rows_dev // BLK
    slot_count = block_order.shape[1]
    group_blocks = PBLK + CONTS
    heads_dev = query_bias.shape[0] // HD
    head_width = heads_dev * HD
    core = lax.axis_index("tp")
    quarter = lax.axis_index("fsdp") * lax.axis_size("pair") + lax.axis_index("pair")
    quarters = lax.axis_size("fsdp") * lax.axis_size("pair")
    hidden_dev = up_weight.shape[1] // quarters

    def own_half(values):
        return lax.dynamic_slice_in_dim(values, core * half_rows, half_rows, axis=0)

    def in_order(mine, other, axis=0):
        first = jnp.where(core == 0, mine, other)
        second = jnp.where(core == 0, other, mine)
        return jnp.concatenate([first, second], axis=axis)


    slot_ids = jnp.arange(slot_count, dtype=jnp.int32)
    ordering = block_order[0]
    inverse = jnp.sum(
        jnp.where(ordering[None, :] == slot_ids[:, None], slot_ids[None, :], 0), axis=1
    )
    ctx_index = lax.axis_index("line") * lax.axis_size("pair") + lax.axis_index("pair")
    first_slot = ctx_index * blocks_dev
    my_slots = first_slot + jnp.arange(blocks_dev, dtype=jnp.int32)
    my_blocks = lax.dynamic_slice_in_dim(ordering, first_slot, blocks_dev)
    positions = my_blocks % group_blocks
    group_base = my_blocks // group_blocks * group_blocks
    prompt_slots = jnp.take(
        inverse, group_base[:, None] + jnp.arange(PBLK, dtype=jnp.int32)[None, :]
    )
    key_slots = jnp.concatenate([prompt_slots, my_slots[:, None]], axis=1)

    vectors = [
        attn_norm_gain,
        attn_norm_bias,
        proj_bias,
        mlp_norm_gain,
        mlp_norm_bias,
        down_bias,
    ]
    vectors = jnp.stack(vectors + [jnp.zeros_like(down_bias)] * 2).astype(F32)

    keyval_cut = lax.dynamic_slice_in_dim(keyval_weight, core * HD, HD, axis=1)
    first_cut = jnp.concatenate([query_weight, keyval_cut], axis=1)
    shard_rows = down_weight.shape[0]
    hidden_half = hidden_dev // 2
    columns = down_weight.shape[1]
    first_rows = shard_rows // 2
    early_rows = shard_rows // 2
    cuts = line_cuts(width, False)
    lines = lax.axis_size("line")
    first_pieces = [(0, slice(0, first_rows), 0)]
    other_pieces = [(0, slice(first_rows, shard_rows), 0)]
    early_pieces = [(1, slice(0, shard_rows), 0), (0, slice(0, early_rows), 1)]
    late_pieces = [(0, slice(early_rows, shard_rows), 1), (1, slice(0, shard_rows), 1)]
    hops = [0.1 * k for k in range(1, 4)] if lines == 4 else spaced(0.1, 0.3, lines - 1)
    levels = spaced(0.4, 0.98, 2 * lines)
    piece_hops = spaced(0.35, 0.75, lines - 1)
    _, first_all, other_cut, early_cut, late_cut, mlp_piece, normed_one, cotangent_line, proj_line = run_programs(
        [
            placed(spread_halves(first_pieces, columns, BF16), 0.0, 0.05),
            placed(rows_gather(first_cut), 0.01, *hops, *levels, 1.0),
            placed(spread_halves(other_pieces, columns, BF16), 0.06, 1.0),
            placed(spread_halves(early_pieces, columns, BF16), 0.06, 1.0),
            placed(spread_halves(late_pieces, columns, BF16), 0.061, 1.0),
            placed(line_gather((quarters, first_rows, hidden_half), BF16), 0.07, *piece_hops, 1.0),
            placed(Work(norm_work, hidden_in.shape, BF16), 0.31, 0.31),
            placed(Work(functools.partial(reorder_work, cuts or [0]), (half_rows, width), BF16), 0.32, 0.32),
            placed(line_gather(proj_weight.shape, BF16), 0.305, *spaced(0.48, 0.88, lines - 1), 1.0),
        ],
        [
            lambda more, outs: more[3:5],
            lambda more, outs: more[5],
            lambda more, outs: more[3:5],
            lambda more, outs: more[3:5],
            lambda more, outs: more[3:5],
            lambda more, outs: outs[0],
            lambda more, outs: more[:2],
            lambda more, outs: more[2],
            lambda more, outs: more[6],
        ],
        1,
        near=[hidden_in, vectors, out_cotangent],
        far=[down_weight, up_weight, first_cut, proj_weight],
    )
    if cuts is None:
        cotangent_line = to_line_order(own_half(out_cotangent))
    first_all = flat(first_all)

    value_shift = jnp.where(core == 1, value_bias.astype(F32), 0.0)
    first_shift = jnp.concatenate([query_bias.astype(F32), value_shift])
    part_like = (rows_dev, HD)
    head_half = head_width // 2
    half_line = jax.ShapeDtypeStruct((lines, shard_rows, head_half), BF16)
    _, query_low, keyval_every, mlp_other, proj_a = run_programs(
        [
            placed(Work(part_work, part_like, BF16), 0.0, 0.0),
            placed(Work(query_work, (rows_dev, head_width), BF16), 0.2, 0.2),
            placed(ctx_gather(part_like, BF16), 0.1, *spaced(0.25, 0.5, lines - 1), *spaced(0.52, 0.9, 2 * lines), 1.0),
            placed(
                line_gather((quarters, shard_rows - first_rows, hidden_half), BF16),
                0.11,
                *spaced(0.3, 0.62, lines - 1),
                1.0,
            ),
            placed(columns_gather(half_line), 0.001, 0.45, 0.85, 1.0),
        ],
        [
            lambda more, outs: more[:3],
            lambda more, outs: more[:3],
            lambda more, outs: outs[0],
            lambda more, outs: more[3],
            lambda more, outs: more[4].at[:, :, :head_half],
        ],
        4,
        near=[normed_one, first_all, first_shift[None]],
        far=[other_cut, proj_line],
    )
    keyval_every, early_cut = lax.optimization_barrier((keyval_every, early_cut))
    mlp_early = lax.all_gather(early_cut, "line", axis=0, tiled=False)
    table = keyval_every.reshape(2, slot_count, BLK, HD)
    mixed_low, logsums, (proj_b, cotangent_all) = attend(
        query_low,
        table,
        positions,
        key_slots,
        [
            placed(columns_gather(half_line), 0.0, 0.9, 1.0, 1.0),
            placed(plane_gather(cotangent_line), 0.0, 0.9, 1.0, 1.0),
        ],
        [proj_line[:, :, head_half:], cotangent_line],
        2,
    )
    proj_a, proj_b = flat(proj_a), flat(proj_b)
    mixed_low, mlp_early, late_cut = lax.optimization_barrier((mixed_low, mlp_early, late_cut))
    mlp_late = lax.all_gather(late_cut, "line", axis=0, tiled=False)
    middle, normed_two_line = project(
        mixed_low, proj_a, proj_b, hidden_in, vectors, 5
    )

    up_shift = lax.dynamic_slice_in_dim(up_bias, quarter * hidden_dev, hidden_dev).astype(F32)
    up_shift = up_shift[None]
    rows_all, act_a, pre_a, back_a, bias_a, weight_grad_a = forward_products(
        normed_two_line, cotangent_all, mlp_piece, mlp_other, mlp_early, up_shift[:, :hidden_half], 6
    )
    rows_all, act_a, pre_a, back_a = flat(rows_all), flat(act_a), flat(pre_a), flat(back_a)
    cotangent_all = flat(cotangent_all)
    cut_a = lax.psum_scatter(weight_grad_a, "line", scatter_dimension=0, tiled=True)
    rows_all, weight_grad_a = lax.optimization_barrier((rows_all, weight_grad_a))
    down_part, weight_grad_b, bias_b, grad_normed_two = second_products(
        rows_all,
        cotangent_all,
        back_a,
        act_a,
        (mlp_piece, mlp_other, mlp_early, mlp_late),
        up_shift[:, hidden_half:],
        7,
    )
    cut_b = lax.psum_scatter(weight_grad_b, "line", scatter_dimension=0, tiled=True)
    cut_a = cut_a.reshape(quarters, 2 * shard_rows, hidden_half)
    cut_b = cut_b.reshape(quarters, 2 * shard_rows, hidden_half)

    grad_middle, grad_mixed, proj_weight_grad, vector = middle_back(
        grad_normed_two, middle, out_cotangent, mixed_low, proj_a, proj_b, vectors, bias_a, bias_b, 8
    )
    grad_mixed, cut_a = lax.optimization_barrier((grad_mixed, cut_a))
    sum_proj, proj_parts = rows_sum(proj_weight_grad)
    sum_down, down_parts = plane_sum(down_part)
    grad_query, grad_sets, query_weight_grad, (grad_proj_weight, mlp_out) = attend_back(
        query_low,
        grad_mixed,
        mixed_low,
        logsums,
        table,
        normed_one,
        positions,
        key_slots,
        [
            placed(sum_proj, 0.0, *spaced(0.13, 0.51, lines), 0.63, 1.06),
            placed(sum_down, 0.0, 0.45, 0.45, 0.45, 0.45, 0.76, 0.95, 1.1, 1.2),
        ],
        [proj_parts, down_parts],
        3,
    )
    grad_table = by_slot(grad_sets, key_slots, slot_count)
    grad_parts = grad_table.reshape(2, lines, 2 * rows_dev, HD)
    along_line, over_pair = ctx_sums(grad_parts)
    sum_query, query_parts = rows_sum(query_weight_grad)
    _, grad_part, grad_query_weight, mlp_grad_a = run_programs(
        [
            placed(along_line, 0.01, 0.75),
            placed(over_pair, 0.76, 0.86, 0.97),
            placed(sum_query, 0.0, 1.0),
            placed(return_half(cut_a, BF16), 0.02, 1.0),
        ],
        [
            grad_parts,
            lambda more, outs: outs[0].reshape(2, rows_dev, HD),
            query_parts,
            cut_a,
        ],
        12,
    )
    input_grad, layer_out, mlp_grad_b, grad_part_weight, summed = first_back(
        grad_query,
        grad_part,
        first_all,
        hidden_in,
        normed_one,
        vectors,
        grad_middle,
        mlp_out,
        middle,
        vector,
        cut_b,
        9,
    )
    grad_down_weight, grad_up_weight = widen(mlp_grad_a, mlp_grad_b)
    grad_keyval_weight = in_order(grad_part_weight[:, :HD], grad_part_weight[:, HD:], axis=1)
    sum_up = summed[:quarters, width : 2 * width - head_width].reshape(quarters * hidden_dev)
    return (
        layer_out,
        input_grad,
        summed[0, :width],
        summed[1, :width],
        grad_query_weight,
        summed[6, :head_width],
        grad_keyval_weight,
        summed[7, :HD],
        grad_proj_weight,
        summed[4, :width],
        summed[2, :width],
        summed[3, :width],
        grad_up_weight,
        sum_up,
        grad_down_weight,
        summed[5, :width],
    )


def solution(mesh):
    fsdp, ctx, tp = mesh.devices.shape
    grid = Mesh(mesh.devices.reshape(fsdp, ctx // 2, 2, tp), EVERY)
    by_rows = P(ROWS, None)
    by_both = P(ROWS, "tp")
    return jax.shard_map(
        body,
        mesh=grid,
        in_specs=(
            by_rows,
            P("fsdp", None),
            P(),
            P(),
            by_both,
            P("tp"),
            by_rows,
            P(),
            by_both,
            P(),
            P(),
            P(),
            by_both,
            P("tp"),
            by_both,
            P(),
            by_rows,
        ),
        out_specs=(
            by_rows,
            by_rows,
            P(),
            P(),
            by_both,
            P("tp"),
            by_rows,
            P(),
            by_both,
            P(),
            P(),
            P(),
            by_both,
            P("tp"),
            by_both,
            P(),
        ),
        check_vma=False,
    )
```

```python
import functools

import jax
import jax.numpy as jnp
from jax import lax
from jax.experimental import pallas as pl
from jax.experimental.pallas import tpu as pltpu
from jax.sharding import Mesh, PartitionSpec as P

HD = 128
BLK = 256
PBLK = 8
CONTS = 8
EPSILON = 1e-05
MASKED = -1e30
F32 = jnp.float32
BF16 = jnp.bfloat16
ROWS = ("fsdp", "line", "pair")
EVERY = ("fsdp", "line", "pair", "tp")


MESH_ID = pl.DeviceIdType.MESH
VMEM_BYTES = 60 * 1024 * 1024
SMALL = pl.CostEstimate(flops=1, bytes_accessed=1, transcendentals=0)
SIDE = ("pair", "fsdp")
FRONT = ("fsdp", "pair")


def here():
    return {name: lax.axis_index(name) for name in EVERY}


def flip(place, step):
    place = dict(place)
    if isinstance(step, str):
        place[step] = 1 - place[step]
    else:
        core = place["tp"]
        for name, used in ((step[0], 1 - core), (step[1], core)):
            place[name] = place[name] + (1 - 2 * place[name]) * used
    return place


def along(place, amount):
    return dict(place, line=place["line"] + amount)


def remote(source, target, send_sem, recv_sem, place):
    return pltpu.make_async_remote_copy(
        src_ref=source,
        dst_ref=target,
        send_sem=send_sem,
        recv_sem=recv_sem,
        device_id=place,
        device_id_type=MESH_ID,
    )


def top_bit(bits):
    return bits.bit_length() - 1


def add_blocks(target, first, second, rows):
    tile = min(rows, 64)

    def one(index, carry):
        cut = pl.ds(pl.multiple_of(index * tile, tile), tile)
        total = first(cut).astype(F32)
        if second is not None:
            total = total + second(cut).astype(F32)
        target[cut, :] = total.astype(target.dtype)
        return carry

    lax.fori_loop(0, rows // tile, one, 0)


def rows_of(ref):
    return lambda cut: ref[cut, :]


class Gather:
    def __init__(self, values, steps, lines, shape, slot):
        self.steps, self.lines, self.slot = steps, lines, slot
        self.out = jax.ShapeDtypeStruct(shape, values.dtype)
        self.in_spec = self.out_spec = pl.BlockSpec(memory_space=pl.ANY)

    def scratch(self):
        parts = 1 << len(self.steps)
        return [
            pltpu.SemaphoreType.DMA(()),
            pltpu.SemaphoreType.DMA((2, self.lines)),
            pltpu.SemaphoreType.DMA((self.lines,)),
            pltpu.SemaphoreType.DMA((self.lines, max(1, len(self.steps)) * parts)),
            pltpu.SemaphoreType.DMA((self.lines, parts)),
        ]

    def stages(self, me, x_ref, out_ref, own_sem, line_send, line_recv, send, recv):
        steps, lines, slot = self.steps, self.lines, self.slot
        count = len(steps)
        my_line = me["line"] if lines > 1 else 0

        def block(bits, shard):
            place = me
            for k in reversed(range(count)):
                if bits >> k & 1:
                    place = flip(place, steps[k])
            return slot(out_ref, dict(place, line=shard))

        def to_step(k, bits, shard, source):
            return remote(
                source,
                block(bits, shard),
                send.at[shard, k * (1 << count) + bits],
                recv.at[shard, bits | 1 << k],
                flip(me, steps[k]),
            )

        def to_line(amount, shard, source):
            return remote(
                source,
                block(0, shard),
                line_send.at[(amount + 1) // 2, shard],
                line_recv.at[shard],
                along(me, amount),
            )

        def send_on(bits, shard, source):
            for k in range(top_bit(bits) + 1, count):
                to_step(k, bits, shard, source).start()

        def at_distance(distance, work):
            if distance == 0:
                work(my_line, 0)
                return
            for amount in (1, -1):
                shard = my_line - amount * distance
                pl.when((shard >= 0) & (shard < lines))(functools.partial(work, shard, amount))

        def line_inside(amount):
            there = my_line + amount
            return (there >= 0) & (there < lines)

        own = pltpu.make_async_copy(x_ref, block(0, my_line), own_sem)

        def begin():
            if lines > 1:
                for amount in (1, -1):
                    pl.when(line_inside(amount))(
                        lambda amount=amount: to_line(amount, my_line, x_ref).start()
                    )
            send_on(0, my_line, x_ref)
            own.start()

        def line_arrival(shard, amount):
            remote(
                block(0, shard), block(0, shard), line_send.at[0, shard], line_recv.at[shard], me
            ).wait_recv()
            pl.when(line_inside(amount))(lambda: to_line(amount, shard, block(0, shard)).start())
            send_on(0, shard, block(0, shard))

        def level_arrival(level, shard, amount):
            for bits in range(1 << level, 2 << level):
                remote(
                    block(bits, shard),
                    block(bits, shard),
                    send.at[shard, 0],
                    recv.at[shard, bits],
                    me,
                ).wait_recv()
                send_on(bits, shard, block(bits, shard))

        def end():
            own.wait()
            if lines > 1:
                for amount in (1, -1):
                    for distance in range(lines):
                        shard = my_line - amount * distance
                        pl.when((shard >= 0) & (shard < lines) & line_inside(amount))(
                            lambda amount=amount, shard=shard: to_line(
                                amount, shard, block(0, shard)
                            ).wait_send()
                        )
            for shard in range(lines):
                for bits in range(1 << count):
                    for k in range(top_bit(bits) + 1, count):
                        to_step(k, bits, shard, block(bits, shard)).wait_send()

        line = [functools.partial(at_distance, number, line_arrival) for number in range(1, lines)]
        levels = [
            functools.partial(at_distance, number - level, functools.partial(level_arrival, level))
            for number in range(lines + count - 1)
            for level in range(count)
            if 0 <= number - level < lines
        ]
        return [begin] + line + levels + [end]


class Sum:
    far_line = True

    def __init__(self, steps, lines, rows, columns, slot, kind=F32):
        self.steps, self.lines, self.rows, self.columns = steps, lines, rows, columns
        self.slot = slot
        self.out = jax.ShapeDtypeStruct((rows, columns), kind)
        self.in_spec = pl.BlockSpec(memory_space=pl.ANY)
        self.out_spec = pl.BlockSpec(memory_space=pltpu.VMEM)

    def scratch(self):
        count, lines = len(self.steps), self.lines
        sizes = [1 << (count - 1 - k) for k in range(count)]
        block = (self.rows, self.columns)
        return (
            [pltpu.VMEM((lines, sizes[0]) + block, BF16)]
            + [pltpu.VMEM((lines, size) + block, BF16) for size in sizes]
            + [pltpu.VMEM((lines,) + (block if lines > 1 else (16, 128)), BF16)]
            + [pltpu.SemaphoreType.DMA((lines, sizes[0]))]
            + [pltpu.SemaphoreType.DMA((lines, size)) for size in sizes] * 2
            + [pltpu.SemaphoreType.DMA((lines,))] * 2
        )

    def stages(self, me, x_ref, out_ref, own, *rest):
        steps, lines, rows, slot = self.steps, self.lines, self.rows, self.slot
        count = len(steps)
        held, rest = rest[:count], rest[count:]
        on_line, own_sem, rest = rest[0], rest[1], rest[2:]
        send, recv = rest[:count], rest[count : 2 * count]
        line_send, line_recv = rest[2 * count :]
        my_line = me["line"] if lines > 1 else 0
        last = count - 1

        def target_of(bits, shard):
            place = me
            for k in range(count):
                if bits >> k & 1:
                    place = flip(place, steps[k])
            return dict(place, line=shard)

        def store(k, shard, bits):
            return held[k].at[shard, bits >> (k + 1)]

        def own_copy(shard, bits):
            return pltpu.make_async_copy(
                slot(x_ref, target_of(bits, shard)),
                own.at[shard, bits >> 1],
                own_sem.at[shard, bits >> 1],
            )

        def copy(k, shard, bits):
            source = slot(x_ref, target_of(bits, shard)) if k == 0 else store(k - 1, shard, bits)
            return remote(
                source,
                store(k, shard, bits ^ (1 << k)),
                send[k].at[shard, bits >> (k + 1)],
                recv[k].at[shard, bits >> (k + 1)],
                flip(me, steps[k]),
            )

        def parts_of(k):
            return [high << (k + 1) for high in reversed(range(1 << (count - 1 - k)))]

        def send_first(shard, amount):
            for bits in parts_of(0):
                copy(0, shard, bits | 1).start()

        def own_first(shard, amount):
            for bits in parts_of(0):
                own_copy(shard, bits).start()

        def take_step(k, shard, amount, parts=None):
            for bits in parts or parts_of(k):
                copy(k, shard, bits | 1 << k).wait_recv()
                arrived = store(k, shard, bits)
                if k == 0:
                    own_copy(shard, bits).wait()
                    mine = own.at[shard, bits >> 1]
                else:
                    mine = store(k - 1, shard, bits)
                add_blocks(arrived, rows_of(mine), rows_of(arrived), rows)
                if k + 1 < count and bits >> (k + 1) & 1:
                    copy(k + 1, shard, bits).start()

        def line_copy(shard):
            return remote(
                held[last].at[shard, 0],
                on_line.at[my_line],
                line_send.at[shard],
                line_recv.at[my_line],
                along(me, shard - my_line),
            )

        def each(distance, work):
            if distance == 0:
                work(my_line, 0)
                return
            for amount in (1, -1):
                shard = my_line + amount * distance
                pl.when((shard >= 0) & (shard < lines))(functools.partial(work, shard, amount))

        order = list(reversed(range(lines)))

        def begin():
            for distance in order:
                each(distance, send_first)
            for distance in order:
                each(distance, own_first)

        def tick(number):
            for k in reversed(range(count)):
                index = number - k
                if 0 <= index < lines:
                    each(order[index], functools.partial(take_step, k))
                    if k == last and order[index] > 0:
                        each(order[index], lambda shard, amount: line_copy(shard).start())

        def end():
            final = held[last].at[my_line, 0]
            if lines == 1:
                add_blocks(out_ref, rows_of(final), None, rows)
            else:
                add_blocks(on_line.at[my_line], rows_of(final), None, rows)

                def arrived(shard, amount):
                    remote(
                        on_line.at[shard], on_line.at[shard], line_send.at[0], line_recv.at[shard], me
                    ).wait_recv()

                for distance in range(1, lines):
                    each(distance, arrived)
                add_blocks(
                    out_ref,
                    lambda cut: sum(on_line[shard, cut, :].astype(F32) for shard in range(lines)),
                    None,
                    rows,
                )
                for distance in range(1, lines):
                    each(distance, lambda shard, amount: line_copy(shard).wait_send())
            for k in range(count):
                for shard in range(lines):
                    for bits in parts_of(k):
                        copy(k, shard, bits | 1 << k).wait_send()

        if lines == 1:
            ticks = [
                functools.partial(take_step, k, 0, 0, [bits]) for k in range(count) for bits in parts_of(k)
            ]
        else:
            ticks = [functools.partial(tick, number) for number in range(lines + count - 1)]
        return [begin] + ticks + [end]


DIRECT = (("pair",), ("fsdp",), ("pair", "fsdp"))


def move(me, names):
    place = me
    for name in names:
        place = flip(place, name)
    return place


def quarter_of(place):
    return place["fsdp"] * 2 + place["pair"]


class Exchange:
    steps, lines = ("pair", "fsdp"), 1

    def __init__(self, moves, shape, kind):
        self.moves = moves
        self.out = jax.ShapeDtypeStruct(shape, kind)
        self.in_spec = self.out_spec = pl.BlockSpec(memory_space=pl.ANY)

    def scratch(self):
        count = len(self.moves)
        return [
            pltpu.SemaphoreType.DMA((count,)),
            pltpu.SemaphoreType.DMA((count, 3)),
            pltpu.SemaphoreType.DMA((count, 3)),
        ]

    def stages(self, me, x_refs, out_ref, own_sem, send, recv):
        copies = []
        for n, (source, target) in enumerate(self.moves):
            there_ref = target(out_ref, quarter_of(me))
            for k, names in reversed(list(enumerate(DIRECT))):
                there = move(me, names)
                copies.append(
                    remote(
                        source(x_refs, quarter_of(there)), there_ref, send.at[n, k], recv.at[n, k], there
                    )
                )
            copies.append(
                pltpu.make_async_copy(source(x_refs, quarter_of(me)), there_ref, own_sem.at[n])
            )

        def begin():
            for one in copies:
                one.start()

        def end():
            for one in copies:
                one.wait()

        return [begin, end]


def half_quarter(ref, quarter, half, rows=None):
    columns = ref.shape[1] // 8
    cut = pl.ds(pl.multiple_of((quarter * 2 + half) * columns, columns), columns)
    return ref.at[:, cut] if rows is None else ref.at[rows, cut]


def spread_halves(pieces, columns, kind):
    moves, start = [], 0
    for index, rows, half in pieces:
        count = rows.stop - rows.start
        moves.append(
            (
                lambda refs, quarter, index=index, rows=rows, half=half: half_quarter(
                    refs[index], quarter, half, rows
                ),
                lambda ref, quarter, start=start, count=count: ref.at[quarter, start : start + count],
            )
        )
        start += count
    return Exchange(moves, (4, start, columns // 8), kind)


def return_half(cut, kind):
    quarters, rows, columns = cut.shape

    def place(ref, quarter):
        return ref.at[:, pl.ds(pl.multiple_of(quarter * columns, columns), columns)]

    return Exchange(
        [(lambda ref, quarter: ref.at[quarter], place)], (rows, quarters * columns), kind
    )


def widen_kernel(a_ref, b_ref, down_ref, up_ref):
    rows, columns = down_ref.shape[0], a_ref.shape[1] // 4
    for start, out_ref in ((0, down_ref), (rows, up_ref)):
        for quarter in range(4):
            for half, ref in enumerate((a_ref, b_ref)):
                at = (quarter * 2 + half) * columns
                cut = slice(quarter * columns, (quarter + 1) * columns)
                out_ref[:, at : at + columns] = ref[start : start + rows, cut].astype(F32)


def widen(half_a, half_b):
    rows, columns = half_a.shape
    shape = jax.ShapeDtypeStruct((rows // 2, 2 * columns), F32)
    return pl.pallas_call(
        widen_kernel,
        out_shape=[shape, shape],
        compiler_params=pltpu.CompilerParams(vmem_limit_bytes=VMEM_BYTES),
        cost_estimate=SMALL,
    )(half_a, half_b)


class Work:
    steps, lines = (), 1

    def __init__(self, work, shape, kind):
        self.work, self.out = work, jax.ShapeDtypeStruct(shape, kind)
        self.in_spec = self.out_spec = pl.BlockSpec(memory_space=pltpu.VMEM)

    def scratch(self):
        return []

    def stages(self, me, x_refs, out_ref):
        return [functools.partial(self.work, me, x_refs, out_ref), lambda: None]


class Direct:
    steps, rows_too = ("tp",), True

    def __init__(self, lines, rows, columns, shared):
        self.lines, self.rows, self.columns, self.shared = lines, rows, columns, shared
        self.out = jax.ShapeDtypeStruct((rows, columns + shared), F32)
        self.in_spec = self.out_spec = pl.BlockSpec(memory_space=pltpu.VMEM)

    def scratch(self):
        lines = self.lines
        return [
            pltpu.VMEM((2, lines, 2, self.rows, self.columns), BF16),
            pltpu.SemaphoreType.DMA((4, 2, lines)),
            pltpu.SemaphoreType.DMA((2, lines, 2)),
            pltpu.SemaphoreType.DMA((2,)),
        ]

    def stages(self, me, x_ref, out_ref, held, send, recv, share_sem):
        def on_others(work):
            for side in range(4):
                for distance in range(self.lines):
                    for way, amount in enumerate((1, -1) if distance else (1,)):
                        if side or distance:
                            place = along(plane_partner(me, side * 2), amount * distance)
                            inside = (place["line"] >= 0) & (place["line"] < self.lines)
                            pl.when(inside)(
                                functools.partial(work, place, send.at[side, way, distance])
                            )

        def copy(place, sem):
            return remote(
                by_rows_slot(x_ref, place),
                by_rows_slot(held, me),
                sem,
                by_rows_slot(recv, me),
                place,
            )

        def arrived(place, sem):
            slot = by_rows_slot(held, place)
            remote(slot, slot, sem, by_rows_slot(recv, place), me).wait_recv()

        def begin():
            on_others(lambda place, sem: copy(place, sem).start())
            held[me["fsdp"], me["line"], me["pair"]] = x_ref[me["fsdp"], me["line"], me["pair"]]

        def end():
            on_others(arrived)
            total = jnp.zeros((self.rows, self.columns), F32)
            for half in range(2):
                for shard in range(self.lines):
                    for side in range(2):
                        total = total + held[half, shard, side].astype(F32)
            out_ref[:, : self.columns] = total
            share = remote(
                out_ref.at[:, : self.columns],
                out_ref.at[:, self.columns :],
                share_sem.at[0],
                share_sem.at[1],
                flip(me, "tp"),
            )
            share.start()
            share.wait()
            on_others(lambda place, sem: copy(place, sem).wait_send())

        return [begin, end]


class Total:
    steps, everyone = (), True

    def __init__(self, shape, lines, special, heads):
        self.lines, self.shape, self.special, self.heads = lines, shape, special, heads
        self.out = jax.ShapeDtypeStruct((shape[0], 2 * shape[1]), F32)
        self.in_spec = self.out_spec = pl.BlockSpec(memory_space=pltpu.VMEM)

    def scratch(self):
        shape, lines = self.shape, self.lines
        return [
            pltpu.VMEM((lines,) + shape, F32),
            pltpu.VMEM((8,) + shape, F32),
            pltpu.SemaphoreType.DMA((2, lines)),
            pltpu.SemaphoreType.DMA((lines,)),
            pltpu.SemaphoreType.DMA((8,)),
            pltpu.SemaphoreType.DMA((8,)),
        ]

    def stages(self, me, x_ref, out_ref, on_line, on_plane, line_send, line_recv, send, recv):
        lines, mine = self.lines, me["line"]
        number = plane_number(me)

        def on_others(work):
            for distance in range(1, lines):
                for way, amount in enumerate((1, -1)):
                    there = mine + amount * distance
                    pl.when((there >= 0) & (there < lines))(
                        functools.partial(work, way, amount, distance, there)
                    )

        def to_line(way, amount, distance):
            return remote(
                on_line.at[mine],
                on_line.at[mine],
                line_send.at[way, distance],
                line_recv.at[mine],
                along(me, amount * distance),
            )

        def to_plane(bits):
            return remote(
                on_plane.at[number],
                on_plane.at[number],
                send.at[bits],
                recv.at[number],
                plane_partner(me, bits),
            )

        def begin():
            on_line[mine] = x_ref[...]
            on_others(lambda way, amount, distance, there: to_line(way, amount, distance).start())

        def arrived(way, amount, distance, there):
            remote(
                on_line.at[there], on_line.at[there], line_send.at[0, 0], line_recv.at[there], me
            ).wait_recv()

        def middle():
            on_others(arrived)
            total = on_line[0]
            for shard in range(1, lines):
                total = total + on_line[shard]
            on_plane[number] = total
            for bits in range(1, 8):
                to_plane(bits).start()

        def end():
            for bits in range(1, 8):
                there = plane_number(plane_partner(me, bits))
                remote(
                    on_plane.at[there], on_plane.at[there], send.at[0], recv.at[there], me
                ).wait_recv()
            total = on_plane[0]
            for other in range(1, 8):
                total = total + on_plane[other]
            width, row, heads = self.shape[1], slice(self.special, self.special + 1), self.heads
            out_ref[...] = jnp.zeros_like(out_ref)
            out_ref[:, :width] = total
            same = [on_plane[quarter * 2 + me["tp"], row, :] for quarter in range(4)]
            out_ref[row, :heads] = sum(part[:, :heads] for part in same)
            for quarter, part in enumerate(same):
                out_ref[quarter : quarter + 1, width : 2 * width - heads] = part[:, heads:]
            for bits in range(1, 8):
                to_plane(bits).wait_send()
            on_others(lambda way, amount, distance, there: to_line(way, amount, distance).wait_send())

        return [begin, middle, end]


def plane_number(place):
    return (place["fsdp"] * 2 + place["pair"]) * 2 + place["tp"]


def plane_partner(me, bits):
    place = me
    for bit, name in ((1, "tp"), (2, "pair"), (4, "fsdp")):
        if bits & bit:
            place = flip(place, name)
    return place


def greet(me, programs, partners=()):
    barrier = pltpu.get_barrier_semaphore()
    plane, reach, lines, corners = set(), 0, 1, False
    for one in programs:
        lines = max(lines, one.lines)
        if one.lines > 1:
            far = hasattr(one, "everyone") or hasattr(one, "far_line")
            reach = max(reach, one.lines - 1 if far else 1)
        if hasattr(one, "everyone"):
            plane |= set(range(1, 8))
        if isinstance(one, Exchange) or hasattr(one, "rows_too"):
            plane |= {2, 4, 6}
        if hasattr(one, "rows_too"):
            reach, corners = one.lines - 1, True
    for step in [step for one in programs for step in one.steps] + list(partners):
        plane |= {"tp": {1}, "pair": {2}, "fsdp": {4}}.get(step, {2, 4})
    for bits in sorted(plane):
        pl.semaphore_signal(
            barrier, inc=1, device_id=plane_partner(me, bits), device_id_type=MESH_ID
        )
    count = len(plane)
    for distance in range(1, reach + 1):
        for amount in (-distance, distance):
            there = me["line"] + amount
            inside = (there >= 0) & (there < lines)

            for bits in (0, 2, 4, 6) if corners else (0,):

                @pl.when(inside)
                def _():
                    pl.semaphore_signal(
                        barrier,
                        inc=1,
                        device_id=along(plane_partner(me, bits), amount),
                        device_id_type=MESH_ID,
                    )

                count = count + inside.astype(jnp.int32)
    pl.semaphore_wait(barrier, count)


def split_scratch(programs, refs):
    parts, start = [], 0
    for one in programs:
        size = len(one.scratch())
        parts.append(refs[start : start + size])
        start += size
    return parts


def schedule(programs, x_refs, out_refs, scratch, partners=()):
    me = here()
    works = [(0.0, functools.partial(greet, me, programs, partners))]
    for one, x_ref, out_ref, held in zip(programs, x_refs, out_refs, split_scratch(programs, scratch)):
        stages = one.stages(me, x_ref, out_ref, *held)
        places = getattr(one, "places", (0.0, 1.0))
        if len(places) == 2:
            places = spaced(places[0], places[1], len(stages))
        last = len(places) - 2
        works += [
            (places[-1] if k == len(stages) - 1 else places[min(k, last)], stage)
            for k, stage in enumerate(stages)
        ]
    return sorted(works, key=lambda work: work[0])


def placed(program, *places):
    program.places = list(places)
    return program


def spaced(start, stop, count):
    return [start + (stop - start) * k / (count - 1) for k in range(count)]


def run_programs(programs, arrays, number, near=(), far=()):
    count = len(programs)
    given = [k for k, array in enumerate(arrays) if not callable(array)]
    others = len(near) + len(far)

    def kernel(*refs):
        (more, refs) = refs[:others], refs[others:]
        plain, out_refs = refs[: len(given)], refs[len(given) : len(given) + count]
        in_refs = [
            array(more, out_refs) if callable(array) else plain[given.index(k)]
            for k, array in enumerate(arrays)
        ]
        for _, work in schedule(programs, in_refs, out_refs, refs[len(given) + count :]):
            work()

    return pl.pallas_call(
        kernel,
        out_shape=[one.out for one in programs],
        in_specs=[pl.BlockSpec(memory_space=pltpu.VMEM)] * len(near)
        + [pl.BlockSpec(memory_space=pl.ANY)] * len(far)
        + [programs[k].in_spec for k in given],
        out_specs=[one.out_spec for one in programs],
        scratch_shapes=[held for one in programs for held in one.scratch()],
        compiler_params=pltpu.CompilerParams(
            collective_id=number, has_side_effects=True, vmem_limit_bytes=VMEM_BYTES
        ),
        cost_estimate=SMALL,
    )(*near, *far, *[arrays[k] for k in given])


def by_rows_slot(ref, at):
    return ref.at[at["fsdp"], at["line"], at["pair"]]


def by_plane_slot(ref, at):
    return ref.at[at["fsdp"], at["pair"], at["tp"]]


def by_ctx_slot(ref, at):
    return ref.at[at["tp"], at["line"], at["pair"]]


def rows_gather(values):
    lines = lax.axis_size("line")
    return Gather(values, (SIDE, FRONT), lines, (2, lines, 2) + values.shape, by_rows_slot)


def line_gather(shape, kind):
    lines = lax.axis_size("line")
    like = jax.ShapeDtypeStruct(shape, kind)
    return Gather(like, (), lines, (lines,) + shape, lambda ref, at: ref.at[at["line"]])


def columns_gather(values):
    lines, rows, columns = values.shape
    return Gather(
        values, (SIDE, FRONT), 1, (2, lines, 2, rows, columns), lambda ref, at: ref.at[at["fsdp"], :, at["pair"]]
    )


def rows_sum(values):
    lines, (total, columns) = lax.axis_size("line"), values.shape
    rows = total // (4 * lines)
    parts = values.astype(BF16).reshape(2, lines, 2, rows, columns)
    return Sum((FRONT, SIDE), lines, rows, columns, by_rows_slot), parts


def plane_gather(values):
    return Gather(values, (SIDE, FRONT, "tp"), 1, (2, 2, 2) + values.shape, by_plane_slot)


def plane_sum(values):
    rows, columns = values.shape[0] // 8, values.shape[1]
    parts = values.astype(BF16).reshape(2, 2, 2, rows, columns)
    return Sum(("tp", FRONT, SIDE), 1, rows, columns, by_plane_slot), parts


def flat(values):
    return values.reshape(-1, values.shape[-1])


def ctx_gather(shape, kind):
    lines = lax.axis_size("line")
    like = jax.ShapeDtypeStruct(shape, kind)
    return Gather(like, ("pair", "tp"), lines, (2, lines, 2) + shape, by_ctx_slot)


def ctx_sums(values):
    _, lines, rows, columns = values.shape
    along_line = Sum(
        ("tp",), lines, rows, columns, lambda ref, at: ref.at[at["tp"], at["line"]], BF16
    )
    over_pair = Sum(("pair",), 1, rows // 2, columns, lambda ref, at: ref.at[at["pair"]])
    return along_line, over_pair


LOG2E = 1.4426950408889634


def visible_bias(bias_ref, position, chunks):
    prompt = position < PBLK
    row = lax.broadcasted_iota(jnp.int32, (BLK, BLK), 0)
    column = lax.broadcasted_iota(jnp.int32, (BLK, BLK), 1)
    limit = jnp.where(prompt, position * BLK + column, PBLK * BLK)
    for chunk in range(chunks - 1):
        bias_ref[chunk] = jnp.where(row + chunk * BLK <= limit, 0.0, MASKED)
    own_limit = jnp.where(prompt, -1, column)
    bias_ref[chunks - 1] = jnp.where(row <= own_limit, 0.0, MASKED)


def rows_by_rows(left, right):
    return lax.dot_general(left, right, (((1,), (1,)), ((), ())), preferred_element_type=F32)


def beside(programs, in_refs, out_refs, scratch, step, steps):
    late = []
    for place, work in schedule(programs, in_refs, out_refs, scratch):
        if place < 1:
            pl.when(step == int(place * steps))(work)
        else:
            late.append((place, work))

    def finish(own=None):
        @pl.when(step == steps - 1)
        def _():
            early = [work for place, work in late if place < 1.05]
            rest = [work for place, work in late if place >= 1.05]
            for work in early + ([own] if own else []) + rest:
                work()

    return finish


def attend_kernel(programs, steps, *refs):
    count = len(programs)
    (position_ref, slot_ref, query_ref, table_ref), refs = refs[:4], refs[4:]
    others, refs = refs[:count], refs[count:]
    (mixed_ref, logsum_ref), refs = refs[:2], refs[2:]
    other_outs, refs = refs[:count], refs[count:]
    (bias_ref, score_ref, value_t_ref), scratch = refs[:3], refs[3:]
    chunks = PBLK + 1
    block = pl.program_id(0)
    factor = HD**-0.5 * LOG2E
    step = pl.program_id(0) * pl.num_programs(1) + pl.program_id(1)
    finish = beside(programs, others, other_outs, scratch, step, steps)

    @pl.when(pl.program_id(1) == 0)
    def _():
        visible_bias(bias_ref, position_ref[block], chunks)
        for chunk in range(chunks):
            value_t_ref[chunk] = table_ref[1, slot_ref[block, chunk]].astype(F32).T.astype(BF16)

    query = query_ref[...]
    largest = None
    for chunk in range(chunks):
        keys = table_ref[0, slot_ref[block, chunk]]
        score = rows_by_rows(keys, query) + bias_ref[chunk]
        score_ref[chunk] = score
        top = jnp.max(score.reshape(BLK // 8, 8, BLK), axis=0)
        largest = top if largest is None else jnp.maximum(largest, top)
    largest = jnp.max(largest, axis=0, keepdims=True)
    total = jnp.zeros((8, BLK), F32)
    mixed = jnp.zeros((HD, BLK), F32)
    for chunk in range(chunks):
        weight = jnp.exp2((score_ref[chunk] - largest) * factor)
        total = total + jnp.sum(weight.reshape(BLK // 8, 8, BLK), axis=0)
        mixed = mixed + jnp.dot(
            value_t_ref[chunk], weight.astype(BF16), preferred_element_type=F32
        )
    total = jnp.sum(total, axis=0, keepdims=True)
    mixed_ref[...] = (mixed / total).T.astype(BF16)
    logsum_ref[0, 0] = largest * factor + jnp.log2(total)
    finish()


def attend(queries, table, positions, key_slots, programs, arrays, number):
    rows, width = queries.shape
    blocks, heads = rows // BLK, width // HD
    count = (PBLK + 1) * BLK
    out = pl.pallas_call(
        functools.partial(attend_kernel, programs, blocks * heads),
        grid=(blocks, heads),
        out_shape=[
            jax.ShapeDtypeStruct((rows, width), BF16),
            jax.ShapeDtypeStruct((blocks, heads, 1, BLK), F32),
        ]
        + [one.out for one in programs],
        in_specs=[
            pl.BlockSpec(memory_space=pltpu.SMEM),
            pl.BlockSpec(memory_space=pltpu.SMEM),
            pl.BlockSpec((BLK, HD), lambda b, h: (b, h)),
            pl.BlockSpec(memory_space=pltpu.VMEM),
        ]
        + [one.in_spec for one in programs],
        out_specs=[
            pl.BlockSpec((BLK, HD), lambda b, h: (b, h)),
            pl.BlockSpec((1, 1, 1, BLK), lambda b, h: (b, h, 0, 0)),
        ]
        + [one.out_spec for one in programs],
        scratch_shapes=[
            pltpu.VMEM((PBLK + 1, BLK, BLK), F32),
            pltpu.VMEM((PBLK + 1, BLK, BLK), F32),
            pltpu.VMEM((PBLK + 1, HD, BLK), BF16),
        ]
        + [held for one in programs for held in one.scratch()],
        compiler_params=pltpu.CompilerParams(
            collective_id=number, has_side_effects=True, vmem_limit_bytes=VMEM_BYTES
        ),
        cost_estimate=SMALL,
    )(positions, key_slots, queries, table, *arrays)
    return out[0], out[1], out[2:]


def attend_back_kernel(programs, steps, *refs):
    count = len(programs)
    (position_ref, slot_ref, query_ref, grad_ref, mixed_ref), refs = refs[:5], refs[5:]
    (logsum_ref, table_ref, normed_ref), refs = refs[:3], refs[3:]
    others, refs = refs[:count], refs[count:]
    (grad_query_ref, set_ref, weight_ref), refs = refs[:3], refs[3:]
    other_outs, refs = refs[:count], refs[count:]
    (bias_ref, key_t_ref, kept_ref), scratch = refs[:3], refs[3:]
    chunks = PBLK + 1
    scale = HD**-0.5
    block, head = pl.program_id(0), pl.program_id(1)
    step = pl.program_id(0) * pl.num_programs(1) + pl.program_id(1)
    finish = beside(programs, others, other_outs, scratch, step, steps)

    @pl.when(head == 0)
    def _():
        visible_bias(bias_ref, position_ref[block], chunks)
        set_ref[...] = jnp.zeros_like(set_ref)
        for chunk in range(chunks):
            key_t_ref[chunk] = table_ref[0, slot_ref[block, chunk]].astype(F32).T.astype(BF16)

    query, grad = query_ref[...], grad_ref[...]
    inner = jnp.sum(grad.astype(F32) * mixed_ref[...].astype(F32), axis=1, keepdims=True)
    inner = jnp.broadcast_to(inner, (BLK, HD)).T[:1, :]
    logsum = logsum_ref[0, 0]
    grad_query = jnp.zeros((HD, BLK), F32)
    for chunk in range(chunks):
        cut = slice(chunk * BLK, (chunk + 1) * BLK)
        slot = slot_ref[block, chunk]
        score = rows_by_rows(table_ref[0, slot], query)
        weight = jnp.exp2(score * (scale * LOG2E) + bias_ref[chunk] - logsum)
        grad_weight = rows_by_rows(table_ref[1, slot], grad)
        grad_score = (weight * (grad_weight - inner)).astype(BF16)
        set_ref[0, cut, :HD] += jnp.dot(grad_score, query, preferred_element_type=F32)
        set_ref[0, cut, HD:] += jnp.dot(weight.astype(BF16), grad, preferred_element_type=F32)
        grad_query = grad_query + jnp.dot(
            key_t_ref[chunk], grad_score, preferred_element_type=F32
        )
    grad_query = (grad_query * scale).T.astype(BF16)
    grad_query_ref[...] = grad_query
    kept_ref[block, head] = grad_query

    @pl.when(head == pl.num_programs(1) - 1)
    def _():
        set_ref[0, :, :HD] = set_ref[0, :, :HD] * scale

    def weights():
        blocks, heads = kept_ref.shape[:2]
        kept = [
            jnp.concatenate([kept_ref[b, h] for h in range(heads)], axis=1) for b in range(blocks)
        ]
        kept = jnp.concatenate(kept, axis=0)

        def work(cut):
            weight_ref[cut, :] = by_columns(normed_ref[:, cut], kept).astype(BF16)

        each_columns(weight_ref.shape[0], 256, work)

    finish(weights)


def attend_back(
    queries, grads, mixed, logsums, table, normed, positions, key_slots, programs, arrays, number
):
    rows, width = queries.shape
    blocks, heads = rows // BLK, width // HD
    count = (PBLK + 1) * BLK
    by_head = pl.BlockSpec((BLK, HD), lambda b, h: (b, h))
    out = pl.pallas_call(
        functools.partial(attend_back_kernel, programs, blocks * heads),
        grid=(blocks, heads),
        out_shape=[
            jax.ShapeDtypeStruct((rows, width), BF16),
            jax.ShapeDtypeStruct((blocks, count, 2 * HD), F32),
            jax.ShapeDtypeStruct((normed.shape[1], width), BF16),
        ]
        + [one.out for one in programs],
        in_specs=[
            pl.BlockSpec(memory_space=pltpu.SMEM),
            pl.BlockSpec(memory_space=pltpu.SMEM),
            by_head,
            by_head,
            by_head,
            pl.BlockSpec((1, 1, 1, BLK), lambda b, h: (b, h, 0, 0)),
            pl.BlockSpec(memory_space=pltpu.VMEM),
            pl.BlockSpec(memory_space=pltpu.VMEM),
        ]
        + [one.in_spec for one in programs],
        out_specs=[
            by_head,
            pl.BlockSpec((1, count, 2 * HD), lambda b, h: (b, 0, 0)),
            pl.BlockSpec(memory_space=pltpu.VMEM),
        ]
        + [one.out_spec for one in programs],
        scratch_shapes=[
            pltpu.VMEM((PBLK + 1, BLK, BLK), F32),
            pltpu.VMEM((PBLK + 1, HD, BLK), BF16),
            pltpu.VMEM((blocks, heads, BLK, HD), BF16),
        ]
        + [held for one in programs for held in one.scratch()],
        compiler_params=pltpu.CompilerParams(
            collective_id=number, has_side_effects=True, vmem_limit_bytes=VMEM_BYTES
        ),
        cost_estimate=SMALL,
    )(positions, key_slots, queries, grads, mixed, logsums, table, normed, *arrays)
    return out[0], out[1], out[2], out[3:]


def by_slot_kernel(slot_ref, set_ref, out_ref, table_ref):
    blocks, chunks = slot_ref.shape

    def clear(index, carry):
        table_ref[index] = jnp.zeros(table_ref.shape[1:], F32)
        return carry

    def give(index, carry):
        out_ref[0, index] = table_ref[index, :, :HD].astype(BF16)
        out_ref[1, index] = table_ref[index, :, HD:].astype(BF16)
        return carry

    lax.fori_loop(0, table_ref.shape[0], clear, 0)
    for block in range(blocks):
        for chunk in range(chunks):
            cut = slice(chunk * BLK, (chunk + 1) * BLK)
            table_ref[slot_ref[block, chunk]] += set_ref[block, cut, :]
    lax.fori_loop(0, table_ref.shape[0], give, 0)


def by_slot(sets, key_slots, slot_count):
    return pl.pallas_call(
        by_slot_kernel,
        out_shape=jax.ShapeDtypeStruct((2, slot_count, BLK, HD), BF16),
        in_specs=[
            pl.BlockSpec(memory_space=pltpu.SMEM),
            pl.BlockSpec(memory_space=pltpu.VMEM),
        ],
        out_specs=pl.BlockSpec(memory_space=pltpu.VMEM),
        scratch_shapes=[pltpu.VMEM((slot_count, BLK, 2 * HD), F32)],
        compiler_params=pltpu.CompilerParams(vmem_limit_bytes=VMEM_BYTES),
        cost_estimate=SMALL,
    )(key_slots, sets)


GELU_OUTER = 0.7978845608028654
GELU_INNER = 0.044715


def weight_copies(parts, target, sems):
    copies, start = [], 0
    for number, (ref, rows) in enumerate(parts):
        count = rows.stop - rows.start
        copies.append(
            pltpu.make_async_copy(
                ref.at[:, :, rows], target.at[:, :, start : start + count], sems.at[number]
            )
        )
        start += count
    return copies


def first_half(rows, refs):
    piece, other, early = refs[:3]
    first = piece.shape[2]
    return [(piece, slice(0, first)), (other, slice(0, rows - first))], [(early, slice(0, rows))]


def second_half(rows, refs):
    early, late = refs[2:]
    there = early.shape[2] - rows
    down = [(early, slice(rows, rows + there)), (late, slice(0, rows - there))]
    return down, [(late, slice(rows - there, 2 * rows - there))]


def gelu_both(value, grad_act):
    square = value * value
    bend = jnp.tanh(GELU_OUTER * value * (1.0 + GELU_INNER * square))
    slope = 0.5 * (1.0 + bend) + 0.5 * GELU_OUTER * value * (1.0 - bend * bend) * (
        1.0 + 3.0 * GELU_INNER * square
    )
    return 0.5 * value * (1.0 + bend), grad_act * slope


def forward_kernel(
    x_ref,
    cotangent_ref,
    piece_ref,
    other_ref,
    early_ref,
    shift_ref,
    all_ref,
    act_ref,
    pre_ref,
    part_ref,
    bias_ref,
    weight_grad_ref,
    up_own,
    down_own,
    grads_own,
    rows_own,
    cotangent_own,
    act_own,
    pre_own,
    part_own,
    weight_sem,
    load_sem,
    store_sem,
    own_sem,
    send,
    recv,
):
    me = here()
    steps = (SIDE, FRONT, "tp")
    half, width = x_ref.shape
    hidden = early_ref.shape[3]

    def place(bits):
        at = me
        for k in (2, 1, 0):
            if bits >> k & 1:
                at = flip(at, steps[k])
        return at

    def block(bits):
        return by_plane_slot(all_ref, place(bits))

    def to_step(k, bits):
        source = block(bits) if bits else x_ref
        return remote(
            source, block(bits), send.at[k, bits], recv.at[bits | 1 << k], flip(me, steps[k])
        )

    def arrived(bits):
        remote(block(bits), block(bits), send.at[0, 0], recv.at[bits], me).wait_recv()

    def loads(number):
        slot, copies = number % 2, []
        for side, bits in enumerate((number, number + 4)):
            rows = pl.ds(side * half, half)
            copies.append(
                pltpu.make_async_copy(
                    by_plane_slot(cotangent_ref, place(bits)),
                    cotangent_own.at[slot, rows],
                    load_sem.at[slot, 0, side],
                )
            )
            copies.append(
                pltpu.make_async_copy(
                    block(bits) if bits else x_ref,
                    rows_own.at[slot, rows],
                    load_sem.at[slot, 1, side],
                )
            )
        return copies

    def stores(number, kind):
        slot = number % 2
        source, target = ((act_own, act_ref), (pre_own, pre_ref), (part_own, part_ref))[kind]
        return [
            pltpu.make_async_copy(
                source.at[slot, pl.ds(side * half, half)],
                by_plane_slot(target, place(bits)),
                store_sem.at[slot, kind, side],
            )
            for side, bits in enumerate((number, number + 4))
        ]

    def products(number):
        slot = number % 2
        tile = 256

        def one(index, carry):
            cut = pl.ds(pl.multiple_of(index * tile, tile), tile)
            down = down_own[:, :, :, cut].reshape(width, tile)
            up = up_own[:, :, :, cut].reshape(width, tile)
            grad_act = jnp.dot(cotangent_own[slot], down, preferred_element_type=F32)
            value = jnp.dot(rows_own[slot], up, preferred_element_type=F32)
            value = value + shift_ref[:, cut]
            act, grad_pre = gelu_both(value, grad_act)
            act_own[slot, :, cut] = act.astype(BF16)
            grad_pre = grad_pre.astype(BF16)
            pre_own[slot, :, cut] = grad_pre
            bias_ref[:, cut] += jnp.sum(
                grad_pre.astype(F32).reshape(2 * half // 8, 8, tile), axis=0
            )
            return carry

        lax.fori_loop(0, hidden // tile, one, 0, unroll=True)

    def back(number):
        slot = number % 2
        tile = up_own.shape[1] * up_own.shape[2]

        def one(index, carry):
            cut = pl.ds(pl.multiple_of(index * tile, tile), tile)
            up = up_own[index].reshape(tile, hidden)
            part_own[slot, :, cut] = rows_by_rows(pre_own[slot], up).astype(BF16)
            return carry

        lax.fori_loop(0, width // tile, one, 0, unroll=2)

    def grads(number):
        tile = 256
        shard_rows = weight_grad_ref.shape[2]
        rows = 4 * half

        def one(index, carry):
            cut = pl.ds(pl.multiple_of(index * tile, tile), tile)
            for kind, (left, right) in enumerate(((cotangent_own, act_own), (rows_own, pre_own))):
                grad = by_columns(
                    left[:, :, cut].reshape(rows, tile), right[...].reshape(rows, hidden)
                )
                if number == 1:
                    grads_own[kind, cut, :] = grad
                else:
                    count = tile // shard_rows
                    shards = pl.ds(pl.multiple_of(index * count, count), count)
                    grad = (grads_own[kind, cut, :] + grad).astype(BF16)
                    weight_grad_ref[shards, kind] = grad.reshape(count, shard_rows, hidden)
            return carry

        lax.fori_loop(0, width // tile, one, 0, unroll=2)

    def pass_on(bits, *ways):
        arrived(bits)
        for k in ways:
            to_step(k, bits).start()

    def second():
        to_step(0, 0).wait_send()
        to_step(1, 0).start()

    def third():
        to_step(1, 0).wait_send()
        to_step(1, 1).start()
        pass_on(2, 2)

    between = [second, third, functools.partial(pass_on, 3, 2), lambda: None]
    barrier = pltpu.get_barrier_semaphore()
    for step in steps:
        pl.semaphore_signal(barrier, inc=1, device_id=flip(me, step), device_id_type=MESH_ID)
    pl.semaphore_wait(barrier, 3)
    to_step(0, 0).start()
    to_step(2, 0).start()
    own = pltpu.make_async_copy(x_ref, block(0), own_sem)
    own.start()
    down_parts, up_parts = first_half(up_own.shape[2], (piece_ref, other_ref, early_ref))
    weights = weight_copies(down_parts, down_own, weight_sem)
    weights += weight_copies(up_parts, up_own, weight_sem.at[2:])
    for one in weights:
        one.start()
    bias_ref[...] = jnp.zeros_like(bias_ref)
    for number in range(4):
        if number == 1:
            pass_on(1, 2)
        arrived(4 + number)
        copies = loads(number)
        for one in copies:
            one.start()
        if number == 0:
            for one in weights:
                one.wait()
        if number >= 2:
            for kind in range(3):
                for one in stores(number - 2, kind):
                    one.wait()
        for one in copies:
            one.wait()
        products(number)
        between[number]()
        for kind in range(2):
            for one in stores(number, kind):
                one.start()
        back(number)
        for one in stores(number, 2):
            one.start()
        if number % 2:
            grads(number)
    for number in (2, 3):
        for kind in range(3):
            for one in stores(number, kind):
                one.wait()
    own.wait()
    for k, bits in ((2, 0), (1, 1), (2, 1), (2, 2), (2, 3)):
        to_step(k, bits).wait_send()


def forward_products(rows, cotangent_all, piece, other, early, shift, number):
    half, width = rows.shape
    lines, quarters, _, hidden = early.shape
    weights = (lines, quarters, width // (lines * quarters), hidden)
    anywhere = pl.BlockSpec(memory_space=pl.ANY)
    inside = pl.BlockSpec(memory_space=pltpu.VMEM)
    lead = (2, 2, 2, half)
    return pl.pallas_call(
        forward_kernel,
        out_shape=[
            jax.ShapeDtypeStruct(lead + (width,), BF16),
            jax.ShapeDtypeStruct(lead + (hidden,), BF16),
            jax.ShapeDtypeStruct(lead + (hidden,), BF16),
            jax.ShapeDtypeStruct(lead + (width,), BF16),
            jax.ShapeDtypeStruct((8, hidden), F32),
            jax.ShapeDtypeStruct((lines * quarters, 2, weights[2], hidden), BF16),
        ],
        in_specs=[anywhere] * 5 + [inside],
        out_specs=[anywhere] * 4 + [inside] * 2,
        scratch_shapes=[
            pltpu.VMEM(weights, BF16),
            pltpu.VMEM(weights, BF16),
            pltpu.VMEM((2, width, hidden), F32),
            pltpu.VMEM((2, 2 * half, width), BF16),
            pltpu.VMEM((2, 2 * half, width), BF16),
            pltpu.VMEM((2, 2 * half, hidden), BF16),
            pltpu.VMEM((2, 2 * half, hidden), BF16),
            pltpu.VMEM((2, 2 * half, width), BF16),
            pltpu.SemaphoreType.DMA((3,)),
            pltpu.SemaphoreType.DMA((2, 2, 2)),
            pltpu.SemaphoreType.DMA((2, 3, 2)),
            pltpu.SemaphoreType.DMA(()),
            pltpu.SemaphoreType.DMA((3, 4)),
            pltpu.SemaphoreType.DMA((8,)),
        ],
        compiler_params=pltpu.CompilerParams(
            collective_id=number, has_side_effects=True, vmem_limit_bytes=VMEM_BYTES
        ),
        cost_estimate=SMALL,
    )(rows, cotangent_all, piece, other, early, shift)


CHIPS = ((1, 1), (1, 0), (0, 1), (0, 0))


def second_kernel(
    rows_ref,
    cotangent_ref,
    before_ref,
    rows_columns_ref,
    cotangent_columns_ref,
    act_a_ref,
    piece_ref,
    other_ref,
    early_ref,
    late_ref,
    shift_ref,
    down_part_ref,
    weight_grad_ref,
    bias_ref,
    sum_ref,
    up_own,
    downs,
    acts,
    pre_own,
    rows_own,
    cotangent_own,
    before_own,
    part_own,
    over_core,
    over_front,
    over_side,
    weight_sem,
    load_sem,
    core_send,
    core_recv,
    front_send,
    front_recv,
    side_sem,
):
    step = pl.program_id(0)
    me = here()
    core = me["tp"]
    width, hidden = rows_ref.shape[1], pre_own.shape[1]
    count = rows_ref.shape[0] // 4
    half = count // 2
    tile = 256
    places = (piece_ref, other_ref, early_ref, late_ref)
    shard_rows = up_own.shape[2]

    def chip(number):
        up, side = CHIPS[number]
        fsdp = me["fsdp"] + up * (1 - 2 * me["fsdp"])
        return fsdp, me["pair"] + side * (1 - 2 * me["pair"])

    def rows_of_chip(number):
        fsdp, pair = chip(number)
        return pl.ds(pl.multiple_of((fsdp * 2 + pair) * count, count), count)

    def loads(number):
        slot, rows = number % 2, rows_of_chip(number)
        pairs = ((rows_ref, rows_own), (cotangent_ref, cotangent_own), (before_ref, before_own))
        return [
            pltpu.make_async_copy(source.at[rows], target.at[slot], load_sem.at[slot, kind])
            for kind, (source, target) in enumerate(pairs)
        ]

    def second_weights():
        down_parts, up_parts = second_half(shard_rows, places)
        copies = weight_copies(down_parts, downs.at[1], weight_sem.at[0])
        return copies + weight_copies(up_parts, up_own, weight_sem.at[1])

    def first_weights():
        copies = weight_copies(first_half(shard_rows, places)[0], downs.at[0], weight_sem.at[2])
        return copies + [pltpu.make_async_copy(act_a_ref, acts.at[0], weight_sem.at[1, 1])]

    def to_core(number):
        fsdp, pair = chip(number)
        up, side = CHIPS[number]
        return remote(
            part_own.at[fsdp, pair, 1 - core],
            over_core.at[up, side],
            core_send.at[up, side],
            core_recv.at[up, side],
            flip(me, "tp"),
        )

    def take_core(number):
        fsdp, pair = chip(number)
        to_core(number).wait_recv()
        held = over_core.at[CHIPS[number]]
        add_blocks(held, rows_of(part_own.at[fsdp, pair, core]), rows_of(held), half)

    def to_front(corner):
        source = over_core.at[1, 1] if corner else over_core.at[1 - core, core]
        return remote(
            source, over_front.at[corner], front_send.at[corner], front_recv.at[corner], flip(me, FRONT)
        )

    def to_side():
        return remote(over_front.at[1], over_side, side_sem.at[0], side_sem.at[1], flip(me, SIDE))

    def take_front(corner):
        to_front(corner).wait_recv()
        held = over_front.at[corner]
        mine = over_core.at[core, 1 - core] if corner else over_core.at[0, 0]
        add_blocks(held, rows_of(mine), rows_of(held), half)

    def products(number):
        slot, rows = number % 2, rows_of_chip(number)

        def one(index, carry):
            cut = pl.ds(pl.multiple_of(index * tile, tile), tile)
            down = downs[1, :, :, :, cut].reshape(width, tile)
            up = up_own[:, :, :, cut].reshape(width, tile)
            grad_act = jnp.dot(cotangent_own[slot], down, preferred_element_type=F32)
            value = jnp.dot(rows_own[slot], up, preferred_element_type=F32) + shift_ref[:, cut]
            act, grad_pre = gelu_both(value, grad_act)
            acts[1, rows, cut] = act.astype(BF16)
            grad_pre = grad_pre.astype(BF16)
            pre_own[rows, cut] = grad_pre
            bias_ref[:, cut] += fold_rows(grad_pre.astype(F32))
            return carry

        lax.fori_loop(0, hidden // tile, one, 0, unroll=True)
        tile_back = up_own.shape[1] * shard_rows
        fsdp, pair = chip(number)

        def back(index, carry):
            cut = pl.ds(pl.multiple_of(index * tile_back, tile_back), tile_back)
            up = up_own[index].reshape(tile_back, hidden)
            part = before_own[slot, :, cut].astype(F32) + rows_by_rows(pre_own[rows, :], up)
            part_own[fsdp, pair, :, :, cut] = part.astype(BF16).reshape(2, half, tile_back)
            return carry

        lax.fori_loop(0, width // tile_back, back, 0, unroll=2)

    def chunk_step(number):
        if number == 0:
            barrier = pltpu.get_barrier_semaphore()
            for bits in (1, 2, 4):
                pl.semaphore_signal(
                    barrier, inc=1, device_id=plane_partner(me, bits), device_id_type=MESH_ID
                )
            for one in loads(0) + second_weights() + first_weights():
                one.start()
            bias_ref[...] = jnp.zeros_like(bias_ref)
            for one in second_weights():
                one.wait()
            pl.semaphore_wait(barrier, 3)
        for one in loads(number):
            one.wait()
        if number < 3:
            for one in loads(number + 1):
                one.start()
        products(number)
        to_core(number).start()
        if number > 0:
            take_core(number - 1)
        if number == 1:
            to_front(1).start()
        if number == 2:
            pl.when(core == 0)(lambda: to_front(0).start())
        if number == 3:
            pl.when(core == 1)(lambda: to_front(0).start())
            for one in first_weights():
                one.wait()

    for number in range(4):
        pl.when(step == number)(functools.partial(chunk_step, number))

    @pl.when(step == 4)
    def _():
        take_core(3)

    @pl.when(step == 5)
    def _():
        take_front(1)
        to_side().start()

    @pl.when(step == 9)
    def _():
        take_front(0)

    @pl.when(step >= 4)
    def _():
        rows_here = down_part_ref.shape[0]
        rows = pl.ds(pl.multiple_of((step - 4) * rows_here, rows_here), rows_here)
        shards = weight_grad_ref.shape[0]
        for kind, (left, right) in enumerate(
            ((cotangent_columns_ref, acts.at[1]), (rows_columns_ref, pre_own))
        ):
            grad = by_columns(left[...], right[...]).astype(BF16)
            weight_grad_ref[:, kind] = grad.reshape(shards, shard_rows, hidden)
        part = rows_by_rows(acts[0, rows, :], downs[0].reshape(width, hidden))
        part = part + rows_by_rows(acts[1, rows, :], downs[1].reshape(width, hidden))
        down_part_ref[...] = part.astype(BF16)

    @pl.when(step == pl.num_programs(0) - 1)
    def _():
        to_side().wait_recv()
        final = over_front.at[0]
        add_blocks(sum_ref, rows_of(final), rows_of(over_side), half)
        for number in range(4):
            to_core(number).wait_send()
        for corner in range(2):
            to_front(corner).wait_send()
        to_side().wait_send()


def second_products(rows_all, cotangent_all, before, act_a, pieces, shift, number):
    rows, width = rows_all.shape
    lines, quarters, _, hidden = pieces[-1].shape
    shards, shard_rows = lines * quarters, width // (lines * quarters)
    weights = (lines, quarters, shard_rows, hidden)
    steps, tiles, half = 12, 8, rows // 8

    def tile(i):
        return jnp.maximum(i - 4, 0)

    columns = pl.BlockSpec((rows, width // tiles), lambda i: (0, tile(i)))
    anywhere = pl.BlockSpec(memory_space=pl.ANY)
    fixed = lambda shape: pl.BlockSpec(shape, lambda i: (0,) * len(shape))
    return pl.pallas_call(
        second_kernel,
        grid=(steps,),
        out_shape=[
            jax.ShapeDtypeStruct((rows, width), BF16),
            jax.ShapeDtypeStruct((shards, 2, shard_rows, hidden), BF16),
            jax.ShapeDtypeStruct((8, hidden), F32),
            jax.ShapeDtypeStruct((half, width), F32),
        ],
        in_specs=[anywhere] * 3 + [columns] * 2 + [anywhere] * 5 + [fixed((1, hidden))],
        out_specs=[
            pl.BlockSpec((rows // tiles, width), lambda i: (tile(i), 0)),
            pl.BlockSpec((shards // tiles, 2, shard_rows, hidden), lambda i: (tile(i), 0, 0, 0)),
            fixed((8, hidden)),
            fixed((half, width)),
        ],
        scratch_shapes=[
            pltpu.VMEM(weights, BF16),
            pltpu.VMEM((2,) + weights, BF16),
            pltpu.VMEM((2, rows, hidden), BF16),
            pltpu.VMEM((rows, hidden), BF16),
            pltpu.VMEM((2, 2 * half, width), BF16),
            pltpu.VMEM((2, 2 * half, width), BF16),
            pltpu.VMEM((2, 2 * half, width), BF16),
            pltpu.VMEM((2, 2, 2, half, width), BF16),
            pltpu.VMEM((2, 2, half, width), BF16),
            pltpu.VMEM((2, half, width), BF16),
            pltpu.VMEM((half, width), BF16),
            pltpu.SemaphoreType.DMA((3, 2)),
            pltpu.SemaphoreType.DMA((2, 3)),
            pltpu.SemaphoreType.DMA((2, 2)),
            pltpu.SemaphoreType.DMA((2, 2)),
            pltpu.SemaphoreType.DMA((2,)),
            pltpu.SemaphoreType.DMA((2,)),
            pltpu.SemaphoreType.DMA((2,)),
        ],
        compiler_params=kernel_params(number),
        cost_estimate=SMALL,
    )(rows_all, cotangent_all, before, rows_all, cotangent_all, act_a, *pieces, shift)


def by_columns(left, right):
    return lax.dot_general(left, right, (((0,), (0,)), ((), ())), preferred_element_type=F32)


def reorder_kernel(cuts, size, x_ref, out_ref):
    for index, cut in enumerate(cuts):
        out_ref[:, index * size : (index + 1) * size] = x_ref[:, cut : cut + size]


def reorder(values, cuts):
    size = values.shape[1] // len(cuts)
    if size % 128:
        return jnp.concatenate([values[:, cut : cut + size] for cut in cuts], axis=1)
    return pl.pallas_call(
        functools.partial(reorder_kernel, cuts, size),
        out_shape=jax.ShapeDtypeStruct(values.shape, values.dtype),
        compiler_params=pltpu.CompilerParams(vmem_limit_bytes=VMEM_BYTES),
        cost_estimate=SMALL,
    )(values)


def to_line_order(values):
    lines = lax.axis_size("line")
    size = values.shape[1] // (2 * lines)
    return reorder(
        values, [(half * lines + shard) * size for shard in range(lines) for half in range(2)]
    )


def from_line_order(values):
    lines = lax.axis_size("line")
    size = values.shape[1] // (2 * lines)
    return reorder(
        values, [(shard * 2 + half) * size for half in range(2) for shard in range(lines)]
    )


def meet_sibling(me):
    barrier = pltpu.get_barrier_semaphore()
    pl.semaphore_signal(barrier, inc=1, device_id=flip(me, "tp"), device_id_type=MESH_ID)
    pl.semaphore_wait(barrier, 1)


def half_rows_of(core, rows):
    return pl.ds(pl.multiple_of(core * rows, rows), rows)


def each_rows(total, tile, work):
    def one(index, carry):
        work(pl.ds(pl.multiple_of(index * tile, tile), tile))
        return carry

    lax.fori_loop(0, total // tile, one, 0)


def each_columns(total, tile, work):
    each_rows(total, tile, work)


def moments(values):
    centered = values - jnp.mean(values, axis=1, keepdims=True)
    spread = jnp.mean(centered * centered, axis=1, keepdims=True)
    return centered, lax.rsqrt(spread + EPSILON)


def norm_back(values, gain, grad):
    centered, rstd = moments(values)
    xhat = centered * rstd
    scaled = grad * gain
    inner = jnp.mean(scaled * xhat, axis=1, keepdims=True)
    return xhat, rstd * (scaled - jnp.mean(scaled, axis=1, keepdims=True) - xhat * inner)


def fold_rows(values):
    return jnp.sum(values.reshape(values.shape[0] // 8, 8, values.shape[1]), axis=0)


def shuffled(cuts, ref, rows):
    if cuts is None:
        return ref[rows, :]
    size = ref.shape[1] // len(cuts)
    return jnp.concatenate([ref[rows, cut : cut + size] for cut in cuts], axis=1)


def norm_work(me, refs, out_ref):
    stream_ref, vectors_ref = refs
    gain, shift = vectors_ref[0:1, :], vectors_ref[1:2, :]

    def work(rows):
        centered, rstd = moments(stream_ref[rows, :].astype(F32))
        out_ref[rows, :] = (centered * rstd * gain + shift).astype(BF16)

    each_rows(out_ref.shape[0], 32, work)


def reorder_work(cuts, me, x_ref, out_ref):
    half, size = out_ref.shape[0], out_ref.shape[1] // len(cuts)
    few = 64

    def work(rows):
        start = pl.multiple_of(me["tp"] * half + rows.start, few)
        for index, cut in enumerate(cuts):
            out_ref[rows, index * size : (index + 1) * size] = x_ref[
                pl.ds(start, few), cut : cut + size
            ]

    each_rows(half, few, work)


def part_work(me, refs, out_ref):
    normed_ref, weight_ref, shift_ref = refs
    heads = weight_ref.shape[1] - out_ref.shape[1]
    part = jnp.dot(normed_ref[...], weight_ref[:, heads:], preferred_element_type=F32)
    out_ref[...] = (part + shift_ref[:, heads:]).astype(BF16)


def query_work(me, refs, out_ref):
    normed_ref, weight_ref, shift_ref = refs

    def work(cut):
        query = jnp.dot(normed_ref[...], weight_ref[:, cut], preferred_element_type=F32)
        out_ref[:, cut] = (query + shift_ref[:, cut]).astype(BF16)

    each_columns(out_ref.shape[1], 256, work)


def project_kernel(cuts, programs, *refs):
    own, refs = refs[:5], refs[5:]
    weights, outs, other_out = refs[:2], refs[2:4], refs[4]
    held, scratch = refs[5:8], refs[8:]
    works = schedule(programs, (weights,), (other_out,), scratch, ("tp",))
    for place, work in works:
        if place < 1:
            work()
    project_work(cuts, *own, *outs, *held)
    for place, work in works:
        if place >= 1:
            work()


def project_work(
    cuts,
    mixed_ref,
    proj_a_ref,
    proj_b_ref,
    stream_ref,
    vectors_ref,
    middle_ref,
    normed_ref,
    sent_ref,
    got_ref,
    sems,
):
    me = here()
    half, width = middle_ref.shape
    mine, other = half_rows_of(me["tp"], half), half_rows_of(1 - me["tp"], half)
    tile = 512
    copy = remote(sent_ref, got_ref, sems.at[0], sems.at[1], flip(me, "tp"))

    def part(rows, target):
        def work(cut):
            heads = proj_a_ref.shape[1]
            part = rows_by_rows(mixed_ref[rows, :heads], proj_a_ref[cut, :])
            target[:, cut] = part + rows_by_rows(mixed_ref[rows, heads:], proj_b_ref[cut, :])

        each_columns(width, tile, work)

    part(other, sent_ref)
    copy.start()
    part(mine, middle_ref)
    copy.wait_recv()
    bias, gain, shift = vectors_ref[2:3, :], vectors_ref[3:4, :], vectors_ref[4:5, :]
    few = 32

    def finish(rows):
        start = pl.multiple_of(me["tp"] * half + rows.start, few)
        stream = stream_ref[pl.ds(start, few), :].astype(F32)
        middle = stream + (middle_ref[rows, :] + got_ref[rows, :] + bias)
        middle_ref[rows, :] = middle
        centered, rstd = moments(middle)
        normed = (centered * rstd * gain + shift).astype(BF16)
        if cuts is None:
            normed_ref[rows, :] = normed
            return
        size = width // len(cuts)
        for index, cut in enumerate(cuts):
            normed_ref[rows, index * size : (index + 1) * size] = normed[:, cut : cut + size]

    each_rows(half, few, finish)
    copy.wait_send()


def in_vmem(count):
    return [pl.BlockSpec(memory_space=pltpu.VMEM)] * count


def kernel_params(number):
    return pltpu.CompilerParams(
        collective_id=number, has_side_effects=True, vmem_limit_bytes=VMEM_BYTES
    )


def line_cuts(width, back):
    lines = lax.axis_size("line")
    size = width // (2 * lines)
    if size % 128:
        return None
    if back:
        return [(shard * 2 + half) * size for half in range(2) for shard in range(lines)]
    return [(half * lines + shard) * size for shard in range(lines) for half in range(2)]


def project(mixed, proj_a, proj_b, stream, vectors, exchange, weights, number):
    rows, width = stream.shape
    half = rows // 2
    cuts = line_cuts(width, False)
    middle, normed, moved = pl.pallas_call(
        functools.partial(project_kernel, cuts, [placed(exchange, 0.0, 1.0)]),
        out_shape=[
            jax.ShapeDtypeStruct((half, width), F32),
            jax.ShapeDtypeStruct((half, width), BF16),
            exchange.out,
        ],
        in_specs=in_vmem(5) + [pl.BlockSpec(memory_space=pl.ANY)] * 2,
        out_specs=in_vmem(2) + [exchange.out_spec],
        scratch_shapes=[
            pltpu.VMEM((half, width), F32),
            pltpu.VMEM((half, width), F32),
            pltpu.SemaphoreType.DMA((2,)),
        ]
        + exchange.scratch(),
        compiler_params=kernel_params(number),
        cost_estimate=SMALL,
    )(mixed, proj_a, proj_b, stream, vectors, *weights)
    return middle, normed if cuts else to_line_order(normed), moved


def middle_back_kernel(
    cuts,
    sum_ref,
    middle_ref,
    cotangent_ref,
    mixed_ref,
    proj_a_ref,
    proj_b_ref,
    vectors_ref,
    hidden_a_ref,
    hidden_b_ref,
    grad_middle_ref,
    grad_mixed_ref,
    proj_grad_ref,
    vector_ref,
    attn_ref,
    sums_own,
    sems,
):
    me = here()
    half, width = middle_ref.shape
    mine, other = half_rows_of(me["tp"], half), half_rows_of(1 - me["tp"], half)
    few = 32
    gain = vectors_ref[3:4, :]
    meet_sibling(me)
    sums_own[...] = jnp.zeros_like(sums_own)

    def norm(rows):
        start = pl.multiple_of(me["tp"] * half + rows.start, few)
        cotangent = cotangent_ref[pl.ds(start, few), :].astype(F32)
        grad = shuffled(cuts, sum_ref, rows)
        xhat, back = norm_back(middle_ref[rows, :], gain, grad)
        grad_middle = cotangent + back
        grad_middle_ref[rows, :] = grad_middle
        attn = grad_middle.astype(BF16)
        attn_ref[pl.ds(start, few), :] = attn
        sums_own[0] += fold_rows(grad * xhat)
        sums_own[1] += fold_rows(grad)
        sums_own[2] += fold_rows(attn.astype(F32))
        sums_own[3] += fold_rows(cotangent)

    each_rows(half, few, norm)
    copy = remote(attn_ref.at[mine], attn_ref.at[mine], sems.at[0], sems.at[1], flip(me, "tp"))
    copy.start()

    def to_heads(rows):
        for number, proj_ref in enumerate((proj_a_ref, proj_b_ref)):
            heads = proj_ref.shape[1]
            grad_ref = grad_mixed_ref.at[:, number * heads : (number + 1) * heads]

            def work(cut):
                grad = jnp.dot(attn_ref[rows, :], proj_ref[:, cut], preferred_element_type=F32)
                grad_ref[rows, cut] = grad.astype(BF16)

            each_columns(heads, 256, work)

    to_heads(mine)
    vector_ref[...] = jnp.zeros_like(vector_ref)
    for kind in range(4):
        vector_ref[2 + kind : 3 + kind, :] = jnp.sum(sums_own[kind], axis=0, keepdims=True)
    size = hidden_a_ref.shape[1]
    for number, hidden_ref in enumerate((hidden_a_ref, hidden_b_ref)):
        start = width - (2 - number) * size
        vector_ref[6:7, start : start + size] = jnp.sum(hidden_ref[...], axis=0, keepdims=True)
    copy.wait_recv()
    to_heads(other)

    def weight(cut):
        grad = lax.dot_general(
            attn_ref[:, cut], mixed_ref[...], (((0,), (0,)), ((), ())), preferred_element_type=F32
        )
        proj_grad_ref[cut, :] = grad.astype(BF16)

    each_columns(width, 256, weight)
    copy.wait_send()


def middle_back(grad_sum, middle, cotangent, mixed, proj_a, proj_b, vectors, hidden_a, hidden_b, number):
    rows, width = cotangent.shape
    half, heads = rows // 2, mixed.shape[1]
    cuts = line_cuts(width, True)
    return pl.pallas_call(
        functools.partial(middle_back_kernel, cuts),
        out_shape=[
            jax.ShapeDtypeStruct((half, width), F32),
            jax.ShapeDtypeStruct((rows, heads), BF16),
            jax.ShapeDtypeStruct((width, heads), BF16),
            jax.ShapeDtypeStruct((8, width), F32),
        ],
        in_specs=in_vmem(9),
        out_specs=in_vmem(4),
        scratch_shapes=[
            pltpu.VMEM((rows, width), BF16),
            pltpu.VMEM((4, 8, width), F32),
            pltpu.SemaphoreType.DMA((2,)),
        ],
        compiler_params=kernel_params(number),
        cost_estimate=SMALL,
    )(
        grad_sum if cuts else from_line_order(grad_sum),
        middle,
        cotangent,
        mixed,
        proj_a,
        proj_b,
        vectors,
        hidden_a,
        hidden_b,
    )


def first_back_kernel(cuts, programs, *refs):
    (
        grad_query_ref,
        grad_part_ref,
        first_ref,
        stream_ref,
        normed_ref,
        vectors_ref,
        grad_middle_ref,
        mlp_ref,
        middle_ref,
        early_ref,
        cut_b_ref,
    ), refs = refs[:11], refs[11:]
    (input_ref, layer_ref, mlp_out, part_out, total_out), refs = refs[:5], refs[5:]
    (weight_ref, vector_ref, sent_ref, got_ref, grad_first_ref, held_ref, sems), scratch = refs[:7], refs[7:]
    me = here()
    rows, width = stream_ref.shape
    half, heads = rows // 2, grad_query_ref.shape[1]
    shard_rows = part_out.shape[0]
    mine, other = half_rows_of(me["tp"], half), half_rows_of(1 - me["tp"], half)
    few = 32
    sibling = flip(me, "tp")
    works = schedule(
        programs,
        (
            cut_b_ref,
            weight_ref.reshape(2, -1, 2, shard_rows, weight_ref.shape[1]),
            vector_ref,
        ),
        (mlp_out, part_out, total_out),
        scratch,
        ("tp",),
    )

    def run_until(stop):
        while works and works[0][0] < stop:
            works.pop(0)[1]()

    run_until(0.1)
    grad_first_ref[:, :heads] = grad_query_ref[...]
    grad_first_ref[:, heads:] = grad_part_ref[...].astype(BF16)

    def weight(cut):
        grad = lax.dot_general(
            normed_ref[:, cut],
            grad_first_ref[:, heads:],
            (((0,), (0,)), ((), ())),
            preferred_element_type=F32,
        )
        weight_ref[cut, :] = grad.astype(BF16)

    each_columns(width, 512, weight)
    run_until(0.2)

    def part(at, target):
        def work(cut):
            target[:, cut] = rows_by_rows(grad_first_ref[at, :], first_ref[cut, :])

        each_columns(width, 512, work)

    part(other, sent_ref)
    sums_copy = remote(sent_ref, got_ref, sems.at[0], sems.at[1], sibling)
    sums_copy.start()
    run_until(0.3)
    bias = vectors_ref[5:6, :]

    def layer(at):
        start = pl.multiple_of(me["tp"] * half + at.start, few)
        out = middle_ref[at, :] + (shuffled(cuts, mlp_ref, at) + bias)
        layer_ref[pl.ds(start, few), :] = out.astype(BF16)

    each_rows(half, few, layer)
    layer_copy = remote(layer_ref.at[mine], layer_ref.at[mine], sems.at[2], sems.at[3], sibling)
    layer_copy.start()
    run_until(0.4)
    grad_own, folded = held_ref.at[0], held_ref.at[1]
    part(mine, grad_own)
    run_until(0.5)
    sums_copy.wait_recv()
    gain = vectors_ref[0:1, :]
    folded[0:16, :] = jnp.zeros((16, width), F32)

    def norm(at):
        start = pl.multiple_of(me["tp"] * half + at.start, few)
        grad = grad_own[at, :] + got_ref[at, :]
        xhat, back = norm_back(stream_ref[pl.ds(start, few), :].astype(F32), gain, grad)
        input_ref[pl.ds(start, few), :] = (grad_middle_ref[at, :] + back).astype(BF16)
        folded[0:8, :] += fold_rows(grad * xhat)
        folded[8:16, :] += fold_rows(grad)

    each_rows(half, few, norm)
    input_copy = remote(input_ref.at[mine], input_ref.at[mine], sems.at[4], sems.at[5], sibling)
    input_copy.start()
    vector_ref[...] = early_ref[...]
    for kind in range(2):
        total = jnp.sum(folded[kind * 8 : kind * 8 + 8, :], axis=0, keepdims=True)
        vector_ref[kind : kind + 1, :] = total
    vector_ref[6:7, :heads] = jnp.sum(
        fold_rows(grad_query_ref[...].astype(F32)), axis=0, keepdims=True
    )
    part_sums = jnp.sum(
        fold_rows(grad_first_ref[:, heads:].astype(F32)), axis=0, keepdims=True
    )
    vector_ref[7:8, : part_sums.shape[1]] = jnp.where(me["tp"] == 1, part_sums, 0.0)
    run_until(2.0)
    layer_copy.wait()
    input_copy.wait()
    sums_copy.wait_send()


def first_back(
    grad_query,
    grad_part,
    first_all,
    stream,
    normed,
    vectors,
    grad_middle,
    mlp_sum,
    middle,
    early,
    cut_b,
    number,
):
    rows, width = stream.shape
    half, heads, part = rows // 2, grad_query.shape[1], grad_part.shape[1]
    lines = lax.axis_size("line")
    cuts = line_cuts(width, True)
    shard_rows = width // (4 * lines)
    vector = early.shape
    programs = [
        placed(return_half(cut_b, BF16), 0.0, 1.0),
        placed(Direct(lines, shard_rows, part, part), 0.1, 0.95),
        placed(Total(vector, lines, 6, heads), 0.9, 0.93, 0.97),
    ]
    anywhere = [pl.BlockSpec(memory_space=pl.ANY)]
    return pl.pallas_call(
        functools.partial(first_back_kernel, cuts, programs),
        out_shape=[
            jax.ShapeDtypeStruct((rows, width), BF16),
            jax.ShapeDtypeStruct((rows, width), BF16),
        ]
        + [one.out for one in programs],
        in_specs=in_vmem(10) + anywhere,
        out_specs=in_vmem(2) + [one.out_spec for one in programs],
        scratch_shapes=[
            pltpu.VMEM((width, part), BF16),
            pltpu.VMEM(vector, F32),
            pltpu.VMEM((half, width), F32),
            pltpu.VMEM((half, width), F32),
            pltpu.VMEM((rows, heads + part), BF16),
            pltpu.VMEM((2, half, width), F32),
            pltpu.SemaphoreType.DMA((6,)),
        ]
        + [held for one in programs for held in one.scratch()],
        compiler_params=kernel_params(number),
        cost_estimate=SMALL,
    )(
        grad_query,
        grad_part,
        first_all,
        stream,
        normed,
        vectors,
        grad_middle,
        mlp_sum if cuts else from_line_order(mlp_sum),
        middle,
        early,
        cut_b,
    )


def body(
    hidden_in,
    block_order,
    attn_norm_gain,
    attn_norm_bias,
    query_weight,
    query_bias,
    keyval_weight,
    value_bias,
    proj_weight,
    proj_bias,
    mlp_norm_gain,
    mlp_norm_bias,
    up_weight,
    up_bias,
    down_weight,
    down_bias,
    out_cotangent,
):
    rows_dev = hidden_in.shape[0]
    half_rows = rows_dev // 2
    width = hidden_in.shape[1]
    blocks_dev = rows_dev // BLK
    slot_count = block_order.shape[1]
    group_blocks = PBLK + CONTS
    heads_dev = query_bias.shape[0] // HD
    head_width = heads_dev * HD
    core = lax.axis_index("tp")
    quarter = lax.axis_index("fsdp") * lax.axis_size("pair") + lax.axis_index("pair")
    quarters = lax.axis_size("fsdp") * lax.axis_size("pair")
    hidden_dev = up_weight.shape[1] // quarters

    def own_half(values):
        return lax.dynamic_slice_in_dim(values, core * half_rows, half_rows, axis=0)

    def in_order(mine, other, axis=0):
        first = jnp.where(core == 0, mine, other)
        second = jnp.where(core == 0, other, mine)
        return jnp.concatenate([first, second], axis=axis)


    slot_ids = jnp.arange(slot_count, dtype=jnp.int32)
    ordering = block_order[0]
    inverse = jnp.sum(
        jnp.where(ordering[None, :] == slot_ids[:, None], slot_ids[None, :], 0), axis=1
    )
    ctx_index = lax.axis_index("line") * lax.axis_size("pair") + lax.axis_index("pair")
    first_slot = ctx_index * blocks_dev
    my_slots = first_slot + jnp.arange(blocks_dev, dtype=jnp.int32)
    my_blocks = lax.dynamic_slice_in_dim(ordering, first_slot, blocks_dev)
    positions = my_blocks % group_blocks
    group_base = my_blocks // group_blocks * group_blocks
    prompt_slots = jnp.take(
        inverse, group_base[:, None] + jnp.arange(PBLK, dtype=jnp.int32)[None, :]
    )
    key_slots = jnp.concatenate([prompt_slots, my_slots[:, None]], axis=1)

    vectors = [
        attn_norm_gain,
        attn_norm_bias,
        proj_bias,
        mlp_norm_gain,
        mlp_norm_bias,
        down_bias,
    ]
    vectors = jnp.stack(vectors + [jnp.zeros_like(down_bias)] * 2).astype(F32)

    keyval_cut = lax.dynamic_slice_in_dim(keyval_weight, core * HD, HD, axis=1)
    first_cut = jnp.concatenate([query_weight, keyval_cut], axis=1)
    shard_rows = down_weight.shape[0]
    hidden_half = hidden_dev // 2
    columns = down_weight.shape[1]
    first_rows = shard_rows // 2
    early_rows = shard_rows // 2
    cuts = line_cuts(width, False)
    lines = lax.axis_size("line")
    first_pieces = [(0, slice(0, first_rows), 0)]
    other_pieces = [(0, slice(first_rows, shard_rows), 0)]
    early_pieces = [(1, slice(0, shard_rows), 0), (0, slice(0, early_rows), 1)]
    late_pieces = [(0, slice(early_rows, shard_rows), 1), (1, slice(0, shard_rows), 1)]
    hops = [0.1 * k for k in range(1, 4)] if lines == 4 else spaced(0.1, 0.3, lines - 1)
    levels = spaced(0.4, 0.98, 2 * lines)
    piece_hops = spaced(0.35, 0.75, lines - 1)
    _, first_all, other_cut, early_cut, mlp_piece, normed_one, cotangent_line, proj_line = run_programs(
        [
            placed(spread_halves(first_pieces, columns, BF16), 0.0, 0.05),
            placed(rows_gather(first_cut), 0.01, *hops, *levels, 1.0),
            placed(spread_halves(other_pieces, columns, BF16), 0.06, 1.0),
            placed(spread_halves(early_pieces, columns, BF16), 0.06, 1.0),
            placed(line_gather((quarters, first_rows, hidden_half), BF16), 0.07, *piece_hops, 1.0),
            placed(Work(norm_work, hidden_in.shape, BF16), 0.31, 0.31),
            placed(Work(functools.partial(reorder_work, cuts or [0]), (half_rows, width), BF16), 0.32, 0.32),
            placed(line_gather(proj_weight.shape, BF16), 0.305, *spaced(0.48, 0.88, lines - 1), 1.0),
        ],
        [
            lambda more, outs: more[3:5],
            lambda more, outs: more[5],
            lambda more, outs: more[3:5],
            lambda more, outs: more[3:5],
            lambda more, outs: outs[0],
            lambda more, outs: more[:2],
            lambda more, outs: more[2],
            lambda more, outs: more[6],
        ],
        1,
        near=[hidden_in, vectors, out_cotangent],
        far=[down_weight, up_weight, first_cut, proj_weight],
    )
    if cuts is None:
        cotangent_line = to_line_order(own_half(out_cotangent))
    first_all = flat(first_all)

    value_shift = jnp.where(core == 1, value_bias.astype(F32), 0.0)
    first_shift = jnp.concatenate([query_bias.astype(F32), value_shift])
    part_like = (rows_dev, HD)
    head_half = head_width // 2
    half_line = jax.ShapeDtypeStruct((lines, shard_rows, head_half), BF16)
    _, query_low, keyval_every, mlp_other, proj_a = run_programs(
        [
            placed(Work(part_work, part_like, BF16), 0.0, 0.0),
            placed(Work(query_work, (rows_dev, head_width), BF16), 0.2, 0.2),
            placed(ctx_gather(part_like, BF16), 0.1, *spaced(0.25, 0.5, lines - 1), *spaced(0.52, 0.9, 2 * lines), 1.0),
            placed(
                line_gather((quarters, shard_rows - first_rows, hidden_half), BF16),
                0.11,
                *spaced(0.3, 0.62, lines - 1),
                1.0,
            ),
            placed(columns_gather(half_line), 0.001, 0.45, 0.85, 1.0),
        ],
        [
            lambda more, outs: more[:3],
            lambda more, outs: more[:3],
            lambda more, outs: outs[0],
            lambda more, outs: more[3],
            lambda more, outs: more[4].at[:, :, :head_half],
        ],
        4,
        near=[normed_one, first_all, first_shift[None]],
        far=[other_cut, proj_line],
    )
    keyval_every, early_cut = lax.optimization_barrier((keyval_every, early_cut))
    mlp_early = lax.all_gather(early_cut, "line", axis=0, tiled=False)
    table = keyval_every.reshape(2, slot_count, BLK, HD)
    mixed_low, logsums, (proj_b, cotangent_all) = attend(
        query_low,
        table,
        positions,
        key_slots,
        [
            placed(columns_gather(half_line), 0.0, 0.9, 1.0, 1.0),
            placed(plane_gather(cotangent_line), 0.0, 0.9, 1.0, 1.0),
        ],
        [proj_line[:, :, head_half:], cotangent_line],
        2,
    )
    proj_a, proj_b = flat(proj_a), flat(proj_b)
    mixed_low, mlp_early = lax.optimization_barrier((mixed_low, mlp_early))
    middle, normed_two_line, late_cut = project(
        mixed_low,
        proj_a,
        proj_b,
        hidden_in,
        vectors,
        spread_halves(late_pieces, columns, BF16),
        (down_weight, up_weight),
        5,
    )
    mlp_late = lax.all_gather(late_cut, "line", axis=0, tiled=False)

    up_shift = lax.dynamic_slice_in_dim(up_bias, quarter * hidden_dev, hidden_dev).astype(F32)
    up_shift = up_shift[None]
    rows_all, act_a, pre_a, back_a, bias_a, weight_grad_a = forward_products(
        normed_two_line, cotangent_all, mlp_piece, mlp_other, mlp_early, up_shift[:, :hidden_half], 6
    )
    rows_all, act_a, pre_a, back_a = flat(rows_all), flat(act_a), flat(pre_a), flat(back_a)
    cotangent_all = flat(cotangent_all)
    cut_a = lax.psum_scatter(weight_grad_a, "line", scatter_dimension=0, tiled=True)
    rows_all, weight_grad_a = lax.optimization_barrier((rows_all, weight_grad_a))
    down_part, weight_grad_b, bias_b, grad_normed_two = second_products(
        rows_all,
        cotangent_all,
        back_a,
        act_a,
        (mlp_piece, mlp_other, mlp_early, mlp_late),
        up_shift[:, hidden_half:],
        7,
    )
    cut_b = lax.psum_scatter(weight_grad_b, "line", scatter_dimension=0, tiled=True)
    cut_a = cut_a.reshape(quarters, 2 * shard_rows, hidden_half)
    cut_b = cut_b.reshape(quarters, 2 * shard_rows, hidden_half)

    grad_middle, grad_mixed, proj_weight_grad, vector = middle_back(
        grad_normed_two, middle, out_cotangent, mixed_low, proj_a, proj_b, vectors, bias_a, bias_b, 8
    )
    grad_mixed, cut_a = lax.optimization_barrier((grad_mixed, cut_a))
    sum_proj, proj_parts = rows_sum(proj_weight_grad)
    sum_down, down_parts = plane_sum(down_part)
    grad_query, grad_sets, query_weight_grad, (grad_proj_weight, mlp_out) = attend_back(
        query_low,
        grad_mixed,
        mixed_low,
        logsums,
        table,
        normed_one,
        positions,
        key_slots,
        [
            placed(sum_proj, 0.0, *spaced(0.13, 0.51, lines), 0.63, 1.06),
            placed(sum_down, 0.0, 0.45, 0.45, 0.45, 0.45, 0.76, 0.95, 1.1, 1.2),
        ],
        [proj_parts, down_parts],
        3,
    )
    grad_table = by_slot(grad_sets, key_slots, slot_count)
    grad_parts = grad_table.reshape(2, lines, 2 * rows_dev, HD)
    along_line, over_pair = ctx_sums(grad_parts)
    sum_query, query_parts = rows_sum(query_weight_grad)
    _, grad_part, grad_query_weight, mlp_grad_a = run_programs(
        [
            placed(along_line, 0.01, 0.75),
            placed(over_pair, 0.76, 0.86, 0.97),
            placed(sum_query, 0.0, 1.0),
            placed(return_half(cut_a, BF16), 0.02, 1.0),
        ],
        [
            grad_parts,
            lambda more, outs: outs[0].reshape(2, rows_dev, HD),
            query_parts,
            cut_a,
        ],
        12,
    )
    input_grad, layer_out, mlp_grad_b, grad_part_weight, summed = first_back(
        grad_query,
        grad_part,
        first_all,
        hidden_in,
        normed_one,
        vectors,
        grad_middle,
        mlp_out,
        middle,
        vector,
        cut_b,
        9,
    )
    grad_down_weight, grad_up_weight = widen(mlp_grad_a, mlp_grad_b)
    grad_keyval_weight = in_order(grad_part_weight[:, :HD], grad_part_weight[:, HD:], axis=1)
    sum_up = summed[:quarters, width : 2 * width - head_width].reshape(quarters * hidden_dev)
    return (
        layer_out,
        input_grad,
        summed[0, :width],
        summed[1, :width],
        grad_query_weight,
        summed[6, :head_width],
        grad_keyval_weight,
        summed[7, :HD],
        grad_proj_weight,
        summed[4, :width],
        summed[2, :width],
        summed[3, :width],
        grad_up_weight,
        sum_up,
        grad_down_weight,
        summed[5, :width],
    )


def solution(mesh):
    fsdp, ctx, tp = mesh.devices.shape
    grid = Mesh(mesh.devices.reshape(fsdp, ctx // 2, 2, tp), EVERY)
    by_rows = P(ROWS, None)
    by_both = P(ROWS, "tp")
    return jax.shard_map(
        body,
        mesh=grid,
        in_specs=(
            by_rows,
            P("fsdp", None),
            P(),
            P(),
            by_both,
            P("tp"),
            by_rows,
            P(),
            by_both,
            P(),
            P(),
            P(),
            by_both,
            P("tp"),
            by_both,
            P(),
            by_rows,
        ),
        out_specs=(
            by_rows,
            by_rows,
            P(),
            P(),
            by_both,
            P("tp"),
            by_rows,
            P(),
            by_both,
            P(),
            P(),
            P(),
            by_both,
            P("tp"),
            by_both,
            P(),
        ),
        check_vma=False,
    )
```

```python
import functools

import jax
import jax.numpy as jnp
from jax import lax
from jax.experimental import pallas as pl
from jax.experimental.pallas import tpu as pltpu
from jax.sharding import Mesh, PartitionSpec as P

HD = 128
BLK = 256
PBLK = 8
CONTS = 8
EPSILON = 1e-05
MASKED = -1e30
F32 = jnp.float32
BF16 = jnp.bfloat16
ROWS = ("fsdp", "line", "pair")
EVERY = ("fsdp", "line", "pair", "tp")


MESH_ID = pl.DeviceIdType.MESH
VMEM_BYTES = 60 * 1024 * 1024
SMALL = pl.CostEstimate(flops=1, bytes_accessed=1, transcendentals=0)
SIDE = ("pair", "fsdp")
FRONT = ("fsdp", "pair")


def here():
    return {name: lax.axis_index(name) for name in EVERY}


def flip(place, step):
    place = dict(place)
    if isinstance(step, str):
        place[step] = 1 - place[step]
    else:
        core = place["tp"]
        for name, used in ((step[0], 1 - core), (step[1], core)):
            place[name] = place[name] + (1 - 2 * place[name]) * used
    return place


def along(place, amount):
    return dict(place, line=place["line"] + amount)


def remote(source, target, send_sem, recv_sem, place):
    return pltpu.make_async_remote_copy(
        src_ref=source,
        dst_ref=target,
        send_sem=send_sem,
        recv_sem=recv_sem,
        device_id=place,
        device_id_type=MESH_ID,
    )


def top_bit(bits):
    return bits.bit_length() - 1


def add_blocks(target, first, second, rows):
    tile = min(rows, 64)

    def one(index, carry):
        cut = pl.ds(pl.multiple_of(index * tile, tile), tile)
        total = first(cut).astype(F32)
        if second is not None:
            total = total + second(cut).astype(F32)
        target[cut, :] = total.astype(target.dtype)
        return carry

    lax.fori_loop(0, rows // tile, one, 0)


def rows_of(ref):
    return lambda cut: ref[cut, :]


class Gather:
    def __init__(self, values, steps, lines, shape, slot):
        self.steps, self.lines, self.slot = steps, lines, slot
        self.out = jax.ShapeDtypeStruct(shape, values.dtype)
        self.in_spec = self.out_spec = pl.BlockSpec(memory_space=pl.ANY)

    def scratch(self):
        parts = 1 << len(self.steps)
        return [
            pltpu.SemaphoreType.DMA(()),
            pltpu.SemaphoreType.DMA((2, self.lines)),
            pltpu.SemaphoreType.DMA((self.lines,)),
            pltpu.SemaphoreType.DMA((self.lines, max(1, len(self.steps)) * parts)),
            pltpu.SemaphoreType.DMA((self.lines, parts)),
        ]

    def stages(self, me, x_ref, out_ref, own_sem, line_send, line_recv, send, recv):
        steps, lines, slot = self.steps, self.lines, self.slot
        count = len(steps)
        my_line = me["line"] if lines > 1 else 0

        def block(bits, shard):
            place = me
            for k in reversed(range(count)):
                if bits >> k & 1:
                    place = flip(place, steps[k])
            return slot(out_ref, dict(place, line=shard))

        def to_step(k, bits, shard, source):
            return remote(
                source,
                block(bits, shard),
                send.at[shard, k * (1 << count) + bits],
                recv.at[shard, bits | 1 << k],
                flip(me, steps[k]),
            )

        def to_line(amount, shard, source):
            return remote(
                source,
                block(0, shard),
                line_send.at[(amount + 1) // 2, shard],
                line_recv.at[shard],
                along(me, amount),
            )

        def send_on(bits, shard, source):
            for k in range(top_bit(bits) + 1, count):
                to_step(k, bits, shard, source).start()

        def at_distance(distance, work):
            if distance == 0:
                work(my_line, 0)
                return
            for amount in (1, -1):
                shard = my_line - amount * distance
                pl.when((shard >= 0) & (shard < lines))(functools.partial(work, shard, amount))

        def line_inside(amount):
            there = my_line + amount
            return (there >= 0) & (there < lines)

        own = pltpu.make_async_copy(x_ref, block(0, my_line), own_sem)

        def begin():
            if lines > 1:
                for amount in (1, -1):
                    pl.when(line_inside(amount))(
                        lambda amount=amount: to_line(amount, my_line, x_ref).start()
                    )
            send_on(0, my_line, x_ref)
            own.start()

        def line_arrival(shard, amount):
            remote(
                block(0, shard), block(0, shard), line_send.at[0, shard], line_recv.at[shard], me
            ).wait_recv()
            pl.when(line_inside(amount))(lambda: to_line(amount, shard, block(0, shard)).start())
            send_on(0, shard, block(0, shard))

        def level_arrival(level, shard, amount):
            for bits in range(1 << level, 2 << level):
                remote(
                    block(bits, shard),
                    block(bits, shard),
                    send.at[shard, 0],
                    recv.at[shard, bits],
                    me,
                ).wait_recv()
                send_on(bits, shard, block(bits, shard))

        def end():
            own.wait()
            if lines > 1:
                for amount in (1, -1):
                    for distance in range(lines):
                        shard = my_line - amount * distance
                        pl.when((shard >= 0) & (shard < lines) & line_inside(amount))(
                            lambda amount=amount, shard=shard: to_line(
                                amount, shard, block(0, shard)
                            ).wait_send()
                        )
            for shard in range(lines):
                for bits in range(1 << count):
                    for k in range(top_bit(bits) + 1, count):
                        to_step(k, bits, shard, block(bits, shard)).wait_send()

        line = [functools.partial(at_distance, number, line_arrival) for number in range(1, lines)]
        levels = [
            functools.partial(at_distance, number - level, functools.partial(level_arrival, level))
            for number in range(lines + count - 1)
            for level in range(count)
            if 0 <= number - level < lines
        ]
        return [begin] + line + levels + [end]


class Sum:
    far_line = True

    def __init__(self, steps, lines, rows, columns, slot, kind=F32):
        self.steps, self.lines, self.rows, self.columns = steps, lines, rows, columns
        self.slot = slot
        self.out = jax.ShapeDtypeStruct((rows, columns), kind)
        self.in_spec = pl.BlockSpec(memory_space=pl.ANY)
        self.out_spec = pl.BlockSpec(memory_space=pltpu.VMEM)

    def scratch(self):
        count, lines = len(self.steps), self.lines
        sizes = [1 << (count - 1 - k) for k in range(count)]
        block = (self.rows, self.columns)
        return (
            [pltpu.VMEM((lines, sizes[0]) + block, BF16)]
            + [pltpu.VMEM((lines, size) + block, BF16) for size in sizes]
            + [pltpu.VMEM((lines,) + (block if lines > 1 else (16, 128)), BF16)]
            + [pltpu.SemaphoreType.DMA((lines, sizes[0]))]
            + [pltpu.SemaphoreType.DMA((lines, size)) for size in sizes] * 2
            + [pltpu.SemaphoreType.DMA((lines,))] * 2
        )

    def stages(self, me, x_ref, out_ref, own, *rest):
        steps, lines, rows, slot = self.steps, self.lines, self.rows, self.slot
        count = len(steps)
        held, rest = rest[:count], rest[count:]
        on_line, own_sem, rest = rest[0], rest[1], rest[2:]
        send, recv = rest[:count], rest[count : 2 * count]
        line_send, line_recv = rest[2 * count :]
        my_line = me["line"] if lines > 1 else 0
        last = count - 1

        def target_of(bits, shard):
            place = me
            for k in range(count):
                if bits >> k & 1:
                    place = flip(place, steps[k])
            return dict(place, line=shard)

        def store(k, shard, bits):
            return held[k].at[shard, bits >> (k + 1)]

        def own_copy(shard, bits):
            return pltpu.make_async_copy(
                slot(x_ref, target_of(bits, shard)),
                own.at[shard, bits >> 1],
                own_sem.at[shard, bits >> 1],
            )

        def copy(k, shard, bits):
            source = slot(x_ref, target_of(bits, shard)) if k == 0 else store(k - 1, shard, bits)
            return remote(
                source,
                store(k, shard, bits ^ (1 << k)),
                send[k].at[shard, bits >> (k + 1)],
                recv[k].at[shard, bits >> (k + 1)],
                flip(me, steps[k]),
            )

        def parts_of(k):
            return [high << (k + 1) for high in reversed(range(1 << (count - 1 - k)))]

        def send_first(shard, amount):
            for bits in parts_of(0):
                copy(0, shard, bits | 1).start()

        def own_first(shard, amount):
            for bits in parts_of(0):
                own_copy(shard, bits).start()

        def take_step(k, shard, amount, parts=None):
            for bits in parts or parts_of(k):
                copy(k, shard, bits | 1 << k).wait_recv()
                arrived = store(k, shard, bits)
                if k == 0:
                    own_copy(shard, bits).wait()
                    mine = own.at[shard, bits >> 1]
                else:
                    mine = store(k - 1, shard, bits)
                add_blocks(arrived, rows_of(mine), rows_of(arrived), rows)
                if k + 1 < count and bits >> (k + 1) & 1:
                    copy(k + 1, shard, bits).start()

        def line_copy(shard):
            return remote(
                held[last].at[shard, 0],
                on_line.at[my_line],
                line_send.at[shard],
                line_recv.at[my_line],
                along(me, shard - my_line),
            )

        def each(distance, work):
            if distance == 0:
                work(my_line, 0)
                return
            for amount in (1, -1):
                shard = my_line + amount * distance
                pl.when((shard >= 0) & (shard < lines))(functools.partial(work, shard, amount))

        order = list(reversed(range(lines)))

        def begin():
            for distance in order:
                each(distance, send_first)
            for distance in order:
                each(distance, own_first)

        def tick(number):
            for k in reversed(range(count)):
                index = number - k
                if 0 <= index < lines:
                    each(order[index], functools.partial(take_step, k))
                    if k == last and order[index] > 0:
                        each(order[index], lambda shard, amount: line_copy(shard).start())

        def end():
            final = held[last].at[my_line, 0]
            if lines == 1:
                add_blocks(out_ref, rows_of(final), None, rows)
            else:
                add_blocks(on_line.at[my_line], rows_of(final), None, rows)

                def arrived(shard, amount):
                    remote(
                        on_line.at[shard], on_line.at[shard], line_send.at[0], line_recv.at[shard], me
                    ).wait_recv()

                for distance in range(1, lines):
                    each(distance, arrived)
                add_blocks(
                    out_ref,
                    lambda cut: sum(on_line[shard, cut, :].astype(F32) for shard in range(lines)),
                    None,
                    rows,
                )
                for distance in range(1, lines):
                    each(distance, lambda shard, amount: line_copy(shard).wait_send())
            for k in range(count):
                for shard in range(lines):
                    for bits in parts_of(k):
                        copy(k, shard, bits | 1 << k).wait_send()

        if lines == 1:
            ticks = [
                functools.partial(take_step, k, 0, 0, [bits]) for k in range(count) for bits in parts_of(k)
            ]
        else:
            ticks = [functools.partial(tick, number) for number in range(lines + count - 1)]
        return [begin] + ticks + [end]


DIRECT = (("pair",), ("fsdp",), ("pair", "fsdp"))


def move(me, names):
    place = me
    for name in names:
        place = flip(place, name)
    return place


def quarter_of(place):
    return place["fsdp"] * 2 + place["pair"]


class Exchange:
    steps, lines = ("pair", "fsdp"), 1

    def __init__(self, moves, shape, kind):
        self.moves = moves
        self.out = jax.ShapeDtypeStruct(shape, kind)
        self.in_spec = self.out_spec = pl.BlockSpec(memory_space=pl.ANY)

    def scratch(self):
        count = len(self.moves)
        return [
            pltpu.SemaphoreType.DMA((count,)),
            pltpu.SemaphoreType.DMA((count, 3)),
            pltpu.SemaphoreType.DMA((count, 3)),
        ]

    def stages(self, me, x_refs, out_ref, own_sem, send, recv):
        copies = []
        for n, (source, target) in enumerate(self.moves):
            there_ref = target(out_ref, quarter_of(me))
            for k, names in reversed(list(enumerate(DIRECT))):
                there = move(me, names)
                copies.append(
                    remote(
                        source(x_refs, quarter_of(there)), there_ref, send.at[n, k], recv.at[n, k], there
                    )
                )
            copies.append(
                pltpu.make_async_copy(source(x_refs, quarter_of(me)), there_ref, own_sem.at[n])
            )

        def begin():
            for one in copies:
                one.start()

        def end():
            for one in copies:
                one.wait()

        return [begin, end]


def half_quarter(ref, quarter, half, rows=None):
    columns = ref.shape[1] // 8
    cut = pl.ds(pl.multiple_of((quarter * 2 + half) * columns, columns), columns)
    return ref.at[:, cut] if rows is None else ref.at[rows, cut]


def spread_halves(pieces, columns, kind):
    moves, start = [], 0
    for index, rows, half in pieces:
        count = rows.stop - rows.start
        moves.append(
            (
                lambda refs, quarter, index=index, rows=rows, half=half: half_quarter(
                    refs[index], quarter, half, rows
                ),
                lambda ref, quarter, start=start, count=count: ref.at[quarter, start : start + count],
            )
        )
        start += count
    return Exchange(moves, (4, start, columns // 8), kind)


def return_half(cut, kind):
    quarters, rows, columns = cut.shape

    def place(ref, quarter):
        return ref.at[:, pl.ds(pl.multiple_of(quarter * columns, columns), columns)]

    return Exchange(
        [(lambda ref, quarter: ref.at[quarter], place)], (rows, quarters * columns), kind
    )


def widen_kernel(a_ref, b_ref, down_ref, up_ref):
    rows, columns = down_ref.shape[0], a_ref.shape[1] // 4
    for start, out_ref in ((0, down_ref), (rows, up_ref)):
        for quarter in range(4):
            for half, ref in enumerate((a_ref, b_ref)):
                at = (quarter * 2 + half) * columns
                cut = slice(quarter * columns, (quarter + 1) * columns)
                out_ref[:, at : at + columns] = ref[start : start + rows, cut].astype(F32)


def widen(half_a, half_b):
    rows, columns = half_a.shape
    shape = jax.ShapeDtypeStruct((rows // 2, 2 * columns), F32)
    return pl.pallas_call(
        widen_kernel,
        out_shape=[shape, shape],
        compiler_params=pltpu.CompilerParams(vmem_limit_bytes=VMEM_BYTES),
        cost_estimate=SMALL,
    )(half_a, half_b)


class Work:
    steps, lines = (), 1

    def __init__(self, work, shape, kind):
        self.work, self.out = work, jax.ShapeDtypeStruct(shape, kind)
        self.in_spec = self.out_spec = pl.BlockSpec(memory_space=pltpu.VMEM)

    def scratch(self):
        return []

    def stages(self, me, x_refs, out_ref):
        return [functools.partial(self.work, me, x_refs, out_ref), lambda: None]


class Direct:
    steps, rows_too = ("tp",), True

    def __init__(self, lines, rows, columns, shared):
        self.lines, self.rows, self.columns, self.shared = lines, rows, columns, shared
        self.out = jax.ShapeDtypeStruct((rows, columns + shared), F32)
        self.in_spec = self.out_spec = pl.BlockSpec(memory_space=pltpu.VMEM)

    def scratch(self):
        lines = self.lines
        return [
            pltpu.VMEM((2, lines, 2, self.rows, self.columns), BF16),
            pltpu.SemaphoreType.DMA((4, 2, lines)),
            pltpu.SemaphoreType.DMA((2, lines, 2)),
            pltpu.SemaphoreType.DMA((2,)),
        ]

    def stages(self, me, x_ref, out_ref, held, send, recv, share_sem):
        def on_others(work):
            for side in range(4):
                for distance in range(self.lines):
                    for way, amount in enumerate((1, -1) if distance else (1,)):
                        if side or distance:
                            place = along(plane_partner(me, side * 2), amount * distance)
                            inside = (place["line"] >= 0) & (place["line"] < self.lines)
                            pl.when(inside)(
                                functools.partial(work, place, send.at[side, way, distance])
                            )

        def copy(place, sem):
            return remote(
                by_rows_slot(x_ref, place),
                by_rows_slot(held, me),
                sem,
                by_rows_slot(recv, me),
                place,
            )

        def arrived(place, sem):
            slot = by_rows_slot(held, place)
            remote(slot, slot, sem, by_rows_slot(recv, place), me).wait_recv()

        def begin():
            on_others(lambda place, sem: copy(place, sem).start())
            held[me["fsdp"], me["line"], me["pair"]] = x_ref[me["fsdp"], me["line"], me["pair"]]

        def end():
            on_others(arrived)
            total = jnp.zeros((self.rows, self.columns), F32)
            for half in range(2):
                for shard in range(self.lines):
                    for side in range(2):
                        total = total + held[half, shard, side].astype(F32)
            out_ref[:, : self.columns] = total
            share = remote(
                out_ref.at[:, : self.columns],
                out_ref.at[:, self.columns :],
                share_sem.at[0],
                share_sem.at[1],
                flip(me, "tp"),
            )
            share.start()
            share.wait()
            on_others(lambda place, sem: copy(place, sem).wait_send())

        return [begin, end]


class Total:
    steps, everyone = (), True

    def __init__(self, shape, lines, special, heads):
        self.lines, self.shape, self.special, self.heads = lines, shape, special, heads
        self.out = jax.ShapeDtypeStruct((shape[0], 2 * shape[1]), F32)
        self.in_spec = self.out_spec = pl.BlockSpec(memory_space=pltpu.VMEM)

    def scratch(self):
        shape, lines = self.shape, self.lines
        return [
            pltpu.VMEM((lines,) + shape, F32),
            pltpu.VMEM((8,) + shape, F32),
            pltpu.SemaphoreType.DMA((2, lines)),
            pltpu.SemaphoreType.DMA((lines,)),
            pltpu.SemaphoreType.DMA((8,)),
            pltpu.SemaphoreType.DMA((8,)),
        ]

    def stages(self, me, x_ref, out_ref, on_line, on_plane, line_send, line_recv, send, recv):
        lines, mine = self.lines, me["line"]
        number = plane_number(me)

        def on_others(work):
            for distance in range(1, lines):
                for way, amount in enumerate((1, -1)):
                    there = mine + amount * distance
                    pl.when((there >= 0) & (there < lines))(
                        functools.partial(work, way, amount, distance, there)
                    )

        def to_line(way, amount, distance):
            return remote(
                on_line.at[mine],
                on_line.at[mine],
                line_send.at[way, distance],
                line_recv.at[mine],
                along(me, amount * distance),
            )

        def to_plane(bits):
            return remote(
                on_plane.at[number],
                on_plane.at[number],
                send.at[bits],
                recv.at[number],
                plane_partner(me, bits),
            )

        def begin():
            on_line[mine] = x_ref[...]
            on_others(lambda way, amount, distance, there: to_line(way, amount, distance).start())

        def arrived(way, amount, distance, there):
            remote(
                on_line.at[there], on_line.at[there], line_send.at[0, 0], line_recv.at[there], me
            ).wait_recv()

        def middle():
            on_others(arrived)
            total = on_line[0]
            for shard in range(1, lines):
                total = total + on_line[shard]
            on_plane[number] = total
            for bits in range(1, 8):
                to_plane(bits).start()

        def end():
            for bits in range(1, 8):
                there = plane_number(plane_partner(me, bits))
                remote(
                    on_plane.at[there], on_plane.at[there], send.at[0], recv.at[there], me
                ).wait_recv()
            total = on_plane[0]
            for other in range(1, 8):
                total = total + on_plane[other]
            width, row, heads = self.shape[1], slice(self.special, self.special + 1), self.heads
            out_ref[...] = jnp.zeros_like(out_ref)
            out_ref[:, :width] = total
            same = [on_plane[quarter * 2 + me["tp"], row, :] for quarter in range(4)]
            out_ref[row, :heads] = sum(part[:, :heads] for part in same)
            for quarter, part in enumerate(same):
                out_ref[quarter : quarter + 1, width : 2 * width - heads] = part[:, heads:]
            for bits in range(1, 8):
                to_plane(bits).wait_send()
            on_others(lambda way, amount, distance, there: to_line(way, amount, distance).wait_send())

        return [begin, middle, end]


def plane_number(place):
    return (place["fsdp"] * 2 + place["pair"]) * 2 + place["tp"]


def plane_partner(me, bits):
    place = me
    for bit, name in ((1, "tp"), (2, "pair"), (4, "fsdp")):
        if bits & bit:
            place = flip(place, name)
    return place


def greet(me, programs, partners=()):
    barrier = pltpu.get_barrier_semaphore()
    plane, reach, lines, corners = set(), 0, 1, False
    for one in programs:
        lines = max(lines, one.lines)
        if one.lines > 1:
            far = hasattr(one, "everyone") or hasattr(one, "far_line")
            reach = max(reach, one.lines - 1 if far else 1)
        if hasattr(one, "everyone"):
            plane |= set(range(1, 8))
        if isinstance(one, Exchange) or hasattr(one, "rows_too"):
            plane |= {2, 4, 6}
        if hasattr(one, "rows_too"):
            reach, corners = one.lines - 1, True
    for step in [step for one in programs for step in one.steps] + list(partners):
        plane |= {"tp": {1}, "pair": {2}, "fsdp": {4}}.get(step, {2, 4})
    for bits in sorted(plane):
        pl.semaphore_signal(
            barrier, inc=1, device_id=plane_partner(me, bits), device_id_type=MESH_ID
        )
    count = len(plane)
    for distance in range(1, reach + 1):
        for amount in (-distance, distance):
            there = me["line"] + amount
            inside = (there >= 0) & (there < lines)

            for bits in (0, 2, 4, 6) if corners else (0,):

                @pl.when(inside)
                def _():
                    pl.semaphore_signal(
                        barrier,
                        inc=1,
                        device_id=along(plane_partner(me, bits), amount),
                        device_id_type=MESH_ID,
                    )

                count = count + inside.astype(jnp.int32)
    pl.semaphore_wait(barrier, count)


def split_scratch(programs, refs):
    parts, start = [], 0
    for one in programs:
        size = len(one.scratch())
        parts.append(refs[start : start + size])
        start += size
    return parts


def schedule(programs, x_refs, out_refs, scratch, partners=()):
    me = here()
    works = [(0.0, functools.partial(greet, me, programs, partners))]
    for one, x_ref, out_ref, held in zip(programs, x_refs, out_refs, split_scratch(programs, scratch)):
        stages = one.stages(me, x_ref, out_ref, *held)
        places = getattr(one, "places", (0.0, 1.0))
        if len(places) == 2:
            places = spaced(places[0], places[1], len(stages))
        last = len(places) - 2
        works += [
            (places[-1] if k == len(stages) - 1 else places[min(k, last)], stage)
            for k, stage in enumerate(stages)
        ]
    return sorted(works, key=lambda work: work[0])


def placed(program, *places):
    program.places = list(places)
    return program


def spaced(start, stop, count):
    return [start + (stop - start) * k / (count - 1) for k in range(count)]


def run_programs(programs, arrays, number, near=(), far=()):
    count = len(programs)
    given = [k for k, array in enumerate(arrays) if not callable(array)]
    others = len(near) + len(far)

    def kernel(*refs):
        (more, refs) = refs[:others], refs[others:]
        plain, out_refs = refs[: len(given)], refs[len(given) : len(given) + count]
        in_refs = [
            array(more, out_refs) if callable(array) else plain[given.index(k)]
            for k, array in enumerate(arrays)
        ]
        for _, work in schedule(programs, in_refs, out_refs, refs[len(given) + count :]):
            work()

    return pl.pallas_call(
        kernel,
        out_shape=[one.out for one in programs],
        in_specs=[pl.BlockSpec(memory_space=pltpu.VMEM)] * len(near)
        + [pl.BlockSpec(memory_space=pl.ANY)] * len(far)
        + [programs[k].in_spec for k in given],
        out_specs=[one.out_spec for one in programs],
        scratch_shapes=[held for one in programs for held in one.scratch()],
        compiler_params=pltpu.CompilerParams(
            collective_id=number, has_side_effects=True, vmem_limit_bytes=VMEM_BYTES
        ),
        cost_estimate=SMALL,
    )(*near, *far, *[arrays[k] for k in given])


def by_rows_slot(ref, at):
    return ref.at[at["fsdp"], at["line"], at["pair"]]


def by_plane_slot(ref, at):
    return ref.at[at["fsdp"], at["pair"], at["tp"]]


def by_ctx_slot(ref, at):
    return ref.at[at["tp"], at["line"], at["pair"]]


def rows_gather(values):
    lines = lax.axis_size("line")
    return Gather(values, (SIDE, FRONT), lines, (2, lines, 2) + values.shape, by_rows_slot)


def line_gather(shape, kind):
    lines = lax.axis_size("line")
    like = jax.ShapeDtypeStruct(shape, kind)
    return Gather(like, (), lines, (lines,) + shape, lambda ref, at: ref.at[at["line"]])


def columns_gather(values):
    lines, rows, columns = values.shape
    return Gather(
        values, (SIDE, FRONT), 1, (2, lines, 2, rows, columns), lambda ref, at: ref.at[at["fsdp"], :, at["pair"]]
    )


def rows_sum(values):
    lines, (total, columns) = lax.axis_size("line"), values.shape
    rows = total // (4 * lines)
    parts = values.astype(BF16).reshape(2, lines, 2, rows, columns)
    return Sum((FRONT, SIDE), lines, rows, columns, by_rows_slot), parts


def plane_gather(values):
    return Gather(values, (SIDE, FRONT, "tp"), 1, (2, 2, 2) + values.shape, by_plane_slot)


def plane_sum(values):
    rows, columns = values.shape[0] // 8, values.shape[1]
    parts = values.astype(BF16).reshape(2, 2, 2, rows, columns)
    return Sum(("tp", FRONT, SIDE), 1, rows, columns, by_plane_slot), parts


def flat(values):
    return values.reshape(-1, values.shape[-1])


def ctx_gather(shape, kind):
    lines = lax.axis_size("line")
    like = jax.ShapeDtypeStruct(shape, kind)
    return Gather(like, ("pair", "tp"), lines, (2, lines, 2) + shape, by_ctx_slot)


def ctx_sums(values):
    _, lines, rows, columns = values.shape
    along_line = Sum(
        ("tp",), lines, rows, columns, lambda ref, at: ref.at[at["tp"], at["line"]], BF16
    )
    over_pair = Sum(("pair",), 1, rows // 2, columns, lambda ref, at: ref.at[at["pair"]])
    return along_line, over_pair


LOG2E = 1.4426950408889634


def visible_bias(bias_ref, position, chunks):
    prompt = position < PBLK
    row = lax.broadcasted_iota(jnp.int32, (BLK, BLK), 0)
    column = lax.broadcasted_iota(jnp.int32, (BLK, BLK), 1)
    limit = jnp.where(prompt, position * BLK + column, PBLK * BLK)
    for chunk in range(chunks - 1):
        bias_ref[chunk] = jnp.where(row + chunk * BLK <= limit, 0.0, MASKED)
    own_limit = jnp.where(prompt, -1, column)
    bias_ref[chunks - 1] = jnp.where(row <= own_limit, 0.0, MASKED)


def rows_by_rows(left, right):
    return lax.dot_general(left, right, (((1,), (1,)), ((), ())), preferred_element_type=F32)


def beside(programs, in_refs, out_refs, scratch, step, steps):
    late = []
    for place, work in schedule(programs, in_refs, out_refs, scratch):
        if place < 1:
            pl.when(step == int(place * steps))(work)
        else:
            late.append((place, work))

    def finish(own=None):
        @pl.when(step == steps - 1)
        def _():
            early = [work for place, work in late if place < 1.05]
            rest = [work for place, work in late if place >= 1.05]
            for work in early + ([own] if own else []) + rest:
                work()

    return finish


def attend_kernel(programs, steps, *refs):
    count = len(programs)
    (position_ref, slot_ref, query_ref, table_ref), refs = refs[:4], refs[4:]
    others, refs = refs[:count], refs[count:]
    (mixed_ref, logsum_ref), refs = refs[:2], refs[2:]
    other_outs, refs = refs[:count], refs[count:]
    (bias_ref, score_ref, value_t_ref), scratch = refs[:3], refs[3:]
    chunks = PBLK + 1
    block = pl.program_id(0)
    factor = HD**-0.5 * LOG2E
    step = pl.program_id(0) * pl.num_programs(1) + pl.program_id(1)
    finish = beside(programs, others, other_outs, scratch, step, steps)

    @pl.when(pl.program_id(1) == 0)
    def _():
        visible_bias(bias_ref, position_ref[block], chunks)
        for chunk in range(chunks):
            value_t_ref[chunk] = table_ref[1, slot_ref[block, chunk]].astype(F32).T.astype(BF16)

    query = query_ref[...]
    largest = None
    for chunk in range(chunks):
        keys = table_ref[0, slot_ref[block, chunk]]
        score = rows_by_rows(keys, query) + bias_ref[chunk]
        score_ref[chunk] = score
        top = jnp.max(score.reshape(BLK // 8, 8, BLK), axis=0)
        largest = top if largest is None else jnp.maximum(largest, top)
    largest = jnp.max(largest, axis=0, keepdims=True)
    total = jnp.zeros((8, BLK), F32)
    mixed = jnp.zeros((HD, BLK), F32)
    for chunk in range(chunks):
        weight = jnp.exp2((score_ref[chunk] - largest) * factor)
        total = total + jnp.sum(weight.reshape(BLK // 8, 8, BLK), axis=0)
        mixed = mixed + jnp.dot(
            value_t_ref[chunk], weight.astype(BF16), preferred_element_type=F32
        )
    total = jnp.sum(total, axis=0, keepdims=True)
    mixed_ref[...] = (mixed / total).T.astype(BF16)
    logsum_ref[0, 0] = largest * factor + jnp.log2(total)
    finish()


def attend(queries, table, positions, key_slots, programs, arrays, number):
    rows, width = queries.shape
    blocks, heads = rows // BLK, width // HD
    count = (PBLK + 1) * BLK
    out = pl.pallas_call(
        functools.partial(attend_kernel, programs, blocks * heads),
        grid=(blocks, heads),
        out_shape=[
            jax.ShapeDtypeStruct((rows, width), BF16),
            jax.ShapeDtypeStruct((blocks, heads, 1, BLK), F32),
        ]
        + [one.out for one in programs],
        in_specs=[
            pl.BlockSpec(memory_space=pltpu.SMEM),
            pl.BlockSpec(memory_space=pltpu.SMEM),
            pl.BlockSpec((BLK, HD), lambda b, h: (b, h)),
            pl.BlockSpec(memory_space=pltpu.VMEM),
        ]
        + [one.in_spec for one in programs],
        out_specs=[
            pl.BlockSpec((BLK, HD), lambda b, h: (b, h)),
            pl.BlockSpec((1, 1, 1, BLK), lambda b, h: (b, h, 0, 0)),
        ]
        + [one.out_spec for one in programs],
        scratch_shapes=[
            pltpu.VMEM((PBLK + 1, BLK, BLK), F32),
            pltpu.VMEM((PBLK + 1, BLK, BLK), F32),
            pltpu.VMEM((PBLK + 1, HD, BLK), BF16),
        ]
        + [held for one in programs for held in one.scratch()],
        compiler_params=pltpu.CompilerParams(
            collective_id=number, has_side_effects=True, vmem_limit_bytes=VMEM_BYTES
        ),
        cost_estimate=SMALL,
    )(positions, key_slots, queries, table, *arrays)
    return out[0], out[1], out[2:]


def attend_back_kernel(programs, steps, *refs):
    count = len(programs)
    (position_ref, slot_ref, query_ref, grad_ref, mixed_ref), refs = refs[:5], refs[5:]
    (logsum_ref, table_ref, normed_ref), refs = refs[:3], refs[3:]
    others, refs = refs[:count], refs[count:]
    (grad_query_ref, set_ref, weight_ref), refs = refs[:3], refs[3:]
    other_outs, refs = refs[:count], refs[count:]
    (bias_ref, key_t_ref, kept_ref), scratch = refs[:3], refs[3:]
    chunks = PBLK + 1
    scale = HD**-0.5
    block, head = pl.program_id(0), pl.program_id(1)
    step = pl.program_id(0) * pl.num_programs(1) + pl.program_id(1)
    finish = beside(programs, others, other_outs, scratch, step, steps)

    @pl.when(head == 0)
    def _():
        visible_bias(bias_ref, position_ref[block], chunks)
        set_ref[...] = jnp.zeros_like(set_ref)
        for chunk in range(chunks):
            key_t_ref[chunk] = table_ref[0, slot_ref[block, chunk]].astype(F32).T.astype(BF16)

    query, grad = query_ref[...], grad_ref[...]
    inner = jnp.sum(grad.astype(F32) * mixed_ref[...].astype(F32), axis=1, keepdims=True)
    inner = jnp.broadcast_to(inner, (BLK, HD)).T[:1, :]
    logsum = logsum_ref[0, 0]
    grad_query = jnp.zeros((HD, BLK), F32)
    for chunk in range(chunks):
        cut = slice(chunk * BLK, (chunk + 1) * BLK)
        slot = slot_ref[block, chunk]
        score = rows_by_rows(table_ref[0, slot], query)
        weight = jnp.exp2(score * (scale * LOG2E) + bias_ref[chunk] - logsum)
        grad_weight = rows_by_rows(table_ref[1, slot], grad)
        grad_score = (weight * (grad_weight - inner)).astype(BF16)
        set_ref[0, cut, :HD] += jnp.dot(grad_score, query, preferred_element_type=F32)
        set_ref[0, cut, HD:] += jnp.dot(weight.astype(BF16), grad, preferred_element_type=F32)
        grad_query = grad_query + jnp.dot(
            key_t_ref[chunk], grad_score, preferred_element_type=F32
        )
    grad_query = (grad_query * scale).T.astype(BF16)
    grad_query_ref[...] = grad_query
    kept_ref[block, head] = grad_query

    @pl.when(head == pl.num_programs(1) - 1)
    def _():
        set_ref[0, :, :HD] = set_ref[0, :, :HD] * scale

    def weights():
        blocks, heads = kept_ref.shape[:2]
        kept = [
            jnp.concatenate([kept_ref[b, h] for h in range(heads)], axis=1) for b in range(blocks)
        ]
        kept = jnp.concatenate(kept, axis=0)

        def work(cut):
            weight_ref[cut, :] = by_columns(normed_ref[:, cut], kept).astype(BF16)

        each_columns(weight_ref.shape[0], 256, work)

    finish(weights)


def attend_back(
    queries, grads, mixed, logsums, table, normed, positions, key_slots, programs, arrays, number
):
    rows, width = queries.shape
    blocks, heads = rows // BLK, width // HD
    count = (PBLK + 1) * BLK
    by_head = pl.BlockSpec((BLK, HD), lambda b, h: (b, h))
    out = pl.pallas_call(
        functools.partial(attend_back_kernel, programs, blocks * heads),
        grid=(blocks, heads),
        out_shape=[
            jax.ShapeDtypeStruct((rows, width), BF16),
            jax.ShapeDtypeStruct((blocks, count, 2 * HD), F32),
            jax.ShapeDtypeStruct((normed.shape[1], width), BF16),
        ]
        + [one.out for one in programs],
        in_specs=[
            pl.BlockSpec(memory_space=pltpu.SMEM),
            pl.BlockSpec(memory_space=pltpu.SMEM),
            by_head,
            by_head,
            by_head,
            pl.BlockSpec((1, 1, 1, BLK), lambda b, h: (b, h, 0, 0)),
            pl.BlockSpec(memory_space=pltpu.VMEM),
            pl.BlockSpec(memory_space=pltpu.VMEM),
        ]
        + [one.in_spec for one in programs],
        out_specs=[
            by_head,
            pl.BlockSpec((1, count, 2 * HD), lambda b, h: (b, 0, 0)),
            pl.BlockSpec(memory_space=pltpu.VMEM),
        ]
        + [one.out_spec for one in programs],
        scratch_shapes=[
            pltpu.VMEM((PBLK + 1, BLK, BLK), F32),
            pltpu.VMEM((PBLK + 1, HD, BLK), BF16),
            pltpu.VMEM((blocks, heads, BLK, HD), BF16),
        ]
        + [held for one in programs for held in one.scratch()],
        compiler_params=pltpu.CompilerParams(
            collective_id=number, has_side_effects=True, vmem_limit_bytes=VMEM_BYTES
        ),
        cost_estimate=SMALL,
    )(positions, key_slots, queries, grads, mixed, logsums, table, normed, *arrays)
    return out[0], out[1], out[2], out[3:]


def by_slot_kernel(slot_ref, set_ref, out_ref, table_ref):
    blocks, chunks = slot_ref.shape

    def clear(index, carry):
        table_ref[index] = jnp.zeros(table_ref.shape[1:], F32)
        return carry

    def give(index, carry):
        out_ref[0, index] = table_ref[index, :, :HD].astype(BF16)
        out_ref[1, index] = table_ref[index, :, HD:].astype(BF16)
        return carry

    lax.fori_loop(0, table_ref.shape[0], clear, 0)
    for block in range(blocks):
        for chunk in range(chunks):
            cut = slice(chunk * BLK, (chunk + 1) * BLK)
            table_ref[slot_ref[block, chunk]] += set_ref[block, cut, :]
    lax.fori_loop(0, table_ref.shape[0], give, 0)


def by_slot(sets, key_slots, slot_count):
    return pl.pallas_call(
        by_slot_kernel,
        out_shape=jax.ShapeDtypeStruct((2, slot_count, BLK, HD), BF16),
        in_specs=[
            pl.BlockSpec(memory_space=pltpu.SMEM),
            pl.BlockSpec(memory_space=pltpu.VMEM),
        ],
        out_specs=pl.BlockSpec(memory_space=pltpu.VMEM),
        scratch_shapes=[pltpu.VMEM((slot_count, BLK, 2 * HD), F32)],
        compiler_params=pltpu.CompilerParams(vmem_limit_bytes=VMEM_BYTES),
        cost_estimate=SMALL,
    )(key_slots, sets)


GELU_OUTER = 0.7978845608028654
GELU_INNER = 0.044715


def weight_copies(parts, target, sems):
    copies, start = [], 0
    for number, (ref, rows) in enumerate(parts):
        count = rows.stop - rows.start
        copies.append(
            pltpu.make_async_copy(
                ref.at[:, :, rows], target.at[:, :, start : start + count], sems.at[number]
            )
        )
        start += count
    return copies


def first_half(rows, refs):
    piece, other, early = refs[:3]
    first = piece.shape[2]
    return [(piece, slice(0, first)), (other, slice(0, rows - first))], [(early, slice(0, rows))]


def second_half(rows, refs):
    early, late = refs[2:]
    there = early.shape[2] - rows
    down = [(early, slice(rows, rows + there)), (late, slice(0, rows - there))]
    return down, [(late, slice(rows - there, 2 * rows - there))]


def gelu_both(value, grad_act):
    square = value * value
    bend = jnp.tanh(GELU_OUTER * value * (1.0 + GELU_INNER * square))
    slope = 0.5 * (1.0 + bend) + 0.5 * GELU_OUTER * value * (1.0 - bend * bend) * (
        1.0 + 3.0 * GELU_INNER * square
    )
    return 0.5 * value * (1.0 + bend), grad_act * slope


def forward_kernel(
    x_ref,
    cotangent_ref,
    piece_ref,
    other_ref,
    early_ref,
    shift_ref,
    all_ref,
    act_ref,
    pre_ref,
    part_ref,
    bias_ref,
    weight_grad_ref,
    up_own,
    down_own,
    grads_own,
    rows_own,
    cotangent_own,
    act_own,
    pre_own,
    part_own,
    weight_sem,
    load_sem,
    store_sem,
    own_sem,
    send,
    recv,
):
    me = here()
    steps = (SIDE, FRONT, "tp")
    half, width = x_ref.shape
    hidden = early_ref.shape[3]

    def place(bits):
        at = me
        for k in (2, 1, 0):
            if bits >> k & 1:
                at = flip(at, steps[k])
        return at

    def block(bits):
        return by_plane_slot(all_ref, place(bits))

    def to_step(k, bits):
        source = block(bits) if bits else x_ref
        return remote(
            source, block(bits), send.at[k, bits], recv.at[bits | 1 << k], flip(me, steps[k])
        )

    def arrived(bits):
        remote(block(bits), block(bits), send.at[0, 0], recv.at[bits], me).wait_recv()

    def loads(number):
        slot, copies = number % 2, []
        for side, bits in enumerate((number, number + 4)):
            rows = pl.ds(side * half, half)
            copies.append(
                pltpu.make_async_copy(
                    by_plane_slot(cotangent_ref, place(bits)),
                    cotangent_own.at[slot, rows],
                    load_sem.at[slot, 0, side],
                )
            )
            copies.append(
                pltpu.make_async_copy(
                    block(bits) if bits else x_ref,
                    rows_own.at[slot, rows],
                    load_sem.at[slot, 1, side],
                )
            )
        return copies

    def stores(number, kind):
        slot = number % 2
        source, target = ((act_own, act_ref), (pre_own, pre_ref), (part_own, part_ref))[kind]
        return [
            pltpu.make_async_copy(
                source.at[slot, pl.ds(side * half, half)],
                by_plane_slot(target, place(bits)),
                store_sem.at[slot, kind, side],
            )
            for side, bits in enumerate((number, number + 4))
        ]

    def products(number):
        slot = number % 2
        tile = 256

        def one(index, carry):
            cut = pl.ds(pl.multiple_of(index * tile, tile), tile)
            down = down_own[:, :, :, cut].reshape(width, tile)
            up = up_own[:, :, :, cut].reshape(width, tile)
            grad_act = jnp.dot(cotangent_own[slot], down, preferred_element_type=F32)
            value = jnp.dot(rows_own[slot], up, preferred_element_type=F32)
            value = value + shift_ref[:, cut]
            act, grad_pre = gelu_both(value, grad_act)
            act_own[slot, :, cut] = act.astype(BF16)
            grad_pre = grad_pre.astype(BF16)
            pre_own[slot, :, cut] = grad_pre
            bias_ref[:, cut] += jnp.sum(
                grad_pre.astype(F32).reshape(2 * half // 8, 8, tile), axis=0
            )
            return carry

        lax.fori_loop(0, hidden // tile, one, 0, unroll=True)

    def back(number):
        slot = number % 2
        tile = up_own.shape[1] * up_own.shape[2]

        def one(index, carry):
            cut = pl.ds(pl.multiple_of(index * tile, tile), tile)
            up = up_own[index].reshape(tile, hidden)
            part_own[slot, :, cut] = rows_by_rows(pre_own[slot], up).astype(BF16)
            return carry

        lax.fori_loop(0, width // tile, one, 0, unroll=2)

    def grads(number):
        tile = 256
        shard_rows = weight_grad_ref.shape[2]
        rows = 4 * half

        def one(index, carry):
            cut = pl.ds(pl.multiple_of(index * tile, tile), tile)
            for kind, (left, right) in enumerate(((cotangent_own, act_own), (rows_own, pre_own))):
                grad = by_columns(
                    left[:, :, cut].reshape(rows, tile), right[...].reshape(rows, hidden)
                )
                if number == 1:
                    grads_own[kind, cut, :] = grad
                else:
                    count = tile // shard_rows
                    shards = pl.ds(pl.multiple_of(index * count, count), count)
                    grad = (grads_own[kind, cut, :] + grad).astype(BF16)
                    weight_grad_ref[shards, kind] = grad.reshape(count, shard_rows, hidden)
            return carry

        lax.fori_loop(0, width // tile, one, 0, unroll=2)

    def pass_on(bits, *ways):
        arrived(bits)
        for k in ways:
            to_step(k, bits).start()

    def second():
        to_step(0, 0).wait_send()
        to_step(1, 0).start()

    def third():
        to_step(1, 0).wait_send()
        to_step(1, 1).start()
        pass_on(2, 2)

    between = [second, third, functools.partial(pass_on, 3, 2), lambda: None]
    barrier = pltpu.get_barrier_semaphore()
    for step in steps:
        pl.semaphore_signal(barrier, inc=1, device_id=flip(me, step), device_id_type=MESH_ID)
    pl.semaphore_wait(barrier, 3)
    to_step(0, 0).start()
    to_step(2, 0).start()
    own = pltpu.make_async_copy(x_ref, block(0), own_sem)
    own.start()
    down_parts, up_parts = first_half(up_own.shape[2], (piece_ref, other_ref, early_ref))
    weights = weight_copies(down_parts, down_own, weight_sem)
    weights += weight_copies(up_parts, up_own, weight_sem.at[2:])
    for one in weights:
        one.start()
    bias_ref[...] = jnp.zeros_like(bias_ref)
    for number in range(4):
        if number == 1:
            pass_on(1, 2)
        arrived(4 + number)
        copies = loads(number)
        for one in copies:
            one.start()
        if number == 0:
            for one in weights:
                one.wait()
        if number >= 2:
            for kind in range(3):
                for one in stores(number - 2, kind):
                    one.wait()
        for one in copies:
            one.wait()
        products(number)
        between[number]()
        for kind in range(2):
            for one in stores(number, kind):
                one.start()
        back(number)
        for one in stores(number, 2):
            one.start()
        if number % 2:
            grads(number)
    for number in (2, 3):
        for kind in range(3):
            for one in stores(number, kind):
                one.wait()
    own.wait()
    for k, bits in ((2, 0), (1, 1), (2, 1), (2, 2), (2, 3)):
        to_step(k, bits).wait_send()


def forward_products(rows, cotangent_all, piece, other, early, shift, number):
    half, width = rows.shape
    lines, quarters, _, hidden = early.shape
    weights = (lines, quarters, width // (lines * quarters), hidden)
    anywhere = pl.BlockSpec(memory_space=pl.ANY)
    inside = pl.BlockSpec(memory_space=pltpu.VMEM)
    lead = (2, 2, 2, half)
    return pl.pallas_call(
        forward_kernel,
        out_shape=[
            jax.ShapeDtypeStruct(lead + (width,), BF16),
            jax.ShapeDtypeStruct(lead + (hidden,), BF16),
            jax.ShapeDtypeStruct(lead + (hidden,), BF16),
            jax.ShapeDtypeStruct(lead + (width,), BF16),
            jax.ShapeDtypeStruct((8, hidden), F32),
            jax.ShapeDtypeStruct((lines * quarters, 2, weights[2], hidden), BF16),
        ],
        in_specs=[anywhere] * 5 + [inside],
        out_specs=[anywhere] * 4 + [inside] * 2,
        scratch_shapes=[
            pltpu.VMEM(weights, BF16),
            pltpu.VMEM(weights, BF16),
            pltpu.VMEM((2, width, hidden), F32),
            pltpu.VMEM((2, 2 * half, width), BF16),
            pltpu.VMEM((2, 2 * half, width), BF16),
            pltpu.VMEM((2, 2 * half, hidden), BF16),
            pltpu.VMEM((2, 2 * half, hidden), BF16),
            pltpu.VMEM((2, 2 * half, width), BF16),
            pltpu.SemaphoreType.DMA((3,)),
            pltpu.SemaphoreType.DMA((2, 2, 2)),
            pltpu.SemaphoreType.DMA((2, 3, 2)),
            pltpu.SemaphoreType.DMA(()),
            pltpu.SemaphoreType.DMA((3, 4)),
            pltpu.SemaphoreType.DMA((8,)),
        ],
        compiler_params=pltpu.CompilerParams(
            collective_id=number, has_side_effects=True, vmem_limit_bytes=VMEM_BYTES
        ),
        cost_estimate=SMALL,
    )(rows, cotangent_all, piece, other, early, shift)


CHIPS = ((1, 1), (1, 0), (0, 1), (0, 0))


def second_kernel(
    rows_ref,
    cotangent_ref,
    before_ref,
    rows_columns_ref,
    cotangent_columns_ref,
    act_a_ref,
    piece_ref,
    other_ref,
    early_ref,
    late_ref,
    shift_ref,
    down_part_ref,
    weight_grad_ref,
    bias_ref,
    sum_ref,
    up_own,
    downs,
    acts,
    pre_own,
    rows_own,
    cotangent_own,
    before_own,
    part_own,
    over_core,
    over_front,
    over_side,
    weight_sem,
    load_sem,
    core_send,
    core_recv,
    front_send,
    front_recv,
    side_sem,
):
    step = pl.program_id(0)
    me = here()
    core = me["tp"]
    width, hidden = rows_ref.shape[1], pre_own.shape[1]
    count = rows_ref.shape[0] // 4
    half = count // 2
    tile = 256
    places = (piece_ref, other_ref, early_ref, late_ref)
    shard_rows = up_own.shape[2]

    def chip(number):
        up, side = CHIPS[number]
        fsdp = me["fsdp"] + up * (1 - 2 * me["fsdp"])
        return fsdp, me["pair"] + side * (1 - 2 * me["pair"])

    def rows_of_chip(number):
        fsdp, pair = chip(number)
        return pl.ds(pl.multiple_of((fsdp * 2 + pair) * count, count), count)

    def loads(number):
        slot, rows = number % 2, rows_of_chip(number)
        pairs = ((rows_ref, rows_own), (cotangent_ref, cotangent_own), (before_ref, before_own))
        return [
            pltpu.make_async_copy(source.at[rows], target.at[slot], load_sem.at[slot, kind])
            for kind, (source, target) in enumerate(pairs)
        ]

    def second_weights():
        down_parts, up_parts = second_half(shard_rows, places)
        copies = weight_copies(down_parts, downs.at[1], weight_sem.at[0])
        return copies + weight_copies(up_parts, up_own, weight_sem.at[1])

    def first_weights():
        copies = weight_copies(first_half(shard_rows, places)[0], downs.at[0], weight_sem.at[2])
        return copies + [pltpu.make_async_copy(act_a_ref, acts.at[0], weight_sem.at[1, 1])]

    def to_core(number):
        fsdp, pair = chip(number)
        up, side = CHIPS[number]
        return remote(
            part_own.at[fsdp, pair, 1 - core],
            over_core.at[up, side],
            core_send.at[up, side],
            core_recv.at[up, side],
            flip(me, "tp"),
        )

    def take_core(number):
        fsdp, pair = chip(number)
        to_core(number).wait_recv()
        held = over_core.at[CHIPS[number]]
        add_blocks(held, rows_of(part_own.at[fsdp, pair, core]), rows_of(held), half)

    def to_front(corner):
        source = over_core.at[1, 1] if corner else over_core.at[1 - core, core]
        return remote(
            source, over_front.at[corner], front_send.at[corner], front_recv.at[corner], flip(me, FRONT)
        )

    def to_side():
        return remote(over_front.at[1], over_side, side_sem.at[0], side_sem.at[1], flip(me, SIDE))

    def take_front(corner):
        to_front(corner).wait_recv()
        held = over_front.at[corner]
        mine = over_core.at[core, 1 - core] if corner else over_core.at[0, 0]
        add_blocks(held, rows_of(mine), rows_of(held), half)

    def products(number):
        slot, rows = number % 2, rows_of_chip(number)

        def one(index, carry):
            cut = pl.ds(pl.multiple_of(index * tile, tile), tile)
            down = downs[1, :, :, :, cut].reshape(width, tile)
            up = up_own[:, :, :, cut].reshape(width, tile)
            grad_act = jnp.dot(cotangent_own[slot], down, preferred_element_type=F32)
            value = jnp.dot(rows_own[slot], up, preferred_element_type=F32) + shift_ref[:, cut]
            act, grad_pre = gelu_both(value, grad_act)
            acts[1, rows, cut] = act.astype(BF16)
            grad_pre = grad_pre.astype(BF16)
            pre_own[rows, cut] = grad_pre
            bias_ref[:, cut] += fold_rows(grad_pre.astype(F32))
            return carry

        lax.fori_loop(0, hidden // tile, one, 0, unroll=True)
        tile_back = up_own.shape[1] * shard_rows
        fsdp, pair = chip(number)

        def back(index, carry):
            cut = pl.ds(pl.multiple_of(index * tile_back, tile_back), tile_back)
            up = up_own[index].reshape(tile_back, hidden)
            part = before_own[slot, :, cut].astype(F32) + rows_by_rows(pre_own[rows, :], up)
            part_own[fsdp, pair, :, :, cut] = part.astype(BF16).reshape(2, half, tile_back)
            return carry

        lax.fori_loop(0, width // tile_back, back, 0, unroll=2)

    def chunk_step(number):
        if number == 0:
            barrier = pltpu.get_barrier_semaphore()
            for bits in (1, 2, 4):
                pl.semaphore_signal(
                    barrier, inc=1, device_id=plane_partner(me, bits), device_id_type=MESH_ID
                )
            for one in loads(0) + second_weights() + first_weights():
                one.start()
            bias_ref[...] = jnp.zeros_like(bias_ref)
            for one in second_weights():
                one.wait()
            pl.semaphore_wait(barrier, 3)
        for one in loads(number):
            one.wait()
        if number < 3:
            for one in loads(number + 1):
                one.start()
        products(number)
        to_core(number).start()
        if number > 0:
            take_core(number - 1)
        if number == 1:
            to_front(1).start()
        if number == 2:
            pl.when(core == 0)(lambda: to_front(0).start())
        if number == 3:
            pl.when(core == 1)(lambda: to_front(0).start())
            for one in first_weights():
                one.wait()

    for number in range(4):
        pl.when(step == number)(functools.partial(chunk_step, number))

    @pl.when(step == 4)
    def _():
        take_core(3)

    @pl.when(step == 5)
    def _():
        take_front(1)
        to_side().start()

    @pl.when(step == 9)
    def _():
        take_front(0)

    @pl.when(step >= 4)
    def _():
        rows_here = down_part_ref.shape[0]
        rows = pl.ds(pl.multiple_of((step - 4) * rows_here, rows_here), rows_here)
        shards = weight_grad_ref.shape[0]
        for kind, (left, right) in enumerate(
            ((cotangent_columns_ref, acts.at[1]), (rows_columns_ref, pre_own))
        ):
            grad = by_columns(left[...], right[...]).astype(BF16)
            weight_grad_ref[:, kind] = grad.reshape(shards, shard_rows, hidden)
        part = rows_by_rows(acts[0, rows, :], downs[0].reshape(width, hidden))
        part = part + rows_by_rows(acts[1, rows, :], downs[1].reshape(width, hidden))
        down_part_ref[...] = part.astype(BF16)

    @pl.when(step == pl.num_programs(0) - 1)
    def _():
        to_side().wait_recv()
        final = over_front.at[0]
        add_blocks(sum_ref, rows_of(final), rows_of(over_side), half)
        for number in range(4):
            to_core(number).wait_send()
        for corner in range(2):
            to_front(corner).wait_send()
        to_side().wait_send()


def second_products(rows_all, cotangent_all, before, act_a, pieces, shift, number):
    rows, width = rows_all.shape
    lines, quarters, _, hidden = pieces[-1].shape
    shards, shard_rows = lines * quarters, width // (lines * quarters)
    weights = (lines, quarters, shard_rows, hidden)
    steps, tiles, half = 12, 8, rows // 8

    def tile(i):
        return jnp.maximum(i - 4, 0)

    columns = pl.BlockSpec((rows, width // tiles), lambda i: (0, tile(i)))
    anywhere = pl.BlockSpec(memory_space=pl.ANY)
    fixed = lambda shape: pl.BlockSpec(shape, lambda i: (0,) * len(shape))
    return pl.pallas_call(
        second_kernel,
        grid=(steps,),
        out_shape=[
            jax.ShapeDtypeStruct((rows, width), BF16),
            jax.ShapeDtypeStruct((shards, 2, shard_rows, hidden), BF16),
            jax.ShapeDtypeStruct((8, hidden), F32),
            jax.ShapeDtypeStruct((half, width), F32),
        ],
        in_specs=[anywhere] * 3 + [columns] * 2 + [anywhere] * 5 + [fixed((1, hidden))],
        out_specs=[
            pl.BlockSpec((rows // tiles, width), lambda i: (tile(i), 0)),
            pl.BlockSpec((shards // tiles, 2, shard_rows, hidden), lambda i: (tile(i), 0, 0, 0)),
            fixed((8, hidden)),
            fixed((half, width)),
        ],
        scratch_shapes=[
            pltpu.VMEM(weights, BF16),
            pltpu.VMEM((2,) + weights, BF16),
            pltpu.VMEM((2, rows, hidden), BF16),
            pltpu.VMEM((rows, hidden), BF16),
            pltpu.VMEM((2, 2 * half, width), BF16),
            pltpu.VMEM((2, 2 * half, width), BF16),
            pltpu.VMEM((2, 2 * half, width), BF16),
            pltpu.VMEM((2, 2, 2, half, width), BF16),
            pltpu.VMEM((2, 2, half, width), BF16),
            pltpu.VMEM((2, half, width), BF16),
            pltpu.VMEM((half, width), BF16),
            pltpu.SemaphoreType.DMA((3, 2)),
            pltpu.SemaphoreType.DMA((2, 3)),
            pltpu.SemaphoreType.DMA((2, 2)),
            pltpu.SemaphoreType.DMA((2, 2)),
            pltpu.SemaphoreType.DMA((2,)),
            pltpu.SemaphoreType.DMA((2,)),
            pltpu.SemaphoreType.DMA((2,)),
        ],
        compiler_params=kernel_params(number),
        cost_estimate=SMALL,
    )(rows_all, cotangent_all, before, rows_all, cotangent_all, act_a, *pieces, shift)


def by_columns(left, right):
    return lax.dot_general(left, right, (((0,), (0,)), ((), ())), preferred_element_type=F32)


def reorder_kernel(cuts, size, x_ref, out_ref):
    for index, cut in enumerate(cuts):
        out_ref[:, index * size : (index + 1) * size] = x_ref[:, cut : cut + size]


def reorder(values, cuts):
    size = values.shape[1] // len(cuts)
    if size % 128:
        return jnp.concatenate([values[:, cut : cut + size] for cut in cuts], axis=1)
    return pl.pallas_call(
        functools.partial(reorder_kernel, cuts, size),
        out_shape=jax.ShapeDtypeStruct(values.shape, values.dtype),
        compiler_params=pltpu.CompilerParams(vmem_limit_bytes=VMEM_BYTES),
        cost_estimate=SMALL,
    )(values)


def to_line_order(values):
    lines = lax.axis_size("line")
    size = values.shape[1] // (2 * lines)
    return reorder(
        values, [(half * lines + shard) * size for shard in range(lines) for half in range(2)]
    )


def from_line_order(values):
    lines = lax.axis_size("line")
    size = values.shape[1] // (2 * lines)
    return reorder(
        values, [(shard * 2 + half) * size for half in range(2) for shard in range(lines)]
    )


def meet_sibling(me):
    barrier = pltpu.get_barrier_semaphore()
    pl.semaphore_signal(barrier, inc=1, device_id=flip(me, "tp"), device_id_type=MESH_ID)
    pl.semaphore_wait(barrier, 1)


def half_rows_of(core, rows):
    return pl.ds(pl.multiple_of(core * rows, rows), rows)


def each_rows(total, tile, work):
    def one(index, carry):
        work(pl.ds(pl.multiple_of(index * tile, tile), tile))
        return carry

    lax.fori_loop(0, total // tile, one, 0, unroll=2)


def each_columns(total, tile, work):
    each_rows(total, tile, work)


def moments(values):
    centered = values - jnp.mean(values, axis=1, keepdims=True)
    spread = jnp.mean(centered * centered, axis=1, keepdims=True)
    return centered, lax.rsqrt(spread + EPSILON)


def norm_back(values, gain, grad):
    centered, rstd = moments(values)
    xhat = centered * rstd
    scaled = grad * gain
    inner = jnp.mean(scaled * xhat, axis=1, keepdims=True)
    return xhat, rstd * (scaled - jnp.mean(scaled, axis=1, keepdims=True) - xhat * inner)


def fold_rows(values):
    return jnp.sum(values.reshape(values.shape[0] // 8, 8, values.shape[1]), axis=0)


def shuffled(cuts, ref, rows):
    if cuts is None:
        return ref[rows, :]
    size = ref.shape[1] // len(cuts)
    return jnp.concatenate([ref[rows, cut : cut + size] for cut in cuts], axis=1)


def norm_work(me, refs, out_ref):
    stream_ref, vectors_ref = refs
    gain, shift = vectors_ref[0:1, :], vectors_ref[1:2, :]

    def work(rows):
        centered, rstd = moments(stream_ref[rows, :].astype(F32))
        out_ref[rows, :] = (centered * rstd * gain + shift).astype(BF16)

    each_rows(out_ref.shape[0], 32, work)


def reorder_work(cuts, me, x_ref, out_ref):
    half, size = out_ref.shape[0], out_ref.shape[1] // len(cuts)
    few = 64

    def work(rows):
        start = pl.multiple_of(me["tp"] * half + rows.start, few)
        for index, cut in enumerate(cuts):
            out_ref[rows, index * size : (index + 1) * size] = x_ref[
                pl.ds(start, few), cut : cut + size
            ]

    each_rows(half, few, work)


def part_work(me, refs, out_ref):
    normed_ref, weight_ref, shift_ref = refs
    heads = weight_ref.shape[1] - out_ref.shape[1]
    part = jnp.dot(normed_ref[...], weight_ref[:, heads:], preferred_element_type=F32)
    out_ref[...] = (part + shift_ref[:, heads:]).astype(BF16)


def query_work(me, refs, out_ref):
    normed_ref, weight_ref, shift_ref = refs

    def work(cut):
        query = jnp.dot(normed_ref[...], weight_ref[:, cut], preferred_element_type=F32)
        out_ref[:, cut] = (query + shift_ref[:, cut]).astype(BF16)

    each_columns(out_ref.shape[1], 256, work)


def project_kernel(
    cuts,
    mixed_ref,
    proj_a_ref,
    proj_b_ref,
    stream_ref,
    vectors_ref,
    middle_ref,
    normed_ref,
    sent_ref,
    got_ref,
    sems,
):
    me = here()
    half, width = middle_ref.shape
    mine, other = half_rows_of(me["tp"], half), half_rows_of(1 - me["tp"], half)
    tile = 512
    meet_sibling(me)
    copy = remote(sent_ref, got_ref, sems.at[0], sems.at[1], flip(me, "tp"))

    def part(rows, target):
        def work(cut):
            heads = proj_a_ref.shape[1]
            part = rows_by_rows(mixed_ref[rows, :heads], proj_a_ref[cut, :])
            target[:, cut] = part + rows_by_rows(mixed_ref[rows, heads:], proj_b_ref[cut, :])

        each_columns(width, tile, work)

    part(other, sent_ref)
    copy.start()
    part(mine, middle_ref)
    copy.wait_recv()
    bias, gain, shift = vectors_ref[2:3, :], vectors_ref[3:4, :], vectors_ref[4:5, :]
    few = 32

    def finish(rows):
        start = pl.multiple_of(me["tp"] * half + rows.start, few)
        stream = stream_ref[pl.ds(start, few), :].astype(F32)
        middle = stream + (middle_ref[rows, :] + got_ref[rows, :] + bias)
        middle_ref[rows, :] = middle
        centered, rstd = moments(middle)
        normed = (centered * rstd * gain + shift).astype(BF16)
        if cuts is None:
            normed_ref[rows, :] = normed
            return
        size = width // len(cuts)
        for index, cut in enumerate(cuts):
            normed_ref[rows, index * size : (index + 1) * size] = normed[:, cut : cut + size]

    each_rows(half, few, finish)
    copy.wait_send()


def in_vmem(count):
    return [pl.BlockSpec(memory_space=pltpu.VMEM)] * count


def kernel_params(number):
    return pltpu.CompilerParams(
        collective_id=number, has_side_effects=True, vmem_limit_bytes=VMEM_BYTES
    )


def line_cuts(width, back):
    lines = lax.axis_size("line")
    size = width // (2 * lines)
    if size % 128:
        return None
    if back:
        return [(shard * 2 + half) * size for half in range(2) for shard in range(lines)]
    return [(half * lines + shard) * size for shard in range(lines) for half in range(2)]


def project(mixed, proj_a, proj_b, stream, vectors, number):
    rows, width = stream.shape
    half = rows // 2
    cuts = line_cuts(width, False)
    middle, normed = pl.pallas_call(
        functools.partial(project_kernel, cuts),
        out_shape=[
            jax.ShapeDtypeStruct((half, width), F32),
            jax.ShapeDtypeStruct((half, width), BF16),
        ],
        in_specs=in_vmem(5),
        out_specs=in_vmem(2),
        scratch_shapes=[
            pltpu.VMEM((half, width), F32),
            pltpu.VMEM((half, width), F32),
            pltpu.SemaphoreType.DMA((2,)),
        ],
        compiler_params=kernel_params(number),
        cost_estimate=SMALL,
    )(mixed, proj_a, proj_b, stream, vectors)
    return middle, normed if cuts else to_line_order(normed)


def middle_back_kernel(
    cuts,
    sum_ref,
    middle_ref,
    cotangent_ref,
    mixed_ref,
    proj_a_ref,
    proj_b_ref,
    vectors_ref,
    hidden_a_ref,
    hidden_b_ref,
    grad_middle_ref,
    grad_mixed_ref,
    proj_grad_ref,
    vector_ref,
    attn_ref,
    sums_own,
    sems,
):
    me = here()
    half, width = middle_ref.shape
    mine, other = half_rows_of(me["tp"], half), half_rows_of(1 - me["tp"], half)
    few = 32
    gain = vectors_ref[3:4, :]
    meet_sibling(me)
    sums_own[...] = jnp.zeros_like(sums_own)

    def norm(rows):
        start = pl.multiple_of(me["tp"] * half + rows.start, few)
        cotangent = cotangent_ref[pl.ds(start, few), :].astype(F32)
        grad = shuffled(cuts, sum_ref, rows)
        xhat, back = norm_back(middle_ref[rows, :], gain, grad)
        grad_middle = cotangent + back
        grad_middle_ref[rows, :] = grad_middle
        attn = grad_middle.astype(BF16)
        attn_ref[pl.ds(start, few), :] = attn
        sums_own[0] += fold_rows(grad * xhat)
        sums_own[1] += fold_rows(grad)
        sums_own[2] += fold_rows(attn.astype(F32))
        sums_own[3] += fold_rows(cotangent)

    each_rows(half, few, norm)
    copy = remote(attn_ref.at[mine], attn_ref.at[mine], sems.at[0], sems.at[1], flip(me, "tp"))
    copy.start()

    def to_heads(rows):
        for number, proj_ref in enumerate((proj_a_ref, proj_b_ref)):
            heads = proj_ref.shape[1]
            grad_ref = grad_mixed_ref.at[:, number * heads : (number + 1) * heads]

            def work(cut):
                grad = jnp.dot(attn_ref[rows, :], proj_ref[:, cut], preferred_element_type=F32)
                grad_ref[rows, cut] = grad.astype(BF16)

            each_columns(heads, 256, work)

    to_heads(mine)
    vector_ref[...] = jnp.zeros_like(vector_ref)
    for kind in range(4):
        vector_ref[2 + kind : 3 + kind, :] = jnp.sum(sums_own[kind], axis=0, keepdims=True)
    size = hidden_a_ref.shape[1]
    for number, hidden_ref in enumerate((hidden_a_ref, hidden_b_ref)):
        start = width - (2 - number) * size
        vector_ref[6:7, start : start + size] = jnp.sum(hidden_ref[...], axis=0, keepdims=True)
    copy.wait_recv()
    to_heads(other)

    def weight(cut):
        grad = lax.dot_general(
            attn_ref[:, cut], mixed_ref[...], (((0,), (0,)), ((), ())), preferred_element_type=F32
        )
        proj_grad_ref[cut, :] = grad.astype(BF16)

    each_columns(width, 256, weight)
    copy.wait_send()


def middle_back(grad_sum, middle, cotangent, mixed, proj_a, proj_b, vectors, hidden_a, hidden_b, number):
    rows, width = cotangent.shape
    half, heads = rows // 2, mixed.shape[1]
    cuts = line_cuts(width, True)
    return pl.pallas_call(
        functools.partial(middle_back_kernel, cuts),
        out_shape=[
            jax.ShapeDtypeStruct((half, width), F32),
            jax.ShapeDtypeStruct((rows, heads), BF16),
            jax.ShapeDtypeStruct((width, heads), BF16),
            jax.ShapeDtypeStruct((8, width), F32),
        ],
        in_specs=in_vmem(9),
        out_specs=in_vmem(4),
        scratch_shapes=[
            pltpu.VMEM((rows, width), BF16),
            pltpu.VMEM((4, 8, width), F32),
            pltpu.SemaphoreType.DMA((2,)),
        ],
        compiler_params=kernel_params(number),
        cost_estimate=SMALL,
    )(
        grad_sum if cuts else from_line_order(grad_sum),
        middle,
        cotangent,
        mixed,
        proj_a,
        proj_b,
        vectors,
        hidden_a,
        hidden_b,
    )


def first_back_kernel(cuts, programs, *refs):
    (
        grad_query_ref,
        grad_part_ref,
        first_ref,
        stream_ref,
        normed_ref,
        vectors_ref,
        grad_middle_ref,
        mlp_ref,
        middle_ref,
        early_ref,
        cut_b_ref,
    ), refs = refs[:11], refs[11:]
    (input_ref, layer_ref, mlp_out, part_out, total_out), refs = refs[:5], refs[5:]
    (weight_ref, vector_ref, sent_ref, got_ref, grad_first_ref, held_ref, sems), scratch = refs[:7], refs[7:]
    me = here()
    rows, width = stream_ref.shape
    half, heads = rows // 2, grad_query_ref.shape[1]
    shard_rows = part_out.shape[0]
    mine, other = half_rows_of(me["tp"], half), half_rows_of(1 - me["tp"], half)
    few = 32
    sibling = flip(me, "tp")
    works = schedule(
        programs,
        (
            cut_b_ref,
            weight_ref.reshape(2, -1, 2, shard_rows, weight_ref.shape[1]),
            vector_ref,
        ),
        (mlp_out, part_out, total_out),
        scratch,
        ("tp",),
    )

    def run_until(stop):
        while works and works[0][0] < stop:
            works.pop(0)[1]()

    run_until(0.1)
    grad_first_ref[:, :heads] = grad_query_ref[...]
    grad_first_ref[:, heads:] = grad_part_ref[...].astype(BF16)

    def weight(cut):
        grad = lax.dot_general(
            normed_ref[:, cut],
            grad_first_ref[:, heads:],
            (((0,), (0,)), ((), ())),
            preferred_element_type=F32,
        )
        weight_ref[cut, :] = grad.astype(BF16)

    each_columns(width, 512, weight)
    run_until(0.2)

    def part(at, target):
        def work(cut):
            target[:, cut] = rows_by_rows(grad_first_ref[at, :], first_ref[cut, :])

        each_columns(width, 512, work)

    part(other, sent_ref)
    sums_copy = remote(sent_ref, got_ref, sems.at[0], sems.at[1], sibling)
    sums_copy.start()
    run_until(0.3)
    bias = vectors_ref[5:6, :]

    def layer(at):
        start = pl.multiple_of(me["tp"] * half + at.start, few)
        out = middle_ref[at, :] + (shuffled(cuts, mlp_ref, at) + bias)
        layer_ref[pl.ds(start, few), :] = out.astype(BF16)

    each_rows(half, few, layer)
    layer_copy = remote(layer_ref.at[mine], layer_ref.at[mine], sems.at[2], sems.at[3], sibling)
    layer_copy.start()
    run_until(0.4)
    grad_own, folded = held_ref.at[0], held_ref.at[1]
    part(mine, grad_own)
    run_until(0.5)
    sums_copy.wait_recv()
    gain = vectors_ref[0:1, :]
    folded[0:16, :] = jnp.zeros((16, width), F32)

    def norm(at):
        start = pl.multiple_of(me["tp"] * half + at.start, few)
        grad = grad_own[at, :] + got_ref[at, :]
        xhat, back = norm_back(stream_ref[pl.ds(start, few), :].astype(F32), gain, grad)
        input_ref[pl.ds(start, few), :] = (grad_middle_ref[at, :] + back).astype(BF16)
        folded[0:8, :] += fold_rows(grad * xhat)
        folded[8:16, :] += fold_rows(grad)

    each_rows(half, few, norm)
    input_copy = remote(input_ref.at[mine], input_ref.at[mine], sems.at[4], sems.at[5], sibling)
    input_copy.start()
    vector_ref[...] = early_ref[...]
    for kind in range(2):
        total = jnp.sum(folded[kind * 8 : kind * 8 + 8, :], axis=0, keepdims=True)
        vector_ref[kind : kind + 1, :] = total
    vector_ref[6:7, :heads] = jnp.sum(
        fold_rows(grad_query_ref[...].astype(F32)), axis=0, keepdims=True
    )
    part_sums = jnp.sum(
        fold_rows(grad_first_ref[:, heads:].astype(F32)), axis=0, keepdims=True
    )
    vector_ref[7:8, : part_sums.shape[1]] = jnp.where(me["tp"] == 1, part_sums, 0.0)
    run_until(2.0)
    layer_copy.wait()
    input_copy.wait()
    sums_copy.wait_send()


def first_back(
    grad_query,
    grad_part,
    first_all,
    stream,
    normed,
    vectors,
    grad_middle,
    mlp_sum,
    middle,
    early,
    cut_b,
    number,
):
    rows, width = stream.shape
    half, heads, part = rows // 2, grad_query.shape[1], grad_part.shape[1]
    lines = lax.axis_size("line")
    cuts = line_cuts(width, True)
    shard_rows = width // (4 * lines)
    vector = early.shape
    programs = [
        placed(return_half(cut_b, BF16), 0.0, 1.0),
        placed(Direct(lines, shard_rows, part, part), 0.1, 0.95),
        placed(Total(vector, lines, 6, heads), 0.9, 0.93, 0.97),
    ]
    anywhere = [pl.BlockSpec(memory_space=pl.ANY)]
    return pl.pallas_call(
        functools.partial(first_back_kernel, cuts, programs),
        out_shape=[
            jax.ShapeDtypeStruct((rows, width), BF16),
            jax.ShapeDtypeStruct((rows, width), BF16),
        ]
        + [one.out for one in programs],
        in_specs=in_vmem(10) + anywhere,
        out_specs=in_vmem(2) + [one.out_spec for one in programs],
        scratch_shapes=[
            pltpu.VMEM((width, part), BF16),
            pltpu.VMEM(vector, F32),
            pltpu.VMEM((half, width), F32),
            pltpu.VMEM((half, width), F32),
            pltpu.VMEM((rows, heads + part), BF16),
            pltpu.VMEM((2, half, width), F32),
            pltpu.SemaphoreType.DMA((6,)),
        ]
        + [held for one in programs for held in one.scratch()],
        compiler_params=kernel_params(number),
        cost_estimate=SMALL,
    )(
        grad_query,
        grad_part,
        first_all,
        stream,
        normed,
        vectors,
        grad_middle,
        mlp_sum if cuts else from_line_order(mlp_sum),
        middle,
        early,
        cut_b,
    )


def body(
    hidden_in,
    block_order,
    attn_norm_gain,
    attn_norm_bias,
    query_weight,
    query_bias,
    keyval_weight,
    value_bias,
    proj_weight,
    proj_bias,
    mlp_norm_gain,
    mlp_norm_bias,
    up_weight,
    up_bias,
    down_weight,
    down_bias,
    out_cotangent,
):
    rows_dev = hidden_in.shape[0]
    half_rows = rows_dev // 2
    width = hidden_in.shape[1]
    blocks_dev = rows_dev // BLK
    slot_count = block_order.shape[1]
    group_blocks = PBLK + CONTS
    heads_dev = query_bias.shape[0] // HD
    head_width = heads_dev * HD
    core = lax.axis_index("tp")
    quarter = lax.axis_index("fsdp") * lax.axis_size("pair") + lax.axis_index("pair")
    quarters = lax.axis_size("fsdp") * lax.axis_size("pair")
    hidden_dev = up_weight.shape[1] // quarters

    def own_half(values):
        return lax.dynamic_slice_in_dim(values, core * half_rows, half_rows, axis=0)

    def in_order(mine, other, axis=0):
        first = jnp.where(core == 0, mine, other)
        second = jnp.where(core == 0, other, mine)
        return jnp.concatenate([first, second], axis=axis)


    slot_ids = jnp.arange(slot_count, dtype=jnp.int32)
    ordering = block_order[0]
    inverse = jnp.sum(
        jnp.where(ordering[None, :] == slot_ids[:, None], slot_ids[None, :], 0), axis=1
    )
    ctx_index = lax.axis_index("line") * lax.axis_size("pair") + lax.axis_index("pair")
    first_slot = ctx_index * blocks_dev
    my_slots = first_slot + jnp.arange(blocks_dev, dtype=jnp.int32)
    my_blocks = lax.dynamic_slice_in_dim(ordering, first_slot, blocks_dev)
    positions = my_blocks % group_blocks
    group_base = my_blocks // group_blocks * group_blocks
    prompt_slots = jnp.take(
        inverse, group_base[:, None] + jnp.arange(PBLK, dtype=jnp.int32)[None, :]
    )
    key_slots = jnp.concatenate([prompt_slots, my_slots[:, None]], axis=1)

    vectors = [
        attn_norm_gain,
        attn_norm_bias,
        proj_bias,
        mlp_norm_gain,
        mlp_norm_bias,
        down_bias,
    ]
    vectors = jnp.stack(vectors + [jnp.zeros_like(down_bias)] * 2).astype(F32)

    keyval_cut = lax.dynamic_slice_in_dim(keyval_weight, core * HD, HD, axis=1)
    first_cut = jnp.concatenate([query_weight, keyval_cut], axis=1)
    shard_rows = down_weight.shape[0]
    hidden_half = hidden_dev // 2
    columns = down_weight.shape[1]
    first_rows = shard_rows // 2
    early_rows = shard_rows // 2
    cuts = line_cuts(width, False)
    lines = lax.axis_size("line")
    first_pieces = [(0, slice(0, first_rows), 0)]
    other_pieces = [(0, slice(first_rows, shard_rows), 0)]
    early_pieces = [(1, slice(0, shard_rows), 0), (0, slice(0, early_rows), 1)]
    late_pieces = [(0, slice(early_rows, shard_rows), 1), (1, slice(0, shard_rows), 1)]
    hops = [0.1 * k for k in range(1, 4)] if lines == 4 else spaced(0.1, 0.3, lines - 1)
    levels = spaced(0.4, 0.98, 2 * lines)
    piece_hops = spaced(0.35, 0.75, lines - 1)
    _, first_all, other_cut, early_cut, late_cut, mlp_piece, normed_one, cotangent_line, proj_line = run_programs(
        [
            placed(spread_halves(first_pieces, columns, BF16), 0.0, 0.05),
            placed(rows_gather(first_cut), 0.01, *hops, *levels, 1.0),
            placed(spread_halves(other_pieces, columns, BF16), 0.06, 1.0),
            placed(spread_halves(early_pieces, columns, BF16), 0.06, 1.0),
            placed(spread_halves(late_pieces, columns, BF16), 0.061, 1.0),
            placed(line_gather((quarters, first_rows, hidden_half), BF16), 0.07, *piece_hops, 1.0),
            placed(Work(norm_work, hidden_in.shape, BF16), 0.31, 0.31),
            placed(Work(functools.partial(reorder_work, cuts or [0]), (half_rows, width), BF16), 0.32, 0.32),
            placed(line_gather(proj_weight.shape, BF16), 0.305, *spaced(0.48, 0.88, lines - 1), 1.0),
        ],
        [
            lambda more, outs: more[3:5],
            lambda more, outs: more[5],
            lambda more, outs: more[3:5],
            lambda more, outs: more[3:5],
            lambda more, outs: more[3:5],
            lambda more, outs: outs[0],
            lambda more, outs: more[:2],
            lambda more, outs: more[2],
            lambda more, outs: more[6],
        ],
        1,
        near=[hidden_in, vectors, out_cotangent],
        far=[down_weight, up_weight, first_cut, proj_weight],
    )
    if cuts is None:
        cotangent_line = to_line_order(own_half(out_cotangent))
    first_all = flat(first_all)

    value_shift = jnp.where(core == 1, value_bias.astype(F32), 0.0)
    first_shift = jnp.concatenate([query_bias.astype(F32), value_shift])
    part_like = (rows_dev, HD)
    head_half = head_width // 2
    half_line = jax.ShapeDtypeStruct((lines, shard_rows, head_half), BF16)
    _, query_low, keyval_every, mlp_other, proj_a = run_programs(
        [
            placed(Work(part_work, part_like, BF16), 0.0, 0.0),
            placed(Work(query_work, (rows_dev, head_width), BF16), 0.2, 0.2),
            placed(ctx_gather(part_like, BF16), 0.1, *spaced(0.25, 0.5, lines - 1), *spaced(0.52, 0.9, 2 * lines), 1.0),
            placed(
                line_gather((quarters, shard_rows - first_rows, hidden_half), BF16),
                0.11,
                *spaced(0.3, 0.62, lines - 1),
                1.0,
            ),
            placed(columns_gather(half_line), 0.001, 0.45, 0.85, 1.0),
        ],
        [
            lambda more, outs: more[:3],
            lambda more, outs: more[:3],
            lambda more, outs: outs[0],
            lambda more, outs: more[3],
            lambda more, outs: more[4].at[:, :, :head_half],
        ],
        4,
        near=[normed_one, first_all, first_shift[None]],
        far=[other_cut, proj_line],
    )
    keyval_every, early_cut = lax.optimization_barrier((keyval_every, early_cut))
    mlp_early = lax.all_gather(early_cut, "line", axis=0, tiled=False)
    table = keyval_every.reshape(2, slot_count, BLK, HD)
    mixed_low, logsums, (proj_b, cotangent_all) = attend(
        query_low,
        table,
        positions,
        key_slots,
        [
            placed(columns_gather(half_line), 0.0, 0.9, 1.0, 1.0),
            placed(plane_gather(cotangent_line), 0.0, 0.9, 1.0, 1.0),
        ],
        [proj_line[:, :, head_half:], cotangent_line],
        2,
    )
    proj_a, proj_b = flat(proj_a), flat(proj_b)
    mixed_low, mlp_early, late_cut = lax.optimization_barrier((mixed_low, mlp_early, late_cut))
    mlp_late = lax.all_gather(late_cut, "line", axis=0, tiled=False)
    middle, normed_two_line = project(
        mixed_low, proj_a, proj_b, hidden_in, vectors, 5
    )

    up_shift = lax.dynamic_slice_in_dim(up_bias, quarter * hidden_dev, hidden_dev).astype(F32)
    up_shift = up_shift[None]
    rows_all, act_a, pre_a, back_a, bias_a, weight_grad_a = forward_products(
        normed_two_line, cotangent_all, mlp_piece, mlp_other, mlp_early, up_shift[:, :hidden_half], 6
    )
    rows_all, act_a, pre_a, back_a = flat(rows_all), flat(act_a), flat(pre_a), flat(back_a)
    cotangent_all = flat(cotangent_all)
    cut_a = lax.psum_scatter(weight_grad_a, "line", scatter_dimension=0, tiled=True)
    rows_all, weight_grad_a = lax.optimization_barrier((rows_all, weight_grad_a))
    down_part, weight_grad_b, bias_b, grad_normed_two = second_products(
        rows_all,
        cotangent_all,
        back_a,
        act_a,
        (mlp_piece, mlp_other, mlp_early, mlp_late),
        up_shift[:, hidden_half:],
        7,
    )
    cut_b = lax.psum_scatter(weight_grad_b, "line", scatter_dimension=0, tiled=True)
    cut_a = cut_a.reshape(quarters, 2 * shard_rows, hidden_half)
    cut_b = cut_b.reshape(quarters, 2 * shard_rows, hidden_half)

    grad_middle, grad_mixed, proj_weight_grad, vector = middle_back(
        grad_normed_two, middle, out_cotangent, mixed_low, proj_a, proj_b, vectors, bias_a, bias_b, 8
    )
    grad_mixed, cut_a = lax.optimization_barrier((grad_mixed, cut_a))
    sum_proj, proj_parts = rows_sum(proj_weight_grad)
    sum_down, down_parts = plane_sum(down_part)
    grad_query, grad_sets, query_weight_grad, (grad_proj_weight, mlp_out) = attend_back(
        query_low,
        grad_mixed,
        mixed_low,
        logsums,
        table,
        normed_one,
        positions,
        key_slots,
        [
            placed(sum_proj, 0.0, *spaced(0.13, 0.51, lines), 0.63, 1.06),
            placed(sum_down, 0.0, 0.45, 0.45, 0.45, 0.45, 0.76, 0.95, 1.1, 1.2),
        ],
        [proj_parts, down_parts],
        3,
    )
    grad_table = by_slot(grad_sets, key_slots, slot_count)
    grad_parts = grad_table.reshape(2, lines, 2 * rows_dev, HD)
    along_line, over_pair = ctx_sums(grad_parts)
    sum_query, query_parts = rows_sum(query_weight_grad)
    _, grad_part, grad_query_weight, mlp_grad_a = run_programs(
        [
            placed(along_line, 0.01, 0.75),
            placed(over_pair, 0.76, 0.86, 0.97),
            placed(sum_query, 0.0, 1.0),
            placed(return_half(cut_a, BF16), 0.02, 1.0),
        ],
        [
            grad_parts,
            lambda more, outs: outs[0].reshape(2, rows_dev, HD),
            query_parts,
            cut_a,
        ],
        12,
    )
    input_grad, layer_out, mlp_grad_b, grad_part_weight, summed = first_back(
        grad_query,
        grad_part,
        first_all,
        hidden_in,
        normed_one,
        vectors,
        grad_middle,
        mlp_out,
        middle,
        vector,
        cut_b,
        9,
    )
    grad_down_weight, grad_up_weight = widen(mlp_grad_a, mlp_grad_b)
    grad_keyval_weight = in_order(grad_part_weight[:, :HD], grad_part_weight[:, HD:], axis=1)
    sum_up = summed[:quarters, width : 2 * width - head_width].reshape(quarters * hidden_dev)
    return (
        layer_out,
        input_grad,
        summed[0, :width],
        summed[1, :width],
        grad_query_weight,
        summed[6, :head_width],
        grad_keyval_weight,
        summed[7, :HD],
        grad_proj_weight,
        summed[4, :width],
        summed[2, :width],
        summed[3, :width],
        grad_up_weight,
        sum_up,
        grad_down_weight,
        summed[5, :width],
    )


def solution(mesh):
    fsdp, ctx, tp = mesh.devices.shape
    grid = Mesh(mesh.devices.reshape(fsdp, ctx // 2, 2, tp), EVERY)
    by_rows = P(ROWS, None)
    by_both = P(ROWS, "tp")
    return jax.shard_map(
        body,
        mesh=grid,
        in_specs=(
            by_rows,
            P("fsdp", None),
            P(),
            P(),
            by_both,
            P("tp"),
            by_rows,
            P(),
            by_both,
            P(),
            P(),
            P(),
            by_both,
            P("tp"),
            by_both,
            P(),
            by_rows,
        ),
        out_specs=(
            by_rows,
            by_rows,
            P(),
            P(),
            by_both,
            P("tp"),
            by_rows,
            P(),
            by_both,
            P(),
            P(),
            P(),
            by_both,
            P("tp"),
            by_both,
            P(),
        ),
        check_vma=False,
    )
```
